32 devices in a mesh: groups: 2 (over x), slab: 8 (over z, y), dom: 2 (over core).
Axes of the slice: x: 2, y: 2, z: 4, core: 2. Of those that a mesh axis runs over, the one named last changes fastest.
Arguments:
- volume: bfloat16 [524288, 128], P(('groups', 'slab')), parts along dimension 0, may hold values from -6 to 6
- kernels: bfloat16 [4, 128, 128], replicated, may hold values from -0.5 to 0.5
- images: bfloat16 [256, 1024, 128], P(('groups', 'slab', 'dom')), parts along dimension 0, may hold values from -6 to 6
- owners: int32 [256, 1024, 1], P(('groups', 'slab', 'dom')), parts along dimension 0, may hold values from 0 to 7; in each aligned block of 8192 rows (0 to 8191, 8192 to 16383, ..., all dimensions but the last counted through in order) at most 2048 rows name the same one
- local_block: int32 [256, 1024], P(('groups', 'slab', 'dom')), parts along dimension 0, may hold values from 0 to 32767
- kinds: int32 [256, 1024], P(('groups', 'slab', 'dom')), parts along dimension 0, may hold values from 0 to 3
- counts: int32 [256], P(('groups', 'slab', 'dom')), parts along dimension 0, may hold values from 512 to 1024
- ctf_code: int32 [256], P(('groups', 'slab', 'dom')), parts along dimension 0, may hold values from 0 to 63
- ctf_table: float32 [64, 2], replicated, may hold values from 5 to 40
- scales: bfloat16 [256], P(('groups', 'slab', 'dom')), parts along dimension 0, may hold values from 0.5 to 2
Outputs:
- gradient_field: float32 [2, 512, 256, 256], P(None, ('groups', 'dom'), 'slab'), parts along dimension 1
- losses: float32 [256], P(('groups', 'slab', 'dom')), parts along dimension 0
The draws below stay inside these ranges and needn't reach their ends.
There are 2 independent parts, one for each index of `groups`. The reference program is written for one: setup_inputs(seed, part) draws one part's arguments, and reference() takes and returns one part's arrays. A program takes and returns all parts, laid end to end along the dimension named above; an argument that names none is the same for every part. Nothing has to cross between parts.
Inputs may be any that keep to these rules, and one draw needn't show every extreme that they name: `owners`: in the rows of one device (aligned blocks of 8192 entries) no slab is named more than 2048 times, a bound that some block reaches.
All inputs are finite; a program needn't handle non-finite values.
Results may differ from the reference program's by a relative error of at most 0.0023.
Values may be sent and summed in bfloat16 or wider, within the bound.
No kernel may reach another device: no remote copies, remote signals or barrier semaphores. Data moves between devices by JAX's collectives and lax.ppermute only.
A program may use at most 320 MiB of HBM per device.

```python
import math
import jax
import jax.numpy as jnp
import numpy as np
from jax import lax

SIDE = 256
P_DEV = 8
NK = 4
NCTF = 64
BLK = 1024
PARTICLES = 128
NBLOCKS = 262144
SLAB_BLOCKS = 32768
CAP = 2048
N_SLAB = 8


def with_ends(result, own_key, low, largest):
    spot = [jax.random.randint(jax.random.fold_in(own_key, axis), (), 0, length) for axis, length in enumerate(result.shape)]
    longest = result.shape.index(max(result.shape))
    beside = spot[:longest] + [(spot[longest] + 1) % result.shape[longest]] + spot[longest + 1:]
    return result.at[tuple(spot)].set(low).at[tuple(beside)].set(largest)


def level_of(own_key, dims, split, low, largest):
    level, own = 1.0, jax.random.fold_in(own_key, 6)
    for axis_at, shards_of in split:
        draws = jnp.exp(jax.random.uniform(jax.random.fold_in(own, axis_at), (shards_of,), jnp.float32, low / len(split), largest / len(split)))
        level = level * jnp.repeat(draws, dims[axis_at] // shards_of).reshape([-1 if axis == axis_at else 1 for axis in range(len(dims))])
    return level


def routed_block(rng, own, number, rows, number_of, top, bound, skew):
    sequence = jax.random.permutation(rng, number_of)
    crowded, ordinary = shares(number_of, rows * top, bound, skew, True), shares(number_of, rows * top, bound, skew, False)
    places = jnp.arange(number_of)

    def named(lengths, offset_by):
        used = int((lengths > 0).sum())
        fixed = max(1, used // 4)
        passed = fixed + (places - fixed + offset_by * (used - fixed)) % max(1, number_of - fixed)
        return jnp.zeros((number_of,), jnp.int32).at[sequence[jnp.where(places < fixed, places, passed)]].set(jnp.asarray(lengths, jnp.int32))

    lengths = jnp.where(number % 4 == 0, named(crowded, number // 4), named(ordinary, number - number // 4 - 1))
    mixed = jax.random.permutation(jax.random.fold_in(own, 3), number_of)
    donor, sink = mixed[0:number_of // 2 * 2:2], mixed[1:number_of // 2 * 2:2]
    room = jnp.minimum(lengths[donor] - 1, bound - lengths[sink]) // 2
    room = jnp.where((donor == sequence[0]) | (sink == sequence[0]) | (lengths[sink] == 0), 0, jnp.maximum(room, 0))
    passed = jax.random.randint(jax.random.fold_in(own, 4), (number_of // 2,), 0, 1 << 20) % (room + 1)
    lengths = lengths.at[donor].add(-passed).at[sink].add(passed)
    members = jnp.searchsorted(jnp.cumsum(lengths), jnp.arange(rows * top), side="right").astype(jnp.int32)
    table = members.reshape(top, rows).T
    table = table[jax.random.permutation(jax.random.fold_in(own, 1), rows)]
    offset_by = jax.random.randint(jax.random.fold_in(own, 2), (rows, 1), 0, top)
    return jnp.take_along_axis(table, (jnp.arange(top)[None, :] + offset_by) % top, axis=1)


def shares(count, total, most, slope, full):
    loads = [(1 << 20) // math.isqrt(standing ** slope) + 1 for standing in range(1, count + 1)]
    largest = most if full else min(most, max(-(-total // count), total * loads[0] // sum(loads)))
    least = 1 if total - largest >= count - 1 else 0
    given, surplus = [largest] + [least] * (count - 1), total - largest - least * (count - 1)
    while surplus > 0:
        free = [i for i in range(1, count) if given[i] < largest] or [i for i in range(1, count) if given[i] < most]
        mass, left = sum([loads[i] for i in free]), surplus
        for i in free:
            addition = min(most - given[i], max(1, left * loads[i] // mass), surplus)
            given[i] = given[i] + addition
            surplus = surplus - addition
    return np.array(given)


def bell_draw(own_key, shape, scale, limit, cuts=(), held_as=jnp.bfloat16):
    entries = jax.random.normal(own_key, shape, jnp.float32) * scale
    if len(cuts) > 0:
        entries = level_of(own_key, shape, cuts, -0.22, 0.18) * entries
    return jnp.clip(entries, min=-limit, max=limit).astype(held_as)


def setup_inputs(seed: int = 0, part: int = 0) -> dict:
    arg_keys = jax.random.split(jax.random.key(seed), 11)
    part_keys = jax.random.split(jax.random.fold_in(arg_keys[10], part), 11)
    volume = bell_draw(part_keys[0], (NBLOCKS, 128), 1.0, 6.0, ((0, 8),))
    kernels = bell_draw(arg_keys[1], (NK, 128, 128), 128 ** -0.5, 0.5)
    images = bell_draw(part_keys[2], (PARTICLES, BLK, 128), 1.0, 6.0, ((0, 16),))
    owners_keys = jax.random.split(jax.random.fold_in(part_keys[3], 1), PARTICLES * BLK // (P_DEV * BLK))
    owners_turns = jax.random.permutation(jax.random.fold_in(part_keys[3], 3), PARTICLES * BLK // (P_DEV * BLK))
    owners = jax.vmap(lambda own, number: routed_block(jax.random.fold_in(part_keys[3], 2), own, number, P_DEV * BLK, N_SLAB, 1, CAP, 2))(owners_keys, owners_turns).reshape((PARTICLES, BLK, 1))
    local_block = with_ends(jax.random.randint(part_keys[4], (PARTICLES, BLK), 0, SLAB_BLOCKS), jax.random.fold_in(part_keys[4], 1), 0, SLAB_BLOCKS - 1).astype(jnp.int32)
    kinds = with_ends(jax.random.randint(part_keys[5], (PARTICLES, BLK), 0, NK), jax.random.fold_in(part_keys[5], 1), 0, NK - 1).astype(jnp.int32)
    counts = with_ends(jax.random.randint(part_keys[6], (PARTICLES,), BLK // 2, BLK + 1), jax.random.fold_in(part_keys[6], 1), BLK // 2, BLK).astype(jnp.int32)
    ctf_code = with_ends(jax.random.randint(part_keys[7], (PARTICLES,), 0, NCTF), jax.random.fold_in(part_keys[7], 1), 0, NCTF - 1).astype(jnp.int32)
    ctf_table = jnp.clip(jax.random.uniform(arg_keys[8], (NCTF, 2), jnp.float32, 5.0, 40.0), 5.0, 40.0)
    scales = jnp.clip(jnp.exp(math.log(2.0) - 1.3862944 * jax.random.uniform(part_keys[9], (PARTICLES,), jnp.float32) ** level_of(part_keys[9], (PARTICLES,), ((0, 16),), -0.2, 0.2)), 0.5, 2.0).astype(jnp.bfloat16)
    return {"volume": volume, "kernels": kernels, "images": images, "owners": owners, "local_block": local_block, "kinds": kinds, "counts": counts, "ctf_code": ctf_code, "ctf_table": ctf_table, "scales": scales}


def pixel_factor(block_pos, scaling, defocus, phase_shift, side_cells):
    per_row = side_cells // 8
    offsets = jnp.arange(64, dtype=jnp.int32)
    vert_pos = (block_pos // per_row)[:, None] * 8 + offsets[None, :] // 8
    horiz_pos = (block_pos % per_row)[:, None] * 8 + offsets[None, :] % 8
    freq_vert = (vert_pos - side_cells // 2).astype(jnp.float32)
    freq_horiz = (horiz_pos - side_cells // 2).astype(jnp.float32)
    radius = (freq_vert * freq_vert + freq_horiz * freq_horiz) / float((side_cells // 2) ** 2)
    factor = scaling[:, None] * jnp.sin(defocus[:, None] * radius + phase_shift[:, None])
    return jnp.concatenate([factor, factor], axis=1)


def block_terms(voxel_rows, pictures, kind_ids, factor, live_mask, kernels):
    kind_count = kernels.shape[0]
    breadth = kernels.shape[1]
    select = (kind_ids[:, None] == jnp.arange(kind_count, dtype=jnp.int32)[None, :]).astype(jnp.bfloat16)
    spread = (select[:, :, None] * voxel_rows[:, None, :]).reshape(-1, kind_count * breadth)
    forward = kernels.reshape(kind_count * breadth, breadth)
    extracted = jnp.dot(spread, forward, preferred_element_type=jnp.float32)
    misfit = jnp.where(live_mask[:, None], factor * extracted - pictures.astype(jnp.float32), 0.0)
    weighted = (factor * misfit).astype(jnp.bfloat16)
    spread_back = (select[:, :, None] * weighted[:, None, :]).reshape(-1, kind_count * breadth)
    backward = jnp.transpose(kernels, (0, 2, 1)).reshape(kind_count * breadth, breadth)
    grad_terms = jnp.dot(spread_back, backward, preferred_element_type=jnp.float32)
    return grad_terms, jnp.sum(misfit * misfit, axis=1)


def reference(volume, kernels, images, owners, local_block, kinds, counts, ctf_code, ctf_table, scales):
    per_row = SIDE // 8
    block_lists = owners[:, :, 0] * SLAB_BLOCKS + local_block
    positions = jnp.arange(BLK, dtype=jnp.int32)

    def visit(carried, record):
        block_list, pictures, kind_ids, live_count, ctf_index, scaling = record
        voxel_rows = volume[block_list]
        table_row = ctf_table[ctf_index]
        factor = pixel_factor(positions, jnp.zeros((BLK,), jnp.float32) + scaling.astype(jnp.float32),
                              jnp.zeros((BLK,), jnp.float32) + table_row[0],
                              jnp.zeros((BLK,), jnp.float32) + table_row[1], SIDE)
        live_mask = positions < live_count
        grad_terms, squares = block_terms(voxel_rows, pictures, kind_ids, factor, live_mask, kernels)
        carried = carried.at[block_list].add(grad_terms)
        return carried, jnp.sum(squares) / (live_count.astype(jnp.float32) * 128.0)

    carried, losses = lax.scan(visit, jnp.zeros((NBLOCKS, 128), jnp.float32),
                               (block_lists, images, kinds, counts, ctf_code, scales))
    grid = carried.reshape(SIDE, per_row, per_row, 2, 8, 8).transpose(3, 0, 1, 4, 2, 5).reshape(2, SIDE, SIDE, SIDE)
    field = jnp.fft.ifftn(grid[0] + 1j * grid[1], norm="ortho")
    gradient_field = jnp.stack([jnp.real(field), jnp.imag(field)]).astype(jnp.float32)
    return gradient_field, losses
```

```python
import functools
import math

import jax
import jax.numpy as jnp
from jax import lax
from jax.experimental import pallas as pl
from jax.experimental.pallas import tpu as pltpu
from jax.sharding import PartitionSpec as P

HIGHEST = lax.Precision.HIGHEST
LANES = 128
GROUP = 8
VMEM_LIMIT = 56 * 1024 * 1024

SMEM_SPEC = pl.BlockSpec(memory_space=pltpu.SMEM)
VMEM_SPEC = pl.BlockSpec(memory_space=pltpu.VMEM)
ANY_SPEC = pl.BlockSpec(memory_space=pl.ANY)


def params(**extra):
    return pltpu.CompilerParams(vmem_limit_bytes=VMEM_LIMIT, **extra)


def bits_of(count):
    return (count - 1).bit_length()


def route_kernel(slabs, cap, local_bits, list_length, owner_ref, local_ref, kind_ref, counts_ref, target_ref, word_ref, totals_ref):
    rows = owner_ref.shape[0]
    rows_each = list_length // LANES
    particles = rows // rows_each
    row_id = lax.broadcasted_iota(jnp.int32, (rows, LANES), 0)
    lane_id = lax.broadcasted_iota(jnp.int32, (rows, LANES), 1)
    particle = row_id // rows_each
    position = (row_id % rows_each) * LANES + lane_id
    limit = jnp.zeros((rows, LANES), jnp.int32)
    for i in range(particles):
        limit = jnp.where(particle == i, counts_ref[i], limit)
    owner = jnp.where(position < limit, owner_ref[...], -1)
    up_to = (
        lax.broadcasted_iota(jnp.int32, (LANES, LANES), 0)
        <= lax.broadcasted_iota(jnp.int32, (LANES, LANES), 1)
    ).astype(jnp.bfloat16)
    ones = jnp.ones((LANES, LANES), jnp.bfloat16)
    before = (
        lax.broadcasted_iota(jnp.int32, (rows, rows), 1)
        < lax.broadcasted_iota(jnp.int32, (rows, rows), 0)
    ).astype(jnp.bfloat16)

    def one_slab(slab, target):
        mine = owner == slab
        hits = mine.astype(jnp.float32).astype(jnp.bfloat16)
        inside = jnp.dot(hits, up_to, preferred_element_type=jnp.float32)
        row_sum = jnp.dot(hits, ones, preferred_element_type=jnp.float32)
        above = jnp.dot(before, row_sum.astype(jnp.bfloat16), preferred_element_type=jnp.float32)
        rank = (inside + above).astype(jnp.int32) - 1
        total = (above[rows - 1:rows, :] + row_sum[rows - 1:rows, :]).astype(jnp.int32)
        totals_ref[pl.ds(slab, 1), :] = total
        return jnp.where(mine, slab * cap + rank, target)

    target = lax.fori_loop(0, slabs, one_slab, jnp.full((rows, LANES), slabs * cap, jnp.int32))
    target_ref[...] = target
    kind_bits = local_bits
    word = local_ref[...] | (kind_ref[...] << kind_bits) | (position << (kind_bits + 2))
    word_ref[...] = word | (particle << (kind_bits + 2 + bits_of(list_length)))


def pack_kernel(slots, target_ref, word_ref, image_ref, out_ref, meta_ref, wide_ref, staged_ref):
    entries = image_ref.shape[0]
    step = 256

    @pl.loop(0, entries // step)
    def _(i):
        at = pl.multiple_of(i * step, step)
        wide_ref[pl.ds(at, step), :] = image_ref[pl.ds(at, step), :].astype(jnp.float32)

    @pl.loop(0, entries // 16)
    def _(i):
        first = i * 16
        targets = [target_ref[first + j] for j in range(16)]
        rows = [wide_ref[pl.ds(first + j, 1), :] for j in range(16)]
        for j in range(16):
            staged_ref[pl.ds(targets[j], 1), :] = rows[j]
        for j in range(16):
            meta_ref[targets[j]] = word_ref[first + j]

    @pl.loop(0, slots // step)
    def _(i):
        at = pl.multiple_of(i * step, step)
        out_ref[pl.ds(at, step), :] = staged_ref[pl.ds(at, step), :].astype(jnp.bfloat16)


def decode_kernel(local_bits, dummy, word_ref, live_ref, index_ref):
    rows = word_ref.shape[0]
    live = live_ref[...] != 0
    index = jnp.where(live, word_ref[...] & ((1 << local_bits) - 1), dummy)
    lane = lax.broadcasted_iota(jnp.int32, (rows, LANES), 1)
    clash = jnp.zeros((rows, LANES), jnp.int32)
    for shift in range(1, GROUP):
        earlier = pltpu.roll(index, shift, 1)
        same = (earlier == index) & (lane % GROUP >= shift) & live
        clash = clash | same.astype(jnp.int32)
    shift = 1
    while shift < GROUP:
        clash = clash | pltpu.roll(clash, LANES - shift, 1)
        shift *= 2
    index_ref[...] = index | (clash << 24)


def gather_kernel(slabs, cap, index_ref, totals_ref, volume_ref, out_ref, wide_ref, staged_ref):
    blocks = volume_ref.shape[0]
    step = 256

    @pl.loop(0, blocks // step)
    def _(i):
        at = pl.multiple_of(i * step, step)
        wide_ref[pl.ds(at, step), :] = volume_ref[pl.ds(at, step), :].astype(jnp.float32)

    @pl.loop(0, slabs)
    def _(source):
        live = totals_ref[source]

        @pl.loop(0, (live + 15) // 16)
        def _(i):
            first = source * cap + i * 16
            places = [index_ref[first + j] & 0xFFFFFF for j in range(16)]
            rows = [wide_ref[pl.ds(places[j], 1), :] for j in range(16)]
            for j in range(16):
                staged_ref[pl.ds(i * 16 + j, 1), :] = rows[j]

        width = min(step, cap)

        @pl.loop(0, (live + width - 1) // width)
        def _(i):
            at = pl.multiple_of(i * width, width)
            to = pl.multiple_of(source * cap + i * width, width)
            out_ref[pl.ds(to, width), :] = staged_ref[pl.ds(at, width), :].astype(jnp.bfloat16)


def sine(angle):
    turns = jnp.floor(angle * (1.0 / math.pi) + 0.5)
    rest = angle - turns * 3.140625
    rest = rest - turns * 9.67502593994140625e-4
    rest = rest - turns * 1.509957990978376e-7
    odd = turns - 2.0 * jnp.floor(turns * 0.5)
    square = rest * rest
    poly = 2.718121e-6
    poly = poly * square - 1.9839334e-4
    poly = poly * square + 8.3333293e-3
    poly = poly * square - 1.6666667e-1
    value = rest + rest * square * poly
    return value * (1.0 - 2.0 * odd)


def slab_kernel(
    side, local_bits, list_length, particles, tile,
    totals_ref, defocus_ref, phase_ref, scale_ref, index_ref,
    word_ref, voxel_ref, image_ref, forward_ref, backward_ref, unit_ref,
    grad_ref, square_ref,
    sum_ref, staged_ref, sem,
):
    source = pl.program_id(0)
    cap = word_ref.shape[2]
    blocks = grad_ref.shape[0]
    features = image_ref.shape[2]
    kinds = forward_ref.shape[0] // features
    position_bits = bits_of(list_length)
    per_row = side // 8
    live = totals_ref[source]

    @pl.when(source == 0)
    def _():
        @pl.loop(0, blocks // 256)
        def _(i):
            at = pl.multiple_of(i * 256, 256)
            sum_ref[pl.ds(at, 256), :] = jnp.zeros((256, features), jnp.float32)

    square_ref[...] = jnp.zeros_like(square_ref)

    @pl.loop(0, (live + tile - 1) // tile)
    def _(t):
        at = pl.multiple_of(t * tile, tile)
        word = word_ref[0, :, pl.ds(at, tile)]
        kind = (word >> local_bits) & 3
        position = (word >> (local_bits + 2)) & (list_length - 1)
        particle = (word >> (local_bits + 2 + position_bits)) & (particles - 1)
        valid = lax.broadcasted_iota(jnp.int32, (1, tile), 1) + at < live
        defocus = jnp.zeros((1, tile), jnp.float32)
        phase = jnp.zeros((1, tile), jnp.float32)
        scale = jnp.zeros((1, tile), jnp.float32)
        for j in range(particles):
            chosen = particle == j
            defocus = jnp.where(chosen, defocus_ref[source * particles + j], defocus)
            phase = jnp.where(chosen, phase_ref[source * particles + j], phase)
            scale = jnp.where(chosen, scale_ref[source * particles + j], scale)
        half = features // 2
        cell = lax.broadcasted_iota(jnp.int32, (half, tile), 0)
        vert = ((position // per_row) * 8 + cell // 8 - side // 2).astype(jnp.float32)
        horiz = ((position % per_row) * 8 + cell % 8 - side // 2).astype(jnp.float32)
        radius = (vert * vert + horiz * horiz) * (1.0 / float((side // 2) ** 2))
        factor = scale * sine(defocus * radius + phase)
        factor = jnp.concatenate([factor, factor], axis=0)
        contract_last = (((1,), (1,)), ((), ()))
        each_kind = lax.dot_general(
            forward_ref[...], voxel_ref[0, pl.ds(at, tile), :], contract_last,
            preferred_element_type=jnp.float32,
        )
        extracted = each_kind[0:features, :]
        for k in range(1, kinds):
            extracted = jnp.where(kind == k, each_kind[k * features:(k + 1) * features, :], extracted)
        picture = lax.dot_general(
            unit_ref[...], image_ref[0, pl.ds(at, tile), :], contract_last,
            preferred_element_type=jnp.float32,
        )
        misfit = jnp.where(valid, factor * extracted - picture, 0.0)
        squares = jnp.sum(misfit * misfit, axis=0, keepdims=True)
        which = lax.broadcasted_iota(jnp.int32, (particles, tile), 0)
        spread = jnp.where(valid & (particle == which), squares, 0.0)
        folded = spread[:, 0:LANES]
        for i in range(1, tile // LANES):
            folded = folded + spread[:, i * LANES:(i + 1) * LANES]
        square_ref[0] = square_ref[0] + folded
        weighted = (factor * misfit).astype(jnp.bfloat16)
        none = jnp.zeros_like(weighted)
        spread_back = jnp.concatenate(
            [jnp.where(kind == k, weighted, none) for k in range(kinds)], axis=0
        )
        terms = jnp.dot(backward_ref[...], spread_back, preferred_element_type=jnp.float32)
        staged_ref[...] = terms.T

        @pl.loop(0, (jnp.minimum(live - at, tile) + GROUP - 1) // GROUP)
        def _(g):
            base = source * cap + at + g * GROUP
            marked = index_ref[base]
            places = [index_ref[base + j] & 0xFFFFFF for j in range(GROUP)]

            @pl.when(marked < (1 << 24))
            def _():
                held = [sum_ref[pl.ds(places[j], 1), :] for j in range(GROUP)]
                new = [staged_ref[pl.ds(g * GROUP + j, 1), :] for j in range(GROUP)]
                for j in range(GROUP):
                    sum_ref[pl.ds(places[j], 1), :] = held[j] + new[j]

            @pl.when(marked >= (1 << 24))
            def _():
                for j in range(GROUP):
                    sum_ref[pl.ds(places[j], 1), :] = (
                        sum_ref[pl.ds(places[j], 1), :] + staged_ref[pl.ds(g * GROUP + j, 1), :]
                    )

    @pl.when(source == pl.num_programs(0) - 1)
    def _():
        copy = pltpu.make_async_copy(sum_ref.at[pl.ds(0, blocks)], grad_ref, sem)
        copy.start()
        copy.wait()


def dft_tables(input_index, side_cells):
    freqs = jnp.arange(side_cells, dtype=jnp.int32)
    product = input_index[:, None] * freqs[None, :] % side_cells
    angles = product.astype(jnp.float32) * (2.0 * math.pi / side_cells)
    norming = 1.0 / math.sqrt(side_cells)
    return (jnp.cos(angles) * norming, jnp.sin(angles) * norming)


def transform(real_part, imag_part, cos_table, sin_table, pattern):
    new_real = jnp.einsum(pattern, real_part, cos_table, precision=HIGHEST) - jnp.einsum(
        pattern, imag_part, sin_table, precision=HIGHEST
    )
    new_imag = jnp.einsum(pattern, real_part, sin_table, precision=HIGHEST) + jnp.einsum(
        pattern, imag_part, cos_table, precision=HIGHEST
    )
    return (new_real, new_imag)


def gradient_of_slab(volume, kernels, images, owners, local_block, kinds, counts, ctf_code, ctf_table, scales):
    slabs = lax.axis_size("slab")
    particles, list_length, features = images.shape
    side = math.isqrt(list_length * 64)
    entries = particles * list_length
    cap = 2 * entries // slabs
    slots = slabs * cap
    blocks = volume.shape[0]
    local_bits = bits_of(blocks)
    kind_count = kernels.shape[0]
    rows = entries // LANES
    int_rows = jax.ShapeDtypeStruct((rows, LANES), jnp.int32)

    target, word, totals = pl.pallas_call(
        functools.partial(route_kernel, slabs, cap, local_bits, list_length),
        out_shape=(int_rows, int_rows, jax.ShapeDtypeStruct((slabs, LANES), jnp.int32)),
        in_specs=[VMEM_SPEC, VMEM_SPEC, VMEM_SPEC, SMEM_SPEC],
        out_specs=(VMEM_SPEC, VMEM_SPEC, VMEM_SPEC),
        compiler_params=params(),
        name="route",
    )(
        owners.reshape(rows, LANES), local_block.reshape(rows, LANES), kinds.reshape(rows, LANES), counts
    )
    packed, meta = pl.pallas_call(
        functools.partial(pack_kernel, slots),
        out_shape=(
            jax.ShapeDtypeStruct((slots, features), jnp.bfloat16),
            jax.ShapeDtypeStruct((slots + 1024,), jnp.int32),
        ),
        in_specs=[SMEM_SPEC, SMEM_SPEC, VMEM_SPEC],
        out_specs=(VMEM_SPEC, SMEM_SPEC),
        scratch_shapes=[
            pltpu.VMEM((entries, features), jnp.float32),
            pltpu.VMEM((slots + 8, features), jnp.float32),
        ],
        compiler_params=params(),
        name="pack",
    )(target.reshape(entries), word.reshape(entries), images.reshape(entries, features))

    code = ctf_code | ((scales.astype(jnp.float32) * 256.0).astype(jnp.int32) << 8)
    header = jnp.concatenate(
        [
            totals[:, 0:1],
            jnp.broadcast_to(code[None, :], (slabs, particles)),
            jnp.zeros((slabs, LANES - 1 - particles), jnp.int32),
        ],
        axis=1,
    )
    sent = jnp.concatenate([meta[:slots].reshape(slabs, cap), header], axis=1)
    arrived = lax.all_to_all(sent, "slab", split_axis=0, concat_axis=0, tiled=True)
    words = arrived[:, :cap]
    totals_in = arrived[:, cap]
    codes_in = arrived[:, cap + 1:cap + 1 + particles]
    live = (jnp.arange(cap, dtype=jnp.int32)[None, :] < totals_in[:, None]).astype(jnp.int32)
    table_rows = ctf_table[(codes_in & 255).reshape(-1)]
    scale_in = (codes_in >> 8).astype(jnp.float32).reshape(-1) * (1.0 / 256.0)

    pictures = lax.all_to_all(
        packed.reshape(slabs, cap, features), "slab", split_axis=0, concat_axis=0, tiled=True
    )

    index = pl.pallas_call(
        functools.partial(decode_kernel, local_bits, blocks),
        out_shape=jax.ShapeDtypeStruct((slots // LANES, LANES), jnp.int32),
        in_specs=[VMEM_SPEC, VMEM_SPEC],
        out_specs=VMEM_SPEC,
        compiler_params=params(),
        name="decode",
    )(words.reshape(slots // LANES, LANES), live.reshape(slots // LANES, LANES))
    index = index.reshape(slots)
    voxels = pl.pallas_call(
        functools.partial(gather_kernel, slabs, cap),
        out_shape=jax.ShapeDtypeStruct((slots, features), jnp.bfloat16),
        in_specs=[SMEM_SPEC, SMEM_SPEC, VMEM_SPEC],
        out_specs=VMEM_SPEC,
        scratch_shapes=[
            pltpu.VMEM((blocks + 8, features), jnp.float32),
            pltpu.VMEM((cap, features), jnp.float32),
        ],
        compiler_params=params(),
        cost_estimate=pl.CostEstimate(flops=0, bytes_accessed=100 * 1024 * 1024, transcendentals=0),
        name="read_voxels",
    )(index, totals_in, volume)

    forward = jnp.transpose(kernels, (0, 2, 1)).reshape(kind_count * features, features)
    backward = jnp.transpose(kernels, (1, 0, 2)).reshape(features, kind_count * features)
    unit = jnp.eye(features, dtype=jnp.bfloat16)
    tile = min(512, cap)
    per_source = lambda length, width: pl.BlockSpec((1, length, width), lambda s: (s, 0, 0))
    whole = lambda shape: pl.BlockSpec(shape, lambda s: (0,) * len(shape))
    grad, squares = pl.pallas_call(
        functools.partial(slab_kernel, side, local_bits, list_length, particles, tile),
        grid=(slabs,),
        out_shape=(
            jax.ShapeDtypeStruct((blocks, features), jnp.float32),
            jax.ShapeDtypeStruct((slabs, particles, LANES), jnp.float32),
        ),
        in_specs=[SMEM_SPEC] * 5 + [
            per_source(1, cap),
            per_source(cap, features),
            per_source(cap, features),
            whole(forward.shape),
            whole(backward.shape),
            whole(unit.shape),
        ],
        out_specs=(ANY_SPEC, per_source(particles, LANES)),
        scratch_shapes=[
            pltpu.VMEM((blocks + 8, features), jnp.float32),
            pltpu.VMEM((tile, features), jnp.float32),
            pltpu.SemaphoreType.DMA(()),
        ],
        compiler_params=params(),
        name="compare_and_add",
    )(
        totals_in, table_rows[:, 0], table_rows[:, 1], scale_in, index,
        words.reshape(slabs, 1, cap), voxels.reshape(slabs, cap, features), pictures,
        forward, backward, unit,
    )
    returned = lax.all_to_all(
        jnp.sum(squares, axis=2), "slab", split_axis=0, concat_axis=0, tiled=True
    )
    losses = jnp.sum(returned, axis=0) / (counts.astype(jnp.float32) * 128.0)
    return grad, losses, side


def body(*arrays):
    grad, losses, side_cells = gradient_of_slab(*arrays)
    per_row = side_cells // 8
    planes_here = grad.shape[0] // (per_row * per_row)
    grid = grad.reshape(planes_here, per_row, per_row, 2, 8, 8).transpose(3, 0, 1, 4, 2, 5)
    grid = grid.reshape(2, planes_here, side_cells, side_cells)
    cells = jnp.arange(side_cells, dtype=jnp.int32)
    cos_table, sin_table = dft_tables(cells, side_cells)
    halves = lax.psum_scatter(grid, "dom", scatter_dimension=3, tiled=True)
    real_part, imag_part = transform(halves[0], halves[1], cos_table, sin_table, "xyz,yk->xkz")
    pencil = lax.all_to_all(
        jnp.stack([real_part, imag_part]), "slab", split_axis=2, concat_axis=1, tiled=True
    )
    real_part, imag_part = transform(pencil[0], pencil[1], cos_table, sin_table, "xyz,xk->kyz")
    rows = lax.all_to_all(
        jnp.stack([real_part, imag_part]), "dom", split_axis=1, concat_axis=3, tiled=True
    )
    real_part, imag_part = transform(rows[0], rows[1], cos_table, sin_table, "xyz,zk->xyk")
    result = jnp.stack([real_part, imag_part])
    return (result, losses)


def solution(mesh):
    in_specs = (
        P(("groups", "slab"), None),
        P(),
        P(("groups", "slab", "dom"), None, None),
        P(("groups", "slab", "dom"), None, None),
        P(("groups", "slab", "dom"), None),
        P(("groups", "slab", "dom"), None),
        P(("groups", "slab", "dom")),
        P(("groups", "slab", "dom")),
        P(),
        P(("groups", "slab", "dom")),
    )
    out_specs = (P(None, ("groups", "dom"), "slab", None), P(("groups", "slab", "dom")))
    return jax.shard_map(body, mesh=mesh, in_specs=in_specs, out_specs=out_specs, check_vma=False)
```

```python
import functools
import math

import jax
import jax.numpy as jnp
import numpy as np
from jax import lax
from jax.experimental import pallas as pl
from jax.experimental.pallas import tpu as pltpu
from jax.sharding import PartitionSpec as P

LANES = 128
QUADS = 1
GROUP = 8
VMEM_LIMIT = 56 * 1024 * 1024

SMEM_SPEC = pl.BlockSpec(memory_space=pltpu.SMEM)
VMEM_SPEC = pl.BlockSpec(memory_space=pltpu.VMEM)
ANY_SPEC = pl.BlockSpec(memory_space=pl.ANY)


def params(**extra):
    return pltpu.CompilerParams(vmem_limit_bytes=VMEM_LIMIT, **extra)


def bits_of(count):
    return (count - 1).bit_length()


def route_kernel(slabs, cap, local_bits, list_length, owner_ref, local_ref, kind_ref, counts_ref, target_ref, word_ref, totals_ref):
    rows = owner_ref.shape[0]
    rows_each = list_length // LANES
    particles = rows // rows_each
    row_id = lax.broadcasted_iota(jnp.int32, (rows, LANES), 0)
    lane_id = lax.broadcasted_iota(jnp.int32, (rows, LANES), 1)
    particle = row_id // rows_each
    position = (row_id % rows_each) * LANES + lane_id
    limit = jnp.zeros((rows, LANES), jnp.int32)
    for i in range(particles):
        limit = jnp.where(particle == i, counts_ref[i], limit)
    owner = jnp.where(position < limit, owner_ref[...], -1)
    up_to = (
        lax.broadcasted_iota(jnp.int32, (LANES, LANES), 0)
        <= lax.broadcasted_iota(jnp.int32, (LANES, LANES), 1)
    ).astype(jnp.bfloat16)
    ones = jnp.ones((LANES, LANES), jnp.bfloat16)
    before = (
        lax.broadcasted_iota(jnp.int32, (rows, rows), 1)
        < lax.broadcasted_iota(jnp.int32, (rows, rows), 0)
    ).astype(jnp.bfloat16)

    def one_slab(slab, target):
        mine = owner == slab
        hits = mine.astype(jnp.float32).astype(jnp.bfloat16)
        inside = jnp.dot(hits, up_to, preferred_element_type=jnp.float32)
        row_sum = jnp.dot(hits, ones, preferred_element_type=jnp.float32)
        above = jnp.dot(before, row_sum.astype(jnp.bfloat16), preferred_element_type=jnp.float32)
        rank = (inside + above).astype(jnp.int32) - 1
        total = (above[rows - 1:rows, :] + row_sum[rows - 1:rows, :]).astype(jnp.int32)
        totals_ref[pl.ds(slab, 1), :] = total
        return jnp.where(mine, slab * cap + rank, target)

    target = lax.fori_loop(0, slabs, one_slab, jnp.full((rows, LANES), slabs * cap, jnp.int32))
    target_ref[...] = target
    kind_bits = local_bits
    word = local_ref[...] | (kind_ref[...] << kind_bits) | (position << (kind_bits + 2))
    word_ref[...] = word | (particle << (kind_bits + 2 + bits_of(list_length)))


def pack_kernel(slots, target_ref, word_ref, image_ref, out_ref, meta_ref, wide_ref, staged_ref):
    entries = image_ref.shape[0]
    step = 256

    @pl.loop(0, entries // step)
    def _(i):
        at = pl.multiple_of(i * step, step)
        wide_ref[pl.ds(at, step), :] = image_ref[pl.ds(at, step), :].astype(jnp.float32)

    @pl.loop(0, entries // 16)
    def _(i):
        first = i * 16
        targets = [target_ref[first + j] for j in range(16)]
        rows = [wide_ref[pl.ds(first + j, 1), :] for j in range(16)]
        for j in range(16):
            staged_ref[pl.ds(targets[j], 1), :] = rows[j]
        for j in range(16):
            meta_ref[targets[j]] = word_ref[first + j]

    @pl.loop(0, slots // step)
    def _(i):
        at = pl.multiple_of(i * step, step)
        out_ref[pl.ds(at, step), :] = staged_ref[pl.ds(at, step), :].astype(jnp.bfloat16)


def decode_kernel(local_bits, dummy, word_ref, live_ref, index_ref):
    rows = word_ref.shape[0]
    live = live_ref[...] != 0
    index = jnp.where(live, word_ref[...] & ((1 << local_bits) - 1), dummy)
    lane = lax.broadcasted_iota(jnp.int32, (rows, LANES), 1)
    clash = jnp.zeros((rows, LANES), jnp.int32)
    for shift in range(1, GROUP):
        earlier = pltpu.roll(index, shift, 1)
        same = (earlier == index) & (lane % GROUP >= shift) & live
        clash = clash | same.astype(jnp.int32)
    shift = 1
    while shift < GROUP:
        clash = clash | pltpu.roll(clash, LANES - shift, 1)
        shift *= 2
    index_ref[...] = index | (clash << 24)


def gather_kernel(slabs, cap, index_ref, totals_ref, volume_ref, out_ref, wide_ref, staged_ref):
    blocks = volume_ref.shape[0]
    step = 256

    @pl.loop(0, blocks // step)
    def _(i):
        at = pl.multiple_of(i * step, step)
        wide_ref[pl.ds(at, step), :] = volume_ref[pl.ds(at, step), :].astype(jnp.float32)

    @pl.loop(0, slabs)
    def _(source):
        live = totals_ref[source]

        @pl.loop(0, (live + 15) // 16)
        def _(i):
            first = source * cap + i * 16
            places = [index_ref[first + j] & 0xFFFFFF for j in range(16)]
            rows = [wide_ref[pl.ds(places[j], 1), :] for j in range(16)]
            for j in range(16):
                staged_ref[pl.ds(i * 16 + j, 1), :] = rows[j]

        width = min(step, cap)

        @pl.loop(0, (live + width - 1) // width)
        def _(i):
            at = pl.multiple_of(i * width, width)
            to = pl.multiple_of(source * cap + i * width, width)
            out_ref[pl.ds(to, width), :] = staged_ref[pl.ds(at, width), :].astype(jnp.bfloat16)


def sine(angle):
    turns = jnp.floor(angle * (1.0 / math.pi) + 0.5)
    rest = angle - turns * 3.140625
    rest = rest - turns * 9.67502593994140625e-4
    rest = rest - turns * 1.509957990978376e-7
    odd = turns - 2.0 * jnp.floor(turns * 0.5)
    square = rest * rest
    poly = 2.718121e-6
    poly = poly * square - 1.9839334e-4
    poly = poly * square + 8.3333293e-3
    poly = poly * square - 1.6666667e-1
    value = rest + rest * square * poly
    return value * (1.0 - 2.0 * odd)


def slab_kernel(
    side, local_bits, list_length, particles, tile,
    totals_ref, defocus_ref, phase_ref, scale_ref, index_ref,
    core_ref, word_ref, voxel_ref, image_ref, forward_ref, backward_ref, unit_ref,
    square_ref, mine_ref, *rest,
):
    theirs_refs, (sum_ref, staged_ref, sems) = rest[:-3], rest[-3:]
    source = pl.program_id(0)
    cap = word_ref.shape[2]
    blocks = sum_ref.shape[0] - 8
    features = image_ref.shape[2]
    kinds = forward_ref.shape[0] // features
    position_bits = bits_of(list_length)
    per_row = side // 8
    live = totals_ref[source]

    @pl.when(source == 0)
    def _():
        @pl.loop(0, blocks // 256)
        def _(i):
            at = pl.multiple_of(i * 256, 256)
            sum_ref[pl.ds(at, 256), :] = jnp.zeros((256, features), jnp.float32)

    square_ref[...] = jnp.zeros_like(square_ref)

    @pl.loop(0, (live + tile - 1) // tile)
    def _(t):
        at = pl.multiple_of(t * tile, tile)
        word = word_ref[0, :, pl.ds(at, tile)]
        kind = (word >> local_bits) & 3
        position = (word >> (local_bits + 2)) & (list_length - 1)
        particle = (word >> (local_bits + 2 + position_bits)) & (particles - 1)
        valid = lax.broadcasted_iota(jnp.int32, (1, tile), 1) + at < live
        defocus = jnp.zeros((1, tile), jnp.float32)
        phase = jnp.zeros((1, tile), jnp.float32)
        scale = jnp.zeros((1, tile), jnp.float32)
        for j in range(particles):
            chosen = particle == j
            defocus = jnp.where(chosen, defocus_ref[source * particles + j], defocus)
            phase = jnp.where(chosen, phase_ref[source * particles + j], phase)
            scale = jnp.where(chosen, scale_ref[source * particles + j], scale)
        half = features // 2
        cell = lax.broadcasted_iota(jnp.int32, (half, tile), 0)
        vert = ((position // per_row) * 8 + cell // 8 - side // 2).astype(jnp.float32)
        horiz = ((position % per_row) * 8 + cell % 8 - side // 2).astype(jnp.float32)
        radius = (vert * vert + horiz * horiz) * (1.0 / float((side // 2) ** 2))
        factor = scale * sine(defocus * radius + phase)
        factor = jnp.concatenate([factor, factor], axis=0)
        contract_last = (((1,), (1,)), ((), ()))
        each_kind = lax.dot_general(
            forward_ref[...], voxel_ref[0, pl.ds(at, tile), :], contract_last,
            preferred_element_type=jnp.float32,
        )
        extracted = each_kind[0:features, :]
        for k in range(1, kinds):
            extracted = jnp.where(kind == k, each_kind[k * features:(k + 1) * features, :], extracted)
        picture = lax.dot_general(
            unit_ref[...], image_ref[0, pl.ds(at, tile), :], contract_last,
            preferred_element_type=jnp.float32,
        )
        misfit = jnp.where(valid, factor * extracted - picture, 0.0)
        squares = jnp.sum(misfit * misfit, axis=0, keepdims=True)
        which = lax.broadcasted_iota(jnp.int32, (particles, tile), 0)
        spread = jnp.where(valid & (particle == which), squares, 0.0)
        folded = spread[:, 0:LANES]
        for i in range(1, tile // LANES):
            folded = folded + spread[:, i * LANES:(i + 1) * LANES]
        square_ref[0] = square_ref[0] + folded
        weighted = (factor * misfit).astype(jnp.bfloat16)
        none = jnp.zeros_like(weighted)
        spread_back = jnp.concatenate(
            [jnp.where(kind == k, weighted, none) for k in range(kinds)], axis=0
        )
        terms = jnp.dot(backward_ref[...], spread_back, preferred_element_type=jnp.float32)
        staged_ref[...] = terms.T

        @pl.loop(0, (jnp.minimum(live - at, tile) + GROUP - 1) // GROUP)
        def _(g):
            base = source * cap + at + g * GROUP
            marked = index_ref[base]
            places = [index_ref[base + j] & 0xFFFFFF for j in range(GROUP)]

            @pl.when(marked < (1 << 24))
            def _():
                held = [sum_ref[pl.ds(places[j], 1), :] for j in range(GROUP)]
                new = [staged_ref[pl.ds(g * GROUP + j, 1), :] for j in range(GROUP)]
                for j in range(GROUP):
                    sum_ref[pl.ds(places[j], 1), :] = held[j] + new[j]

            @pl.when(marked >= (1 << 24))
            def _():
                for j in range(GROUP):
                    sum_ref[pl.ds(places[j], 1), :] = (
                        sum_ref[pl.ds(places[j], 1), :] + staged_ref[pl.ds(g * GROUP + j, 1), :]
                    )

    @pl.when(source == pl.num_programs(0) - 1)
    def _():
        half = blocks // 2
        length = half // len(theirs_refs)
        copies = []
        for i, theirs_ref in enumerate(theirs_refs):
            at = pl.multiple_of((1 - core_ref[0]) * half + i * length, length)
            copies.append(pltpu.make_async_copy(sum_ref.at[pl.ds(at, length)], theirs_ref, sems.at[i + 1]))
        at = pl.multiple_of(core_ref[0] * half, half)
        copies.append(pltpu.make_async_copy(sum_ref.at[pl.ds(at, half)], mine_ref, sems.at[0]))
        for copy in copies:
            copy.start()
        for copy in copies:
            copy.wait()


def rotated(value, turn, length):
    real, imag = value
    if turn == 0:
        return value
    if 4 * turn == length:
        return (-imag, real)
    root = math.sqrt(0.5)
    if 8 * turn == length:
        return ((real - imag) * root, (real + imag) * root)
    if 8 * turn == 3 * length:
        return ((real + imag) * -root, (real - imag) * root)
    cos, sin = math.cos(2 * math.pi * turn / length), math.sin(2 * math.pi * turn / length)
    return (real * cos - imag * sin, real * sin + imag * cos)


def small_dft(values):
    length = len(values)
    if length == 1:
        return values
    even, odd = small_dft(values[0::2]), small_dft(values[1::2])
    low, high = [], []
    for k in range(length // 2):
        turned = rotated(odd[k], k, length)
        low.append((even[k][0] + turned[0], even[k][1] + turned[1]))
        high.append((even[k][0] - turned[0], even[k][1] - turned[1]))
    return low + high


def swap_quarters(values):
    lane = lax.broadcasted_iota(jnp.int32, values[0].shape, 1)
    low, even = lane < 64, (lane // 32) % 2 == 0
    roll = lambda value, shift: pltpu.roll(value, shift, 1)
    for first, second, shift, keep in ((0, 2, 64, low), (1, 3, 64, low), (0, 1, 32, even), (2, 3, 32, even)):
        one, two = values[first], values[second]
        values[first] = jnp.where(keep, one, roll(two, shift))
        values[second] = jnp.where(keep, roll(one, LANES - shift), two)
    return values


def in_halves(value):
    high = value.astype(jnp.bfloat16)
    return high, (value - high.astype(jnp.float32)).astype(jnp.bfloat16)


def planes_kernel(mine_ref, theirs_ref, zblock_ref, turn_ref, wide_ref, fine_ref, out_ref, high_ref, low_ref):
    step = pl.program_id(1)
    count = mine_ref.shape[1]
    groups, side = out_ref.shape[0], out_ref.shape[4]
    height = side // groups

    @pl.loop(0, count)
    def _(i):
        block = (mine_ref[:, i] + theirs_ref[:, i]).reshape(LANES, LANES)
        high, low = in_halves(block.T)
        both = jnp.dot(
            jnp.concatenate([high, low, high], axis=1), zblock_ref[...],
            preferred_element_type=jnp.float32,
        )
        by_cos = both[:, :LANES].reshape(8, 2, 8, LANES)
        by_sin = both[:, LANES:].reshape(8, 2, 8, LANES)
        real = by_cos[:, 0] - by_sin[:, 1]
        imag = by_sin[:, 0] + by_cos[:, 1]
        values = []
        for z in range(8):
            cos, sin = turn_ref[0, z:z + 1, :], turn_ref[1, z:z + 1, :]
            values.append((real[z] * cos - imag[z] * sin, real[z] * sin + imag[z] * cos))
        values = [jnp.concatenate(value, axis=0) for value in small_dft(values)]
        at = pl.ds(pl.multiple_of((step * count + i) * 16, 16), 16)
        for half in range(2):
            planes = swap_quarters(values[4 * half:4 * half + 4])
            for x in range(4):
                columns = slice((2 * x + half) * LANES, (2 * x + half + 1) * LANES)
                high, low = in_halves(planes[x])
                high_ref[at, columns] = high
                low_ref[at, columns] = low

    @pl.when(step == pl.num_programs(1) - 1)
    def _():
        @pl.loop(0, 4)
        def _(x):
            columns = pl.ds(pl.multiple_of(x * side, side), side)
            product = functools.partial(jnp.dot, preferred_element_type=jnp.float32)
            high = high_ref[:, columns]
            result = product(wide_ref[...], high) + (
                product(wide_ref[...], low_ref[:, columns]) + product(fine_ref[...], high)
            )
            for part in range(2):
                for group in range(groups):
                    start = part * side + group * height
                    out_ref[group, x, part] = result[start:start + height, :].astype(jnp.bfloat16)


def first_dimension_kernel(slabs, each, core_ref, *refs):
    arrays, (out_ref, mid_ref) = refs[:-2], refs[-2:]
    chunks = len(arrays) // 2
    own, other = arrays[:chunks], arrays[chunks:]
    held = own[0].shape[1]
    core = core_ref[0]
    is_first = core == 0
    sign = (1 - 2 * core).astype(jnp.float32)

    def plane(x):
        slab, rest = x // (2 * each), x % (2 * each)
        half, inner = rest // each, rest % each
        loaded = []
        for part in range(2):
            here = own[inner // held][slab, inner % held, part].astype(jnp.float32)
            there = other[inner // held][slab, inner % held, part].astype(jnp.float32)
            loaded.append(jnp.where(is_first, here, there) if half == 0 else jnp.where(is_first, there, here))
        return tuple(loaded)

    for low in range(16):
        values = small_dft([plane(low + 16 * high) for high in range(16)])
        for k in range(16):
            real, imag = rotated(values[k], low * k, 256)
            if low % 2:
                real, imag = real * sign, imag * sign
            mid_ref[k, low, 0] = real
            mid_ref[k, low, 1] = imag

    @pl.loop(0, 16)
    def _(k):
        values = [(mid_ref[k, low, 0], mid_ref[k, low, 1]) for low in range(16)]
        even, odd = small_dft(values[0::2]), small_dft(values[1::2])
        for m in range(8):
            turned = rotated(odd[m], m, 16)
            out_ref[0, k + 16 * m] = even[m][0] + turned[0]
            out_ref[1, k + 16 * m] = even[m][1] + turned[1]


def host_halves(table):
    high = table.astype(jnp.bfloat16)
    return high, (table - high.astype(np.float64)).astype(jnp.bfloat16)


def transform_tables(side):
    per_row = side // 8
    grid = np.arange(per_row)
    angle = 2 * np.pi * np.outer(grid, grid) / per_row
    zblock = np.concatenate([np.kron(np.eye(4), np.cos(angle)), np.kron(np.eye(4), np.sin(angle))], axis=1)
    high, low = host_halves(zblock)
    zblock = np.concatenate([high, high, low], axis=0)
    angle = 2 * np.pi * np.outer(np.arange(8), grid) / side
    turns = np.stack([np.tile(np.cos(angle), (1, 4)), np.tile(np.sin(angle), (1, 4))]).astype(np.float32)
    cells = np.arange(side)
    angle = 2 * np.pi * (np.outer(cells, cells) % side) / side
    cos, sin = np.cos(angle).reshape(side, per_row, 1, 8), np.sin(angle).reshape(side, per_row, 1, 8)
    matrix = np.concatenate(
        [np.concatenate([cos, -sin], axis=2), np.concatenate([sin, cos], axis=2)], axis=0
    ).reshape(2 * side, 2 * side) / float(side) ** 1.5
    return (zblock, turns) + host_halves(matrix)


def to_field(mine, theirs_sent, side):
    slabs = lax.axis_size("slab")
    per_row = side // 8
    each = side // slabs // 2
    chunks = len(theirs_sent)
    real_planes = each // chunks
    held = max(4, real_planes)
    height = side // slabs
    groups = slabs if height % 16 == 0 else 1
    tables = [jnp.asarray(table) for table in transform_tables(side)]
    swap = [(0, 1), (1, 0)]
    theirs = [lax.ppermute(chunk, "dom", swap) for chunk in theirs_sent]
    grid_shape = (-1, per_row, per_row, LANES)
    mine = mine.reshape(grid_shape)
    short = held - real_planes
    if short:
        mine = jnp.pad(mine, ((0, short), (0, 0), (0, 0), (0, 0)))
    yblocks = 8
    own, other = [], []
    for chunk in range(chunks):
        added = theirs[chunk].reshape(grid_shape)
        if short:
            added = jnp.pad(added, ((0, short), (0, 0), (0, 0), (0, 0)))
        quads = held // 4
        whole = lambda table: pl.BlockSpec(table.shape, lambda q, y: (0,) * table.ndim)
        sent = pl.pallas_call(
            planes_kernel,
            grid=(quads, per_row // yblocks),
            out_shape=jax.ShapeDtypeStruct((groups, held, 2, side // groups, side), jnp.bfloat16),
            in_specs=[
                pl.BlockSpec((4, yblocks, per_row, LANES), lambda q, y, at=chunk * quads: (at + q, y, 0, 0)),
                pl.BlockSpec((4, yblocks, per_row, LANES), lambda q, y: (q, y, 0, 0)),
            ] + [whole(table) for table in tables],
            out_specs=pl.BlockSpec((groups, 4, 2, side // groups, side), lambda q, y: (0, q, 0, 0, 0)),
            scratch_shapes=[
                pltpu.VMEM((2 * side, 4 * side), jnp.bfloat16),
                pltpu.VMEM((2 * side, 4 * side), jnp.bfloat16),
            ],
            compiler_params=params(),
            cost_estimate=pl.CostEstimate(
                flops=held * 8 * side**3, bytes_accessed=held * 4 * side**2 * 8, transcendentals=0
            ),
            name="transform_planes",
        )(mine, added, *tables)
        if groups != slabs:
            sent = sent.reshape(held, 2, slabs, height, side).transpose(2, 0, 1, 3, 4)[:, :real_planes]
        got = lax.all_to_all(sent, "slab", split_axis=0, concat_axis=0, tiled=True)
        own.append(got)
        other.append(lax.ppermute(got, "dom", swap))
    rows = min(16, height)
    arrays = own + other
    return pl.pallas_call(
        functools.partial(first_dimension_kernel, slabs, each),
        grid=(height // rows, side // LANES),
        out_shape=jax.ShapeDtypeStruct((2, side // 2, height, side), jnp.float32),
        in_specs=[SMEM_SPEC] + [
            pl.BlockSpec((slabs, real_planes, 2, rows, LANES), lambda y, z: (0, 0, 0, y, z))
            for _ in arrays
        ],
        out_specs=pl.BlockSpec((2, side // 2, rows, LANES), lambda y, z: (0, 0, y, z)),
        scratch_shapes=[pltpu.VMEM((16, 16, 2, rows, LANES), jnp.float32)],
        compiler_params=params(),
        name="transform_first",
    )(lax.axis_index("dom").astype(jnp.int32).reshape(1), *arrays)


def gradient_of_slab(volume, kernels, images, owners, local_block, kinds, counts, ctf_code, ctf_table, scales):
    slabs = lax.axis_size("slab")
    particles, list_length, features = images.shape
    side = math.isqrt(list_length * 64)
    entries = particles * list_length
    cap = 2 * entries // slabs
    slots = slabs * cap
    blocks = volume.shape[0]
    local_bits = bits_of(blocks)
    kind_count = kernels.shape[0]
    rows = entries // LANES
    int_rows = jax.ShapeDtypeStruct((rows, LANES), jnp.int32)

    target, word, totals = pl.pallas_call(
        functools.partial(route_kernel, slabs, cap, local_bits, list_length),
        out_shape=(int_rows, int_rows, jax.ShapeDtypeStruct((slabs, LANES), jnp.int32)),
        in_specs=[VMEM_SPEC, VMEM_SPEC, VMEM_SPEC, SMEM_SPEC],
        out_specs=(VMEM_SPEC, VMEM_SPEC, VMEM_SPEC),
        compiler_params=params(),
        name="route",
    )(
        owners.reshape(rows, LANES), local_block.reshape(rows, LANES), kinds.reshape(rows, LANES), counts
    )
    packed, meta = pl.pallas_call(
        functools.partial(pack_kernel, slots),
        out_shape=(
            jax.ShapeDtypeStruct((slots, features), jnp.bfloat16),
            jax.ShapeDtypeStruct((slots + 1024,), jnp.int32),
        ),
        in_specs=[SMEM_SPEC, SMEM_SPEC, VMEM_SPEC],
        out_specs=(VMEM_SPEC, SMEM_SPEC),
        scratch_shapes=[
            pltpu.VMEM((entries, features), jnp.float32),
            pltpu.VMEM((slots + 8, features), jnp.float32),
        ],
        compiler_params=params(),
        name="pack",
    )(target.reshape(entries), word.reshape(entries), images.reshape(entries, features))

    code = ctf_code | ((scales.astype(jnp.float32) * 256.0).astype(jnp.int32) << 8)
    header = jnp.concatenate(
        [
            totals[:, 0:1],
            jnp.broadcast_to(code[None, :], (slabs, particles)),
            jnp.zeros((slabs, LANES - 1 - particles), jnp.int32),
        ],
        axis=1,
    )
    sent = jnp.concatenate([meta[:slots].reshape(slabs, cap), header], axis=1)
    arrived = lax.all_to_all(sent, "slab", split_axis=0, concat_axis=0, tiled=True)
    words = arrived[:, :cap]
    totals_in = arrived[:, cap]
    codes_in = arrived[:, cap + 1:cap + 1 + particles]
    live = (jnp.arange(cap, dtype=jnp.int32)[None, :] < totals_in[:, None]).astype(jnp.int32)
    table_rows = ctf_table[(codes_in & 255).reshape(-1)]
    scale_in = (codes_in >> 8).astype(jnp.float32).reshape(-1) * (1.0 / 256.0)

    pictures = lax.all_to_all(
        packed.reshape(slabs, cap, features), "slab", split_axis=0, concat_axis=0, tiled=True
    )

    index = pl.pallas_call(
        functools.partial(decode_kernel, local_bits, blocks),
        out_shape=jax.ShapeDtypeStruct((slots // LANES, LANES), jnp.int32),
        in_specs=[VMEM_SPEC, VMEM_SPEC],
        out_specs=VMEM_SPEC,
        compiler_params=params(),
        name="decode",
    )(words.reshape(slots // LANES, LANES), live.reshape(slots // LANES, LANES))
    index = index.reshape(slots)
    voxels = pl.pallas_call(
        functools.partial(gather_kernel, slabs, cap),
        out_shape=jax.ShapeDtypeStruct((slots, features), jnp.bfloat16),
        in_specs=[SMEM_SPEC, SMEM_SPEC, VMEM_SPEC],
        out_specs=VMEM_SPEC,
        scratch_shapes=[
            pltpu.VMEM((blocks + 8, features), jnp.float32),
            pltpu.VMEM((cap, features), jnp.float32),
        ],
        compiler_params=params(),
        cost_estimate=pl.CostEstimate(flops=0, bytes_accessed=100 * 1024 * 1024, transcendentals=0),
        name="read_voxels",
    )(index, totals_in, volume)

    forward = jnp.transpose(kernels, (0, 2, 1)).reshape(kind_count * features, features)
    backward = kernels.reshape(kind_count, 2, 8, 8, features).transpose(3, 1, 2, 0, 4)
    backward = backward.reshape(features, kind_count * features)
    unit = jnp.eye(features, dtype=jnp.bfloat16)
    tile = min(512, cap)
    per_source = lambda length, width: pl.BlockSpec((1, length, width), lambda s: (s, 0, 0))
    whole = lambda shape: pl.BlockSpec(shape, lambda s: (0,) * len(shape))
    planes_each = side // slabs // 2
    chunks = max(1, planes_each // (4 * QUADS))
    squares, mine, *theirs = pl.pallas_call(
        functools.partial(slab_kernel, side, local_bits, list_length, particles, tile),
        grid=(slabs,),
        out_shape=(
            jax.ShapeDtypeStruct((slabs, particles, LANES), jnp.float32),
            jax.ShapeDtypeStruct((blocks // 2, features), jnp.float32),
        ) + (jax.ShapeDtypeStruct((blocks // 2 // chunks, features), jnp.float32),) * chunks,
        in_specs=[SMEM_SPEC] * 6 + [
            per_source(1, cap),
            per_source(cap, features),
            per_source(cap, features),
            whole(forward.shape),
            whole(backward.shape),
            whole(unit.shape),
        ],
        out_specs=(per_source(particles, LANES),) + (ANY_SPEC,) * (1 + chunks),
        scratch_shapes=[
            pltpu.VMEM((blocks + 8, features), jnp.float32),
            pltpu.VMEM((tile, features), jnp.float32),
            pltpu.SemaphoreType.DMA((1 + chunks,)),
        ],
        compiler_params=params(),
        name="compare_and_add",
    )(
        totals_in, table_rows[:, 0], table_rows[:, 1], scale_in, index,
        lax.axis_index("dom").astype(jnp.int32).reshape(1),
        words.reshape(slabs, 1, cap), voxels.reshape(slabs, cap, features), pictures,
        forward, backward, unit,
    )
    returned = lax.all_to_all(
        jnp.sum(squares, axis=2), "slab", split_axis=0, concat_axis=0, tiled=True
    )
    losses = jnp.sum(returned, axis=0) / (counts.astype(jnp.float32) * 128.0)
    return mine, theirs, losses, side


def body(*arrays):
    mine, theirs, losses, side = gradient_of_slab(*arrays)
    return to_field(mine, theirs, side), losses


def solution(mesh):
    in_specs = (
        P(("groups", "slab"), None),
        P(),
        P(("groups", "slab", "dom"), None, None),
        P(("groups", "slab", "dom"), None, None),
        P(("groups", "slab", "dom"), None),
        P(("groups", "slab", "dom"), None),
        P(("groups", "slab", "dom")),
        P(("groups", "slab", "dom")),
        P(),
        P(("groups", "slab", "dom")),
    )
    out_specs = (P(None, ("groups", "dom"), "slab", None), P(("groups", "slab", "dom")))
    return jax.shard_map(body, mesh=mesh, in_specs=in_specs, out_specs=out_specs, check_vma=False)
```

```python
import functools
import math

import jax
import jax.numpy as jnp
import numpy as np
from jax import lax
from jax.experimental import pallas as pl
from jax.experimental.pallas import tpu as pltpu
from jax.sharding import PartitionSpec as P

LANES = 128
TILE = 512
GROUP = 16
VMEM_LIMIT = 56 * 1024 * 1024

SMEM_SPEC = pl.BlockSpec(memory_space=pltpu.SMEM)
VMEM_SPEC = pl.BlockSpec(memory_space=pltpu.VMEM)
ANY_SPEC = pl.BlockSpec(memory_space=pl.ANY)


def params(**extra):
    return pltpu.CompilerParams(vmem_limit_bytes=VMEM_LIMIT, **extra)


def bits_of(count):
    return (count - 1).bit_length()


def route_kernel(slabs, cap, local_bits, list_length, owner_ref, local_ref, kind_ref, counts_ref, target_ref, word_ref, totals_ref):
    rows = owner_ref.shape[0]
    rows_each = list_length // LANES
    particles = rows // rows_each
    row_id = lax.broadcasted_iota(jnp.int32, (rows, LANES), 0)
    lane_id = lax.broadcasted_iota(jnp.int32, (rows, LANES), 1)
    particle = row_id // rows_each
    position = (row_id % rows_each) * LANES + lane_id
    limit = jnp.zeros((rows, LANES), jnp.int32)
    for i in range(particles):
        limit = jnp.where(particle == i, counts_ref[i], limit)
    owner = jnp.where(position < limit, owner_ref[...], -1)
    up_to = (
        lax.broadcasted_iota(jnp.int32, (LANES, LANES), 0)
        <= lax.broadcasted_iota(jnp.int32, (LANES, LANES), 1)
    ).astype(jnp.bfloat16)
    ones = jnp.ones((LANES, LANES), jnp.bfloat16)
    before = (
        lax.broadcasted_iota(jnp.int32, (rows, rows), 1)
        < lax.broadcasted_iota(jnp.int32, (rows, rows), 0)
    ).astype(jnp.bfloat16)

    def one_slab(slab, target):
        mine = owner == slab
        hits = mine.astype(jnp.float32).astype(jnp.bfloat16)
        inside = jnp.dot(hits, up_to, preferred_element_type=jnp.float32)
        row_sum = jnp.dot(hits, ones, preferred_element_type=jnp.float32)
        above = jnp.dot(before, row_sum.astype(jnp.bfloat16), preferred_element_type=jnp.float32)
        rank = (inside + above).astype(jnp.int32) - 1
        total = (above[rows - 1:rows, :] + row_sum[rows - 1:rows, :]).astype(jnp.int32)
        totals_ref[pl.ds(slab, 1), :] = total
        return jnp.where(mine, slab * cap + rank, target)

    target = lax.fori_loop(0, slabs, one_slab, jnp.full((rows, LANES), slabs * cap, jnp.int32))
    target_ref[...] = target
    kind_bits = local_bits
    word = local_ref[...] | (kind_ref[...] << kind_bits) | (position << (kind_bits + 2))
    word_ref[...] = word | (particle << (kind_bits + 2 + bits_of(list_length)))


def pack_words_kernel(list_length, target_ref, word_ref, counts_ref, meta_ref):
    @pl.loop(0, counts_ref.shape[0])
    def _(particle):
        @pl.loop(0, (counts_ref[particle] + 15) // 16)
        def _(i):
            first = particle * list_length + i * 16
            targets = [target_ref[first + j] for j in range(16)]
            words = [word_ref[first + j] for j in range(16)]
            for j in range(16):
                meta_ref[targets[j]] = words[j]


def pack_images_kernel(slabs, cap, list_length, target_ref, counts_ref, image_ref, *refs):
    out_refs, (wide_ref, staged_ref) = refs[:-2], refs[-2:]
    step = 256

    @pl.loop(0, image_ref.shape[0] // step)
    def _(i):
        at = pl.multiple_of(i * step, step)
        wide_ref[pl.ds(at, step), :] = image_ref[pl.ds(at, step), :].astype(jnp.float32)

    @pl.loop(0, counts_ref.shape[0])
    def _(particle):
        @pl.loop(0, (counts_ref[particle] + 15) // 16)
        def _(i):
            first = particle * list_length + i * 16
            targets = [target_ref[first + j] for j in range(16)]
            rows = [wide_ref[pl.ds(first + j, 1), :] for j in range(16)]
            for j in range(16):
                staged_ref[pl.ds(targets[j], 1), :] = rows[j]

    for chunk, out_ref in enumerate(out_refs):
        width = out_ref.shape[1]

        @pl.loop(0, slabs)
        def _(slab):
            at = pl.multiple_of(slab * cap + chunk * width, width)
            out_ref[slab] = staged_ref[pl.ds(at, width), :].astype(jnp.bfloat16)


def decode_kernel(local_bits, dummy, word_ref, live_ref, index_ref):
    rows = word_ref.shape[0]
    live = live_ref[...] != 0
    index = jnp.where(live, word_ref[...] & ((1 << local_bits) - 1), dummy)
    lane = lax.broadcasted_iota(jnp.int32, (rows, LANES), 1)
    clash = jnp.zeros((rows, LANES), jnp.int32)
    for shift in range(1, GROUP):
        earlier = pltpu.roll(index, shift, 1)
        same = (earlier == index) & (lane % GROUP >= shift) & live
        clash = clash | same.astype(jnp.int32)
    shift = 1
    while shift < GROUP:
        clash = clash | pltpu.roll(clash, LANES - shift, 1)
        shift *= 2
    index_ref[...] = index | (clash << 24)


def gather_kernel(slabs, cap, index_ref, totals_ref, volume_ref, out_ref, wide_ref, staged_ref):
    blocks = volume_ref.shape[0]
    step = 256

    @pl.loop(0, blocks // step)
    def _(i):
        at = pl.multiple_of(i * step, step)
        wide_ref[pl.ds(at, step), :] = volume_ref[pl.ds(at, step), :].astype(jnp.float32)

    @pl.loop(0, slabs)
    def _(source):
        live = totals_ref[source]

        @pl.loop(0, (live + 15) // 16)
        def _(i):
            first = source * cap + i * 16
            places = [index_ref[first + j] & 0xFFFFFF for j in range(16)]
            rows = [wide_ref[pl.ds(places[j], 1), :] for j in range(16)]
            for j in range(16):
                staged_ref[pl.ds(i * 16 + j, 1), :] = rows[j]

        width = min(step, cap)

        @pl.loop(0, (live + width - 1) // width)
        def _(i):
            at = pl.multiple_of(i * width, width)
            to = pl.multiple_of(source * cap + i * width, width)
            out_ref[pl.ds(to, width), :] = staged_ref[pl.ds(at, width), :].astype(jnp.bfloat16)


def sine(angle):
    turns = jnp.floor(angle * (1.0 / math.pi) + 0.5)
    rest = angle - turns * 3.140625
    rest = rest - turns * 9.67502593994140625e-4
    rest = rest - turns * 1.509957990978376e-7
    odd = turns - 2.0 * jnp.floor(turns * 0.5)
    square = rest * rest
    poly = 2.718121e-6
    poly = poly * square - 1.9839334e-4
    poly = poly * square + 8.3333293e-3
    poly = poly * square - 1.6666667e-1
    value = rest + rest * square * poly
    return value * (1.0 - 2.0 * odd)


def slab_kernel(
    side, local_bits, list_length, particles, cap, offset, first, last,
    totals_ref, defocus_ref, phase_ref, scale_ref, index_ref, core_ref,
    word_ref, voxel_ref, image_ref, forward_ref, backward_ref, unit_ref, *rest,
):
    if not first:
        before_ref, rest = rest[0], rest[1:]
    square_ref, sum_refs, (sum_ref, staged_ref, sems) = rest[0], rest[1:-3], rest[-3:]
    source = pl.program_id(0)
    tile = word_ref.shape[2]
    blocks = sum_ref.shape[0] - 8
    features = image_ref.shape[2]
    kinds = forward_ref.shape[0] // features
    position_bits = bits_of(list_length)
    per_row = side // 8
    live = jnp.clip(totals_ref[source] - offset, 0, tile)

    @pl.when(source == 0)
    def _():
        if first:
            @pl.loop(0, blocks // 256)
            def _(i):
                at = pl.multiple_of(i * 256, 256)
                sum_ref[pl.ds(at, 256), :] = jnp.zeros((256, features), jnp.float32)
        else:
            pltpu.make_async_copy(before_ref, sum_ref.at[pl.ds(0, blocks)], sems.at[0]).start()

    @pl.when(live == 0)
    def _():
        square_ref[...] = jnp.zeros_like(square_ref)

    @pl.when(live > 0)
    def _():
        word = word_ref[0]
        kind = (word >> local_bits) & 3
        position = (word >> (local_bits + 2)) & (list_length - 1)
        particle = (word >> (local_bits + 2 + position_bits)) & (particles - 1)
        valid = lax.broadcasted_iota(jnp.int32, (1, tile), 1) < live
        defocus = jnp.zeros((1, tile), jnp.float32)
        phase = jnp.zeros((1, tile), jnp.float32)
        scale = jnp.zeros((1, tile), jnp.float32)
        for j in range(particles):
            chosen = particle == j
            defocus = jnp.where(chosen, defocus_ref[source * particles + j], defocus)
            phase = jnp.where(chosen, phase_ref[source * particles + j], phase)
            scale = jnp.where(chosen, scale_ref[source * particles + j], scale)
        half = features // 2
        cell = lax.broadcasted_iota(jnp.int32, (half, tile), 0)
        vert = ((position // per_row) * 8 - side // 2 + cell // 8).astype(jnp.float32)
        horiz = ((position % per_row) * 8 - side // 2 + cell % 8).astype(jnp.float32)
        radius = (vert * vert + horiz * horiz) * (1.0 / float((side // 2) ** 2))
        factor = scale * sine(defocus * radius + phase)
        factor = jnp.concatenate([factor, factor], axis=0)
        contract_last = (((1,), (1,)), ((), ()))
        each_kind = lax.dot_general(
            forward_ref[...], voxel_ref[0], contract_last, preferred_element_type=jnp.float32
        )
        extracted = each_kind[0:features, :]
        for k in range(1, kinds):
            extracted = jnp.where(kind == k, each_kind[k * features:(k + 1) * features, :], extracted)
        picture = lax.dot_general(
            unit_ref[...], image_ref[0], contract_last, preferred_element_type=jnp.float32
        )
        misfit = jnp.where(valid, factor * extracted - picture, 0.0)
        squares = jnp.sum(misfit * misfit, axis=0, keepdims=True)
        which = lax.broadcasted_iota(jnp.int32, (particles, tile), 0)
        spread = jnp.where(valid & (particle == which), squares, 0.0)
        folded = spread[:, 0:LANES]
        for i in range(1, tile // LANES):
            folded = folded + spread[:, i * LANES:(i + 1) * LANES]
        square_ref[0] = folded
        weighted = (factor * misfit).astype(jnp.bfloat16)
        none = jnp.zeros_like(weighted)
        spread_back = jnp.concatenate(
            [jnp.where(kind == k, weighted, none) for k in range(kinds)], axis=0
        )
        terms = jnp.dot(backward_ref[...], spread_back, preferred_element_type=jnp.float32)
        staged_ref[...] = terms.T

    if not first:
        @pl.when(source == 0)
        def _():
            pltpu.make_async_copy(before_ref, sum_ref.at[pl.ds(0, blocks)], sems.at[0]).wait()

    @pl.loop(0, (live + GROUP - 1) // GROUP)
    def _(g):
        base = source * cap + offset + g * GROUP
        marked = index_ref[base]
        places = [index_ref[base + j] & 0xFFFFFF for j in range(GROUP)]

        @pl.when(marked < (1 << 24))
        def _():
            held = [sum_ref[pl.ds(places[j], 1), :] for j in range(GROUP)]
            new = [staged_ref[pl.ds(g * GROUP + j, 1), :] for j in range(GROUP)]
            for j in range(GROUP):
                sum_ref[pl.ds(places[j], 1), :] = held[j] + new[j]

        @pl.when(marked >= (1 << 24))
        def _():
            for j in range(GROUP):
                sum_ref[pl.ds(places[j], 1), :] = (
                    sum_ref[pl.ds(places[j], 1), :] + staged_ref[pl.ds(g * GROUP + j, 1), :]
                )

    @pl.when(source == pl.num_programs(0) - 1)
    def _():
        copies = []
        if last:
            half = blocks // 2
            start = (1 - core_ref[0]) * half
            places = [core_ref[0] * half]
            for out_ref in sum_refs[1:]:
                places.append(start)
                start = start + out_ref.shape[0]
        else:
            places = [0]
        for i, (place, out_ref) in enumerate(zip(places, sum_refs)):
            length = out_ref.shape[0]
            at = pl.multiple_of(place, 8)
            copies.append(pltpu.make_async_copy(sum_ref.at[pl.ds(at, length)], out_ref, sems.at[i]))
        for copy in copies:
            copy.start()
        for copy in copies:
            copy.wait()


def pieces_of(planes):
    if planes < 16:
        return [planes]
    return [4, 4, planes - 8]


def rotated(value, turn, length):
    real, imag = value
    if turn == 0:
        return value
    if 4 * turn == length:
        return (-imag, real)
    root = math.sqrt(0.5)
    if 8 * turn == length:
        return ((real - imag) * root, (real + imag) * root)
    if 8 * turn == 3 * length:
        return ((real + imag) * -root, (real - imag) * root)
    cos, sin = math.cos(2 * math.pi * turn / length), math.sin(2 * math.pi * turn / length)
    return (real * cos - imag * sin, real * sin + imag * cos)


def small_dft(values):
    length = len(values)
    if length == 1:
        return values
    even, odd = small_dft(values[0::2]), small_dft(values[1::2])
    low, high = [], []
    for k in range(length // 2):
        turned = rotated(odd[k], k, length)
        low.append((even[k][0] + turned[0], even[k][1] + turned[1]))
        high.append((even[k][0] - turned[0], even[k][1] - turned[1]))
    return low + high


def swap_quarters(values):
    lane = lax.broadcasted_iota(jnp.int32, values[0].shape, 1)
    low, even = lane < 64, (lane // 32) % 2 == 0
    roll = lambda value, shift: pltpu.roll(value, shift, 1)
    for first, second, shift, keep in ((0, 2, 64, low), (1, 3, 64, low), (0, 1, 32, even), (2, 3, 32, even)):
        one, two = values[first], values[second]
        values[first] = jnp.where(keep, one, roll(two, shift))
        values[second] = jnp.where(keep, roll(one, LANES - shift), two)
    return values


def in_halves(value):
    high = value.astype(jnp.bfloat16)
    return high, (value - high.astype(jnp.float32)).astype(jnp.bfloat16)


def planes_kernel(mine_ref, theirs_ref, zblock_ref, turn_ref, wide_ref, fine_ref, out_ref, high_ref, low_ref):
    step = pl.program_id(1)
    count = mine_ref.shape[1]
    groups, side = out_ref.shape[0], out_ref.shape[4]
    height = side // groups

    @pl.loop(0, count, unroll=4)
    def _(i):
        block = (mine_ref[:, i] + theirs_ref[:, i]).reshape(LANES, LANES)
        high, low = in_halves(block.T)
        both = jnp.dot(
            jnp.concatenate([high, low, high], axis=1), zblock_ref[...],
            preferred_element_type=jnp.float32,
        )
        by_cos = both[:, :LANES].reshape(8, 2, 8, LANES)
        by_sin = both[:, LANES:].reshape(8, 2, 8, LANES)
        real = by_cos[:, 0] - by_sin[:, 1]
        imag = by_sin[:, 0] + by_cos[:, 1]
        values = []
        for z in range(8):
            cos, sin = turn_ref[0, z:z + 1, :], turn_ref[1, z:z + 1, :]
            values.append((real[z] * cos - imag[z] * sin, real[z] * sin + imag[z] * cos))
        values = [jnp.concatenate(value, axis=0) for value in small_dft(values)]
        at = pl.ds(pl.multiple_of((step * count + i) * 16, 16), 16)
        for half in range(2):
            planes = swap_quarters(values[4 * half:4 * half + 4])
            for x in range(4):
                columns = slice((2 * x + half) * LANES, (2 * x + half + 1) * LANES)
                high, low = in_halves(planes[x])
                high_ref[at, columns] = high
                low_ref[at, columns] = low

    @pl.when(step == pl.num_programs(1) - 1)
    def _():
        @pl.loop(0, 4)
        def _(x):
            columns = pl.ds(pl.multiple_of(x * side, side), side)
            product = functools.partial(jnp.dot, preferred_element_type=jnp.float32)
            high = high_ref[:, columns]
            result = product(wide_ref[...], high) + (
                product(wide_ref[...], low_ref[:, columns]) + product(fine_ref[...], high)
            )
            for part in range(2):
                for group in range(groups):
                    start = part * side + group * height
                    out_ref[group, x, part] = result[start:start + height, :].astype(jnp.bfloat16)


def first_dimension_kernel(slabs, each, core_ref, *refs):
    arrays, (out_ref, mid_ref) = refs[:-2], refs[-2:]
    chunks = len(arrays) // 2
    own, other = arrays[:chunks], arrays[chunks:]
    spots = [(i, at) for i, ref in enumerate(own) for at in range(ref.shape[1])]
    core = core_ref[0]
    is_first = core == 0
    sign = (1 - 2 * core).astype(jnp.float32)

    def plane(x):
        slab, rest = x // (2 * each), x % (2 * each)
        half, inner = rest // each, rest % each
        loaded = []
        for part in range(2):
            chunk, at = spots[inner]
            here = own[chunk][slab, at, part].astype(jnp.float32)
            there = other[chunk][slab, at, part].astype(jnp.float32)
            loaded.append(jnp.where(is_first, here, there) if half == 0 else jnp.where(is_first, there, here))
        return tuple(loaded)

    for low in range(16):
        values = small_dft([plane(low + 16 * high) for high in range(16)])
        for k in range(16):
            real, imag = rotated(values[k], low * k, 256)
            if low % 2:
                real, imag = real * sign, imag * sign
            mid_ref[k, low, 0] = real
            mid_ref[k, low, 1] = imag

    @pl.loop(0, 16)
    def _(k):
        values = [(mid_ref[k, low, 0], mid_ref[k, low, 1]) for low in range(16)]
        even, odd = small_dft(values[0::2]), small_dft(values[1::2])
        for m in range(8):
            turned = rotated(odd[m], m, 16)
            out_ref[0, k + 16 * m] = even[m][0] + turned[0]
            out_ref[1, k + 16 * m] = even[m][1] + turned[1]


def host_halves(table):
    high = table.astype(jnp.bfloat16)
    return high, (table - high.astype(np.float64)).astype(jnp.bfloat16)


def transform_tables(side):
    per_row = side // 8
    grid = np.arange(per_row)
    angle = 2 * np.pi * np.outer(grid, grid) / per_row
    zblock = np.concatenate([np.kron(np.eye(4), np.cos(angle)), np.kron(np.eye(4), np.sin(angle))], axis=1)
    high, low = host_halves(zblock)
    zblock = np.concatenate([high, high, low], axis=0)
    angle = 2 * np.pi * np.outer(np.arange(8), grid) / side
    turns = np.stack([np.tile(np.cos(angle), (1, 4)), np.tile(np.sin(angle), (1, 4))]).astype(np.float32)
    cells = np.arange(side)
    angle = 2 * np.pi * (np.outer(cells, cells) % side) / side
    cos, sin = np.cos(angle).reshape(side, per_row, 1, 8), np.sin(angle).reshape(side, per_row, 1, 8)
    matrix = np.concatenate(
        [np.concatenate([cos, -sin], axis=2), np.concatenate([sin, cos], axis=2)], axis=0
    ).reshape(2 * side, 2 * side) / float(side) ** 1.5
    return (zblock, turns) + host_halves(matrix)


def to_field(mine, theirs_sent, side):
    slabs = lax.axis_size("slab")
    per_row = side // 8
    each = side // slabs // 2
    height = side // slabs
    groups = slabs if height % 16 == 0 else 1
    tables = [jnp.asarray(table) for table in transform_tables(side)]
    swap = [(0, 1), (1, 0)]
    theirs = [lax.ppermute(chunk, "dom", swap) for chunk in theirs_sent]
    grid_shape = (-1, per_row, per_row, LANES)
    mine = mine.reshape(grid_shape)
    short = max(0, 4 - each)
    if short:
        mine = jnp.pad(mine, ((0, short), (0, 0), (0, 0), (0, 0)))
    yblocks = 8
    own, other = [], []
    first_quad = 0
    for real_planes, added in zip(pieces_of(each), theirs):
        added = added.reshape(grid_shape)
        if short:
            added = jnp.pad(added, ((0, short), (0, 0), (0, 0), (0, 0)))
        held = real_planes + short
        quads = held // 4
        whole = lambda table: pl.BlockSpec(table.shape, lambda q, y: (0,) * table.ndim)
        sent = pl.pallas_call(
            planes_kernel,
            grid=(quads, per_row // yblocks),
            out_shape=jax.ShapeDtypeStruct((groups, held, 2, side // groups, side), jnp.bfloat16),
            in_specs=[
                pl.BlockSpec((4, yblocks, per_row, LANES), lambda q, y, at=first_quad: (at + q, y, 0, 0)),
                pl.BlockSpec((4, yblocks, per_row, LANES), lambda q, y: (q, y, 0, 0)),
            ] + [whole(table) for table in tables],
            out_specs=pl.BlockSpec((groups, 4, 2, side // groups, side), lambda q, y: (0, q, 0, 0, 0)),
            scratch_shapes=[
                pltpu.VMEM((2 * side, 4 * side), jnp.bfloat16),
                pltpu.VMEM((2 * side, 4 * side), jnp.bfloat16),
            ],
            compiler_params=params(),
            cost_estimate=pl.CostEstimate(
                flops=held * 8 * side**3, bytes_accessed=held * 4 * side**2 * 8, transcendentals=0
            ),
            name="transform_planes",
        )(mine, added, *tables)
        if groups != slabs:
            sent = sent.reshape(-1, 2, slabs, height, side).transpose(2, 0, 1, 3, 4)[:, :real_planes]
        first_quad += quads
        got = lax.all_to_all(sent, "slab", split_axis=0, concat_axis=0, tiled=True)
        own.append(got)
        other.append(lax.ppermute(got, "dom", swap))
    rows = min(16, height)
    arrays = own + other
    return pl.pallas_call(
        functools.partial(first_dimension_kernel, slabs, each),
        grid=(height // rows, side // LANES),
        out_shape=jax.ShapeDtypeStruct((2, side // 2, height, side), jnp.float32),
        in_specs=[SMEM_SPEC] + [
            pl.BlockSpec(array.shape[:3] + (rows, LANES), lambda y, z: (0, 0, 0, y, z))
            for array in arrays
        ],
        out_specs=pl.BlockSpec((2, side // 2, rows, LANES), lambda y, z: (0, 0, y, z)),
        scratch_shapes=[pltpu.VMEM((16, 16, 2, rows, LANES), jnp.float32)],
        compiler_params=params(),
        name="transform_first",
    )(lax.axis_index("dom").astype(jnp.int32).reshape(1), *arrays)


def gradient_of_slab(volume, kernels, images, owners, local_block, kinds, counts, ctf_code, ctf_table, scales):
    slabs = lax.axis_size("slab")
    particles, list_length, features = images.shape
    side = math.isqrt(list_length * 64)
    entries = particles * list_length
    cap = 2 * entries // slabs
    slots = slabs * cap
    blocks = volume.shape[0]
    local_bits = bits_of(blocks)
    kind_count = kernels.shape[0]
    rows = entries // LANES
    int_rows = jax.ShapeDtypeStruct((rows, LANES), jnp.int32)

    target, word, totals = pl.pallas_call(
        functools.partial(route_kernel, slabs, cap, local_bits, list_length),
        out_shape=(int_rows, int_rows, jax.ShapeDtypeStruct((slabs, LANES), jnp.int32)),
        in_specs=[VMEM_SPEC, VMEM_SPEC, VMEM_SPEC, SMEM_SPEC],
        out_specs=(VMEM_SPEC, VMEM_SPEC, VMEM_SPEC),
        compiler_params=params(),
        name="route",
    )(
        owners.reshape(rows, LANES), local_block.reshape(rows, LANES), kinds.reshape(rows, LANES), counts
    )
    target, word = target.reshape(entries), word.reshape(entries)
    meta = pl.pallas_call(
        functools.partial(pack_words_kernel, list_length),
        out_shape=jax.ShapeDtypeStruct((slots + 1024,), jnp.int32),
        in_specs=[SMEM_SPEC, SMEM_SPEC, SMEM_SPEC],
        out_specs=SMEM_SPEC,
        compiler_params=params(),
        name="pack_words",
    )(target, word, counts)
    parts = max(1, cap // TILE)
    tile = cap // parts
    packed = pl.pallas_call(
        functools.partial(pack_images_kernel, slabs, cap, list_length),
        out_shape=(jax.ShapeDtypeStruct((slabs, tile, features), jnp.bfloat16),) * parts,
        in_specs=[SMEM_SPEC, SMEM_SPEC, VMEM_SPEC],
        out_specs=(VMEM_SPEC,) * parts,
        scratch_shapes=[
            pltpu.VMEM((entries, features), jnp.float32),
            pltpu.VMEM((slots + 8, features), jnp.float32),
        ],
        compiler_params=params(),
        cost_estimate=pl.CostEstimate(flops=0, bytes_accessed=50 * 1024 * 1024, transcendentals=0),
        name="pack_images",
    )(target, counts, images.reshape(entries, features))

    code = ctf_code | ((scales.astype(jnp.float32) * 256.0).astype(jnp.int32) << 8)
    header = jnp.concatenate(
        [
            totals[:, 0:1],
            jnp.broadcast_to(code[None, :], (slabs, particles)),
            jnp.zeros((slabs, LANES - 1 - particles), jnp.int32),
        ],
        axis=1,
    )
    sent = jnp.concatenate([meta[:slots].reshape(slabs, cap), header], axis=1)
    arrived = lax.all_to_all(sent, "slab", split_axis=0, concat_axis=0, tiled=True)
    words = arrived[:, :cap]
    totals_in = arrived[:, cap]
    codes_in = arrived[:, cap + 1:cap + 1 + particles]
    live = (jnp.arange(cap, dtype=jnp.int32)[None, :] < totals_in[:, None]).astype(jnp.int32)
    table_rows = ctf_table[(codes_in & 255).reshape(-1)]
    scale_in = (codes_in >> 8).astype(jnp.float32).reshape(-1) * (1.0 / 256.0)

    index = pl.pallas_call(
        functools.partial(decode_kernel, local_bits, blocks),
        out_shape=jax.ShapeDtypeStruct((slots // LANES, LANES), jnp.int32),
        in_specs=[VMEM_SPEC, VMEM_SPEC],
        out_specs=VMEM_SPEC,
        compiler_params=params(),
        name="decode",
    )(words.reshape(slots // LANES, LANES), live.reshape(slots // LANES, LANES))
    index = index.reshape(slots)
    voxels = pl.pallas_call(
        functools.partial(gather_kernel, slabs, cap),
        out_shape=jax.ShapeDtypeStruct((slots, features), jnp.bfloat16),
        in_specs=[SMEM_SPEC, SMEM_SPEC, VMEM_SPEC],
        out_specs=VMEM_SPEC,
        scratch_shapes=[
            pltpu.VMEM((blocks + 8, features), jnp.float32),
            pltpu.VMEM((cap, features), jnp.float32),
        ],
        compiler_params=params(),
        cost_estimate=pl.CostEstimate(flops=0, bytes_accessed=100 * 1024 * 1024, transcendentals=0),
        name="read_voxels",
    )(index, totals_in, volume)

    forward = jnp.transpose(kernels, (0, 2, 1)).reshape(kind_count * features, features)
    backward = kernels.reshape(kind_count, 2, 8, 8, features).transpose(3, 1, 2, 0, 4)
    backward = backward.reshape(features, kind_count * features)
    unit = jnp.eye(features, dtype=jnp.bfloat16)
    per_source = lambda length, width, at=0: pl.BlockSpec((1, length, width), lambda s: (s, at, 0))
    whole = lambda table: pl.BlockSpec(table.shape, lambda s: (0,) * table.ndim)
    voxels = voxels.reshape(slabs, cap, features)
    core = lax.axis_index("dom").astype(jnp.int32).reshape(1)
    plane_blocks = (side // 8) ** 2
    pieces = [planes * plane_blocks for planes in pieces_of(side // slabs // 2)]
    squares, sums = 0.0, ()
    for part in range(parts):
        first, last = part == 0, part == parts - 1
        picture = lax.all_to_all(packed[part], "slab", split_axis=0, concat_axis=0, tiled=True)
        lengths = [blocks // 2] + pieces if last else [blocks]
        more, *sums = pl.pallas_call(
            functools.partial(
                slab_kernel, side, local_bits, list_length, particles, cap, part * tile, first, last
            ),
            grid=(slabs,),
            out_shape=(jax.ShapeDtypeStruct((slabs, particles, LANES), jnp.float32),)
            + tuple(jax.ShapeDtypeStruct((length, features), jnp.float32) for length in lengths),
            in_specs=[SMEM_SPEC] * 6 + [
                per_source(1, tile),
                per_source(tile, features, part),
                per_source(tile, features),
                whole(forward),
                whole(backward),
                whole(unit),
            ] + [ANY_SPEC] * len(sums),
            out_specs=(per_source(particles, LANES),) + (ANY_SPEC,) * len(lengths),
            scratch_shapes=[
                pltpu.VMEM((blocks + 8, features), jnp.float32),
                pltpu.VMEM((tile, features), jnp.float32),
                pltpu.SemaphoreType.DMA((len(lengths),)),
            ],
            compiler_params=params(),
            cost_estimate=pl.CostEstimate(
                flops=slabs * tile * features * features * 9, bytes_accessed=80 * 1024 * 1024, transcendentals=0
            ),
            name="compare_and_add",
        )(
            totals_in, table_rows[:, 0], table_rows[:, 1], scale_in, index, core,
            words[:, part * tile:(part + 1) * tile].reshape(slabs, 1, tile), voxels, picture,
            forward, backward, unit, *sums,
        )
        squares = squares + more
    mine, *theirs = sums
    shared = lax.all_gather(jnp.sum(squares, axis=2), "slab")
    returned = lax.dynamic_index_in_dim(shared, lax.axis_index("slab"), axis=1, keepdims=False)
    losses = jnp.sum(returned, axis=0) / (counts.astype(jnp.float32) * 128.0)
    return mine, theirs, losses, side


def body(*arrays):
    mine, theirs, losses, side = gradient_of_slab(*arrays)
    return to_field(mine, theirs, side), losses


def solution(mesh):
    in_specs = (
        P(("groups", "slab"), None),
        P(),
        P(("groups", "slab", "dom"), None, None),
        P(("groups", "slab", "dom"), None, None),
        P(("groups", "slab", "dom"), None),
        P(("groups", "slab", "dom"), None),
        P(("groups", "slab", "dom")),
        P(("groups", "slab", "dom")),
        P(),
        P(("groups", "slab", "dom")),
    )
    out_specs = (P(None, ("groups", "dom"), "slab", None), P(("groups", "slab", "dom")))
    return jax.shard_map(body, mesh=mesh, in_specs=in_specs, out_specs=out_specs, check_vma=False)
```

```python
import functools
import math

import jax
import jax.numpy as jnp
import numpy as np
from jax import lax
from jax.experimental import pallas as pl
from jax.experimental.pallas import tpu as pltpu
from jax.sharding import PartitionSpec as P

LANES = 128
TILE = 512
COPIES = 8
GROUP = 16
VMEM_LIMIT = 56 * 1024 * 1024

SMEM_SPEC = pl.BlockSpec(memory_space=pltpu.SMEM)
VMEM_SPEC = pl.BlockSpec(memory_space=pltpu.VMEM)
ANY_SPEC = pl.BlockSpec(memory_space=pl.ANY)


def params(**extra):
    return pltpu.CompilerParams(vmem_limit_bytes=VMEM_LIMIT, **extra)


def bits_of(count):
    return (count - 1).bit_length()


def route_kernel(slabs, cap, local_bits, list_length, owner_ref, local_ref, kind_ref, counts_ref, target_ref, word_ref, totals_ref):
    rows = owner_ref.shape[0]
    rows_each = list_length // LANES
    particles = rows // rows_each
    row_id = lax.broadcasted_iota(jnp.int32, (rows, LANES), 0)
    lane_id = lax.broadcasted_iota(jnp.int32, (rows, LANES), 1)
    particle = row_id // rows_each
    position = (row_id % rows_each) * LANES + lane_id
    limit = jnp.zeros((rows, LANES), jnp.int32)
    for i in range(particles):
        limit = jnp.where(particle == i, counts_ref[i], limit)
    owner = jnp.where(position < limit, owner_ref[...], -1)
    up_to = (
        lax.broadcasted_iota(jnp.int32, (LANES, LANES), 0)
        <= lax.broadcasted_iota(jnp.int32, (LANES, LANES), 1)
    ).astype(jnp.bfloat16)
    ones = jnp.ones((LANES, LANES), jnp.bfloat16)
    before = (
        lax.broadcasted_iota(jnp.int32, (rows, rows), 1)
        < lax.broadcasted_iota(jnp.int32, (rows, rows), 0)
    ).astype(jnp.bfloat16)

    def one_slab(slab, target):
        mine = owner == slab
        hits = mine.astype(jnp.float32).astype(jnp.bfloat16)
        inside = jnp.dot(hits, up_to, preferred_element_type=jnp.float32)
        row_sum = jnp.dot(hits, ones, preferred_element_type=jnp.float32)
        above = jnp.dot(before, row_sum.astype(jnp.bfloat16), preferred_element_type=jnp.float32)
        rank = (inside + above).astype(jnp.int32) - 1
        total = (above[rows - 1:rows, :] + row_sum[rows - 1:rows, :]).astype(jnp.int32)
        totals_ref[pl.ds(slab, 1), :] = total
        return jnp.where(mine, slab * cap + rank, target)

    target = lax.fori_loop(0, slabs, one_slab, jnp.full((rows, LANES), slabs * cap, jnp.int32))
    target_ref[...] = target
    kind_bits = local_bits
    word = local_ref[...] | (kind_ref[...] << kind_bits) | (position << (kind_bits + 2))
    word_ref[...] = word | (particle << (kind_bits + 2 + bits_of(list_length)))


def pack_kernel(slabs, cap, list_length, target_ref, word_ref, counts_ref, image_ref, meta_ref, *refs):
    out_refs, (wide_ref, staged_ref) = refs[:-2], refs[-2:]
    step = 256

    @pl.loop(0, image_ref.shape[0] // step)
    def _(i):
        at = pl.multiple_of(i * step, step)
        wide_ref[pl.ds(at, step), :] = image_ref[pl.ds(at, step), :].astype(jnp.float32)

    @pl.loop(0, counts_ref.shape[0])
    def _(particle):
        @pl.loop(0, (counts_ref[particle] + 15) // 16)
        def _(i):
            first = particle * list_length + i * 16
            targets = [target_ref[first + j] for j in range(16)]
            rows = [wide_ref[pl.ds(first + j, 1), :] for j in range(16)]
            words = [word_ref[first + j] for j in range(16)]
            for j in range(16):
                staged_ref[pl.ds(targets[j], 1), :] = rows[j]
                meta_ref[targets[j]] = words[j]

    for chunk, out_ref in enumerate(out_refs):
        width = out_ref.shape[1]

        @pl.loop(0, slabs)
        def _(slab):
            at = pl.multiple_of(slab * cap + chunk * width, width)
            out_ref[slab] = staged_ref[pl.ds(at, width), :].astype(jnp.bfloat16)


def decode_kernel(local_bits, dummy, word_ref, live_ref, index_ref):
    rows = word_ref.shape[0]
    live = live_ref[...] != 0
    index = jnp.where(live, word_ref[...] & ((1 << local_bits) - 1), dummy)
    lane = lax.broadcasted_iota(jnp.int32, (rows, LANES), 1)
    clash = jnp.zeros((rows, LANES), jnp.int32)
    for shift in range(1, GROUP):
        earlier = pltpu.roll(index, shift, 1)
        same = (earlier == index) & (lane % GROUP >= shift) & live
        clash = clash | same.astype(jnp.int32)
    shift = 1
    while shift < GROUP:
        clash = clash | pltpu.roll(clash, LANES - shift, 1)
        shift *= 2
    index_ref[...] = index | (clash << 24)


def gather_kernel(slabs, cap, index_ref, totals_ref, volume_ref, out_ref, wide_ref, staged_ref):
    blocks = volume_ref.shape[0]
    step = 256

    @pl.loop(0, blocks // step)
    def _(i):
        at = pl.multiple_of(i * step, step)
        wide_ref[pl.ds(at, step), :] = volume_ref[pl.ds(at, step), :].astype(jnp.float32)

    @pl.loop(0, slabs)
    def _(source):
        live = totals_ref[source]

        @pl.loop(0, (live + 15) // 16)
        def _(i):
            first = source * cap + i * 16
            places = [index_ref[first + j] & 0xFFFFFF for j in range(16)]
            rows = [wide_ref[pl.ds(places[j], 1), :] for j in range(16)]
            for j in range(16):
                staged_ref[pl.ds(i * 16 + j, 1), :] = rows[j]

        width = min(step, cap)

        @pl.loop(0, (live + width - 1) // width)
        def _(i):
            at = pl.multiple_of(i * width, width)
            to = pl.multiple_of(source * cap + i * width, width)
            out_ref[pl.ds(to, width), :] = staged_ref[pl.ds(at, width), :].astype(jnp.bfloat16)


def sine(angle):
    turns = jnp.floor(angle * (1.0 / math.pi) + 0.5)
    rest = angle - turns * 3.140625
    rest = rest - turns * 9.67502593994140625e-4
    rest = rest - turns * 1.509957990978376e-7
    odd = turns - 2.0 * jnp.floor(turns * 0.5)
    square = rest * rest
    poly = 2.718121e-6
    poly = poly * square - 1.9839334e-4
    poly = poly * square + 8.3333293e-3
    poly = poly * square - 1.6666667e-1
    value = rest + rest * square * poly
    return value * (1.0 - 2.0 * odd)


def slab_kernel(
    side, local_bits, list_length, particles, cap, offset, first, last,
    totals_ref, defocus_ref, phase_ref, scale_ref, index_ref, core_ref,
    word_ref, voxel_ref, image_ref, forward_ref, backward_ref, unit_ref, *rest,
):
    if not first:
        before_ref, rest = rest[0], rest[1:]
    square_ref, sum_refs, (sum_ref, staged_ref, sems) = rest[0], rest[1:-3], rest[-3:]
    source = pl.program_id(0)
    tile = word_ref.shape[2]
    blocks = sum_ref.shape[0] - 8
    features = image_ref.shape[2]
    kinds = forward_ref.shape[0] // features
    position_bits = bits_of(list_length)
    per_row = side // 8
    live = jnp.clip(totals_ref[source] - offset, 0, tile)

    def fetches():
        length = blocks // COPIES
        return [
            pltpu.make_async_copy(
                before_ref.at[pl.ds(i * length, length)], sum_ref.at[pl.ds(i * length, length)], sems.at[i]
            )
            for i in range(COPIES)
        ]

    @pl.when(source == 0)
    def _():
        if first:
            @pl.loop(0, blocks // 256)
            def _(i):
                at = pl.multiple_of(i * 256, 256)
                sum_ref[pl.ds(at, 256), :] = jnp.zeros((256, features), jnp.float32)
        else:
            for copy in fetches():
                copy.start()

    @pl.when(live == 0)
    def _():
        square_ref[...] = jnp.zeros_like(square_ref)

    @pl.when(live > 0)
    def _():
        word = word_ref[0]
        kind = (word >> local_bits) & 3
        position = (word >> (local_bits + 2)) & (list_length - 1)
        particle = (word >> (local_bits + 2 + position_bits)) & (particles - 1)
        valid = lax.broadcasted_iota(jnp.int32, (1, tile), 1) < live
        defocus = jnp.zeros((1, tile), jnp.float32)
        phase = jnp.zeros((1, tile), jnp.float32)
        scale = jnp.zeros((1, tile), jnp.float32)
        for j in range(particles):
            chosen = particle == j
            defocus = jnp.where(chosen, defocus_ref[source * particles + j], defocus)
            phase = jnp.where(chosen, phase_ref[source * particles + j], phase)
            scale = jnp.where(chosen, scale_ref[source * particles + j], scale)
        half = features // 2
        cell = lax.broadcasted_iota(jnp.int32, (half, tile), 0)
        vert = ((position // per_row) * 8 - side // 2 + cell // 8).astype(jnp.float32)
        horiz = ((position % per_row) * 8 - side // 2 + cell % 8).astype(jnp.float32)
        radius = (vert * vert + horiz * horiz) * (1.0 / float((side // 2) ** 2))
        factor = scale * sine(defocus * radius + phase)
        factor = jnp.concatenate([factor, factor], axis=0)
        contract_last = (((1,), (1,)), ((), ()))
        each_kind = lax.dot_general(
            forward_ref[...], voxel_ref[0], contract_last, preferred_element_type=jnp.float32
        )
        extracted = each_kind[0:features, :]
        for k in range(1, kinds):
            extracted = jnp.where(kind == k, each_kind[k * features:(k + 1) * features, :], extracted)
        picture = lax.dot_general(
            unit_ref[...], image_ref[0], contract_last, preferred_element_type=jnp.float32
        )
        misfit = jnp.where(valid, factor * extracted - picture, 0.0)
        squares = jnp.sum(misfit * misfit, axis=0, keepdims=True)
        which = lax.broadcasted_iota(jnp.int32, (particles, tile), 0)
        spread = jnp.where(valid & (particle == which), squares, 0.0)
        folded = spread[:, 0:LANES]
        for i in range(1, tile // LANES):
            folded = folded + spread[:, i * LANES:(i + 1) * LANES]
        square_ref[0] = folded
        weighted = (factor * misfit).astype(jnp.bfloat16)
        none = jnp.zeros_like(weighted)
        spread_back = jnp.concatenate(
            [jnp.where(kind == k, weighted, none) for k in range(kinds)], axis=0
        )
        terms = jnp.dot(backward_ref[...], spread_back, preferred_element_type=jnp.float32)
        staged_ref[...] = terms.T

    if not first:
        @pl.when(source == 0)
        def _():
            for copy in fetches():
                copy.wait()

    @pl.loop(0, (live + GROUP - 1) // GROUP)
    def _(g):
        base = source * cap + offset + g * GROUP
        marked = index_ref[base]
        places = [index_ref[base + j] & 0xFFFFFF for j in range(GROUP)]

        @pl.when(marked < (1 << 24))
        def _():
            held = [sum_ref[pl.ds(places[j], 1), :] for j in range(GROUP)]
            new = [staged_ref[pl.ds(g * GROUP + j, 1), :] for j in range(GROUP)]
            for j in range(GROUP):
                sum_ref[pl.ds(places[j], 1), :] = held[j] + new[j]

        @pl.when(marked >= (1 << 24))
        def _():
            for j in range(GROUP):
                sum_ref[pl.ds(places[j], 1), :] = (
                    sum_ref[pl.ds(places[j], 1), :] + staged_ref[pl.ds(g * GROUP + j, 1), :]
                )

    @pl.when(source == pl.num_programs(0) - 1)
    def _():
        copies = []
        if last:
            half = blocks // 2
            start = (1 - core_ref[0]) * half
            places = [core_ref[0] * half]
            for out_ref in sum_refs[1:]:
                places.append(start)
                start = start + out_ref.shape[0]
        else:
            places = [0]
        cuts = max(1, COPIES // len(places))
        for place, out_ref in zip(places, sum_refs):
            length = out_ref.shape[0] // cuts
            for i in range(cuts):
                at = pl.multiple_of(place + i * length, 8)
                copies.append(
                    pltpu.make_async_copy(
                        sum_ref.at[pl.ds(at, length)],
                        out_ref.at[pl.ds(i * length, length)],
                        sems.at[len(copies)],
                    )
                )
        for copy in copies:
            copy.start()
        for copy in copies:
            copy.wait()


def pieces_of(planes):
    if planes < 16:
        return [planes]
    return [4, 4, planes - 8]


def rotated(value, turn, length):
    real, imag = value
    if turn == 0:
        return value
    if 4 * turn == length:
        return (-imag, real)
    root = math.sqrt(0.5)
    if 8 * turn == length:
        return ((real - imag) * root, (real + imag) * root)
    if 8 * turn == 3 * length:
        return ((real + imag) * -root, (real - imag) * root)
    cos, sin = math.cos(2 * math.pi * turn / length), math.sin(2 * math.pi * turn / length)
    return (real * cos - imag * sin, real * sin + imag * cos)


def small_dft(values):
    length = len(values)
    if length == 1:
        return values
    even, odd = small_dft(values[0::2]), small_dft(values[1::2])
    low, high = [], []
    for k in range(length // 2):
        turned = rotated(odd[k], k, length)
        low.append((even[k][0] + turned[0], even[k][1] + turned[1]))
        high.append((even[k][0] - turned[0], even[k][1] - turned[1]))
    return low + high


def swap_quarters(values):
    lane = lax.broadcasted_iota(jnp.int32, values[0].shape, 1)
    low, even = lane < 64, (lane // 32) % 2 == 0
    roll = lambda value, shift: pltpu.roll(value, shift, 1)
    for first, second, shift, keep in ((0, 2, 64, low), (1, 3, 64, low), (0, 1, 32, even), (2, 3, 32, even)):
        one, two = values[first], values[second]
        values[first] = jnp.where(keep, one, roll(two, shift))
        values[second] = jnp.where(keep, roll(one, LANES - shift), two)
    return values


def in_halves(value):
    high = value.astype(jnp.bfloat16)
    return high, (value - high.astype(jnp.float32)).astype(jnp.bfloat16)


def planes_kernel(me_ref, mine_ref, theirs_ref, zblock_ref, turn_ref, wide_ref, fine_ref, *refs):
    out_refs, (high_ref, low_ref, wide_here_ref, fine_here_ref) = refs[:-4], refs[-4:]
    step = pl.program_id(1)
    count = mine_ref.shape[1]
    groups = len(out_refs)
    height, side = out_refs[0].shape[2:]

    @pl.when((step == 0) & (pl.program_id(0) == 0))
    def _():
        for part in range(2):
            for group in range(groups):
                at = pl.multiple_of(part * side + (group ^ me_ref[0]) * height, height)
                to = slice(part * side + group * height, part * side + (group + 1) * height)
                wide_here_ref[to, :] = wide_ref[pl.ds(at, height), :]
                fine_here_ref[to, :] = fine_ref[pl.ds(at, height), :]

    @pl.loop(0, count, unroll=4)
    def _(i):
        block = (mine_ref[:, i] + theirs_ref[:, i]).reshape(LANES, LANES)
        high, low = in_halves(block.T)
        both = jnp.dot(
            jnp.concatenate([high, low, high], axis=1), zblock_ref[...],
            preferred_element_type=jnp.float32,
        )
        by_cos = both[:, :LANES].reshape(8, 2, 8, LANES)
        by_sin = both[:, LANES:].reshape(8, 2, 8, LANES)
        real = by_cos[:, 0] - by_sin[:, 1]
        imag = by_sin[:, 0] + by_cos[:, 1]
        values = []
        for z in range(8):
            cos, sin = turn_ref[0, z:z + 1, :], turn_ref[1, z:z + 1, :]
            values.append((real[z] * cos - imag[z] * sin, real[z] * sin + imag[z] * cos))
        values = [jnp.concatenate(value, axis=0) for value in small_dft(values)]
        at = pl.ds(pl.multiple_of((step * count + i) * 16, 16), 16)
        for half in range(2):
            planes = swap_quarters(values[4 * half:4 * half + 4])
            for x in range(4):
                columns = slice((2 * x + half) * LANES, (2 * x + half + 1) * LANES)
                high, low = in_halves(planes[x])
                high_ref[at, columns] = high
                low_ref[at, columns] = low

    @pl.when(step == pl.num_programs(1) - 1)
    def _():
        @pl.loop(0, 4)
        def _(x):
            columns = pl.ds(pl.multiple_of(x * side, side), side)
            product = functools.partial(jnp.dot, preferred_element_type=jnp.float32)
            high = high_ref[:, columns]
            wide = wide_here_ref[...]
            result = product(wide, high) + (
                product(wide, low_ref[:, columns]) + product(fine_here_ref[...], high)
            )
            for part in range(2):
                for group in range(groups):
                    start = part * side + group * height
                    out_refs[group][x, part] = result[start:start + height, :].astype(jnp.bfloat16)


def first_dimension_kernel(slabs, each, core_ref, *refs):
    arrays, (out_ref, mid_ref) = refs[:-2], refs[-2:]
    me = core_ref[1]
    chunks = len(arrays) // 2
    own, other = arrays[:chunks], arrays[chunks:]
    spots = [(i, at) for i, ref in enumerate(own) for at in range(ref.shape[1])]
    core = core_ref[0]
    is_first = core == 0
    sign = (1 - 2 * core).astype(jnp.float32)

    def plane(x):
        slab, rest = x // (2 * each), x % (2 * each)
        half, inner = rest // each, rest % each
        loaded = []
        for part in range(2):
            chunk, at = spots[inner]
            here = own[chunk][slab ^ me, at, part].astype(jnp.float32)
            there = other[chunk][slab ^ me, at, part].astype(jnp.float32)
            loaded.append(jnp.where(is_first, here, there) if half == 0 else jnp.where(is_first, there, here))
        return tuple(loaded)

    for low in range(16):
        values = small_dft([plane(low + 16 * high) for high in range(16)])
        for k in range(16):
            real, imag = rotated(values[k], low * k, 256)
            if low % 2:
                real, imag = real * sign, imag * sign
            mid_ref[k, low, 0] = real
            mid_ref[k, low, 1] = imag

    @pl.loop(0, 16)
    def _(k):
        values = [(mid_ref[k, low, 0], mid_ref[k, low, 1]) for low in range(16)]
        even, odd = small_dft(values[0::2]), small_dft(values[1::2])
        for m in range(8):
            turned = rotated(odd[m], m, 16)
            out_ref[0, k + 16 * m] = even[m][0] + turned[0]
            out_ref[1, k + 16 * m] = even[m][1] + turned[1]


def host_halves(table):
    high = table.astype(jnp.bfloat16)
    return high, (table - high.astype(np.float64)).astype(jnp.bfloat16)


def transform_tables(side):
    per_row = side // 8
    grid = np.arange(per_row)
    angle = 2 * np.pi * np.outer(grid, grid) / per_row
    zblock = np.concatenate([np.kron(np.eye(4), np.cos(angle)), np.kron(np.eye(4), np.sin(angle))], axis=1)
    high, low = host_halves(zblock)
    zblock = np.concatenate([high, high, low], axis=0)
    angle = 2 * np.pi * np.outer(np.arange(8), grid) / side
    turns = np.stack([np.tile(np.cos(angle), (1, 4)), np.tile(np.sin(angle), (1, 4))]).astype(np.float32)
    cells = np.arange(side)
    angle = 2 * np.pi * (np.outer(cells, cells) % side) / side
    cos, sin = np.cos(angle).reshape(side, per_row, 1, 8), np.sin(angle).reshape(side, per_row, 1, 8)
    matrix = np.concatenate(
        [np.concatenate([cos, -sin], axis=2), np.concatenate([sin, cos], axis=2)], axis=0
    ).reshape(2 * side, 2 * side) / float(side) ** 1.5
    return (zblock, turns) + host_halves(matrix)


def to_field(mine, theirs_sent, side):
    slabs = lax.axis_size("slab")
    per_row = side // 8
    each = side // slabs // 2
    height = side // slabs
    groups = slabs if height % 16 == 0 else 1
    me = lax.axis_index("slab").astype(jnp.int32) if groups == slabs else jnp.int32(0)
    tables = [jnp.asarray(table) for table in transform_tables(side)]
    swap = [(0, 1), (1, 0)]
    theirs = [lax.ppermute(chunk, "dom", swap) for chunk in theirs_sent]
    grid_shape = (-1, per_row, per_row, LANES)
    mine = mine.reshape(grid_shape)
    short = max(0, 4 - each)
    if short:
        mine = jnp.pad(mine, ((0, short), (0, 0), (0, 0), (0, 0)))
    yblocks = 8
    own, other = [], []
    first_quad = 0
    for real_planes, added in zip(pieces_of(each), theirs):
        added = added.reshape(grid_shape)
        if short:
            added = jnp.pad(added, ((0, short), (0, 0), (0, 0), (0, 0)))
        held = real_planes + short
        quads = held // 4
        whole = lambda table: pl.BlockSpec(table.shape, lambda q, y: (0,) * table.ndim)
        sent = pl.pallas_call(
            planes_kernel,
            grid=(quads, per_row // yblocks),
            out_shape=(jax.ShapeDtypeStruct((held, 2, side // groups, side), jnp.bfloat16),) * groups,
            in_specs=[SMEM_SPEC] + [
                pl.BlockSpec((4, yblocks, per_row, LANES), lambda q, y, at=first_quad: (at + q, y, 0, 0)),
                pl.BlockSpec((4, yblocks, per_row, LANES), lambda q, y: (q, y, 0, 0)),
            ] + [whole(table) for table in tables],
            out_specs=(pl.BlockSpec((4, 2, side // groups, side), lambda q, y: (q, 0, 0, 0)),) * groups,
            scratch_shapes=[
                pltpu.VMEM((2 * side, 4 * side), jnp.bfloat16),
                pltpu.VMEM((2 * side, 4 * side), jnp.bfloat16),
                pltpu.VMEM((2 * side, 2 * side), jnp.bfloat16),
                pltpu.VMEM((2 * side, 2 * side), jnp.bfloat16),
            ],
            compiler_params=params(),
            cost_estimate=pl.CostEstimate(
                flops=held * 8 * side**3, bytes_accessed=held * 4 * side**2 * 8, transcendentals=0
            ),
            name="transform_planes",
        )(me.reshape(1), mine, added, *tables)
        if groups != slabs:
            sent = sent[0].reshape(-1, 2, slabs, height, side).transpose(2, 0, 1, 3, 4)[:, :real_planes]
            got = lax.all_to_all(sent, "slab", split_axis=0, concat_axis=0, tiled=True)
        else:
            got = jnp.stack([sent[0]] + [
                lax.ppermute(sent[i], "slab", [(slab, slab ^ i) for slab in range(slabs)])
                for i in range(1, slabs)
            ])
        first_quad += quads
        own.append(got)
        other.append(lax.ppermute(got, "dom", swap))
    rows = min(16, height)
    arrays = own + other
    return pl.pallas_call(
        functools.partial(first_dimension_kernel, slabs, each),
        grid=(height // rows, side // LANES),
        out_shape=jax.ShapeDtypeStruct((2, side // 2, height, side), jnp.float32),
        in_specs=[SMEM_SPEC] + [
            pl.BlockSpec(array.shape[:3] + (rows, LANES), lambda y, z: (0, 0, 0, y, z))
            for array in arrays
        ],
        out_specs=pl.BlockSpec((2, side // 2, rows, LANES), lambda y, z: (0, 0, y, z)),
        scratch_shapes=[pltpu.VMEM((16, 16, 2, rows, LANES), jnp.float32)],
        compiler_params=params(),
        name="transform_first",
    )(jnp.stack([lax.axis_index("dom").astype(jnp.int32), me]), *arrays)


def gradient_of_slab(volume, kernels, images, owners, local_block, kinds, counts, ctf_code, ctf_table, scales):
    slabs = lax.axis_size("slab")
    particles, list_length, features = images.shape
    side = math.isqrt(list_length * 64)
    entries = particles * list_length
    cap = 2 * entries // slabs
    slots = slabs * cap
    blocks = volume.shape[0]
    local_bits = bits_of(blocks)
    kind_count = kernels.shape[0]
    rows = entries // LANES
    int_rows = jax.ShapeDtypeStruct((rows, LANES), jnp.int32)

    target, word, totals = pl.pallas_call(
        functools.partial(route_kernel, slabs, cap, local_bits, list_length),
        out_shape=(int_rows, int_rows, jax.ShapeDtypeStruct((slabs, LANES), jnp.int32)),
        in_specs=[VMEM_SPEC, VMEM_SPEC, VMEM_SPEC, SMEM_SPEC],
        out_specs=(VMEM_SPEC, VMEM_SPEC, VMEM_SPEC),
        compiler_params=params(),
        name="route",
    )(
        owners.reshape(rows, LANES), local_block.reshape(rows, LANES), kinds.reshape(rows, LANES), counts
    )
    target, word = target.reshape(entries), word.reshape(entries)
    parts = max(1, cap // TILE)
    tile = cap // parts
    meta, *packed = pl.pallas_call(
        functools.partial(pack_kernel, slabs, cap, list_length),
        out_shape=(jax.ShapeDtypeStruct((slots + 1024,), jnp.int32),)
        + (jax.ShapeDtypeStruct((slabs, tile, features), jnp.bfloat16),) * parts,
        in_specs=[SMEM_SPEC, SMEM_SPEC, SMEM_SPEC, VMEM_SPEC],
        out_specs=(SMEM_SPEC,) + (VMEM_SPEC,) * parts,
        scratch_shapes=[
            pltpu.VMEM((entries, features), jnp.float32),
            pltpu.VMEM((slots + 8, features), jnp.float32),
        ],
        compiler_params=params(),
        name="pack",
    )(target, word, counts, images.reshape(entries, features))

    code = ctf_code | ((scales.astype(jnp.float32) * 256.0).astype(jnp.int32) << 8)
    header = jnp.concatenate(
        [
            totals[:, 0:1],
            jnp.broadcast_to(code[None, :], (slabs, particles)),
            jnp.zeros((slabs, LANES - 1 - particles), jnp.int32),
        ],
        axis=1,
    )
    sent = jnp.concatenate([meta[:slots].reshape(slabs, cap), header], axis=1)
    arrived = lax.all_to_all(sent, "slab", split_axis=0, concat_axis=0, tiled=True)
    words = arrived[:, :cap]
    totals_in = arrived[:, cap]
    codes_in = arrived[:, cap + 1:cap + 1 + particles]
    live = (jnp.arange(cap, dtype=jnp.int32)[None, :] < totals_in[:, None]).astype(jnp.int32)
    table_rows = ctf_table[(codes_in & 255).reshape(-1)]
    scale_in = (codes_in >> 8).astype(jnp.float32).reshape(-1) * (1.0 / 256.0)

    index = pl.pallas_call(
        functools.partial(decode_kernel, local_bits, blocks),
        out_shape=jax.ShapeDtypeStruct((slots // LANES, LANES), jnp.int32),
        in_specs=[VMEM_SPEC, VMEM_SPEC],
        out_specs=VMEM_SPEC,
        compiler_params=params(),
        name="decode",
    )(words.reshape(slots // LANES, LANES), live.reshape(slots // LANES, LANES))
    index = index.reshape(slots)
    voxels = pl.pallas_call(
        functools.partial(gather_kernel, slabs, cap),
        out_shape=jax.ShapeDtypeStruct((slots, features), jnp.bfloat16),
        in_specs=[SMEM_SPEC, SMEM_SPEC, VMEM_SPEC],
        out_specs=VMEM_SPEC,
        scratch_shapes=[
            pltpu.VMEM((blocks + 8, features), jnp.float32),
            pltpu.VMEM((cap, features), jnp.float32),
        ],
        compiler_params=params(),
        cost_estimate=pl.CostEstimate(flops=0, bytes_accessed=100 * 1024 * 1024, transcendentals=0),
        name="read_voxels",
    )(index, totals_in, volume)

    forward = jnp.transpose(kernels, (0, 2, 1)).reshape(kind_count * features, features)
    backward = kernels.reshape(kind_count, 2, 8, 8, features).transpose(3, 1, 2, 0, 4)
    backward = backward.reshape(features, kind_count * features)
    unit = jnp.eye(features, dtype=jnp.bfloat16)
    per_source = lambda length, width, at=0: pl.BlockSpec((1, length, width), lambda s: (s, at, 0))
    whole = lambda table: pl.BlockSpec(table.shape, lambda s: (0,) * table.ndim)
    voxels = voxels.reshape(slabs, cap, features)
    core = lax.axis_index("dom").astype(jnp.int32).reshape(1)
    plane_blocks = (side // 8) ** 2
    pieces = [planes * plane_blocks for planes in pieces_of(side // slabs // 2)]
    squares, sums, behind = 0.0, (), [voxels]
    for part in range(parts):
        first, last = part == 0, part == parts - 1
        if not first:
            packed[part], earlier = lax.optimization_barrier((packed[part], behind[part - 1]))
            if part == 1:
                voxels = earlier
        picture = lax.all_to_all(packed[part], "slab", split_axis=0, concat_axis=0, tiled=True)
        lengths = [blocks // 2] + pieces if last else [blocks]
        more, *sums = pl.pallas_call(
            functools.partial(
                slab_kernel, side, local_bits, list_length, particles, cap, part * tile, first, last
            ),
            grid=(slabs,),
            out_shape=(jax.ShapeDtypeStruct((slabs, particles, LANES), jnp.float32),)
            + tuple(jax.ShapeDtypeStruct((length, features), jnp.float32) for length in lengths),
            in_specs=[SMEM_SPEC] * 6 + [
                per_source(1, tile),
                per_source(tile, features, part),
                per_source(tile, features),
                whole(forward),
                whole(backward),
                whole(unit),
            ] + [ANY_SPEC] * len(sums),
            out_specs=(per_source(particles, LANES),) + (ANY_SPEC,) * len(lengths),
            scratch_shapes=[
                pltpu.VMEM((blocks + 8, features), jnp.float32),
                pltpu.VMEM((tile, features), jnp.float32),
                pltpu.SemaphoreType.DMA((COPIES,)),
            ],
            compiler_params=params(),
            cost_estimate=pl.CostEstimate(flops=0, bytes_accessed=16 * 1024 * 1024, transcendentals=0),
            name="compare_and_add",
        )(
            totals_in, table_rows[:, 0], table_rows[:, 1], scale_in, index, core,
            words[:, part * tile:(part + 1) * tile].reshape(slabs, 1, tile), voxels, picture,
            forward, backward, unit, *sums,
        )
        squares = squares + more
        behind.append(more)
    mine, *theirs = sums
    shared = lax.all_gather(jnp.sum(squares, axis=2), "slab")
    returned = lax.dynamic_index_in_dim(shared, lax.axis_index("slab"), axis=1, keepdims=False)
    losses = jnp.sum(returned, axis=0) / (counts.astype(jnp.float32) * 128.0)
    return mine, theirs, losses, side


def body(*arrays):
    mine, theirs, losses, side = gradient_of_slab(*arrays)
    return to_field(mine, theirs, side), losses


def solution(mesh):
    in_specs = (
        P(("groups", "slab"), None),
        P(),
        P(("groups", "slab", "dom"), None, None),
        P(("groups", "slab", "dom"), None, None),
        P(("groups", "slab", "dom"), None),
        P(("groups", "slab", "dom"), None),
        P(("groups", "slab", "dom")),
        P(("groups", "slab", "dom")),
        P(),
        P(("groups", "slab", "dom")),
    )
    out_specs = (P(None, ("groups", "dom"), "slab", None), P(("groups", "slab", "dom")))
    return jax.shard_map(body, mesh=mesh, in_specs=in_specs, out_specs=out_specs, check_vma=False)
```

```python
import functools
import math

import jax
import jax.numpy as jnp
import numpy as np
from jax import lax
from jax.experimental import pallas as pl
from jax.experimental.pallas import tpu as pltpu
from jax.sharding import PartitionSpec as P

LANES = 128
TILE = 512
GROUP = 16
VMEM_LIMIT = 56 * 1024 * 1024

SMEM_SPEC = pl.BlockSpec(memory_space=pltpu.SMEM)
VMEM_SPEC = pl.BlockSpec(memory_space=pltpu.VMEM)
ANY_SPEC = pl.BlockSpec(memory_space=pl.ANY)


def params(**extra):
    return pltpu.CompilerParams(vmem_limit_bytes=VMEM_LIMIT, **extra)


def bits_of(count):
    return (count - 1).bit_length()


def route_kernel(slabs, cap, local_bits, list_length, owner_ref, local_ref, kind_ref, counts_ref, target_ref, word_ref, totals_ref):
    rows = owner_ref.shape[0]
    rows_each = list_length // LANES
    particles = rows // rows_each
    row_id = lax.broadcasted_iota(jnp.int32, (rows, LANES), 0)
    lane_id = lax.broadcasted_iota(jnp.int32, (rows, LANES), 1)
    particle = row_id // rows_each
    position = (row_id % rows_each) * LANES + lane_id
    limit = jnp.zeros((rows, LANES), jnp.int32)
    for i in range(particles):
        limit = jnp.where(particle == i, counts_ref[i], limit)
    owner = jnp.where(position < limit, owner_ref[...], -1)
    up_to = (
        lax.broadcasted_iota(jnp.int32, (LANES, LANES), 0)
        <= lax.broadcasted_iota(jnp.int32, (LANES, LANES), 1)
    ).astype(jnp.bfloat16)
    ones = jnp.ones((LANES, LANES), jnp.bfloat16)
    before = (
        lax.broadcasted_iota(jnp.int32, (rows, rows), 1)
        < lax.broadcasted_iota(jnp.int32, (rows, rows), 0)
    ).astype(jnp.bfloat16)

    def one_slab(slab, target):
        mine = owner == slab
        hits = mine.astype(jnp.float32).astype(jnp.bfloat16)
        inside = jnp.dot(hits, up_to, preferred_element_type=jnp.float32)
        row_sum = jnp.dot(hits, ones, preferred_element_type=jnp.float32)
        above = jnp.dot(before, row_sum.astype(jnp.bfloat16), preferred_element_type=jnp.float32)
        rank = (inside + above).astype(jnp.int32) - 1
        total = (above[rows - 1:rows, :] + row_sum[rows - 1:rows, :]).astype(jnp.int32)
        totals_ref[pl.ds(slab, 1), :] = total
        return jnp.where(mine, slab * cap + rank, target)

    target = lax.fori_loop(0, slabs, one_slab, jnp.full((rows, LANES), slabs * cap, jnp.int32))
    target_ref[...] = target
    kind_bits = local_bits
    word = local_ref[...] | (kind_ref[...] << kind_bits) | (position << (kind_bits + 2))
    word_ref[...] = word | (particle << (kind_bits + 2 + bits_of(list_length)))


def pack_kernel(slabs, cap, list_length, target_ref, word_ref, counts_ref, image_ref, meta_ref, *refs):
    out_refs, (wide_ref, staged_ref) = refs[:-2], refs[-2:]
    step = 256

    @pl.loop(0, image_ref.shape[0] // step)
    def _(i):
        at = pl.multiple_of(i * step, step)
        wide_ref[pl.ds(at, step), :] = image_ref[pl.ds(at, step), :].astype(jnp.float32)

    @pl.loop(0, counts_ref.shape[0])
    def _(particle):
        @pl.loop(0, (counts_ref[particle] + 15) // 16)
        def _(i):
            first = particle * list_length + i * 16
            targets = [target_ref[first + j] for j in range(16)]
            rows = [wide_ref[pl.ds(first + j, 1), :] for j in range(16)]
            words = [word_ref[first + j] for j in range(16)]
            for j in range(16):
                staged_ref[pl.ds(targets[j], 1), :] = rows[j]
                meta_ref[targets[j]] = words[j]

    for chunk, out_ref in enumerate(out_refs):
        width = out_ref.shape[1]

        @pl.loop(0, slabs)
        def _(slab):
            at = pl.multiple_of(slab * cap + chunk * width, width)
            out_ref[slab] = staged_ref[pl.ds(at, width), :].astype(jnp.bfloat16)


def decode_kernel(local_bits, dummy, word_ref, live_ref, index_ref):
    rows = word_ref.shape[0]
    live = live_ref[...] != 0
    index = jnp.where(live, word_ref[...] & ((1 << local_bits) - 1), dummy)
    lane = lax.broadcasted_iota(jnp.int32, (rows, LANES), 1)
    clash = jnp.zeros((rows, LANES), jnp.int32)
    for shift in range(1, GROUP):
        earlier = pltpu.roll(index, shift, 1)
        same = (earlier == index) & (lane % GROUP >= shift) & live
        clash = clash | same.astype(jnp.int32)
    shift = 1
    while shift < GROUP:
        clash = clash | pltpu.roll(clash, LANES - shift, 1)
        shift *= 2
    index_ref[...] = index | (clash << 24)


def gather_kernel(slabs, cap, index_ref, totals_ref, volume_ref, *refs):
    out_refs, (wide_ref, staged_ref) = refs[:-2], refs[-2:]
    blocks = volume_ref.shape[0]
    step = 256

    @pl.loop(0, blocks // step)
    def _(i):
        at = pl.multiple_of(i * step, step)
        wide_ref[pl.ds(at, step), :] = volume_ref[pl.ds(at, step), :].astype(jnp.float32)

    @pl.loop(0, slabs)
    def _(source):
        live = totals_ref[source]

        @pl.loop(0, (live + 15) // 16)
        def _(i):
            first = source * cap + i * 16
            places = [index_ref[first + j] & 0xFFFFFF for j in range(16)]
            rows = [wide_ref[pl.ds(places[j], 1), :] for j in range(16)]
            for j in range(16):
                staged_ref[pl.ds(i * 16 + j, 1), :] = rows[j]

        for chunk, out_ref in enumerate(out_refs):
            width = out_ref.shape[1]

            @pl.when(live > chunk * width)
            def _():
                out_ref[source] = staged_ref[chunk * width:(chunk + 1) * width, :].astype(jnp.bfloat16)


def sine(angle):
    turns = jnp.floor(angle * (1.0 / math.pi) + 0.5)
    rest = angle - turns * 3.140625
    rest = rest - turns * 9.67502593994140625e-4
    rest = rest - turns * 1.509957990978376e-7
    odd = turns - 2.0 * jnp.floor(turns * 0.5)
    square = rest * rest
    poly = 2.718121e-6
    poly = poly * square - 1.9839334e-4
    poly = poly * square + 8.3333293e-3
    poly = poly * square - 1.6666667e-1
    value = rest + rest * square * poly
    return value * (1.0 - 2.0 * odd)


def slab_kernel(
    side, local_bits, list_length, particles, cap, offset, first, last,
    totals_ref, defocus_ref, phase_ref, scale_ref, index_ref, core_ref,
    word_ref, voxel_ref, image_ref, forward_ref, backward_ref, unit_ref, *rest,
):
    if not first:
        rest = rest[1:]
    square_ref, sum_ref, out_refs, (staged_ref, sems) = rest[0], rest[1], rest[2:-2], rest[-2:]
    slabs, _, tile = word_ref.shape
    blocks = sum_ref.shape[0] - 8
    features = image_ref.shape[2]
    kinds = forward_ref.shape[0] // features
    position_bits = bits_of(list_length)
    per_row = side // 8

    if first:
        @pl.loop(0, blocks // 256)
        def _(i):
            at = pl.multiple_of(i * 256, 256)
            sum_ref[pl.ds(at, 256), :] = jnp.zeros((256, features), jnp.float32)

    @pl.loop(0, slabs)
    def _(source):
        live = jnp.clip(totals_ref[source] - offset, 0, tile)

        @pl.when(live == 0)
        def _():
            square_ref[source] = jnp.zeros((particles, LANES), jnp.float32)

        @pl.when(live > 0)
        def _():
            word = word_ref[source]
            kind = (word >> local_bits) & 3
            position = (word >> (local_bits + 2)) & (list_length - 1)
            particle = (word >> (local_bits + 2 + position_bits)) & (particles - 1)
            valid = lax.broadcasted_iota(jnp.int32, (1, tile), 1) < live
            defocus = jnp.zeros((1, tile), jnp.float32)
            phase = jnp.zeros((1, tile), jnp.float32)
            scale = jnp.zeros((1, tile), jnp.float32)
            for j in range(particles):
                chosen = particle == j
                defocus = jnp.where(chosen, defocus_ref[source * particles + j], defocus)
                phase = jnp.where(chosen, phase_ref[source * particles + j], phase)
                scale = jnp.where(chosen, scale_ref[source * particles + j], scale)
            half = features // 2
            cell = lax.broadcasted_iota(jnp.int32, (half, tile), 0)
            vert = ((position // per_row) * 8 - side // 2 + cell // 8).astype(jnp.float32)
            horiz = ((position % per_row) * 8 - side // 2 + cell % 8).astype(jnp.float32)
            radius = (vert * vert + horiz * horiz) * (1.0 / float((side // 2) ** 2))
            factor = scale * sine(defocus * radius + phase)
            factor = jnp.concatenate([factor, factor], axis=0)
            contract_last = (((1,), (1,)), ((), ()))
            each_kind = lax.dot_general(
                forward_ref[...], voxel_ref[source], contract_last, preferred_element_type=jnp.float32
            )
            extracted = each_kind[0:features, :]
            for k in range(1, kinds):
                extracted = jnp.where(kind == k, each_kind[k * features:(k + 1) * features, :], extracted)
            picture = lax.dot_general(
                unit_ref[...], image_ref[source], contract_last, preferred_element_type=jnp.float32
            )
            misfit = jnp.where(valid, factor * extracted - picture, 0.0)
            squares = jnp.sum(misfit * misfit, axis=0, keepdims=True)
            which = lax.broadcasted_iota(jnp.int32, (particles, tile), 0)
            spread = jnp.where(valid & (particle == which), squares, 0.0)
            folded = spread[:, 0:LANES]
            for i in range(1, tile // LANES):
                folded = folded + spread[:, i * LANES:(i + 1) * LANES]
            square_ref[source] = folded
            weighted = (factor * misfit).astype(jnp.bfloat16)
            none = jnp.zeros_like(weighted)
            spread_back = jnp.concatenate(
                [jnp.where(kind == k, weighted, none) for k in range(kinds)], axis=0
            )
            terms = jnp.dot(backward_ref[...], spread_back, preferred_element_type=jnp.float32)
            staged_ref[...] = terms.T

        @pl.loop(0, (live + GROUP - 1) // GROUP)
        def _(g):
            base = source * cap + offset + g * GROUP
            marked = index_ref[base]
            places = [index_ref[base + j] & 0xFFFFFF for j in range(GROUP)]

            @pl.when(marked < (1 << 24))
            def _():
                held = [sum_ref[pl.ds(places[j], 1), :] for j in range(GROUP)]
                new = [staged_ref[pl.ds(g * GROUP + j, 1), :] for j in range(GROUP)]
                for j in range(GROUP):
                    sum_ref[pl.ds(places[j], 1), :] = held[j] + new[j]

            @pl.when(marked >= (1 << 24))
            def _():
                for j in range(GROUP):
                    sum_ref[pl.ds(places[j], 1), :] = (
                        sum_ref[pl.ds(places[j], 1), :] + staged_ref[pl.ds(g * GROUP + j, 1), :]
                    )

    if last:
        half = blocks // 2
        start = (1 - core_ref[0]) * half
        places = [core_ref[0] * half]
        for out_ref in out_refs[1:]:
            places.append(start)
            start = start + out_ref.shape[0]
        copies = []
        for i, (place, out_ref) in enumerate(zip(places, out_refs)):
            length = out_ref.shape[0]
            at = pl.multiple_of(place, 8)
            copies.append(pltpu.make_async_copy(sum_ref.at[pl.ds(at, length)], out_ref, sems.at[i]))
        for copy in copies:
            copy.start()
        for copy in copies:
            copy.wait()


def pieces_of(planes):
    if planes < 16:
        return [planes]
    return [4, planes - 4]


def rotated(value, turn, length):
    real, imag = value
    if turn == 0:
        return value
    if 4 * turn == length:
        return (-imag, real)
    root = math.sqrt(0.5)
    if 8 * turn == length:
        return ((real - imag) * root, (real + imag) * root)
    if 8 * turn == 3 * length:
        return ((real + imag) * -root, (real - imag) * root)
    cos, sin = math.cos(2 * math.pi * turn / length), math.sin(2 * math.pi * turn / length)
    return (real * cos - imag * sin, real * sin + imag * cos)


def small_dft(values):
    length = len(values)
    if length == 1:
        return values
    even, odd = small_dft(values[0::2]), small_dft(values[1::2])
    low, high = [], []
    for k in range(length // 2):
        turned = rotated(odd[k], k, length)
        low.append((even[k][0] + turned[0], even[k][1] + turned[1]))
        high.append((even[k][0] - turned[0], even[k][1] - turned[1]))
    return low + high


def swap_quarters(values):
    lane = lax.broadcasted_iota(jnp.int32, values[0].shape, 1)
    low, even = lane < 64, (lane // 32) % 2 == 0
    roll = lambda value, shift: pltpu.roll(value, shift, 1)
    for first, second, shift, keep in ((0, 2, 64, low), (1, 3, 64, low), (0, 1, 32, even), (2, 3, 32, even)):
        one, two = values[first], values[second]
        values[first] = jnp.where(keep, one, roll(two, shift))
        values[second] = jnp.where(keep, roll(one, LANES - shift), two)
    return values


def in_halves(value):
    high = value.astype(jnp.bfloat16)
    return high, (value - high.astype(jnp.float32)).astype(jnp.bfloat16)


def planes_kernel(mine_ref, theirs_ref, zblock_ref, turn_ref, wide_ref, fine_ref, out_ref, high_ref, low_ref):
    step = pl.program_id(1)
    count = mine_ref.shape[1]
    groups, side = out_ref.shape[0], out_ref.shape[4]
    height = side // groups

    @pl.loop(0, count, unroll=4)
    def _(i):
        block = (mine_ref[:, i] + theirs_ref[:, i]).reshape(LANES, LANES)
        high, low = in_halves(block.T)
        both = jnp.dot(
            jnp.concatenate([high, low, high], axis=1), zblock_ref[...],
            preferred_element_type=jnp.float32,
        )
        by_cos = both[:, :LANES].reshape(8, 2, 8, LANES)
        by_sin = both[:, LANES:].reshape(8, 2, 8, LANES)
        real = by_cos[:, 0] - by_sin[:, 1]
        imag = by_sin[:, 0] + by_cos[:, 1]
        values = []
        for z in range(8):
            cos, sin = turn_ref[0, z:z + 1, :], turn_ref[1, z:z + 1, :]
            values.append((real[z] * cos - imag[z] * sin, real[z] * sin + imag[z] * cos))
        values = [jnp.concatenate(value, axis=0) for value in small_dft(values)]
        at = pl.ds(pl.multiple_of((step * count + i) * 16, 16), 16)
        for half in range(2):
            planes = swap_quarters(values[4 * half:4 * half + 4])
            for x in range(4):
                columns = slice((2 * x + half) * LANES, (2 * x + half + 1) * LANES)
                high, low = in_halves(planes[x])
                high_ref[at, columns] = high
                low_ref[at, columns] = low

    @pl.when(step == pl.num_programs(1) - 1)
    def _():
        @pl.loop(0, 4)
        def _(x):
            columns = pl.ds(pl.multiple_of(x * side, side), side)
            product = functools.partial(jnp.dot, preferred_element_type=jnp.float32)
            high = high_ref[:, columns]
            result = product(wide_ref[...], high) + (
                product(wide_ref[...], low_ref[:, columns]) + product(fine_ref[...], high)
            )
            for part in range(2):
                for group in range(groups):
                    start = part * side + group * height
                    out_ref[group, x, part] = result[start:start + height, :].astype(jnp.bfloat16)


def first_dimension_kernel(slabs, each, core_ref, *refs):
    arrays, (out_ref, mid_ref) = refs[:-2], refs[-2:]
    chunks = len(arrays) // 2
    own, other = arrays[:chunks], arrays[chunks:]
    spots = [(i, at) for i, ref in enumerate(own) for at in range(ref.shape[1])]
    core = core_ref[0]
    is_first = core == 0
    sign = (1 - 2 * core).astype(jnp.float32)

    def plane(x):
        slab, rest = x // (2 * each), x % (2 * each)
        half, inner = rest // each, rest % each
        loaded = []
        for part in range(2):
            chunk, at = spots[inner]
            here = own[chunk][slab, at, part].astype(jnp.float32)
            there = other[chunk][slab, at, part].astype(jnp.float32)
            loaded.append(jnp.where(is_first, here, there) if half == 0 else jnp.where(is_first, there, here))
        return tuple(loaded)

    for low in range(16):
        values = small_dft([plane(low + 16 * high) for high in range(16)])
        for k in range(16):
            real, imag = rotated(values[k], low * k, 256)
            if low % 2:
                real, imag = real * sign, imag * sign
            mid_ref[k, low, 0] = real
            mid_ref[k, low, 1] = imag

    @pl.loop(0, 16)
    def _(k):
        values = [(mid_ref[k, low, 0], mid_ref[k, low, 1]) for low in range(16)]
        even, odd = small_dft(values[0::2]), small_dft(values[1::2])
        for m in range(8):
            turned = rotated(odd[m], m, 16)
            out_ref[0, k + 16 * m] = even[m][0] + turned[0]
            out_ref[1, k + 16 * m] = even[m][1] + turned[1]


def host_halves(table):
    high = table.astype(jnp.bfloat16)
    return high, (table - high.astype(np.float64)).astype(jnp.bfloat16)


def transform_tables(side):
    per_row = side // 8
    grid = np.arange(per_row)
    angle = 2 * np.pi * np.outer(grid, grid) / per_row
    zblock = np.concatenate([np.kron(np.eye(4), np.cos(angle)), np.kron(np.eye(4), np.sin(angle))], axis=1)
    high, low = host_halves(zblock)
    zblock = np.concatenate([high, high, low], axis=0)
    angle = 2 * np.pi * np.outer(np.arange(8), grid) / side
    turns = np.stack([np.tile(np.cos(angle), (1, 4)), np.tile(np.sin(angle), (1, 4))]).astype(np.float32)
    cells = np.arange(side)
    angle = 2 * np.pi * (np.outer(cells, cells) % side) / side
    cos, sin = np.cos(angle).reshape(side, per_row, 1, 8), np.sin(angle).reshape(side, per_row, 1, 8)
    matrix = np.concatenate(
        [np.concatenate([cos, -sin], axis=2), np.concatenate([sin, cos], axis=2)], axis=0
    ).reshape(2 * side, 2 * side) / float(side) ** 1.5
    return (zblock, turns) + host_halves(matrix)


def to_field(mine, theirs_sent, losses, side):
    slabs = lax.axis_size("slab")
    per_row = side // 8
    each = side // slabs // 2
    height = side // slabs
    groups = slabs if height % 16 == 0 else 1
    tables = [jnp.asarray(table) for table in transform_tables(side)]
    swap = [(0, 1), (1, 0)]
    theirs = [lax.ppermute(chunk, "dom", swap) for chunk in theirs_sent]
    grid_shape = (-1, per_row, per_row, LANES)
    mine = mine.reshape(grid_shape)
    short = max(0, 4 - each)
    if short:
        mine = jnp.pad(mine, ((0, short), (0, 0), (0, 0), (0, 0)))
    yblocks = 8
    own, other = [], []
    theirs[-1], losses = lax.optimization_barrier((theirs[-1], losses))
    first_quad = 0
    for real_planes, added in zip(pieces_of(each), theirs):
        added = added.reshape(grid_shape)
        if short:
            added = jnp.pad(added, ((0, short), (0, 0), (0, 0), (0, 0)))
        held = real_planes + short
        quads = held // 4
        whole = lambda table: pl.BlockSpec(table.shape, lambda q, y: (0,) * table.ndim)
        sent = pl.pallas_call(
            planes_kernel,
            grid=(quads, per_row // yblocks),
            out_shape=jax.ShapeDtypeStruct((groups, held, 2, side // groups, side), jnp.bfloat16),
            in_specs=[
                pl.BlockSpec((4, yblocks, per_row, LANES), lambda q, y, at=first_quad: (at + q, y, 0, 0)),
                pl.BlockSpec((4, yblocks, per_row, LANES), lambda q, y: (q, y, 0, 0)),
            ] + [whole(table) for table in tables],
            out_specs=pl.BlockSpec((groups, 4, 2, side // groups, side), lambda q, y: (0, q, 0, 0, 0)),
            scratch_shapes=[
                pltpu.VMEM((2 * side, 4 * side), jnp.bfloat16),
                pltpu.VMEM((2 * side, 4 * side), jnp.bfloat16),
            ],
            compiler_params=params(),
            cost_estimate=pl.CostEstimate(
                flops=held * 8 * side**3, bytes_accessed=held * 4 * side**2 * 8, transcendentals=0
            ),
            name="transform_planes",
        )(mine, added, *tables)
        if groups != slabs:
            sent = sent.reshape(-1, 2, slabs, height, side).transpose(2, 0, 1, 3, 4)[:, :real_planes]
        first_quad += quads
        got = lax.all_to_all(sent, "slab", split_axis=0, concat_axis=0, tiled=True)
        own.append(got)
        other.append(lax.ppermute(got, "dom", swap))
    rows = min(16, height)
    arrays = own + other
    field = pl.pallas_call(
        functools.partial(first_dimension_kernel, slabs, each),
        grid=(height // rows, side // LANES),
        out_shape=jax.ShapeDtypeStruct((2, side // 2, height, side), jnp.float32),
        in_specs=[SMEM_SPEC] + [
            pl.BlockSpec(array.shape[:3] + (rows, LANES), lambda y, z: (0, 0, 0, y, z))
            for array in arrays
        ],
        out_specs=pl.BlockSpec((2, side // 2, rows, LANES), lambda y, z: (0, 0, y, z)),
        scratch_shapes=[pltpu.VMEM((16, 16, 2, rows, LANES), jnp.float32)],
        compiler_params=params(),
        name="transform_first",
    )(lax.axis_index("dom").astype(jnp.int32).reshape(1), *arrays)
    return field, losses


def gradient_of_slab(volume, kernels, images, owners, local_block, kinds, counts, ctf_code, ctf_table, scales):
    slabs = lax.axis_size("slab")
    particles, list_length, features = images.shape
    side = math.isqrt(list_length * 64)
    entries = particles * list_length
    cap = 2 * entries // slabs
    slots = slabs * cap
    blocks = volume.shape[0]
    local_bits = bits_of(blocks)
    kind_count = kernels.shape[0]
    rows = entries // LANES
    int_rows = jax.ShapeDtypeStruct((rows, LANES), jnp.int32)

    target, word, totals = pl.pallas_call(
        functools.partial(route_kernel, slabs, cap, local_bits, list_length),
        out_shape=(int_rows, int_rows, jax.ShapeDtypeStruct((slabs, LANES), jnp.int32)),
        in_specs=[VMEM_SPEC, VMEM_SPEC, VMEM_SPEC, SMEM_SPEC],
        out_specs=(VMEM_SPEC, VMEM_SPEC, VMEM_SPEC),
        compiler_params=params(),
        name="route",
    )(
        owners.reshape(rows, LANES), local_block.reshape(rows, LANES), kinds.reshape(rows, LANES), counts
    )
    target, word = target.reshape(entries), word.reshape(entries)
    parts = max(1, cap // TILE)
    tile = cap // parts
    meta, *packed = pl.pallas_call(
        functools.partial(pack_kernel, slabs, cap, list_length),
        out_shape=(jax.ShapeDtypeStruct((slots + 1024,), jnp.int32),)
        + (jax.ShapeDtypeStruct((slabs, tile, features), jnp.bfloat16),) * parts,
        in_specs=[SMEM_SPEC, SMEM_SPEC, SMEM_SPEC, VMEM_SPEC],
        out_specs=(SMEM_SPEC,) + (VMEM_SPEC,) * parts,
        scratch_shapes=[
            pltpu.VMEM((entries, features), jnp.float32),
            pltpu.VMEM((slots + 8, features), jnp.float32),
        ],
        compiler_params=params(),
        name="pack",
    )(target, word, counts, images.reshape(entries, features))

    code = ctf_code | ((scales.astype(jnp.float32) * 256.0).astype(jnp.int32) << 8)
    header = jnp.concatenate(
        [
            totals[:, 0:1],
            jnp.broadcast_to(code[None, :], (slabs, particles)),
            jnp.zeros((slabs, LANES - 1 - particles), jnp.int32),
        ],
        axis=1,
    )
    sent = jnp.concatenate([meta[:slots].reshape(slabs, cap), header], axis=1)
    arrived = lax.all_to_all(sent, "slab", split_axis=0, concat_axis=0, tiled=True)
    words = arrived[:, :cap]
    totals_in = arrived[:, cap]
    codes_in = arrived[:, cap + 1:cap + 1 + particles]
    live = (jnp.arange(cap, dtype=jnp.int32)[None, :] < totals_in[:, None]).astype(jnp.int32)
    table_rows = ctf_table[(codes_in & 255).reshape(-1)]
    scale_in = (codes_in >> 8).astype(jnp.float32).reshape(-1) * (1.0 / 256.0)

    index = pl.pallas_call(
        functools.partial(decode_kernel, local_bits, blocks),
        out_shape=jax.ShapeDtypeStruct((slots // LANES, LANES), jnp.int32),
        in_specs=[VMEM_SPEC, VMEM_SPEC],
        out_specs=VMEM_SPEC,
        compiler_params=params(),
        name="decode",
    )(words.reshape(slots // LANES, LANES), live.reshape(slots // LANES, LANES))
    index = index.reshape(slots)
    voxels = list(pl.pallas_call(
        functools.partial(gather_kernel, slabs, cap),
        out_shape=(jax.ShapeDtypeStruct((slabs, tile, features), jnp.bfloat16),) * parts,
        in_specs=[SMEM_SPEC, SMEM_SPEC, VMEM_SPEC],
        out_specs=(VMEM_SPEC,) * parts,
        scratch_shapes=[
            pltpu.VMEM((blocks + 8, features), jnp.float32),
            pltpu.VMEM((cap, features), jnp.float32),
        ],
        compiler_params=params(),
        cost_estimate=pl.CostEstimate(flops=0, bytes_accessed=100 * 1024 * 1024, transcendentals=0),
        name="read_voxels",
    )(index, totals_in, volume))

    forward = jnp.transpose(kernels, (0, 2, 1)).reshape(kind_count * features, features)
    backward = kernels.reshape(kind_count, 2, 8, 8, features).transpose(3, 1, 2, 0, 4)
    backward = backward.reshape(features, kind_count * features)
    unit = jnp.eye(features, dtype=jnp.bfloat16)
    core = lax.axis_index("dom").astype(jnp.int32).reshape(1)
    plane_blocks = (side // 8) ** 2
    pieces = [planes * plane_blocks for planes in pieces_of(side // slabs // 2)]
    squares, sums, behind = 0.0, None, [voxels[0]]
    for part in range(parts):
        first, last = part == 0, part == parts - 1
        if not first:
            packed[part], earlier = lax.optimization_barrier((packed[part], behind[part - 1]))
            if part == 1:
                voxels[0] = earlier
        picture = lax.all_to_all(packed[part], "slab", split_axis=0, concat_axis=0, tiled=True)
        lengths = [blocks // 2] + pieces if last else []
        arguments = [
            totals_in, table_rows[:, 0], table_rows[:, 1], scale_in, index, core,
            words[:, part * tile:(part + 1) * tile].reshape(slabs, 1, tile), voxels[part], picture,
            forward, backward, unit,
        ]
        aliases = {}
        if not first:
            aliases = {len(arguments): 1}
            arguments.append(pltpu.with_memory_space_constraint(sums, pltpu.VMEM))
        more, sums, *halves = pl.pallas_call(
            functools.partial(
                slab_kernel, side, local_bits, list_length, particles, cap, part * tile, first, last
            ),
            out_shape=(
                jax.ShapeDtypeStruct((slabs, particles, LANES), jnp.float32),
                pltpu.VMEM((blocks + 8, features), jnp.float32),
            )
            + tuple(jax.ShapeDtypeStruct((length, features), jnp.float32) for length in lengths),
            in_specs=[SMEM_SPEC] * 6 + [VMEM_SPEC] * (len(arguments) - 6),
            out_specs=(VMEM_SPEC, VMEM_SPEC) + (ANY_SPEC,) * len(lengths),
            scratch_shapes=[
                pltpu.VMEM((tile, features), jnp.float32),
                pltpu.SemaphoreType.DMA((max(1, len(lengths)),)),
            ],
            input_output_aliases=aliases,
            compiler_params=pltpu.CompilerParams(vmem_limit_bytes=24 * 1024 * 1024),
            cost_estimate=pl.CostEstimate(flops=0, bytes_accessed=16 * 1024 * 1024, transcendentals=0),
            name="compare_and_add",
        )(*arguments)
        squares = squares + more
        behind.append(more)
    mine, *theirs = halves
    shared = lax.all_gather(jnp.sum(squares, axis=2), "slab")
    returned = lax.dynamic_index_in_dim(shared, lax.axis_index("slab"), axis=1, keepdims=False)
    losses = jnp.sum(returned, axis=0) / (counts.astype(jnp.float32) * 128.0)
    return mine, theirs, losses, side


def body(*arrays):
    mine, theirs, losses, side = gradient_of_slab(*arrays)
    return to_field(mine, theirs, losses, side)


def solution(mesh):
    in_specs = (
        P(("groups", "slab"), None),
        P(),
        P(("groups", "slab", "dom"), None, None),
        P(("groups", "slab", "dom"), None, None),
        P(("groups", "slab", "dom"), None),
        P(("groups", "slab", "dom"), None),
        P(("groups", "slab", "dom")),
        P(("groups", "slab", "dom")),
        P(),
        P(("groups", "slab", "dom")),
    )
    out_specs = (P(None, ("groups", "dom"), "slab", None), P(("groups", "slab", "dom")))
    return jax.shard_map(body, mesh=mesh, in_specs=in_specs, out_specs=out_specs, check_vma=False)
```

```python
import functools
import math

import jax
import jax.numpy as jnp
import numpy as np
from jax import lax
from jax.experimental import pallas as pl
from jax.experimental.pallas import tpu as pltpu
from jax.sharding import PartitionSpec as P

LANES = 128
TILE = 1024
GROUP = 16
VMEM_LIMIT = 56 * 1024 * 1024

SMEM_SPEC = pl.BlockSpec(memory_space=pltpu.SMEM)
VMEM_SPEC = pl.BlockSpec(memory_space=pltpu.VMEM)
ANY_SPEC = pl.BlockSpec(memory_space=pl.ANY)


def params(**extra):
    return pltpu.CompilerParams(vmem_limit_bytes=VMEM_LIMIT, **extra)


def bits_of(count):
    return (count - 1).bit_length()


def route_kernel(slabs, cap, local_bits, list_length, owner_ref, local_ref, kind_ref, counts_ref, target_ref, word_ref, totals_ref):
    rows = owner_ref.shape[0]
    rows_each = list_length // LANES
    particles = rows // rows_each
    row_id = lax.broadcasted_iota(jnp.int32, (rows, LANES), 0)
    lane_id = lax.broadcasted_iota(jnp.int32, (rows, LANES), 1)
    particle = row_id // rows_each
    position = (row_id % rows_each) * LANES + lane_id
    limit = jnp.zeros((rows, LANES), jnp.int32)
    for i in range(particles):
        limit = jnp.where(particle == i, counts_ref[i], limit)
    owner = jnp.where(position < limit, owner_ref[...], -1)
    up_to = (
        lax.broadcasted_iota(jnp.int32, (LANES, LANES), 0)
        <= lax.broadcasted_iota(jnp.int32, (LANES, LANES), 1)
    ).astype(jnp.bfloat16)
    ones = jnp.ones((LANES, LANES), jnp.bfloat16)
    before = (
        lax.broadcasted_iota(jnp.int32, (rows, rows), 1)
        < lax.broadcasted_iota(jnp.int32, (rows, rows), 0)
    ).astype(jnp.bfloat16)

    def one_slab(slab, target):
        mine = owner == slab
        hits = mine.astype(jnp.float32).astype(jnp.bfloat16)
        inside = jnp.dot(hits, up_to, preferred_element_type=jnp.float32)
        row_sum = jnp.dot(hits, ones, preferred_element_type=jnp.float32)
        above = jnp.dot(before, row_sum.astype(jnp.bfloat16), preferred_element_type=jnp.float32)
        rank = (inside + above).astype(jnp.int32) - 1
        total = (above[rows - 1:rows, :] + row_sum[rows - 1:rows, :]).astype(jnp.int32)
        totals_ref[pl.ds(slab, 1), :] = total
        return jnp.where(mine, slab * cap + rank, target)

    target = lax.fori_loop(0, slabs, one_slab, jnp.full((rows, LANES), slabs * cap, jnp.int32))
    target_ref[...] = target
    kind_bits = local_bits
    word = local_ref[...] | (kind_ref[...] << kind_bits) | (position << (kind_bits + 2))
    word_ref[...] = word | (particle << (kind_bits + 2 + bits_of(list_length)))


def pack_kernel(slabs, cap, list_length, target_ref, word_ref, counts_ref, image_ref, meta_ref, *refs):
    out_refs, (wide_ref, staged_ref) = refs[:-2], refs[-2:]
    step = 256

    @pl.loop(0, image_ref.shape[0] // step)
    def _(i):
        at = pl.multiple_of(i * step, step)
        wide_ref[pl.ds(at, step), :] = image_ref[pl.ds(at, step), :].astype(jnp.float32)

    @pl.loop(0, counts_ref.shape[0])
    def _(particle):
        @pl.loop(0, (counts_ref[particle] + 15) // 16)
        def _(i):
            first = particle * list_length + i * 16
            targets = [target_ref[first + j] for j in range(16)]
            rows = [wide_ref[pl.ds(first + j, 1), :] for j in range(16)]
            words = [word_ref[first + j] for j in range(16)]
            for j in range(16):
                staged_ref[pl.ds(targets[j], 1), :] = rows[j]
                meta_ref[targets[j]] = words[j]

    for chunk, out_ref in enumerate(out_refs):
        width = out_ref.shape[1]

        @pl.loop(0, slabs)
        def _(slab):
            at = pl.multiple_of(slab * cap + chunk * width, width)
            out_ref[slab] = staged_ref[pl.ds(at, width), :].astype(jnp.bfloat16)


def decode_kernel(local_bits, dummy, word_ref, live_ref, index_ref):
    rows = word_ref.shape[0]
    live = live_ref[...] != 0
    index = jnp.where(live, word_ref[...] & ((1 << local_bits) - 1), dummy)
    lane = lax.broadcasted_iota(jnp.int32, (rows, LANES), 1)
    clash = jnp.zeros((rows, LANES), jnp.int32)
    for shift in range(1, GROUP):
        earlier = pltpu.roll(index, shift, 1)
        same = (earlier == index) & (lane % GROUP >= shift) & live
        clash = clash | same.astype(jnp.int32)
    shift = 1
    while shift < GROUP:
        clash = clash | pltpu.roll(clash, LANES - shift, 1)
        shift *= 2
    index_ref[...] = index | (clash << 24)


def gather_kernel(slabs, cap, index_ref, totals_ref, volume_ref, *refs):
    out_refs, (wide_ref, staged_ref) = refs[:-2], refs[-2:]
    blocks = volume_ref.shape[0]
    step = 256

    @pl.loop(0, blocks // step)
    def _(i):
        at = pl.multiple_of(i * step, step)
        wide_ref[pl.ds(at, step), :] = volume_ref[pl.ds(at, step), :].astype(jnp.float32)

    @pl.loop(0, slabs)
    def _(source):
        live = totals_ref[source]

        @pl.loop(0, (live + 15) // 16)
        def _(i):
            first = source * cap + i * 16
            places = [index_ref[first + j] & 0xFFFFFF for j in range(16)]
            rows = [wide_ref[pl.ds(places[j], 1), :] for j in range(16)]
            for j in range(16):
                staged_ref[pl.ds(i * 16 + j, 1), :] = rows[j]

        for chunk, out_ref in enumerate(out_refs):
            width = out_ref.shape[1]

            @pl.when(live > chunk * width)
            def _():
                out_ref[source] = staged_ref[chunk * width:(chunk + 1) * width, :].astype(jnp.bfloat16)


def sine(angle):
    turns = jnp.floor(angle * (1.0 / math.pi) + 0.5)
    rest = angle - turns * 3.140625
    rest = rest - turns * 9.67502593994140625e-4
    rest = rest - turns * 1.509957990978376e-7
    odd = turns - 2.0 * jnp.floor(turns * 0.5)
    square = rest * rest
    poly = 2.718121e-6
    poly = poly * square - 1.9839334e-4
    poly = poly * square + 8.3333293e-3
    poly = poly * square - 1.6666667e-1
    value = rest + rest * square * poly
    return value * (1.0 - 2.0 * odd)


def slab_kernel(
    side, local_bits, list_length, particles, cap, offset, first, last,
    totals_ref, defocus_ref, phase_ref, scale_ref, index_ref, core_ref,
    word_ref, voxel_ref, image_ref, forward_ref, backward_ref, unit_ref, *rest,
):
    if not first:
        rest = rest[1:]
    square_ref, sum_ref, out_refs, (staged_ref, sems) = rest[0], rest[1], rest[2:-2], rest[-2:]
    slabs, _, tile = word_ref.shape
    blocks = sum_ref.shape[0] - 8
    features = image_ref.shape[2]
    kinds = forward_ref.shape[0] // features
    position_bits = bits_of(list_length)
    per_row = side // 8

    if first:
        @pl.loop(0, blocks // 256)
        def _(i):
            at = pl.multiple_of(i * 256, 256)
            sum_ref[pl.ds(at, 256), :] = jnp.zeros((256, features), jnp.float32)

    @pl.loop(0, slabs)
    def _(source):
        live = jnp.clip(totals_ref[source] - offset, 0, tile)

        @pl.when(live == 0)
        def _():
            square_ref[source] = jnp.zeros((particles, LANES), jnp.float32)

        @pl.when(live > 0)
        def _():
            word = word_ref[source]
            kind = (word >> local_bits) & 3
            position = (word >> (local_bits + 2)) & (list_length - 1)
            particle = (word >> (local_bits + 2 + position_bits)) & (particles - 1)
            valid = lax.broadcasted_iota(jnp.int32, (1, tile), 1) < live
            defocus = jnp.zeros((1, tile), jnp.float32)
            phase = jnp.zeros((1, tile), jnp.float32)
            scale = jnp.zeros((1, tile), jnp.float32)
            for j in range(particles):
                chosen = particle == j
                defocus = jnp.where(chosen, defocus_ref[source * particles + j], defocus)
                phase = jnp.where(chosen, phase_ref[source * particles + j], phase)
                scale = jnp.where(chosen, scale_ref[source * particles + j], scale)
            half = features // 2
            cell = lax.broadcasted_iota(jnp.int32, (half, tile), 0)
            vert = ((position // per_row) * 8 - side // 2 + cell // 8).astype(jnp.float32)
            horiz = ((position % per_row) * 8 - side // 2 + cell % 8).astype(jnp.float32)
            radius = (vert * vert + horiz * horiz) * (1.0 / float((side // 2) ** 2))
            factor = scale * sine(defocus * radius + phase)
            factor = jnp.concatenate([factor, factor], axis=0)
            contract_last = (((1,), (1,)), ((), ()))
            each_kind = lax.dot_general(
                forward_ref[...], voxel_ref[source], contract_last, preferred_element_type=jnp.float32
            )
            extracted = each_kind[0:features, :]
            for k in range(1, kinds):
                extracted = jnp.where(kind == k, each_kind[k * features:(k + 1) * features, :], extracted)
            picture = lax.dot_general(
                unit_ref[...], image_ref[source], contract_last, preferred_element_type=jnp.float32
            )
            misfit = jnp.where(valid, factor * extracted - picture, 0.0)
            squares = jnp.sum(misfit * misfit, axis=0, keepdims=True)
            which = lax.broadcasted_iota(jnp.int32, (particles, tile), 0)
            spread = jnp.where(valid & (particle == which), squares, 0.0)
            folded = spread[:, 0:LANES]
            for i in range(1, tile // LANES):
                folded = folded + spread[:, i * LANES:(i + 1) * LANES]
            square_ref[source] = folded
            weighted = (factor * misfit).astype(jnp.bfloat16)
            none = jnp.zeros_like(weighted)
            spread_back = jnp.concatenate(
                [jnp.where(kind == k, weighted, none) for k in range(kinds)], axis=0
            )
            terms = jnp.dot(backward_ref[...], spread_back, preferred_element_type=jnp.float32)
            staged_ref[...] = terms.T

        @pl.loop(0, (live + GROUP - 1) // GROUP)
        def _(g):
            base = source * cap + offset + g * GROUP
            marked = index_ref[base]
            places = [index_ref[base + j] & 0xFFFFFF for j in range(GROUP)]

            @pl.when(marked < (1 << 24))
            def _():
                held = [sum_ref[pl.ds(places[j], 1), :] for j in range(GROUP)]
                new = [staged_ref[pl.ds(g * GROUP + j, 1), :] for j in range(GROUP)]
                for j in range(GROUP):
                    sum_ref[pl.ds(places[j], 1), :] = held[j] + new[j]

            @pl.when(marked >= (1 << 24))
            def _():
                for j in range(GROUP):
                    sum_ref[pl.ds(places[j], 1), :] = (
                        sum_ref[pl.ds(places[j], 1), :] + staged_ref[pl.ds(g * GROUP + j, 1), :]
                    )

    if last:
        half = blocks // 2
        start = (1 - core_ref[0]) * half
        places = [core_ref[0] * half]
        for out_ref in out_refs[1:]:
            places.append(start)
            start = start + out_ref.shape[0]
        copies = []
        for i, (place, out_ref) in enumerate(zip(places, out_refs)):
            length = out_ref.shape[0]
            at = pl.multiple_of(place, 8)
            copies.append(pltpu.make_async_copy(sum_ref.at[pl.ds(at, length)], out_ref, sems.at[i]))
        for copy in copies:
            copy.start()
        for copy in copies:
            copy.wait()


def pieces_of(planes):
    if planes < 16:
        return [planes]
    return [4, planes - 4]


def rotated(value, turn, length):
    real, imag = value
    if turn == 0:
        return value
    if 4 * turn == length:
        return (-imag, real)
    root = math.sqrt(0.5)
    if 8 * turn == length:
        return ((real - imag) * root, (real + imag) * root)
    if 8 * turn == 3 * length:
        return ((real + imag) * -root, (real - imag) * root)
    cos, sin = math.cos(2 * math.pi * turn / length), math.sin(2 * math.pi * turn / length)
    return (real * cos - imag * sin, real * sin + imag * cos)


def small_dft(values):
    length = len(values)
    if length == 1:
        return values
    even, odd = small_dft(values[0::2]), small_dft(values[1::2])
    low, high = [], []
    for k in range(length // 2):
        turned = rotated(odd[k], k, length)
        low.append((even[k][0] + turned[0], even[k][1] + turned[1]))
        high.append((even[k][0] - turned[0], even[k][1] - turned[1]))
    return low + high


def swap_quarters(values):
    lane = lax.broadcasted_iota(jnp.int32, values[0].shape, 1)
    low, even = lane < 64, (lane // 32) % 2 == 0
    roll = lambda value, shift: pltpu.roll(value, shift, 1)
    for first, second, shift, keep in ((0, 2, 64, low), (1, 3, 64, low), (0, 1, 32, even), (2, 3, 32, even)):
        one, two = values[first], values[second]
        values[first] = jnp.where(keep, one, roll(two, shift))
        values[second] = jnp.where(keep, roll(one, LANES - shift), two)
    return values


def in_halves(value):
    high = value.astype(jnp.bfloat16)
    return high, (value - high.astype(jnp.float32)).astype(jnp.bfloat16)


def planes_kernel(mine_ref, theirs_ref, zblock_ref, turn_ref, wide_ref, fine_ref, out_ref, high_ref, low_ref):
    step = pl.program_id(1)
    count = mine_ref.shape[1]
    groups, side = out_ref.shape[0], out_ref.shape[4]
    height = side // groups

    @pl.loop(0, count, unroll=4)
    def _(i):
        block = (mine_ref[:, i] + theirs_ref[:, i]).reshape(LANES, LANES)
        high, low = in_halves(block.T)
        both = jnp.dot(
            jnp.concatenate([high, low, high], axis=1), zblock_ref[...],
            preferred_element_type=jnp.float32,
        )
        by_cos = both[:, :LANES].reshape(8, 2, 8, LANES)
        by_sin = both[:, LANES:].reshape(8, 2, 8, LANES)
        real = by_cos[:, 0] - by_sin[:, 1]
        imag = by_sin[:, 0] + by_cos[:, 1]
        values = []
        for z in range(8):
            cos, sin = turn_ref[0, z:z + 1, :], turn_ref[1, z:z + 1, :]
            values.append((real[z] * cos - imag[z] * sin, real[z] * sin + imag[z] * cos))
        values = [jnp.concatenate(value, axis=0) for value in small_dft(values)]
        at = pl.ds(pl.multiple_of((step * count + i) * 16, 16), 16)
        for half in range(2):
            planes = swap_quarters(values[4 * half:4 * half + 4])
            for x in range(4):
                columns = slice((2 * x + half) * LANES, (2 * x + half + 1) * LANES)
                high, low = in_halves(planes[x])
                high_ref[at, columns] = high
                low_ref[at, columns] = low

    @pl.when(step == pl.num_programs(1) - 1)
    def _():
        @pl.loop(0, 4)
        def _(x):
            columns = pl.ds(pl.multiple_of(x * side, side), side)
            product = functools.partial(jnp.dot, preferred_element_type=jnp.float32)
            high = high_ref[:, columns]
            result = product(wide_ref[...], high) + (
                product(wide_ref[...], low_ref[:, columns]) + product(fine_ref[...], high)
            )
            for part in range(2):
                for group in range(groups):
                    start = part * side + group * height
                    out_ref[group, x, part] = result[start:start + height, :].astype(jnp.bfloat16)


def first_dimension_kernel(slabs, each, core_ref, *refs):
    arrays, (out_ref, mid_ref) = refs[:-2], refs[-2:]
    chunks = len(arrays) // 2
    own, other = arrays[:chunks], arrays[chunks:]
    spots = [(i, at) for i, ref in enumerate(own) for at in range(ref.shape[1])]
    core = core_ref[0]
    is_first = core == 0
    sign = (1 - 2 * core).astype(jnp.float32)

    def plane(x):
        slab, rest = x // (2 * each), x % (2 * each)
        half, inner = rest // each, rest % each
        loaded = []
        for part in range(2):
            chunk, at = spots[inner]
            here = own[chunk][slab, at, part].astype(jnp.float32)
            there = other[chunk][slab, at, part].astype(jnp.float32)
            loaded.append(jnp.where(is_first, here, there) if half == 0 else jnp.where(is_first, there, here))
        return tuple(loaded)

    for low in range(16):
        values = small_dft([plane(low + 16 * high) for high in range(16)])
        for k in range(16):
            real, imag = rotated(values[k], low * k, 256)
            if low % 2:
                real, imag = real * sign, imag * sign
            mid_ref[k, low, 0] = real
            mid_ref[k, low, 1] = imag

    @pl.loop(0, 16)
    def _(k):
        values = [(mid_ref[k, low, 0], mid_ref[k, low, 1]) for low in range(16)]
        even, odd = small_dft(values[0::2]), small_dft(values[1::2])
        for m in range(8):
            turned = rotated(odd[m], m, 16)
            out_ref[0, k + 16 * m] = even[m][0] + turned[0]
            out_ref[1, k + 16 * m] = even[m][1] + turned[1]


def host_halves(table):
    high = table.astype(jnp.bfloat16)
    return high, (table - high.astype(np.float64)).astype(jnp.bfloat16)


def transform_tables(side):
    per_row = side // 8
    grid = np.arange(per_row)
    angle = 2 * np.pi * np.outer(grid, grid) / per_row
    zblock = np.concatenate([np.kron(np.eye(4), np.cos(angle)), np.kron(np.eye(4), np.sin(angle))], axis=1)
    high, low = host_halves(zblock)
    zblock = np.concatenate([high, high, low], axis=0)
    angle = 2 * np.pi * np.outer(np.arange(8), grid) / side
    turns = np.stack([np.tile(np.cos(angle), (1, 4)), np.tile(np.sin(angle), (1, 4))]).astype(np.float32)
    cells = np.arange(side)
    angle = 2 * np.pi * (np.outer(cells, cells) % side) / side
    cos, sin = np.cos(angle).reshape(side, per_row, 1, 8), np.sin(angle).reshape(side, per_row, 1, 8)
    matrix = np.concatenate(
        [np.concatenate([cos, -sin], axis=2), np.concatenate([sin, cos], axis=2)], axis=0
    ).reshape(2 * side, 2 * side) / float(side) ** 1.5
    return (zblock, turns) + host_halves(matrix)


def sum_over_slabs(partial_sums):
    slabs = partial_sums.shape[0]
    if slabs <= 8:
        me = lax.axis_index("slab")
        row = lambda i: lax.dynamic_index_in_dim(partial_sums, me ^ i, axis=0, keepdims=True)
        returned = [row(0)] + [
            lax.ppermute(row(i), "slab", [(slab, slab ^ i) for slab in range(slabs)])
            for i in range(1, slabs)
        ]
        returned = jnp.concatenate(returned)
    else:
        returned = lax.all_to_all(partial_sums, "slab", split_axis=0, concat_axis=0, tiled=True)
    return jnp.sum(returned, axis=0)


def to_field(mine, theirs_sent, partial_sums, side):
    slabs = lax.axis_size("slab")
    per_row = side // 8
    each = side // slabs // 2
    height = side // slabs
    groups = slabs if height % 16 == 0 else 1
    tables = [jnp.asarray(table) for table in transform_tables(side)]
    swap = [(0, 1), (1, 0)]
    theirs = [lax.ppermute(chunk, "dom", swap) for chunk in theirs_sent]
    grid_shape = (-1, per_row, per_row, LANES)
    mine = mine.reshape(grid_shape)
    short = max(0, 4 - each)
    if short:
        mine = jnp.pad(mine, ((0, short), (0, 0), (0, 0), (0, 0)))
    yblocks = 8
    own = []
    first_quad = 0
    before = []
    for real_planes, added in zip(pieces_of(each), theirs):
        if before:
            added, before[0] = lax.optimization_barrier((added, before[0]))
        added = added.reshape(grid_shape)
        if short:
            added = jnp.pad(added, ((0, short), (0, 0), (0, 0), (0, 0)))
        held = real_planes + short
        quads = held // 4
        whole = lambda table: pl.BlockSpec(table.shape, lambda q, y: (0,) * table.ndim)
        sent = pl.pallas_call(
            planes_kernel,
            grid=(quads, per_row // yblocks),
            out_shape=jax.ShapeDtypeStruct((groups, held, 2, side // groups, side), jnp.bfloat16),
            in_specs=[
                pl.BlockSpec((4, yblocks, per_row, LANES), lambda q, y, at=first_quad: (at + q, y, 0, 0)),
                pl.BlockSpec((4, yblocks, per_row, LANES), lambda q, y: (q, y, 0, 0)),
            ] + [whole(table) for table in tables],
            out_specs=pl.BlockSpec((groups, 4, 2, side // groups, side), lambda q, y: (0, q, 0, 0, 0)),
            scratch_shapes=[
                pltpu.VMEM((2 * side, 4 * side), jnp.bfloat16),
                pltpu.VMEM((2 * side, 4 * side), jnp.bfloat16),
            ],
            compiler_params=params(),
            cost_estimate=pl.CostEstimate(
                flops=held * 8 * side**3, bytes_accessed=held * 4 * side**2 * 8, transcendentals=0
            ),
            name="transform_planes",
        )(mine, added, *tables)
        if groups != slabs:
            sent = sent.reshape(-1, 2, slabs, height, side).transpose(2, 0, 1, 3, 4)[:, :real_planes]
        first_quad += quads
        if before:
            sent, own[-1] = lax.optimization_barrier((sent, own[-1]))
        if first_quad * 4 >= each:
            sent, partial_sums = lax.optimization_barrier((sent, partial_sums))
        before = [sent]
        got = lax.all_to_all(sent, "slab", split_axis=0, concat_axis=0, tiled=True)
        own.append(got)
    own[-1], losses = lax.optimization_barrier((own[-1], sum_over_slabs(partial_sums)))
    other = [lax.ppermute(got, "dom", swap) for got in own]
    rows = min(16, height)
    arrays = own + other
    field = pl.pallas_call(
        functools.partial(first_dimension_kernel, slabs, each),
        grid=(height // rows, side // LANES),
        out_shape=jax.ShapeDtypeStruct((2, side // 2, height, side), jnp.float32),
        in_specs=[SMEM_SPEC] + [
            pl.BlockSpec(array.shape[:3] + (rows, LANES), lambda y, z: (0, 0, 0, y, z))
            for array in arrays
        ],
        out_specs=pl.BlockSpec((2, side // 2, rows, LANES), lambda y, z: (0, 0, y, z)),
        scratch_shapes=[pltpu.VMEM((16, 16, 2, rows, LANES), jnp.float32)],
        compiler_params=params(),
        name="transform_first",
    )(lax.axis_index("dom").astype(jnp.int32).reshape(1), *arrays)
    return field, losses


def gradient_of_slab(volume, kernels, images, owners, local_block, kinds, counts, ctf_code, ctf_table, scales):
    slabs = lax.axis_size("slab")
    particles, list_length, features = images.shape
    side = math.isqrt(list_length * 64)
    entries = particles * list_length
    cap = 2 * entries // slabs
    slots = slabs * cap
    blocks = volume.shape[0]
    local_bits = bits_of(blocks)
    kind_count = kernels.shape[0]
    rows = entries // LANES
    int_rows = jax.ShapeDtypeStruct((rows, LANES), jnp.int32)

    target, word, totals = pl.pallas_call(
        functools.partial(route_kernel, slabs, cap, local_bits, list_length),
        out_shape=(int_rows, int_rows, jax.ShapeDtypeStruct((slabs, LANES), jnp.int32)),
        in_specs=[VMEM_SPEC, VMEM_SPEC, VMEM_SPEC, SMEM_SPEC],
        out_specs=(VMEM_SPEC, VMEM_SPEC, VMEM_SPEC),
        compiler_params=params(),
        name="route",
    )(
        owners.reshape(rows, LANES), local_block.reshape(rows, LANES), kinds.reshape(rows, LANES), counts
    )
    target, word = target.reshape(entries), word.reshape(entries)
    parts = max(1, cap // TILE)
    tile = cap // parts
    meta, *packed = pl.pallas_call(
        functools.partial(pack_kernel, slabs, cap, list_length),
        out_shape=(jax.ShapeDtypeStruct((slots + 1024,), jnp.int32),)
        + (jax.ShapeDtypeStruct((slabs, tile, features), jnp.bfloat16),) * parts,
        in_specs=[SMEM_SPEC, SMEM_SPEC, SMEM_SPEC, VMEM_SPEC],
        out_specs=(SMEM_SPEC,) + (VMEM_SPEC,) * parts,
        scratch_shapes=[
            pltpu.VMEM((entries, features), jnp.float32),
            pltpu.VMEM((slots + 8, features), jnp.float32),
        ],
        compiler_params=params(),
        name="pack",
    )(target, word, counts, images.reshape(entries, features))

    code = ctf_code | ((scales.astype(jnp.float32) * 256.0).astype(jnp.int32) << 8)
    header = jnp.concatenate(
        [
            totals[:, 0:1],
            jnp.broadcast_to(code[None, :], (slabs, particles)),
            jnp.zeros((slabs, LANES - 1 - particles), jnp.int32),
        ],
        axis=1,
    )
    sent = jnp.concatenate([meta[:slots].reshape(slabs, cap), header], axis=1)
    arrived = lax.all_to_all(sent, "slab", split_axis=0, concat_axis=0, tiled=True)
    words = arrived[:, :cap]
    totals_in = arrived[:, cap]
    codes_in = arrived[:, cap + 1:cap + 1 + particles]
    live = (jnp.arange(cap, dtype=jnp.int32)[None, :] < totals_in[:, None]).astype(jnp.int32)
    table_rows = ctf_table[(codes_in & 255).reshape(-1)]
    scale_in = (codes_in >> 8).astype(jnp.float32).reshape(-1) * (1.0 / 256.0)

    index = pl.pallas_call(
        functools.partial(decode_kernel, local_bits, blocks),
        out_shape=jax.ShapeDtypeStruct((slots // LANES, LANES), jnp.int32),
        in_specs=[VMEM_SPEC, VMEM_SPEC],
        out_specs=VMEM_SPEC,
        compiler_params=params(),
        name="decode",
    )(words.reshape(slots // LANES, LANES), live.reshape(slots // LANES, LANES))
    index = index.reshape(slots)
    voxels = list(pl.pallas_call(
        functools.partial(gather_kernel, slabs, cap),
        out_shape=(jax.ShapeDtypeStruct((slabs, tile, features), jnp.bfloat16),) * parts,
        in_specs=[SMEM_SPEC, SMEM_SPEC, VMEM_SPEC],
        out_specs=(VMEM_SPEC,) * parts,
        scratch_shapes=[
            pltpu.VMEM((blocks + 8, features), jnp.float32),
            pltpu.VMEM((cap, features), jnp.float32),
        ],
        compiler_params=params(),
        cost_estimate=pl.CostEstimate(flops=0, bytes_accessed=100 * 1024 * 1024, transcendentals=0),
        name="read_voxels",
    )(index, totals_in, volume))

    forward = jnp.transpose(kernels, (0, 2, 1)).reshape(kind_count * features, features)
    backward = kernels.reshape(kind_count, 2, 8, 8, features).transpose(3, 1, 2, 0, 4)
    backward = backward.reshape(features, kind_count * features)
    unit = jnp.eye(features, dtype=jnp.bfloat16)
    core = lax.axis_index("dom").astype(jnp.int32).reshape(1)
    plane_blocks = (side // 8) ** 2
    pieces = [planes * plane_blocks for planes in pieces_of(side // slabs // 2)]
    squares, sums, behind = 0.0, None, [voxels[0]]
    for part in range(parts):
        first, last = part == 0, part == parts - 1
        if not first:
            packed[part], earlier = lax.optimization_barrier((packed[part], behind[part - 1]))
            if part == 1:
                voxels[0] = earlier
        picture = lax.all_to_all(packed[part], "slab", split_axis=0, concat_axis=0, tiled=True)
        lengths = [blocks // 2] + pieces if last else []
        arguments = [
            totals_in, table_rows[:, 0], table_rows[:, 1], scale_in, index, core,
            words[:, part * tile:(part + 1) * tile].reshape(slabs, 1, tile), voxels[part], picture,
            forward, backward, unit,
        ]
        aliases = {}
        if not first:
            aliases = {len(arguments): 1}
            arguments.append(pltpu.with_memory_space_constraint(sums, pltpu.VMEM))
        more, sums, *halves = pl.pallas_call(
            functools.partial(
                slab_kernel, side, local_bits, list_length, particles, cap, part * tile, first, last
            ),
            out_shape=(
                jax.ShapeDtypeStruct((slabs, particles, LANES), jnp.float32),
                pltpu.VMEM((blocks + 8, features), jnp.float32),
            )
            + tuple(jax.ShapeDtypeStruct((length, features), jnp.float32) for length in lengths),
            in_specs=[SMEM_SPEC] * 6 + [VMEM_SPEC] * (len(arguments) - 6),
            out_specs=(VMEM_SPEC, VMEM_SPEC) + (ANY_SPEC,) * len(lengths),
            scratch_shapes=[
                pltpu.VMEM((tile, features), jnp.float32),
                pltpu.SemaphoreType.DMA((max(1, len(lengths)),)),
            ],
            input_output_aliases=aliases,
            compiler_params=pltpu.CompilerParams(vmem_limit_bytes=24 * 1024 * 1024),
            cost_estimate=pl.CostEstimate(flops=0, bytes_accessed=16 * 1024 * 1024, transcendentals=0),
            name="compare_and_add",
        )(*arguments)
        squares = squares + more
        behind.append(more)
    mine, *theirs = halves
    partial_sums = jnp.sum(squares, axis=2)
    return mine, theirs, partial_sums, side


def body(*arrays):
    mine, theirs, partial_sums, side = gradient_of_slab(*arrays)
    field, squares = to_field(mine, theirs, partial_sums, side)
    counts = arrays[6]
    return field, squares / (counts.astype(jnp.float32) * 128.0)


def solution(mesh):
    in_specs = (
        P(("groups", "slab"), None),
        P(),
        P(("groups", "slab", "dom"), None, None),
        P(("groups", "slab", "dom"), None, None),
        P(("groups", "slab", "dom"), None),
        P(("groups", "slab", "dom"), None),
        P(("groups", "slab", "dom")),
        P(("groups", "slab", "dom")),
        P(),
        P(("groups", "slab", "dom")),
    )
    out_specs = (P(None, ("groups", "dom"), "slab", None), P(("groups", "slab", "dom")))
    return jax.shard_map(body, mesh=mesh, in_specs=in_specs, out_specs=out_specs, check_vma=False)
```

```python
import functools
import math

import jax
import jax.numpy as jnp
import numpy as np
from jax import lax
from jax.experimental import pallas as pl
from jax.experimental.pallas import tpu as pltpu
from jax.sharding import PartitionSpec as P

LANES = 128
GROUP = 32
UNUSED = 100
MIB = 1024 * 1024

SMEM_SPEC = pl.BlockSpec(memory_space=pltpu.SMEM)
VMEM_SPEC = pl.BlockSpec(memory_space=pltpu.VMEM)
ANY_SPEC = pl.BlockSpec(memory_space=pl.ANY)


def params(mib):
    return pltpu.CompilerParams(vmem_limit_bytes=mib * MIB)


def bits_of(count):
    return (count - 1).bit_length()


def route_kernel(slabs, cap, local_bits, owner_ref, local_ref, kind_ref, counts_ref, target_ref, word_ref, totals_ref):
    particles, list_length = local_ref.shape
    rows_each = list_length // LANES
    rows = particles * rows_each
    gathered = lambda ref: jnp.concatenate(
        [ref[:, j * LANES:(j + 1) * LANES] for j in range(rows_each)], axis=0
    )
    row_id = lax.broadcasted_iota(jnp.int32, (rows, LANES), 0)
    lane_id = lax.broadcasted_iota(jnp.int32, (rows, LANES), 1)
    particle = row_id % particles
    position = (row_id // particles) * LANES + lane_id
    limit = jnp.zeros((rows, LANES), jnp.int32)
    for i in range(particles):
        limit = jnp.where(particle == i, counts_ref[i], limit)
    owner = jnp.concatenate(
        [owner_ref[pl.ds(j, particles, stride=rows_each), :] for j in range(rows_each)], axis=0
    )
    owner = jnp.where(position < limit, owner, -1)
    up_to = (
        lax.broadcasted_iota(jnp.int32, (LANES, LANES), 0)
        <= lax.broadcasted_iota(jnp.int32, (LANES, LANES), 1)
    ).astype(jnp.bfloat16)
    ones = jnp.ones((LANES, LANES), jnp.bfloat16)
    before = (
        lax.broadcasted_iota(jnp.int32, (rows, rows), 1)
        < lax.broadcasted_iota(jnp.int32, (rows, rows), 0)
    ).astype(jnp.bfloat16)

    def one_slab(slab, target):
        mine = owner == slab
        hits = mine.astype(jnp.float32).astype(jnp.bfloat16)
        inside = jnp.dot(hits, up_to, preferred_element_type=jnp.float32)
        row_sum = jnp.dot(hits, ones, preferred_element_type=jnp.float32)
        above = jnp.dot(before, row_sum.astype(jnp.bfloat16), preferred_element_type=jnp.float32)
        rank = (inside + above).astype(jnp.int32) - 1
        total = (above[rows - 1:rows, :] + row_sum[rows - 1:rows, :]).astype(jnp.int32)
        totals_ref[pl.ds(slab, 1), :] = total
        return jnp.where(mine, slab * (cap + LANES) + rank, target)

    target = lax.fori_loop(0, slabs, one_slab, jnp.full((rows, LANES), cap + UNUSED, jnp.int32))
    target_ref[...] = target
    kind_bits = local_bits
    word = gathered(local_ref) | (gathered(kind_ref) << kind_bits) | (position << (kind_bits + 2))
    word_ref[...] = word | (particle << (kind_bits + 2 + bits_of(list_length)))


def pack_kernel(slabs, cap, list_length, target_ref, word_ref, counts_ref, totals_ref, code_ref, image_ref, meta_ref, *refs):
    out_refs, (wide_ref, staged_ref) = refs[:-2], refs[-2:]
    particles = counts_ref.shape[0]
    stride = cap + LANES
    step = 256

    @pl.loop(0, image_ref.shape[0] // step)
    def _(i):
        at = pl.multiple_of(i * step, step)
        wide_ref[pl.ds(at, step), :] = image_ref[pl.ds(at, step), :].astype(jnp.float32)

    @pl.loop(0, particles)
    def _(particle):
        @pl.loop(0, (counts_ref[particle] + 15) // 16)
        def _(i):
            first = (i // 8) * (particles * LANES) + particle * LANES + (i % 8) * 16
            row = particle * list_length + i * 16
            targets = [target_ref[first + j] for j in range(16)]
            words = [word_ref[first + j] for j in range(16)]
            rows = [wide_ref[pl.ds(row + j, 1), :] for j in range(16)]
            for j in range(16):
                staged_ref[pl.ds(targets[j], 1), :] = rows[j]
                meta_ref[targets[j]] = words[j]

    @pl.loop(0, slabs)
    def _(slab):
        header = slab * stride + cap
        meta_ref[header] = totals_ref[slab, 0]
        for j in range(particles):
            meta_ref[header + 1 + j] = code_ref[j]

    offset = 0
    for out_ref in out_refs:
        width = out_ref.shape[1]

        @pl.loop(0, slabs)
        def _(slab, offset=offset):
            at = pl.multiple_of(slab * stride + offset, LANES)
            out_ref[slab] = staged_ref[pl.ds(at, width), :].astype(jnp.bfloat16)

        offset += width


def decode_kernel(local_bits, dummy, word_ref, live_ref, index_ref):
    rows = word_ref.shape[0]
    live = live_ref[...] != 0
    index = jnp.where(live, word_ref[...] & ((1 << local_bits) - 1), dummy)
    lane = lax.broadcasted_iota(jnp.int32, (rows, LANES), 1)
    clash = jnp.zeros((rows, LANES), jnp.int32)
    for shift in range(1, GROUP):
        earlier = pltpu.roll(index, shift, 1)
        same = (earlier == index) & (lane % GROUP >= shift) & live
        clash = clash | same.astype(jnp.int32)
    shift = 1
    while shift < GROUP:
        clash = clash | pltpu.roll(clash, LANES - shift, 1)
        shift *= 2
    index_ref[...] = index | jnp.where(lane % GROUP == 0, clash << 24, 0)


def gather_kernel(slabs, cap, index_ref, totals_ref, volume_ref, *refs):
    out_refs, (wide_ref, staged_ref) = refs[:-2], refs[-2:]
    blocks = volume_ref.shape[0]
    step = 256

    @pl.loop(0, blocks // step)
    def _(i):
        at = pl.multiple_of(i * step, step)
        wide_ref[pl.ds(at, step), :] = volume_ref[pl.ds(at, step), :].astype(jnp.float32)

    @pl.loop(0, slabs)
    def _(source):
        live = totals_ref[source]

        @pl.loop(0, (live + 15) // 16)
        def _(i):
            first = source * cap + i * 16
            places = [index_ref[first] & 0xFFFFFF] + [index_ref[first + j] for j in range(1, 16)]
            rows = [wide_ref[pl.ds(places[j], 1), :] for j in range(16)]
            for j in range(16):
                staged_ref[pl.ds(i * 16 + j, 1), :] = rows[j]

        offset = 0
        for out_ref in out_refs:
            width = out_ref.shape[1]

            @pl.when(live > offset)
            def _(offset=offset):
                out_ref[source] = staged_ref[offset:offset + width, :].astype(jnp.bfloat16)

            offset += width


def sine(angle):
    turns = jnp.floor(angle * (1.0 / math.pi) + 0.5)
    rest = angle - turns * 3.140625
    rest = rest - turns * 9.67502593994140625e-4
    rest = rest - turns * 1.509957990978376e-7
    odd = turns - 2.0 * jnp.floor(turns * 0.5)
    square = rest * rest
    poly = 2.718121e-6
    poly = poly * square - 1.9839334e-4
    poly = poly * square + 8.3333293e-3
    poly = poly * square - 1.6666667e-1
    value = rest + rest * square * poly
    return value * (1.0 - 2.0 * odd)


def slab_kernel(
    side, local_bits, list_length, particles, cap, offset, first, last,
    totals_ref, defocus_ref, phase_ref, scale_ref, index_ref, core_ref,
    word_ref, voxel_ref, image_ref, forward_ref, backward_ref, unit_ref, *rest,
):
    if not first:
        rest = rest[1:]
    square_ref, sum_ref, out_refs, (staged_ref, sems) = rest[0], rest[1], rest[2:-2], rest[-2:]
    slabs, _, tile = word_ref.shape
    blocks = sum_ref.shape[0] - 8
    features = image_ref.shape[2]
    kinds = forward_ref.shape[0] // features
    position_bits = bits_of(list_length)
    per_row = side // 8

    if first:
        @pl.loop(0, blocks // 256)
        def _(i):
            at = pl.multiple_of(i * 256, 256)
            sum_ref[pl.ds(at, 256), :] = jnp.zeros((256, features), jnp.float32)

    @pl.loop(0, slabs)
    def _(source):
        live = jnp.clip(totals_ref[source] - offset, 0, tile)

        @pl.when(live == 0)
        def _():
            square_ref[source] = jnp.zeros((particles, LANES), jnp.float32)

        @pl.when(live > 0)
        def _():
            word = word_ref[source]
            kind = (word >> local_bits) & 3
            position = (word >> (local_bits + 2)) & (list_length - 1)
            particle = (word >> (local_bits + 2 + position_bits)) & (particles - 1)
            valid = lax.broadcasted_iota(jnp.int32, (1, tile), 1) < live
            defocus = jnp.zeros((1, tile), jnp.float32)
            phase = jnp.zeros((1, tile), jnp.float32)
            scale = jnp.zeros((1, tile), jnp.float32)
            for j in range(particles):
                chosen = particle == j
                defocus = jnp.where(chosen, defocus_ref[source * particles + j], defocus)
                phase = jnp.where(chosen, phase_ref[source * particles + j], phase)
                scale = jnp.where(chosen, scale_ref[source * particles + j], scale)
            half = features // 2
            cell = lax.broadcasted_iota(jnp.int32, (half, tile), 0)
            vert = ((position // per_row) * 8 - side // 2 + cell // 8).astype(jnp.float32)
            horiz = ((position % per_row) * 8 - side // 2 + cell % 8).astype(jnp.float32)
            radius = (vert * vert + horiz * horiz) * (1.0 / float((side // 2) ** 2))
            factor = scale * sine(defocus * radius + phase)
            factor = jnp.concatenate([factor, factor], axis=0)
            contract_last = (((1,), (1,)), ((), ()))
            each_kind = lax.dot_general(
                forward_ref[...], voxel_ref[source], contract_last, preferred_element_type=jnp.float32
            )
            extracted = each_kind[0:features, :]
            for k in range(1, kinds):
                extracted = jnp.where(kind == k, each_kind[k * features:(k + 1) * features, :], extracted)
            picture = lax.dot_general(
                unit_ref[...], image_ref[source], contract_last, preferred_element_type=jnp.float32
            )
            misfit = jnp.where(valid, factor * extracted - picture, 0.0)
            squares = jnp.sum(misfit * misfit, axis=0, keepdims=True)
            which = lax.broadcasted_iota(jnp.int32, (particles, tile), 0)
            spread = jnp.where(valid & (particle == which), squares, 0.0)
            folded = spread[:, 0:LANES]
            for i in range(1, tile // LANES):
                folded = folded + spread[:, i * LANES:(i + 1) * LANES]
            square_ref[source] = folded
            weighted = (factor * misfit).astype(jnp.bfloat16)
            none = jnp.zeros_like(weighted)
            spread_back = jnp.concatenate(
                [jnp.where(kind == k, weighted, none) for k in range(kinds)], axis=0
            )
            terms = jnp.dot(backward_ref[...], spread_back, preferred_element_type=jnp.float32)
            staged_ref[...] = terms.T

        @pl.loop(0, (live + GROUP - 1) // GROUP)
        def _(g):
            base = source * cap + offset + g * GROUP
            marked = index_ref[base]
            places = [marked & 0xFFFFFF] + [index_ref[base + j] for j in range(1, GROUP)]

            @pl.when(marked < (1 << 24))
            def _():
                held = [sum_ref[pl.ds(places[j], 1), :] for j in range(GROUP)]
                new = [staged_ref[pl.ds(g * GROUP + j, 1), :] for j in range(GROUP)]
                for j in range(GROUP):
                    sum_ref[pl.ds(places[j], 1), :] = held[j] + new[j]

            @pl.when(marked >= (1 << 24))
            def _():
                for j in range(GROUP):
                    sum_ref[pl.ds(places[j], 1), :] = (
                        sum_ref[pl.ds(places[j], 1), :] + staged_ref[pl.ds(g * GROUP + j, 1), :]
                    )

    if last:
        out_ref = out_refs[0]
        at = pl.multiple_of((1 - core_ref[0]) * (blocks // 2), 8)
        copy = pltpu.make_async_copy(sum_ref.at[pl.ds(at, out_ref.shape[0])], out_ref, sems.at[0])
        copy.start()
        copy.wait()


def split_kernel(core_ref, sum_ref, *refs):
    out_refs, sems = refs[:-1], refs[-1]
    half = out_refs[0].shape[0]
    places = [core_ref[0] * half]
    start = (2 - core_ref[0]) * half
    for out_ref in reversed(out_refs[1:]):
        start = start - out_ref.shape[0]
        places.insert(1, start)
    copies = []
    for i, (place, out_ref) in enumerate(zip(places, out_refs)):
        at = pl.multiple_of(place, 8)
        copies.append(pltpu.make_async_copy(sum_ref.at[pl.ds(at, out_ref.shape[0])], out_ref, sems.at[i]))
    for copy in copies:
        copy.start()
    for copy in copies:
        copy.wait()


def pieces_of(planes):
    if planes < 16:
        return [planes]
    return [4, 4, planes - 8]


def rotated(value, turn, length):
    real, imag = value
    if turn == 0:
        return value
    if 4 * turn == length:
        return (-imag, real)
    root = math.sqrt(0.5)
    if 8 * turn == length:
        return ((real - imag) * root, (real + imag) * root)
    if 8 * turn == 3 * length:
        return ((real + imag) * -root, (real - imag) * root)
    cos, sin = math.cos(2 * math.pi * turn / length), math.sin(2 * math.pi * turn / length)
    return (real * cos - imag * sin, real * sin + imag * cos)


def small_dft(values):
    length = len(values)
    if length == 1:
        return values
    even, odd = small_dft(values[0::2]), small_dft(values[1::2])
    low, high = [], []
    for k in range(length // 2):
        turned = rotated(odd[k], k, length)
        low.append((even[k][0] + turned[0], even[k][1] + turned[1]))
        high.append((even[k][0] - turned[0], even[k][1] - turned[1]))
    return low + high


def swap_quarters(values):
    lane = lax.broadcasted_iota(jnp.int32, values[0].shape, 1)
    low, even = lane < 64, (lane // 32) % 2 == 0
    roll = lambda value, shift: pltpu.roll(value, shift, 1)
    for first, second, shift, keep in ((0, 2, 64, low), (1, 3, 64, low), (0, 1, 32, even), (2, 3, 32, even)):
        one, two = values[first], values[second]
        values[first] = jnp.where(keep, one, roll(two, shift))
        values[second] = jnp.where(keep, roll(one, LANES - shift), two)
    return values


def in_halves(value):
    high = value.astype(jnp.bfloat16)
    return high, (value - high.astype(jnp.float32)).astype(jnp.bfloat16)


def planes_kernel(mine_ref, theirs_ref, zblock_ref, turn_ref, wide_ref, fine_ref, out_ref, high_ref, low_ref):
    step = pl.program_id(1)
    count = mine_ref.shape[1]
    groups, side = out_ref.shape[0], out_ref.shape[4]
    height = side // groups

    @pl.loop(0, count, unroll=4)
    def _(i):
        block = (mine_ref[:, i] + theirs_ref[:, i]).reshape(LANES, LANES)
        high, low = in_halves(block.T)
        both = jnp.dot(
            jnp.concatenate([high, low, high], axis=1), zblock_ref[...],
            preferred_element_type=jnp.float32,
        )
        by_cos = both[:, :LANES].reshape(8, 2, 8, LANES)
        by_sin = both[:, LANES:].reshape(8, 2, 8, LANES)
        real = by_cos[:, 0] - by_sin[:, 1]
        imag = by_sin[:, 0] + by_cos[:, 1]
        values = []
        for z in range(8):
            cos, sin = turn_ref[0, z:z + 1, :], turn_ref[1, z:z + 1, :]
            values.append((real[z] * cos - imag[z] * sin, real[z] * sin + imag[z] * cos))
        values = [jnp.concatenate(value, axis=0) for value in small_dft(values)]
        at = pl.ds(pl.multiple_of((step * count + i) * 16, 16), 16)
        for half in range(2):
            planes = swap_quarters(values[4 * half:4 * half + 4])
            for x in range(4):
                columns = slice((2 * x + half) * LANES, (2 * x + half + 1) * LANES)
                high, low = in_halves(planes[x])
                high_ref[at, columns] = high
                low_ref[at, columns] = low

    @pl.when(step == pl.num_programs(1) - 1)
    def _():
        @pl.loop(0, 4)
        def _(x):
            columns = pl.ds(pl.multiple_of(x * side, side), side)
            product = functools.partial(jnp.dot, preferred_element_type=jnp.float32)
            high = high_ref[:, columns]
            result = product(wide_ref[...], high) + (
                product(wide_ref[...], low_ref[:, columns]) + product(fine_ref[...], high)
            )
            for part in range(2):
                for group in range(groups):
                    start = part * side + group * height
                    out_ref[group, x, part] = result[start:start + height, :].astype(jnp.bfloat16)


def first_dimension_kernel(slabs, each, core_ref, *refs):
    arrays, (out_ref, mid_ref) = refs[:-2], refs[-2:]
    chunks = len(arrays) // 2
    own, other = arrays[:chunks], arrays[chunks:]
    spots = [(i, at) for i, ref in enumerate(own) for at in range(ref.shape[1])]
    core = core_ref[0]
    is_first = core == 0
    sign = (1 - 2 * core).astype(jnp.float32)

    def plane(x):
        slab, rest = x // (2 * each), x % (2 * each)
        half, inner = rest // each, rest % each
        loaded = []
        for part in range(2):
            chunk, at = spots[inner]
            here = own[chunk][slab, at, part].astype(jnp.float32)
            there = other[chunk][slab, at, part].astype(jnp.float32)
            loaded.append(jnp.where(is_first, here, there) if half == 0 else jnp.where(is_first, there, here))
        return tuple(loaded)

    for low in range(16):
        values = small_dft([plane(low + 16 * high) for high in range(16)])
        for k in range(16):
            real, imag = rotated(values[k], low * k, 256)
            if low % 2:
                real, imag = real * sign, imag * sign
            mid_ref[k, low, 0] = real
            mid_ref[k, low, 1] = imag

    @pl.loop(0, 16)
    def _(k):
        values = [(mid_ref[k, low, 0], mid_ref[k, low, 1]) for low in range(16)]
        even, odd = small_dft(values[0::2]), small_dft(values[1::2])
        for m in range(8):
            turned = rotated(odd[m], m, 16)
            out_ref[0, k + 16 * m] = even[m][0] + turned[0]
            out_ref[1, k + 16 * m] = even[m][1] + turned[1]


def host_halves(table):
    high = table.astype(jnp.bfloat16)
    return high, (table - high.astype(np.float64)).astype(jnp.bfloat16)


def transform_tables(side):
    per_row = side // 8
    grid = np.arange(per_row)
    angle = 2 * np.pi * np.outer(grid, grid) / per_row
    zblock = np.concatenate([np.kron(np.eye(4), np.cos(angle)), np.kron(np.eye(4), np.sin(angle))], axis=1)
    high, low = host_halves(zblock)
    zblock = np.concatenate([high, high, low], axis=0)
    angle = 2 * np.pi * np.outer(np.arange(8), grid) / side
    turns = np.stack([np.tile(np.cos(angle), (1, 4)), np.tile(np.sin(angle), (1, 4))]).astype(np.float32)
    cells = np.arange(side)
    angle = 2 * np.pi * (np.outer(cells, cells) % side) / side
    cos, sin = np.cos(angle).reshape(side, per_row, 1, 8), np.sin(angle).reshape(side, per_row, 1, 8)
    matrix = np.concatenate(
        [np.concatenate([cos, -sin], axis=2), np.concatenate([sin, cos], axis=2)], axis=0
    ).reshape(2 * side, 2 * side) / float(side) ** 1.5
    return (zblock, turns) + host_halves(matrix)


def sum_over_slabs(partial_sums):
    slabs = partial_sums.shape[0]
    if slabs <= 8:
        me = lax.axis_index("slab")
        row = lambda i: lax.dynamic_index_in_dim(partial_sums, me ^ i, axis=0, keepdims=True)
        returned = [row(0)] + [
            lax.ppermute(row(i), "slab", [(slab, slab ^ i) for slab in range(slabs)])
            for i in range(1, slabs)
        ]
        returned = jnp.concatenate(returned)
    else:
        returned = lax.all_to_all(partial_sums, "slab", split_axis=0, concat_axis=0, tiled=True)
    return jnp.sum(returned, axis=0)


def to_field(mine, theirs_sent, partial_sums, side):
    slabs = lax.axis_size("slab")
    per_row = side // 8
    each = side // slabs // 2
    height = side // slabs
    groups = slabs if height % 16 == 0 else 1
    tables = [jnp.asarray(table) for table in transform_tables(side)]
    swap = [(0, 1), (1, 0)]
    theirs = [lax.ppermute(chunk, "dom", swap) for chunk in theirs_sent]
    grid_shape = (-1, per_row, per_row, LANES)
    mine = mine.reshape(grid_shape)
    short = max(0, 4 - each)
    if short:
        mine = jnp.pad(mine, ((0, short), (0, 0), (0, 0), (0, 0)))
    yblocks = 8
    own = []
    first_quad = 0
    before = []
    for real_planes, added in zip(pieces_of(each), theirs):
        if before:
            added, before[0] = lax.optimization_barrier((added, before[0]))
        added = added.reshape(grid_shape)
        if short:
            added = jnp.pad(added, ((0, short), (0, 0), (0, 0), (0, 0)))
        held = real_planes + short
        quads = held // 4
        whole = lambda table: pl.BlockSpec(table.shape, lambda q, y: (0,) * table.ndim)
        sent = pl.pallas_call(
            planes_kernel,
            grid=(quads, per_row // yblocks),
            out_shape=jax.ShapeDtypeStruct((groups, held, 2, side // groups, side), jnp.bfloat16),
            in_specs=[
                pl.BlockSpec((4, yblocks, per_row, LANES), lambda q, y, at=first_quad: (at + q, y, 0, 0)),
                pl.BlockSpec((4, yblocks, per_row, LANES), lambda q, y: (q, y, 0, 0)),
            ] + [whole(table) for table in tables],
            out_specs=pl.BlockSpec((groups, 4, 2, side // groups, side), lambda q, y: (0, q, 0, 0, 0)),
            scratch_shapes=[
                pltpu.VMEM((2 * side, 4 * side), jnp.bfloat16),
                pltpu.VMEM((2 * side, 4 * side), jnp.bfloat16),
            ],
            compiler_params=params(24),
            cost_estimate=pl.CostEstimate(
                flops=held * 8 * side**3, bytes_accessed=held * 4 * side**2 * 8, transcendentals=0
            ),
            name="transform_planes",
        )(mine, added, *tables)
        if groups != slabs:
            sent = sent.reshape(-1, 2, slabs, height, side).transpose(2, 0, 1, 3, 4)[:, :real_planes]
        first_quad += quads
        if before:
            sent, own[-1] = lax.optimization_barrier((sent, own[-1]))
        if first_quad * 4 >= each:
            sent, partial_sums = lax.optimization_barrier((sent, partial_sums))
        before = [sent]
        got = lax.all_to_all(sent, "slab", split_axis=0, concat_axis=0, tiled=True)
        own.append(got)
    own[-1], losses = lax.optimization_barrier((own[-1], sum_over_slabs(partial_sums)))
    other = [lax.ppermute(got, "dom", swap) for got in own]
    rows = min(16, height)
    arrays = own + other
    field = pl.pallas_call(
        functools.partial(first_dimension_kernel, slabs, each),
        grid=(height // rows, side // LANES),
        out_shape=jax.ShapeDtypeStruct((2, side // 2, height, side), jnp.float32),
        in_specs=[SMEM_SPEC] + [
            pl.BlockSpec(array.shape[:3] + (rows, LANES), lambda y, z: (0, 0, 0, y, z))
            for array in arrays
        ],
        out_specs=pl.BlockSpec((2, side // 2, rows, LANES), lambda y, z: (0, 0, y, z)),
        scratch_shapes=[pltpu.VMEM((16, 16, 2, rows, LANES), jnp.float32)],
        compiler_params=params(28),
        name="transform_first",
    )(lax.axis_index("dom").astype(jnp.int32).reshape(1), *arrays)
    return field, losses


def gradient_of_slab(volume, kernels, images, owners, local_block, kinds, counts, ctf_code, ctf_table, scales):
    slabs = lax.axis_size("slab")
    particles, list_length, features = images.shape
    side = math.isqrt(list_length * 64)
    entries = particles * list_length
    cap = 2 * entries // slabs
    slots = slabs * cap
    blocks = volume.shape[0]
    local_bits = bits_of(blocks)
    kind_count = kernels.shape[0]
    rows = entries // LANES
    int_rows = jax.ShapeDtypeStruct((rows, LANES), jnp.int32)

    target, word, totals = pl.pallas_call(
        functools.partial(route_kernel, slabs, cap, local_bits),
        out_shape=(int_rows, int_rows, jax.ShapeDtypeStruct((slabs, LANES), jnp.int32)),
        in_specs=[VMEM_SPEC, VMEM_SPEC, VMEM_SPEC, SMEM_SPEC],
        out_specs=(VMEM_SPEC, VMEM_SPEC, VMEM_SPEC),
        compiler_params=params(16),
        name="route",
    )(owners.reshape(rows, LANES), local_block, kinds, counts)
    target, word = target.reshape(entries), word.reshape(entries)
    tiles = [cap // 2, cap // 2] if cap >= 2048 else [cap]
    parts = len(tiles)
    code = ctf_code | ((scales.astype(jnp.float32) * 256.0).astype(jnp.int32) << 8)
    stride = cap + LANES
    meta, *packed = pl.pallas_call(
        functools.partial(pack_kernel, slabs, cap, list_length),
        out_shape=(jax.ShapeDtypeStruct((slabs * stride,), jnp.int32),)
        + tuple(jax.ShapeDtypeStruct((slabs, tile, features), jnp.bfloat16) for tile in tiles),
        in_specs=[SMEM_SPEC] * 5 + [VMEM_SPEC],
        out_specs=(SMEM_SPEC,) + (VMEM_SPEC,) * parts,
        scratch_shapes=[
            pltpu.VMEM((entries, features), jnp.float32),
            pltpu.VMEM((slabs * stride, features), jnp.float32),
        ],
        compiler_params=params(32),
        name="pack",
    )(target, word, counts, totals, code, images.reshape(entries, features))
    arrived = lax.all_to_all(
        meta.reshape(slabs, stride), "slab", split_axis=0, concat_axis=0, tiled=True
    )
    words = arrived[:, :cap]
    totals_in = arrived[:, cap]
    codes_in = arrived[:, cap + 1:cap + 1 + particles]
    live = (jnp.arange(cap, dtype=jnp.int32)[None, :] < totals_in[:, None]).astype(jnp.int32)
    table_rows = ctf_table[(codes_in & 255).reshape(-1)]
    scale_in = (codes_in >> 8).astype(jnp.float32).reshape(-1) * (1.0 / 256.0)

    index = pl.pallas_call(
        functools.partial(decode_kernel, local_bits, blocks),
        out_shape=jax.ShapeDtypeStruct((slots // LANES, LANES), jnp.int32),
        in_specs=[VMEM_SPEC, VMEM_SPEC],
        out_specs=VMEM_SPEC,
        compiler_params=params(16),
        name="decode",
    )(words.reshape(slots // LANES, LANES), live.reshape(slots // LANES, LANES))
    index = index.reshape(slots)
    voxels = list(pl.pallas_call(
        functools.partial(gather_kernel, slabs, cap),
        out_shape=tuple(
            jax.ShapeDtypeStruct((slabs, tile, features), jnp.bfloat16) for tile in tiles
        ),
        in_specs=[SMEM_SPEC, SMEM_SPEC, VMEM_SPEC],
        out_specs=(VMEM_SPEC,) * parts,
        scratch_shapes=[
            pltpu.VMEM((blocks + 8, features), jnp.float32),
            pltpu.VMEM((cap, features), jnp.float32),
        ],
        compiler_params=params(40),
        cost_estimate=pl.CostEstimate(flops=0, bytes_accessed=100 * MIB, transcendentals=0),
        name="read_voxels",
    )(index, totals_in, volume))

    forward = jnp.transpose(kernels, (0, 2, 1)).reshape(kind_count * features, features)
    backward = kernels.reshape(kind_count, 2, 8, 8, features).transpose(3, 1, 2, 0, 4)
    backward = backward.reshape(features, kind_count * features)
    unit = jnp.eye(features, dtype=jnp.bfloat16)
    core = lax.axis_index("dom").astype(jnp.int32).reshape(1)
    plane_blocks = (side // 8) ** 2
    pieces = [planes * plane_blocks for planes in pieces_of(side // slabs // 2)]
    squares, sums, behind, offset = 0.0, None, [voxels[0]], 0
    for part, tile in enumerate(tiles):
        first, last = part == 0, part == parts - 1
        if not first:
            packed[part], earlier = lax.optimization_barrier((packed[part], behind[part - 1]))
            if part == 1:
                voxels[0] = earlier
        picture = lax.all_to_all(packed[part], "slab", split_axis=0, concat_axis=0, tiled=True)
        lengths = pieces[:1] if last else []
        arguments = [
            totals_in, table_rows[:, 0], table_rows[:, 1], scale_in, index, core,
            words[:, offset:offset + tile].reshape(slabs, 1, tile), voxels[part], picture,
            forward, backward, unit,
        ]
        aliases = {}
        if not first:
            aliases = {len(arguments): 1}
            arguments.append(pltpu.with_memory_space_constraint(sums, pltpu.VMEM))
        more, sums, *first_piece = pl.pallas_call(
            functools.partial(
                slab_kernel, side, local_bits, list_length, particles, cap, offset, first, last
            ),
            out_shape=(
                jax.ShapeDtypeStruct((slabs, particles, LANES), jnp.float32),
                pltpu.VMEM((blocks + 8, features), jnp.float32),
            )
            + tuple(jax.ShapeDtypeStruct((length, features), jnp.float32) for length in lengths),
            in_specs=[SMEM_SPEC] * 6 + [VMEM_SPEC] * (len(arguments) - 6),
            out_specs=(VMEM_SPEC, VMEM_SPEC) + (ANY_SPEC,) * len(lengths),
            scratch_shapes=[
                pltpu.VMEM((tile, features), jnp.float32),
                pltpu.SemaphoreType.DMA((max(1, len(lengths)),)),
            ],
            input_output_aliases=aliases,
            compiler_params=params(24),
            cost_estimate=pl.CostEstimate(flops=0, bytes_accessed=16 * MIB, transcendentals=0),
            name="compare_and_add",
        )(*arguments)
        squares = squares + more
        behind.append(more)
        offset += tile
    lengths = [blocks // 2] + pieces[1:]
    mine, *theirs = pl.pallas_call(
        split_kernel,
        out_shape=tuple(jax.ShapeDtypeStruct((length, features), jnp.float32) for length in lengths),
        in_specs=[SMEM_SPEC, VMEM_SPEC],
        out_specs=(ANY_SPEC,) * len(lengths),
        scratch_shapes=[pltpu.SemaphoreType.DMA((len(lengths),))],
        compiler_params=params(16),
        cost_estimate=pl.CostEstimate(flops=0, bytes_accessed=16 * MIB, transcendentals=0),
        name="split_sums",
    )(core, pltpu.with_memory_space_constraint(sums, pltpu.VMEM))
    theirs = first_piece + theirs
    partial_sums = jnp.sum(squares, axis=2)
    return mine, theirs, partial_sums, side


def body(*arrays):
    mine, theirs, partial_sums, side = gradient_of_slab(*arrays)
    field, squares = to_field(mine, theirs, partial_sums, side)
    counts = arrays[6]
    return field, squares / (counts.astype(jnp.float32) * 128.0)


def solution(mesh):
    in_specs = (
        P(("groups", "slab"), None),
        P(),
        P(("groups", "slab", "dom"), None, None),
        P(("groups", "slab", "dom"), None, None),
        P(("groups", "slab", "dom"), None),
        P(("groups", "slab", "dom"), None),
        P(("groups", "slab", "dom")),
        P(("groups", "slab", "dom")),
        P(),
        P(("groups", "slab", "dom")),
    )
    out_specs = (P(None, ("groups", "dom"), "slab", None), P(("groups", "slab", "dom")))
    return jax.shard_map(body, mesh=mesh, in_specs=in_specs, out_specs=out_specs, check_vma=False)
```

```python
import functools
import math

import jax
import jax.numpy as jnp
import numpy as np
from jax import lax
from jax.experimental import pallas as pl
from jax.experimental.pallas import tpu as pltpu
from jax.sharding import PartitionSpec as P

LANES = 128
GROUP = 16
UNUSED = 100
MIB = 1024 * 1024

SMEM_SPEC = pl.BlockSpec(memory_space=pltpu.SMEM)
VMEM_SPEC = pl.BlockSpec(memory_space=pltpu.VMEM)
ANY_SPEC = pl.BlockSpec(memory_space=pl.ANY)


def params(mib):
    return pltpu.CompilerParams(vmem_limit_bytes=mib * MIB)


def bits_of(count):
    return (count - 1).bit_length()


def route_kernel(slabs, cap, local_bits, owner_ref, local_ref, kind_ref, counts_ref, target_ref, word_ref, totals_ref):
    particles, list_length = local_ref.shape
    rows_each = list_length // LANES
    rows = particles * rows_each
    gathered = lambda ref: jnp.concatenate(
        [ref[:, j * LANES:(j + 1) * LANES] for j in range(rows_each)], axis=0
    )
    row_id = lax.broadcasted_iota(jnp.int32, (rows, LANES), 0)
    lane_id = lax.broadcasted_iota(jnp.int32, (rows, LANES), 1)
    particle = row_id % particles
    position = (row_id // particles) * LANES + lane_id
    limit = jnp.zeros((rows, LANES), jnp.int32)
    for i in range(particles):
        limit = jnp.where(particle == i, counts_ref[i], limit)
    owner = jnp.concatenate(
        [owner_ref[pl.ds(j, particles, stride=rows_each), :] for j in range(rows_each)], axis=0
    )
    owner = jnp.where(position < limit, owner, -1)
    up_to = (
        lax.broadcasted_iota(jnp.int32, (LANES, LANES), 0)
        <= lax.broadcasted_iota(jnp.int32, (LANES, LANES), 1)
    ).astype(jnp.bfloat16)
    ones = jnp.ones((LANES, LANES), jnp.bfloat16)
    before = (
        lax.broadcasted_iota(jnp.int32, (rows, rows), 1)
        < lax.broadcasted_iota(jnp.int32, (rows, rows), 0)
    ).astype(jnp.bfloat16)

    def one_slab(slab, target):
        mine = owner == slab
        hits = mine.astype(jnp.float32).astype(jnp.bfloat16)
        inside = jnp.dot(hits, up_to, preferred_element_type=jnp.float32)
        row_sum = jnp.dot(hits, ones, preferred_element_type=jnp.float32)
        above = jnp.dot(before, row_sum.astype(jnp.bfloat16), preferred_element_type=jnp.float32)
        rank = (inside + above).astype(jnp.int32) - 1
        total = (above[rows - 1:rows, :] + row_sum[rows - 1:rows, :]).astype(jnp.int32)
        totals_ref[pl.ds(slab, 1), :] = total
        return jnp.where(mine, slab * (cap + LANES) + rank, target)

    target = lax.fori_loop(0, slabs, one_slab, jnp.full((rows, LANES), cap + UNUSED, jnp.int32))
    target_ref[...] = target
    kind_bits = local_bits
    word = gathered(local_ref) | (gathered(kind_ref) << kind_bits) | (position << (kind_bits + 2))
    word_ref[...] = word | (particle << (kind_bits + 2 + bits_of(list_length)))


def pack_kernel(slabs, cap, list_length, target_ref, word_ref, counts_ref, totals_ref, code_ref, image_ref, meta_ref, *refs):
    out_refs, (wide_ref, staged_ref) = refs[:-2], refs[-2:]
    particles = counts_ref.shape[0]
    stride = cap + LANES
    step = 256

    @pl.loop(0, image_ref.shape[0] // step)
    def _(i):
        at = pl.multiple_of(i * step, step)
        wide_ref[pl.ds(at, step), :] = image_ref[pl.ds(at, step), :].astype(jnp.float32)

    @pl.loop(0, particles)
    def _(particle):
        @pl.loop(0, (counts_ref[particle] + 15) // 16)
        def _(i):
            first = (i // 8) * (particles * LANES) + particle * LANES + (i % 8) * 16
            row = particle * list_length + i * 16
            targets = [target_ref[first + j] for j in range(16)]
            words = [word_ref[first + j] for j in range(16)]
            rows = [wide_ref[pl.ds(row + j, 1), :] for j in range(16)]
            for j in range(16):
                staged_ref[pl.ds(targets[j], 1), :] = rows[j]
                meta_ref[targets[j]] = words[j]

    @pl.loop(0, slabs)
    def _(slab):
        header = slab * stride + cap
        meta_ref[header] = totals_ref[slab, 0]
        for j in range(particles):
            meta_ref[header + 1 + j] = code_ref[j]

    offset = 0
    for out_ref in out_refs:
        width = out_ref.shape[1]

        @pl.loop(0, slabs)
        def _(slab, offset=offset):
            at = pl.multiple_of(slab * stride + offset, LANES)
            out_ref[slab] = staged_ref[pl.ds(at, width), :].astype(jnp.bfloat16)

        offset += width


def decode_kernel(local_bits, dummy, word_ref, live_ref, index_ref):
    rows = word_ref.shape[0]
    live = live_ref[...] != 0
    index = jnp.where(live, word_ref[...] & ((1 << local_bits) - 1), dummy)
    lane = lax.broadcasted_iota(jnp.int32, (rows, LANES), 1)
    clash = jnp.zeros((rows, LANES), jnp.int32)
    for shift in range(1, GROUP):
        earlier = pltpu.roll(index, shift, 1)
        same = (earlier == index) & (lane % GROUP >= shift) & live
        clash = clash | same.astype(jnp.int32)
    shift = 1
    while shift < GROUP:
        clash = clash | pltpu.roll(clash, LANES - shift, 1)
        shift *= 2
    index_ref[...] = index | jnp.where(lane % GROUP == 0, clash << 24, 0)


def gather_kernel(slabs, cap, index_ref, totals_ref, volume_ref, *refs):
    out_refs, (wide_ref, staged_ref) = refs[:-2], refs[-2:]
    blocks = volume_ref.shape[0]
    step = 256

    @pl.loop(0, blocks // step)
    def _(i):
        at = pl.multiple_of(i * step, step)
        wide_ref[pl.ds(at, step), :] = volume_ref[pl.ds(at, step), :].astype(jnp.float32)

    @pl.loop(0, slabs)
    def _(source):
        live = totals_ref[source]

        @pl.loop(0, (live + 15) // 16)
        def _(i):
            first = source * cap + i * 16
            places = [index_ref[first] & 0xFFFFFF] + [index_ref[first + j] for j in range(1, 16)]
            rows = [wide_ref[pl.ds(places[j], 1), :] for j in range(16)]
            for j in range(16):
                staged_ref[pl.ds(i * 16 + j, 1), :] = rows[j]

        offset = 0
        for out_ref in out_refs:
            width = out_ref.shape[1]

            @pl.when(live > offset)
            def _(offset=offset):
                out_ref[source] = staged_ref[offset:offset + width, :].astype(jnp.bfloat16)

            offset += width


def sine(angle):
    turns = jnp.floor(angle * (1.0 / math.pi) + 0.5)
    rest = angle - turns * 3.140625
    rest = rest - turns * 9.67502593994140625e-4
    rest = rest - turns * 1.509957990978376e-7
    odd = turns - 2.0 * jnp.floor(turns * 0.5)
    square = rest * rest
    poly = 2.718121e-6
    poly = poly * square - 1.9839334e-4
    poly = poly * square + 8.3333293e-3
    poly = poly * square - 1.6666667e-1
    value = rest + rest * square * poly
    return value * (1.0 - 2.0 * odd)


def slab_kernel(
    side, local_bits, list_length, particles, cap, offset, first, last,
    totals_ref, defocus_ref, phase_ref, scale_ref, index_ref, core_ref,
    word_ref, voxel_ref, image_ref, forward_ref, backward_ref, unit_ref, *rest,
):
    if not first:
        rest = rest[1:]
    square_ref, sum_ref, out_refs, (staged_ref, sems) = rest[0], rest[1], rest[2:-2], rest[-2:]
    slabs, _, tile = word_ref.shape
    blocks = sum_ref.shape[0] - 8
    features = image_ref.shape[2]
    kinds = forward_ref.shape[0] // features
    position_bits = bits_of(list_length)
    per_row = side // 8

    if first:
        @pl.loop(0, blocks // 256)
        def _(i):
            at = pl.multiple_of(i * 256, 256)
            sum_ref[pl.ds(at, 256), :] = jnp.zeros((256, features), jnp.float32)

    @pl.loop(0, slabs)
    def _(source):
        live = jnp.clip(totals_ref[source] - offset, 0, tile)

        @pl.when(live == 0)
        def _():
            square_ref[source] = jnp.zeros((particles, LANES), jnp.float32)

        @pl.when(live > 0)
        def _():
            word = word_ref[source]
            kind = (word >> local_bits) & 3
            position = (word >> (local_bits + 2)) & (list_length - 1)
            particle = (word >> (local_bits + 2 + position_bits)) & (particles - 1)
            valid = lax.broadcasted_iota(jnp.int32, (1, tile), 1) < live
            defocus = jnp.zeros((1, tile), jnp.float32)
            phase = jnp.zeros((1, tile), jnp.float32)
            scale = jnp.zeros((1, tile), jnp.float32)
            for j in range(particles):
                chosen = particle == j
                defocus = jnp.where(chosen, defocus_ref[source * particles + j], defocus)
                phase = jnp.where(chosen, phase_ref[source * particles + j], phase)
                scale = jnp.where(chosen, scale_ref[source * particles + j], scale)
            half = features // 2
            cell = lax.broadcasted_iota(jnp.int32, (half, tile), 0)
            vert = ((position // per_row) * 8 - side // 2 + cell // 8).astype(jnp.float32)
            horiz = ((position % per_row) * 8 - side // 2 + cell % 8).astype(jnp.float32)
            radius = (vert * vert + horiz * horiz) * (1.0 / float((side // 2) ** 2))
            factor = scale * sine(defocus * radius + phase)
            factor = jnp.concatenate([factor, factor], axis=0)
            contract_last = (((1,), (1,)), ((), ()))
            each_kind = lax.dot_general(
                forward_ref[...], voxel_ref[source], contract_last, preferred_element_type=jnp.float32
            )
            extracted = each_kind[0:features, :]
            for k in range(1, kinds):
                extracted = jnp.where(kind == k, each_kind[k * features:(k + 1) * features, :], extracted)
            picture = lax.dot_general(
                unit_ref[...], image_ref[source], contract_last, preferred_element_type=jnp.float32
            )
            misfit = jnp.where(valid, factor * extracted - picture, 0.0)
            squares = jnp.sum(misfit * misfit, axis=0, keepdims=True)
            which = lax.broadcasted_iota(jnp.int32, (particles, tile), 0)
            spread = jnp.where(valid & (particle == which), squares, 0.0)
            folded = spread[:, 0:LANES]
            for i in range(1, tile // LANES):
                folded = folded + spread[:, i * LANES:(i + 1) * LANES]
            square_ref[source] = folded
            weighted = (factor * misfit).astype(jnp.bfloat16)
            none = jnp.zeros_like(weighted)
            spread_back = jnp.concatenate(
                [jnp.where(kind == k, weighted, none) for k in range(kinds)], axis=0
            )
            terms = jnp.dot(backward_ref[...], spread_back, preferred_element_type=jnp.float32)
            staged_ref[...] = terms.T

        @pl.loop(0, (live + GROUP - 1) // GROUP)
        def _(g):
            base = source * cap + offset + g * GROUP
            marked = index_ref[base]
            places = [marked & 0xFFFFFF] + [index_ref[base + j] for j in range(1, GROUP)]

            @pl.when(marked < (1 << 24))
            def _():
                held = [sum_ref[pl.ds(places[j], 1), :] for j in range(GROUP)]
                new = [staged_ref[pl.ds(g * GROUP + j, 1), :] for j in range(GROUP)]
                for j in range(GROUP):
                    sum_ref[pl.ds(places[j], 1), :] = held[j] + new[j]

            @pl.when(marked >= (1 << 24))
            def _():
                for j in range(GROUP):
                    sum_ref[pl.ds(places[j], 1), :] = (
                        sum_ref[pl.ds(places[j], 1), :] + staged_ref[pl.ds(g * GROUP + j, 1), :]
                    )

    if last:
        half = blocks // 2
        start = (1 - core_ref[0]) * half
        places = [core_ref[0] * half]
        for out_ref in out_refs[1:]:
            places.append(start)
            start = start + out_ref.shape[0]
        copies = []
        for i, (place, out_ref) in enumerate(zip(places, out_refs)):
            length = out_ref.shape[0]
            at = pl.multiple_of(place, 8)
            copies.append(pltpu.make_async_copy(sum_ref.at[pl.ds(at, length)], out_ref, sems.at[i]))
        for copy in copies:
            copy.start()
        for copy in copies:
            copy.wait()


def pieces_of(planes):
    if planes < 16:
        return [planes]
    return [4, planes - 4]


def rotated(value, turn, length):
    real, imag = value
    if turn == 0:
        return value
    if 4 * turn == length:
        return (-imag, real)
    root = math.sqrt(0.5)
    if 8 * turn == length:
        return ((real - imag) * root, (real + imag) * root)
    if 8 * turn == 3 * length:
        return ((real + imag) * -root, (real - imag) * root)
    cos, sin = math.cos(2 * math.pi * turn / length), math.sin(2 * math.pi * turn / length)
    return (real * cos - imag * sin, real * sin + imag * cos)


def small_dft(values):
    length = len(values)
    if length == 1:
        return values
    even, odd = small_dft(values[0::2]), small_dft(values[1::2])
    low, high = [], []
    for k in range(length // 2):
        turned = rotated(odd[k], k, length)
        low.append((even[k][0] + turned[0], even[k][1] + turned[1]))
        high.append((even[k][0] - turned[0], even[k][1] - turned[1]))
    return low + high


def swap_quarters(values):
    lane = lax.broadcasted_iota(jnp.int32, values[0].shape, 1)
    low, even = lane < 64, (lane // 32) % 2 == 0
    roll = lambda value, shift: pltpu.roll(value, shift, 1)
    for first, second, shift, keep in ((0, 2, 64, low), (1, 3, 64, low), (0, 1, 32, even), (2, 3, 32, even)):
        one, two = values[first], values[second]
        values[first] = jnp.where(keep, one, roll(two, shift))
        values[second] = jnp.where(keep, roll(one, LANES - shift), two)
    return values


def in_halves(value):
    high = value.astype(jnp.bfloat16)
    return high, (value - high.astype(jnp.float32)).astype(jnp.bfloat16)


def planes_kernel(mine_ref, theirs_ref, zblock_ref, turn_ref, wide_ref, fine_ref, out_ref, high_ref, low_ref):
    step = pl.program_id(1)
    count = mine_ref.shape[1]
    groups, side = out_ref.shape[0], out_ref.shape[4]
    height = side // groups

    @pl.loop(0, count, unroll=8)
    def _(i):
        block = (mine_ref[:, i] + theirs_ref[:, i]).reshape(LANES, LANES)
        high, low = in_halves(block.T)
        both = jnp.dot(
            jnp.concatenate([high, low, high], axis=1), zblock_ref[...],
            preferred_element_type=jnp.float32,
        )
        by_cos = both[:, :LANES].reshape(8, 2, 8, LANES)
        by_sin = both[:, LANES:].reshape(8, 2, 8, LANES)
        real = by_cos[:, 0] - by_sin[:, 1]
        imag = by_sin[:, 0] + by_cos[:, 1]
        values = []
        for z in range(8):
            cos, sin = turn_ref[0, z:z + 1, :], turn_ref[1, z:z + 1, :]
            values.append((real[z] * cos - imag[z] * sin, real[z] * sin + imag[z] * cos))
        values = [jnp.concatenate(value, axis=0) for value in small_dft(values)]
        at = pl.ds(pl.multiple_of((step * count + i) * 16, 16), 16)
        for half in range(2):
            planes = swap_quarters(values[4 * half:4 * half + 4])
            for x in range(4):
                columns = slice((2 * x + half) * LANES, (2 * x + half + 1) * LANES)
                high, low = in_halves(planes[x])
                high_ref[at, columns] = high
                low_ref[at, columns] = low

    @pl.when(step == pl.num_programs(1) - 1)
    def _():
        @pl.loop(0, 4)
        def _(x):
            columns = pl.ds(pl.multiple_of(x * side, side), side)
            product = functools.partial(jnp.dot, preferred_element_type=jnp.float32)
            high = high_ref[:, columns]
            result = product(wide_ref[...], high) + (
                product(wide_ref[...], low_ref[:, columns]) + product(fine_ref[...], high)
            )
            for part in range(2):
                for group in range(groups):
                    start = part * side + group * height
                    out_ref[group, x, part] = result[start:start + height, :].astype(jnp.bfloat16)


def first_dimension_kernel(slabs, each, core_ref, *refs):
    arrays, (out_ref, mid_ref) = refs[:-2], refs[-2:]
    chunks = len(arrays) // 2
    own, other = arrays[:chunks], arrays[chunks:]
    spots = [(i, at) for i, ref in enumerate(own) for at in range(ref.shape[1])]
    core = core_ref[0]
    is_first = core == 0
    sign = (1 - 2 * core).astype(jnp.float32)

    rows = out_ref.shape[2]
    strips = [slice(at, min(at + 8, rows)) for at in range(0, rows, 8)]

    def plane(x, strip):
        slab, rest = x // (2 * each), x % (2 * each)
        half, inner = rest // each, rest % each
        chunk, at = spots[inner]
        loaded = []
        for part in range(2):
            here, there = own[chunk][slab, at, part], other[chunk][slab, at, part]
            value = jnp.where(is_first, here, there) if half == 0 else jnp.where(is_first, there, here)
            loaded.append(value.astype(jnp.float32)[strip])
        return tuple(loaded)

    for low in range(16):
        for strip in strips:
            values = small_dft([plane(low + 16 * high, strip) for high in range(16)])
            for k in range(16):
                real, imag = rotated(values[k], low * k, 256)
                if low % 2:
                    real, imag = real * sign, imag * sign
                mid_ref[k, low, 0, strip] = real
                mid_ref[k, low, 1, strip] = imag

    @pl.loop(0, 16)
    def _(k):
        for strip in strips:
            values = [(mid_ref[k, low, 0, strip], mid_ref[k, low, 1, strip]) for low in range(16)]
            even, odd = small_dft(values[0::2]), small_dft(values[1::2])
            for m in range(8):
                turned = rotated(odd[m], m, 16)
                out_ref[0, k + 16 * m, strip] = even[m][0] + turned[0]
                out_ref[1, k + 16 * m, strip] = even[m][1] + turned[1]


def host_halves(table):
    high = table.astype(jnp.bfloat16)
    return high, (table - high.astype(np.float64)).astype(jnp.bfloat16)


def transform_tables(side):
    per_row = side // 8
    grid = np.arange(per_row)
    angle = 2 * np.pi * np.outer(grid, grid) / per_row
    zblock = np.concatenate([np.kron(np.eye(4), np.cos(angle)), np.kron(np.eye(4), np.sin(angle))], axis=1)
    high, low = host_halves(zblock)
    zblock = np.concatenate([high, high, low], axis=0)
    angle = 2 * np.pi * np.outer(np.arange(8), grid) / side
    turns = np.stack([np.tile(np.cos(angle), (1, 4)), np.tile(np.sin(angle), (1, 4))]).astype(np.float32)
    cells = np.arange(side)
    angle = 2 * np.pi * (np.outer(cells, cells) % side) / side
    cos, sin = np.cos(angle).reshape(side, per_row, 1, 8), np.sin(angle).reshape(side, per_row, 1, 8)
    matrix = np.concatenate(
        [np.concatenate([cos, -sin], axis=2), np.concatenate([sin, cos], axis=2)], axis=0
    ).reshape(2 * side, 2 * side) / float(side) ** 1.5
    return (zblock, turns) + host_halves(matrix)


def sum_over_slabs(partial_sums):
    slabs = partial_sums.shape[0]
    if slabs <= 8:
        me = lax.axis_index("slab")
        row = lambda i: lax.dynamic_index_in_dim(partial_sums, me ^ i, axis=0, keepdims=True)
        returned = [row(0)] + [
            lax.ppermute(row(i), "slab", [(slab, slab ^ i) for slab in range(slabs)])
            for i in range(1, slabs)
        ]
        returned = jnp.concatenate(returned)
    else:
        returned = lax.all_to_all(partial_sums, "slab", split_axis=0, concat_axis=0, tiled=True)
    return jnp.sum(returned, axis=0)


def to_field(mine, theirs_sent, partial_sums, side):
    slabs = lax.axis_size("slab")
    per_row = side // 8
    each = side // slabs // 2
    height = side // slabs
    groups = slabs if height % 16 == 0 else 1
    tables = [jnp.asarray(table) for table in transform_tables(side)]
    swap = [(0, 1), (1, 0)]
    theirs = [lax.ppermute(chunk, "dom", swap) for chunk in theirs_sent]
    grid_shape = (-1, per_row, per_row, LANES)
    mine = mine.reshape(grid_shape)
    short = max(0, 4 - each)
    if short:
        mine = jnp.pad(mine, ((0, short), (0, 0), (0, 0), (0, 0)))
    yblocks = 8
    own = []
    first_quad = 0
    before = []
    for real_planes, added in zip(pieces_of(each), theirs):
        if before:
            added, before[0] = lax.optimization_barrier((added, before[0]))
        added = added.reshape(grid_shape)
        if short:
            added = jnp.pad(added, ((0, short), (0, 0), (0, 0), (0, 0)))
        held = real_planes + short
        quads = held // 4
        whole = lambda table: pl.BlockSpec(table.shape, lambda q, y: (0,) * table.ndim)
        sent = pl.pallas_call(
            planes_kernel,
            grid=(quads, per_row // yblocks),
            out_shape=jax.ShapeDtypeStruct((groups, held, 2, side // groups, side), jnp.bfloat16),
            in_specs=[
                pl.BlockSpec((4, yblocks, per_row, LANES), lambda q, y, at=first_quad: (at + q, y, 0, 0)),
                pl.BlockSpec((4, yblocks, per_row, LANES), lambda q, y: (q, y, 0, 0)),
            ] + [whole(table) for table in tables],
            out_specs=pl.BlockSpec((groups, 4, 2, side // groups, side), lambda q, y: (0, q, 0, 0, 0)),
            scratch_shapes=[
                pltpu.VMEM((2 * side, 4 * side), jnp.bfloat16),
                pltpu.VMEM((2 * side, 4 * side), jnp.bfloat16),
            ],
            compiler_params=params(56),
            cost_estimate=pl.CostEstimate(
                flops=held * 8 * side**3, bytes_accessed=held * 4 * side**2 * 8, transcendentals=0
            ),
            name="transform_planes",
        )(mine, added, *tables)
        if groups != slabs:
            sent = sent.reshape(-1, 2, slabs, height, side).transpose(2, 0, 1, 3, 4)[:, :real_planes]
        first_quad += quads
        if before:
            sent, own[-1] = lax.optimization_barrier((sent, own[-1]))
        if first_quad * 4 >= each:
            sent, partial_sums = lax.optimization_barrier((sent, partial_sums))
        before = [sent]
        got = lax.all_to_all(sent, "slab", split_axis=0, concat_axis=0, tiled=True)
        own.append(got)
    own[-1], losses = lax.optimization_barrier((own[-1], sum_over_slabs(partial_sums)))
    other = [lax.ppermute(got, "dom", swap) for got in own]
    rows = min(16, height)
    arrays = own + other
    field = pl.pallas_call(
        functools.partial(first_dimension_kernel, slabs, each),
        grid=(height // rows, side // LANES),
        out_shape=jax.ShapeDtypeStruct((2, side // 2, height, side), jnp.float32),
        in_specs=[SMEM_SPEC] + [
            pl.BlockSpec(array.shape[:3] + (rows, LANES), lambda y, z: (0, 0, 0, y, z))
            for array in arrays
        ],
        out_specs=pl.BlockSpec((2, side // 2, rows, LANES), lambda y, z: (0, 0, y, z)),
        scratch_shapes=[pltpu.VMEM((16, 16, 2, rows, LANES), jnp.float32)],
        compiler_params=params(56),
        name="transform_first",
    )(lax.axis_index("dom").astype(jnp.int32).reshape(1), *arrays)
    return field, losses


def gradient_of_slab(volume, kernels, images, owners, local_block, kinds, counts, ctf_code, ctf_table, scales):
    slabs = lax.axis_size("slab")
    particles, list_length, features = images.shape
    side = math.isqrt(list_length * 64)
    entries = particles * list_length
    cap = 2 * entries // slabs
    slots = slabs * cap
    blocks = volume.shape[0]
    local_bits = bits_of(blocks)
    kind_count = kernels.shape[0]
    rows = entries // LANES
    int_rows = jax.ShapeDtypeStruct((rows, LANES), jnp.int32)

    target, word, totals = pl.pallas_call(
        functools.partial(route_kernel, slabs, cap, local_bits),
        out_shape=(int_rows, int_rows, jax.ShapeDtypeStruct((slabs, LANES), jnp.int32)),
        in_specs=[VMEM_SPEC, VMEM_SPEC, VMEM_SPEC, SMEM_SPEC],
        out_specs=(VMEM_SPEC, VMEM_SPEC, VMEM_SPEC),
        compiler_params=params(56),
        name="route",
    )(owners.reshape(rows, LANES), local_block, kinds, counts)
    target, word = target.reshape(entries), word.reshape(entries)
    tiles = [cap // 2, cap // 2] if cap >= 2048 else [cap]
    parts = len(tiles)
    code = ctf_code | ((scales.astype(jnp.float32) * 256.0).astype(jnp.int32) << 8)
    stride = cap + LANES
    meta, *packed = pl.pallas_call(
        functools.partial(pack_kernel, slabs, cap, list_length),
        out_shape=(jax.ShapeDtypeStruct((slabs * stride,), jnp.int32),)
        + tuple(jax.ShapeDtypeStruct((slabs, tile, features), jnp.bfloat16) for tile in tiles),
        in_specs=[SMEM_SPEC] * 5 + [VMEM_SPEC],
        out_specs=(SMEM_SPEC,) + (VMEM_SPEC,) * parts,
        scratch_shapes=[
            pltpu.VMEM((entries, features), jnp.float32),
            pltpu.VMEM((slabs * stride, features), jnp.float32),
        ],
        compiler_params=params(56),
        name="pack",
    )(target, word, counts, totals, code, images.reshape(entries, features))
    arrived = lax.all_to_all(
        meta.reshape(slabs, stride), "slab", split_axis=0, concat_axis=0, tiled=True
    )
    words = arrived[:, :cap]
    totals_in = arrived[:, cap]
    codes_in = arrived[:, cap + 1:cap + 1 + particles]
    live = (jnp.arange(cap, dtype=jnp.int32)[None, :] < totals_in[:, None]).astype(jnp.int32)
    table_rows = ctf_table[(codes_in & 255).reshape(-1)]
    scale_in = (codes_in >> 8).astype(jnp.float32).reshape(-1) * (1.0 / 256.0)

    index = pl.pallas_call(
        functools.partial(decode_kernel, local_bits, blocks),
        out_shape=jax.ShapeDtypeStruct((slots // LANES, LANES), jnp.int32),
        in_specs=[VMEM_SPEC, VMEM_SPEC],
        out_specs=VMEM_SPEC,
        compiler_params=params(56),
        name="decode",
    )(words.reshape(slots // LANES, LANES), live.reshape(slots // LANES, LANES))
    index = index.reshape(slots)
    voxels = list(pl.pallas_call(
        functools.partial(gather_kernel, slabs, cap),
        out_shape=tuple(
            jax.ShapeDtypeStruct((slabs, tile, features), jnp.bfloat16) for tile in tiles
        ),
        in_specs=[SMEM_SPEC, SMEM_SPEC, VMEM_SPEC],
        out_specs=(VMEM_SPEC,) * parts,
        scratch_shapes=[
            pltpu.VMEM((blocks + 8, features), jnp.float32),
            pltpu.VMEM((cap, features), jnp.float32),
        ],
        compiler_params=params(56),
        cost_estimate=pl.CostEstimate(flops=0, bytes_accessed=100 * MIB, transcendentals=0),
        name="read_voxels",
    )(index, totals_in, volume))

    forward = jnp.transpose(kernels, (0, 2, 1)).reshape(kind_count * features, features)
    backward = kernels.reshape(kind_count, 2, 8, 8, features).transpose(3, 1, 2, 0, 4)
    backward = backward.reshape(features, kind_count * features)
    unit = jnp.eye(features, dtype=jnp.bfloat16)
    core = lax.axis_index("dom").astype(jnp.int32).reshape(1)
    plane_blocks = (side // 8) ** 2
    pieces = [planes * plane_blocks for planes in pieces_of(side // slabs // 2)]
    squares, sums, behind, offset = 0.0, None, [voxels[0]], 0
    for part, tile in enumerate(tiles):
        first, last = part == 0, part == parts - 1
        if not first:
            packed[part], earlier = lax.optimization_barrier((packed[part], behind[part - 1]))
            if part == 1:
                voxels[0] = earlier
        picture = lax.all_to_all(packed[part], "slab", split_axis=0, concat_axis=0, tiled=True)
        lengths = [blocks // 2] + pieces if last else []
        arguments = [
            totals_in, table_rows[:, 0], table_rows[:, 1], scale_in, index, core,
            words[:, offset:offset + tile].reshape(slabs, 1, tile), voxels[part], picture,
            forward, backward, unit,
        ]
        aliases = {}
        if not first:
            aliases = {len(arguments): 1}
            arguments.append(pltpu.with_memory_space_constraint(sums, pltpu.VMEM))
        more, sums, *halves = pl.pallas_call(
            functools.partial(
                slab_kernel, side, local_bits, list_length, particles, cap, offset, first, last
            ),
            out_shape=(
                jax.ShapeDtypeStruct((slabs, particles, LANES), jnp.float32),
                pltpu.VMEM((blocks + 8, features), jnp.float32),
            )
            + tuple(jax.ShapeDtypeStruct((length, features), jnp.float32) for length in lengths),
            in_specs=[SMEM_SPEC] * 6 + [VMEM_SPEC] * (len(arguments) - 6),
            out_specs=(VMEM_SPEC, VMEM_SPEC) + (ANY_SPEC,) * len(lengths),
            scratch_shapes=[
                pltpu.VMEM((tile, features), jnp.float32),
                pltpu.SemaphoreType.DMA((max(1, len(lengths)),)),
            ],
            input_output_aliases=aliases,
            compiler_params=params(24),
            cost_estimate=pl.CostEstimate(flops=0, bytes_accessed=16 * MIB, transcendentals=0),
            name="compare_and_add",
        )(*arguments)
        squares = squares + more
        behind.append(more)
        offset += tile
    mine, *theirs = halves
    partial_sums = jnp.sum(squares, axis=2)
    return mine, theirs, partial_sums, side


def body(*arrays):
    mine, theirs, partial_sums, side = gradient_of_slab(*arrays)
    field, squares = to_field(mine, theirs, partial_sums, side)
    counts = arrays[6]
    return field, squares / (counts.astype(jnp.float32) * 128.0)


def solution(mesh):
    in_specs = (
        P(("groups", "slab"), None),
        P(),
        P(("groups", "slab", "dom"), None, None),
        P(("groups", "slab", "dom"), None, None),
        P(("groups", "slab", "dom"), None),
        P(("groups", "slab", "dom"), None),
        P(("groups", "slab", "dom")),
        P(("groups", "slab", "dom")),
        P(),
        P(("groups", "slab", "dom")),
    )
    out_specs = (P(None, ("groups", "dom"), "slab", None), P(("groups", "slab", "dom")))
    return jax.shard_map(body, mesh=mesh, in_specs=in_specs, out_specs=out_specs, check_vma=False)
```

```python
import functools
import math

import jax
import jax.numpy as jnp
import numpy as np
from jax import lax
from jax.experimental import pallas as pl
from jax.experimental.pallas import tpu as pltpu
from jax.sharding import PartitionSpec as P

LANES = 128
GROUP = 16
UNUSED = 100
STEP = 256
MIB = 1024 * 1024

SMEM_SPEC = pl.BlockSpec(memory_space=pltpu.SMEM)
VMEM_SPEC = pl.BlockSpec(memory_space=pltpu.VMEM)
ANY_SPEC = pl.BlockSpec(memory_space=pl.ANY)


def params(mib):
    return pltpu.CompilerParams(vmem_limit_bytes=mib * MIB)


def bits_of(count):
    return (count - 1).bit_length()


def route_kernel(slabs, cap, local_bits, owner_ref, local_ref, kind_ref, counts_ref, target_ref, word_ref, totals_ref):
    particles, list_length = local_ref.shape
    rows_each = list_length // LANES
    rows = particles * rows_each
    gathered = lambda ref: jnp.concatenate(
        [ref[:, j * LANES:(j + 1) * LANES] for j in range(rows_each)], axis=0
    )
    row_id = lax.broadcasted_iota(jnp.int32, (rows, LANES), 0)
    lane_id = lax.broadcasted_iota(jnp.int32, (rows, LANES), 1)
    particle = row_id % particles
    position = (row_id // particles) * LANES + lane_id
    limit = jnp.zeros((rows, LANES), jnp.int32)
    for i in range(particles):
        limit = jnp.where(particle == i, counts_ref[i], limit)
    owner = jnp.concatenate(
        [owner_ref[pl.ds(j, particles, stride=rows_each), :] for j in range(rows_each)], axis=0
    )
    owner = jnp.where(position < limit, owner, -1)
    up_to = (
        lax.broadcasted_iota(jnp.int32, (LANES, LANES), 0)
        <= lax.broadcasted_iota(jnp.int32, (LANES, LANES), 1)
    ).astype(jnp.bfloat16)
    ones = jnp.ones((LANES, LANES), jnp.bfloat16)
    before = (
        lax.broadcasted_iota(jnp.int32, (rows, rows), 1)
        < lax.broadcasted_iota(jnp.int32, (rows, rows), 0)
    ).astype(jnp.bfloat16)

    def one_slab(slab, target):
        mine = owner == slab
        hits = mine.astype(jnp.float32).astype(jnp.bfloat16)
        inside = jnp.dot(hits, up_to, preferred_element_type=jnp.float32)
        row_sum = jnp.dot(hits, ones, preferred_element_type=jnp.float32)
        above = jnp.dot(before, row_sum.astype(jnp.bfloat16), preferred_element_type=jnp.float32)
        rank = (inside + above).astype(jnp.int32) - 1
        total = (above[rows - 1:rows, :] + row_sum[rows - 1:rows, :]).astype(jnp.int32)
        totals_ref[pl.ds(slab, 1), :] = total
        return jnp.where(mine, slab * (cap + LANES) + rank, target)

    target = lax.fori_loop(0, slabs, one_slab, jnp.full((rows, LANES), cap + UNUSED, jnp.int32))
    target_ref[...] = target
    kind_bits = local_bits
    word = gathered(local_ref) | (gathered(kind_ref) << kind_bits) | (position << (kind_bits + 2))
    word_ref[...] = word | (particle << (kind_bits + 2 + bits_of(list_length)))


def pack_kernel(slabs, cap, list_length, target_ref, word_ref, counts_ref, totals_ref, code_ref, image_ref, meta_ref, *refs):
    out_refs, (wide_ref, staged_ref) = refs[:-2], refs[-2:]
    particles = counts_ref.shape[0]
    stride = cap + LANES
    step = 256

    @pl.loop(0, image_ref.shape[0] // step)
    def _(i):
        at = pl.multiple_of(i * step, step)
        wide_ref[pl.ds(at, step), :] = image_ref[pl.ds(at, step), :].astype(jnp.float32)

    @pl.loop(0, particles)
    def _(particle):
        @pl.loop(0, (counts_ref[particle] + 15) // 16)
        def _(i):
            first = (i // 8) * (particles * LANES) + particle * LANES + (i % 8) * 16
            row = particle * list_length + i * 16
            targets = [target_ref[first + j] for j in range(16)]
            words = [word_ref[first + j] for j in range(16)]
            rows = [wide_ref[pl.ds(row + j, 1), :] for j in range(16)]
            for j in range(16):
                staged_ref[pl.ds(targets[j], 1), :] = rows[j]
                meta_ref[targets[j]] = words[j]

    @pl.loop(0, slabs)
    def _(slab):
        header = slab * stride + cap
        meta_ref[header] = totals_ref[slab, 0]
        for j in range(particles):
            meta_ref[header + 1 + j] = code_ref[j]

    offset = 0
    for out_ref in out_refs:
        width = out_ref.shape[1]

        @pl.loop(0, slabs)
        def _(slab, offset=offset):
            at = pl.multiple_of(slab * stride + offset, LANES)
            out_ref[slab] = staged_ref[pl.ds(at, width), :].astype(jnp.bfloat16)

        offset += width


def decode_kernel(local_bits, dummy, word_ref, live_ref, index_ref):
    rows = word_ref.shape[0]
    live = live_ref[...] != 0
    index = jnp.where(live, word_ref[...] & ((1 << local_bits) - 1), dummy)
    lane = lax.broadcasted_iota(jnp.int32, (rows, LANES), 1)
    clash = jnp.zeros((rows, LANES), jnp.int32)
    for shift in range(1, GROUP):
        earlier = pltpu.roll(index, shift, 1)
        same = (earlier == index) & (lane % GROUP >= shift) & live
        clash = clash | same.astype(jnp.int32)
    shift = 1
    while shift < LANES:
        if shift == GROUP:
            index = index | jnp.where(lane % GROUP == 0, clash << 24, 0)
        clash = clash | pltpu.roll(clash, LANES - shift, 1)
        shift *= 2
    index_ref[0:rows, :] = index | jnp.where(lane == 0, clash << 25, 0)
    index_ref[rows:, :] = jnp.full((index_ref.shape[0] - rows, LANES), dummy, jnp.int32)


def gather_kernel(slabs, cap, index_ref, totals_ref, volume_ref, *refs):
    out_refs, (wide_ref, staged_ref) = refs[:-2], refs[-2:]
    blocks = volume_ref.shape[0]
    step = 256

    @pl.loop(0, blocks // step)
    def _(i):
        at = pl.multiple_of(i * step, step)
        wide_ref[pl.ds(at, step), :] = volume_ref[pl.ds(at, step), :].astype(jnp.float32)

    @pl.loop(0, slabs)
    def _(source):
        live = totals_ref[source]

        @pl.loop(0, (live + 15) // 16)
        def _(i):
            first = source * cap + i * 16
            places = [index_ref[first] & 0xFFFFFF] + [index_ref[first + j] for j in range(1, 16)]
            rows = [wide_ref[pl.ds(places[j], 1), :] for j in range(16)]
            for j in range(16):
                staged_ref[pl.ds(i * 16 + j, 1), :] = rows[j]

        offset = 0
        for out_ref in out_refs:
            width = out_ref.shape[1]

            @pl.when(live > offset)
            def _(offset=offset):
                out_ref[source] = staged_ref[offset:offset + width, :].astype(jnp.bfloat16)

            offset += width


def sine(angle):
    turns = jnp.floor(angle * (1.0 / math.pi) + 0.5)
    rest = angle - turns * 3.140625
    rest = rest - turns * (math.pi - 3.140625)
    odd = turns - 2.0 * jnp.floor(turns * 0.5)
    square = rest * rest
    poly = 2.718121e-6
    poly = poly * square - 1.9839334e-4
    poly = poly * square + 8.3333293e-3
    poly = poly * square - 1.6666667e-1
    value = rest + rest * square * poly
    return value * (1.0 - 2.0 * odd)


def slab_kernel(
    side, local_bits, list_length, particles, cap, offset, first, last,
    totals_ref, defocus_ref, phase_ref, scale_ref, index_ref, core_ref,
    word_ref, voxel_ref, image_ref, forward_ref, backward_ref, unit_ref, *rest,
):
    if not first:
        rest = rest[1:]
    square_ref, sum_ref, out_refs, (staged_ref, steps_ref, sems) = rest[0], rest[1], rest[2:-3], rest[-3:]
    slabs, _, tile = word_ref.shape
    step = staged_ref.shape[0]
    steps_each = tile // step
    blocks = sum_ref.shape[0] - 8
    features = image_ref.shape[2]
    kinds = forward_ref.shape[0] // features
    position_bits = bits_of(list_length)
    per_row = side // 8
    half = features // 2

    if first:
        @pl.loop(0, blocks // 256)
        def _(i):
            at = pl.multiple_of(i * 256, 256)
            sum_ref[pl.ds(at, 256), :] = jnp.zeros((256, features), jnp.float32)

    square_ref[...] = jnp.zeros_like(square_ref)
    live_of = lambda source: jnp.clip(totals_ref[source] - offset, 0, tile)

    def list_source(source, count):
        def list_step(i, count):
            steps_ref[count] = source * steps_each + i
            return count + 1

        return lax.fori_loop(0, (live_of(source) + step - 1) // step, list_step, count)

    steps_ref[0] = 0
    count = lax.fori_loop(0, slabs, list_source, 0)

    def compare(number):
        which_step = steps_ref[jnp.minimum(number, jnp.maximum(count - 1, 0))]
        source, at = which_step // steps_each, (which_step % steps_each) * step
        at = pl.multiple_of(at, step)
        live = jnp.where(number < count, live_of(source) - at, 0)
        word = word_ref[source, :, pl.ds(at, step)]
        kind = (word >> local_bits) & 3
        position = (word >> (local_bits + 2)) & (list_length - 1)
        particle = (word >> (local_bits + 2 + position_bits)) & (particles - 1)
        valid = lax.broadcasted_iota(jnp.int32, (1, step), 1) < live
        defocus = jnp.zeros((1, step), jnp.float32)
        phase = jnp.zeros((1, step), jnp.float32)
        scale = jnp.zeros((1, step), jnp.float32)
        for j in range(particles):
            chosen = particle == j
            defocus = jnp.where(chosen, defocus_ref[source * particles + j], defocus)
            phase = jnp.where(chosen, phase_ref[source * particles + j], phase)
            scale = jnp.where(chosen, scale_ref[source * particles + j], scale)
        defocus = defocus * (1.0 / float((side // 2) ** 2))
        cell = lax.broadcasted_iota(jnp.int32, (half, LANES), 0)
        cell_vert, cell_horiz = (cell // 8).astype(jnp.float32), (cell % 8).astype(jnp.float32)
        repeat = lambda table: jnp.concatenate([table] * (step // LANES), axis=1)
        vert = ((position // per_row) * 8 - side // 2).astype(jnp.float32) + repeat(cell_vert)
        horiz = ((position % per_row) * 8 - side // 2).astype(jnp.float32) + repeat(cell_horiz)
        factor = scale * sine(defocus * (vert * vert + horiz * horiz) + phase)
        factor = jnp.concatenate([factor, factor], axis=0)
        contract_last = (((1,), (1,)), ((), ()))
        each_kind = lax.dot_general(
            forward_ref[...], voxel_ref[source, pl.ds(at, step), :], contract_last,
            preferred_element_type=jnp.float32,
        )
        extracted = each_kind[0:features, :]
        for k in range(1, kinds):
            extracted = jnp.where(kind == k, each_kind[k * features:(k + 1) * features, :], extracted)
        picture = lax.dot_general(
            unit_ref[...], image_ref[source, pl.ds(at, step), :], contract_last,
            preferred_element_type=jnp.float32,
        )
        misfit = jnp.where(valid, factor * extracted - picture, 0.0)
        squares = jnp.sum(misfit * misfit, axis=0, keepdims=True)
        which = lax.broadcasted_iota(jnp.int32, (particles, step), 0)
        spread = jnp.where(valid & (particle == which), squares, 0.0)
        folded = spread[:, 0:LANES]
        for i in range(1, step // LANES):
            folded = folded + spread[:, i * LANES:(i + 1) * LANES]
        square_ref[source] = square_ref[source] + folded
        weighted = (factor * misfit).astype(jnp.bfloat16)
        none = jnp.zeros_like(weighted)
        spread_back = jnp.concatenate(
            [jnp.where(kind == k, weighted, none) for k in range(kinds)], axis=0
        )
        terms = jnp.dot(backward_ref[...], spread_back, preferred_element_type=jnp.float32)
        staged_ref[...] = terms.T

    def places_of(base):
        return [index_ref[base] & 0xFFFFFF] + [index_ref[base + j] for j in range(1, GROUP)]

    def add_group(base, at):
        places = places_of(base)
        held = [sum_ref[pl.ds(place, 1), :] for place in places]
        new = [staged_ref[pl.ds(at + j, 1), :] for j in range(GROUP)]
        for j in range(GROUP):
            sum_ref[pl.ds(places[j], 1), :] = held[j] + new[j]

    @pl.loop(0, count + 1)
    def _(number):
        earlier = steps_ref[jnp.maximum(number - 1, 0)]
        base = (earlier // steps_each) * cap + offset + (earlier % steps_each) * step
        base = jnp.where(number > 0, base, slabs * cap)
        marks = index_ref[base]
        for i in range(1, step // LANES):
            marks = marks | index_ref[base + i * LANES]

        @pl.when(marks < (1 << 25))
        def _():
            for g in range(step // GROUP):
                add_group(base + g * GROUP, g * GROUP)
            compare(number)

        @pl.when(marks >= (1 << 25))
        def _():
            @pl.loop(0, step // GROUP)
            def _(g):
                start = base + g * GROUP
                clashes = (index_ref[start] >> 24) & 1

                @pl.when(clashes == 0)
                def _():
                    add_group(start, g * GROUP)

                @pl.when(clashes == 1)
                def _():
                    places = places_of(start)
                    for j in range(GROUP):
                        sum_ref[pl.ds(places[j], 1), :] = (
                            sum_ref[pl.ds(places[j], 1), :] + staged_ref[pl.ds(g * GROUP + j, 1), :]
                        )

            compare(number)

    if last:
        half = blocks // 2
        start = (1 - core_ref[0]) * half
        places = [core_ref[0] * half]
        for out_ref in out_refs[1:]:
            places.append(start)
            start = start + out_ref.shape[0]
        copies = []
        for i, (place, out_ref) in enumerate(zip(places, out_refs)):
            length = out_ref.shape[0]
            at = pl.multiple_of(place, 8)
            copies.append(pltpu.make_async_copy(sum_ref.at[pl.ds(at, length)], out_ref, sems.at[i]))
        for copy in copies:
            copy.start()
        for copy in copies:
            copy.wait()


def pieces_of(planes):
    if planes < 16:
        return [planes]
    return [4, planes - 4]


def rotated(value, turn, length, sign=None):
    real, imag = value
    if turn == 0 or 4 * turn == length:
        if turn:
            real, imag = -imag, real
        return (real, imag) if sign is None else (real * sign, imag * sign)
    if sign is None and 8 * turn in (length, 3 * length):
        root = math.sqrt(0.5)
        if 8 * turn == length:
            return ((real - imag) * root, (real + imag) * root)
        return ((real + imag) * -root, (real - imag) * root)
    cos, sin = math.cos(2 * math.pi * turn / length), math.sin(2 * math.pi * turn / length)
    if sign is not None:
        cos, sin = cos * sign, sin * sign
    return (real * cos - imag * sin, real * sin + imag * cos)


def small_dft(values):
    length = len(values)
    if length == 1:
        return values
    even, odd = small_dft(values[0::2]), small_dft(values[1::2])
    low, high = [], []
    for k in range(length // 2):
        turned = rotated(odd[k], k, length)
        low.append((even[k][0] + turned[0], even[k][1] + turned[1]))
        high.append((even[k][0] - turned[0], even[k][1] - turned[1]))
    return low + high


def swap_quarters(values):
    lane = lax.broadcasted_iota(jnp.int32, values[0].shape, 1)
    low, even = lane < 64, (lane // 32) % 2 == 0
    roll = lambda value, shift: pltpu.roll(value, shift, 1)
    for first, second, shift, keep in ((0, 2, 64, low), (1, 3, 64, low), (0, 1, 32, even), (2, 3, 32, even)):
        one, two = values[first], values[second]
        values[first] = jnp.where(keep, one, roll(two, shift))
        values[second] = jnp.where(keep, roll(one, LANES - shift), two)
    return values


def in_halves(value):
    high = value.astype(jnp.bfloat16)
    return high, (value - high.astype(jnp.float32)).astype(jnp.bfloat16)


def planes_kernel(mine_ref, theirs_ref, zblock_ref, turn_ref, wide_ref, fine_ref, out_ref, high_ref, low_ref):
    step = pl.program_id(1)
    count = mine_ref.shape[1]
    groups, side = out_ref.shape[0], out_ref.shape[4]
    height = side // groups

    @pl.loop(0, count, unroll=8)
    def _(i):
        block = (mine_ref[:, i] + theirs_ref[:, i]).reshape(LANES, LANES)
        high, low = in_halves(block.T)
        both = jnp.dot(
            jnp.concatenate([high, low, high], axis=1), zblock_ref[...],
            preferred_element_type=jnp.float32,
        )
        by_cos = both[:, :LANES].reshape(8, 2, 8, LANES)
        by_sin = both[:, LANES:].reshape(8, 2, 8, LANES)
        real = by_cos[:, 0] - by_sin[:, 1]
        imag = by_sin[:, 0] + by_cos[:, 1]
        values = []
        for z in range(8):
            cos, sin = turn_ref[0, z:z + 1, :], turn_ref[1, z:z + 1, :]
            values.append((real[z] * cos - imag[z] * sin, real[z] * sin + imag[z] * cos))
        values = [jnp.concatenate(value, axis=0) for value in small_dft(values)]
        at = pl.ds(pl.multiple_of((step * count + i) * 16, 16), 16)
        for half in range(2):
            planes = swap_quarters(values[4 * half:4 * half + 4])
            for x in range(4):
                columns = slice((2 * x + half) * LANES, (2 * x + half + 1) * LANES)
                high, low = in_halves(planes[x])
                high_ref[at, columns] = high
                low_ref[at, columns] = low

    @pl.when(step == pl.num_programs(1) - 1)
    def _():
        @pl.loop(0, 4)
        def _(x):
            columns = pl.ds(pl.multiple_of(x * side, side), side)
            product = functools.partial(jnp.dot, preferred_element_type=jnp.float32)
            high = high_ref[:, columns]
            result = product(wide_ref[...], high) + (
                product(wide_ref[...], low_ref[:, columns]) + product(fine_ref[...], high)
            )
            for part in range(2):
                for group in range(groups):
                    start = part * side + group * height
                    out_ref[group, x, part] = result[start:start + height, :].astype(jnp.bfloat16)


def first_dimension_kernel(slabs, each, core_ref, *refs):
    arrays, (out_ref, mid_ref) = refs[:-2], refs[-2:]
    chunks = len(arrays) // 2
    own, other = arrays[:chunks], arrays[chunks:]
    spots = [(i, at) for i, ref in enumerate(own) for at in range(ref.shape[1])]
    core = core_ref[0]
    is_first = core == 0
    sign = (1 - 2 * core).astype(jnp.float32)

    rows = out_ref.shape[2]
    strips = [slice(at, min(at + 8, rows)) for at in range(0, rows, 8)]

    def plane(x, strip):
        slab, rest = x // (2 * each), x % (2 * each)
        half, inner = rest // each, rest % each
        chunk, at = spots[inner]
        loaded = []
        for part in range(2):
            here, there = own[chunk][slab, at, part], other[chunk][slab, at, part]
            value = jnp.where(is_first, here, there) if half == 0 else jnp.where(is_first, there, here)
            loaded.append(value.astype(jnp.float32)[strip])
        return tuple(loaded)

    for low in range(16):
        for strip in strips:
            values = small_dft([plane(low + 16 * high, strip) for high in range(16)])
            for k in range(16):
                real, imag = rotated(values[k], low * k, 256, sign if low % 2 else None)
                mid_ref[k, low, 0, strip] = real
                mid_ref[k, low, 1, strip] = imag

    @pl.loop(0, 16)
    def _(k):
        for strip in strips:
            values = [(mid_ref[k, low, 0, strip], mid_ref[k, low, 1, strip]) for low in range(16)]
            even, odd = small_dft(values[0::2]), small_dft(values[1::2])
            for m in range(8):
                turned = rotated(odd[m], m, 16)
                out_ref[0, k + 16 * m, strip] = even[m][0] + turned[0]
                out_ref[1, k + 16 * m, strip] = even[m][1] + turned[1]


def host_halves(table):
    high = table.astype(jnp.bfloat16)
    return high, (table - high.astype(np.float64)).astype(jnp.bfloat16)


def transform_tables(side):
    per_row = side // 8
    grid = np.arange(per_row)
    angle = 2 * np.pi * np.outer(grid, grid) / per_row
    zblock = np.concatenate([np.kron(np.eye(4), np.cos(angle)), np.kron(np.eye(4), np.sin(angle))], axis=1)
    high, low = host_halves(zblock)
    zblock = np.concatenate([high, high, low], axis=0)
    angle = 2 * np.pi * np.outer(np.arange(8), grid) / side
    turns = np.stack([np.tile(np.cos(angle), (1, 4)), np.tile(np.sin(angle), (1, 4))]).astype(np.float32)
    cells = np.arange(side)
    angle = 2 * np.pi * (np.outer(cells, cells) % side) / side
    cos, sin = np.cos(angle).reshape(side, per_row, 1, 8), np.sin(angle).reshape(side, per_row, 1, 8)
    matrix = np.concatenate(
        [np.concatenate([cos, -sin], axis=2), np.concatenate([sin, cos], axis=2)], axis=0
    ).reshape(2 * side, 2 * side) / float(side) ** 1.5
    return (zblock, turns) + host_halves(matrix)


def sum_over_slabs(partial_sums):
    slabs = partial_sums.shape[0]
    if slabs <= 8:
        me = lax.axis_index("slab")
        row = lambda i: lax.dynamic_index_in_dim(partial_sums, me ^ i, axis=0, keepdims=True)
        returned = [row(0)] + [
            lax.ppermute(row(i), "slab", [(slab, slab ^ i) for slab in range(slabs)])
            for i in range(1, slabs)
        ]
        returned = jnp.concatenate(returned)
    else:
        returned = lax.all_to_all(partial_sums, "slab", split_axis=0, concat_axis=0, tiled=True)
    return jnp.sum(returned, axis=0)


def to_field(mine, theirs_sent, partial_sums, side):
    slabs = lax.axis_size("slab")
    per_row = side // 8
    each = side // slabs // 2
    height = side // slabs
    groups = slabs if height % 16 == 0 else 1
    tables = [jnp.asarray(table) for table in transform_tables(side)]
    swap = [(0, 1), (1, 0)]
    theirs = [lax.ppermute(chunk, "dom", swap) for chunk in theirs_sent]
    grid_shape = (-1, per_row, per_row, LANES)
    mine = mine.reshape(grid_shape)
    short = max(0, 4 - each)
    if short:
        mine = jnp.pad(mine, ((0, short), (0, 0), (0, 0), (0, 0)))
    yblocks = 8
    own = []
    first_quad = 0
    before = []
    for real_planes, added in zip(pieces_of(each), theirs):
        if before:
            added, before[0] = lax.optimization_barrier((added, before[0]))
        added = added.reshape(grid_shape)
        if short:
            added = jnp.pad(added, ((0, short), (0, 0), (0, 0), (0, 0)))
        held = real_planes + short
        quads = held // 4
        whole = lambda table: pl.BlockSpec(table.shape, lambda q, y: (0,) * table.ndim)
        sent = pl.pallas_call(
            planes_kernel,
            grid=(quads, per_row // yblocks),
            out_shape=jax.ShapeDtypeStruct((groups, held, 2, side // groups, side), jnp.bfloat16),
            in_specs=[
                pl.BlockSpec((4, yblocks, per_row, LANES), lambda q, y, at=first_quad: (at + q, y, 0, 0)),
                pl.BlockSpec((4, yblocks, per_row, LANES), lambda q, y: (q, y, 0, 0)),
            ] + [whole(table) for table in tables],
            out_specs=pl.BlockSpec((groups, 4, 2, side // groups, side), lambda q, y: (0, q, 0, 0, 0)),
            scratch_shapes=[
                pltpu.VMEM((2 * side, 4 * side), jnp.bfloat16),
                pltpu.VMEM((2 * side, 4 * side), jnp.bfloat16),
            ],
            compiler_params=params(56),
            cost_estimate=pl.CostEstimate(
                flops=held * 8 * side**3, bytes_accessed=held * 4 * side**2 * 8, transcendentals=0
            ),
            name="transform_planes",
        )(mine, added, *tables)
        if groups != slabs:
            sent = sent.reshape(-1, 2, slabs, height, side).transpose(2, 0, 1, 3, 4)[:, :real_planes]
        first_quad += quads
        if before:
            sent, own[-1] = lax.optimization_barrier((sent, own[-1]))
        if first_quad * 4 >= each:
            sent, partial_sums = lax.optimization_barrier((sent, partial_sums))
        before = [sent]
        got = lax.all_to_all(sent, "slab", split_axis=0, concat_axis=0, tiled=True)
        own.append(got)
    own[-1], losses = lax.optimization_barrier((own[-1], sum_over_slabs(partial_sums)))
    other = [lax.ppermute(got, "dom", swap) for got in own]
    rows = min(16, height)
    arrays = own + other
    field = pl.pallas_call(
        functools.partial(first_dimension_kernel, slabs, each),
        grid=(height // rows, side // LANES),
        out_shape=jax.ShapeDtypeStruct((2, side // 2, height, side), jnp.float32),
        in_specs=[SMEM_SPEC] + [
            pl.BlockSpec(array.shape[:3] + (rows, LANES), lambda y, z: (0, 0, 0, y, z))
            for array in arrays
        ],
        out_specs=pl.BlockSpec((2, side // 2, rows, LANES), lambda y, z: (0, 0, y, z)),
        scratch_shapes=[pltpu.VMEM((16, 16, 2, rows, LANES), jnp.float32)],
        compiler_params=params(56),
        name="transform_first",
    )(lax.axis_index("dom").astype(jnp.int32).reshape(1), *arrays)
    return field, losses


def gradient_of_slab(volume, kernels, images, owners, local_block, kinds, counts, ctf_code, ctf_table, scales):
    slabs = lax.axis_size("slab")
    particles, list_length, features = images.shape
    side = math.isqrt(list_length * 64)
    entries = particles * list_length
    cap = 2 * entries // slabs
    slots = slabs * cap
    blocks = volume.shape[0]
    local_bits = bits_of(blocks)
    kind_count = kernels.shape[0]
    rows = entries // LANES
    int_rows = jax.ShapeDtypeStruct((rows, LANES), jnp.int32)

    target, word, totals = pl.pallas_call(
        functools.partial(route_kernel, slabs, cap, local_bits),
        out_shape=(int_rows, int_rows, jax.ShapeDtypeStruct((slabs, LANES), jnp.int32)),
        in_specs=[VMEM_SPEC, VMEM_SPEC, VMEM_SPEC, SMEM_SPEC],
        out_specs=(VMEM_SPEC, VMEM_SPEC, VMEM_SPEC),
        compiler_params=params(56),
        name="route",
    )(owners.reshape(rows, LANES), local_block, kinds, counts)
    target, word = target.reshape(entries), word.reshape(entries)
    tiles = [cap // 2, cap // 2] if cap >= 2048 else [cap]
    parts = len(tiles)
    code = ctf_code | ((scales.astype(jnp.float32) * 256.0).astype(jnp.int32) << 8)
    stride = cap + LANES
    meta, *packed = pl.pallas_call(
        functools.partial(pack_kernel, slabs, cap, list_length),
        out_shape=(jax.ShapeDtypeStruct((slabs * stride,), jnp.int32),)
        + tuple(jax.ShapeDtypeStruct((slabs, tile, features), jnp.bfloat16) for tile in tiles),
        in_specs=[SMEM_SPEC] * 5 + [VMEM_SPEC],
        out_specs=(SMEM_SPEC,) + (VMEM_SPEC,) * parts,
        scratch_shapes=[
            pltpu.VMEM((entries, features), jnp.float32),
            pltpu.VMEM((slabs * stride, features), jnp.float32),
        ],
        compiler_params=params(56),
        name="pack",
    )(target, word, counts, totals, code, images.reshape(entries, features))
    arrived = lax.all_to_all(
        meta.reshape(slabs, stride), "slab", split_axis=0, concat_axis=0, tiled=True
    )
    words = arrived[:, :cap]
    totals_in = arrived[:, cap]
    codes_in = arrived[:, cap + 1:cap + 1 + particles]
    live = (jnp.arange(cap, dtype=jnp.int32)[None, :] < totals_in[:, None]).astype(jnp.int32)
    table_rows = ctf_table[(codes_in & 255).reshape(-1)]
    scale_in = (codes_in >> 8).astype(jnp.float32).reshape(-1) * (1.0 / 256.0)

    index = pl.pallas_call(
        functools.partial(decode_kernel, local_bits, blocks),
        out_shape=jax.ShapeDtypeStruct((slots // LANES + 8, LANES), jnp.int32),
        in_specs=[VMEM_SPEC, VMEM_SPEC],
        out_specs=VMEM_SPEC,
        compiler_params=params(56),
        name="decode",
    )(words.reshape(slots // LANES, LANES), live.reshape(slots // LANES, LANES))
    index = index.reshape(slots + 8 * LANES)
    voxels = list(pl.pallas_call(
        functools.partial(gather_kernel, slabs, cap),
        out_shape=tuple(
            jax.ShapeDtypeStruct((slabs, tile, features), jnp.bfloat16) for tile in tiles
        ),
        in_specs=[SMEM_SPEC, SMEM_SPEC, VMEM_SPEC],
        out_specs=(VMEM_SPEC,) * parts,
        scratch_shapes=[
            pltpu.VMEM((blocks + 8, features), jnp.float32),
            pltpu.VMEM((cap, features), jnp.float32),
        ],
        compiler_params=params(56),
        cost_estimate=pl.CostEstimate(flops=0, bytes_accessed=100 * MIB, transcendentals=0),
        name="read_voxels",
    )(index, totals_in, volume))

    forward = jnp.transpose(kernels, (0, 2, 1)).reshape(kind_count * features, features)
    backward = kernels.reshape(kind_count, 2, 8, 8, features).transpose(3, 1, 2, 0, 4)
    backward = backward.reshape(features, kind_count * features)
    unit = jnp.eye(features, dtype=jnp.bfloat16)
    core = lax.axis_index("dom").astype(jnp.int32).reshape(1)
    plane_blocks = (side // 8) ** 2
    pieces = [planes * plane_blocks for planes in pieces_of(side // slabs // 2)]
    squares, sums, behind, offset = 0.0, None, [voxels[0]], 0
    for part, tile in enumerate(tiles):
        first, last = part == 0, part == parts - 1
        if not first:
            packed[part], earlier = lax.optimization_barrier((packed[part], behind[part - 1]))
            if part == 1:
                voxels[0] = earlier
        picture = lax.all_to_all(packed[part], "slab", split_axis=0, concat_axis=0, tiled=True)
        lengths = [blocks // 2] + pieces if last else []
        arguments = [
            totals_in, table_rows[:, 0], table_rows[:, 1], scale_in, index, core,
            words[:, offset:offset + tile].reshape(slabs, 1, tile), voxels[part], picture,
            forward, backward, unit,
        ]
        aliases = {}
        if not first:
            aliases = {len(arguments): 1}
            arguments.append(pltpu.with_memory_space_constraint(sums, pltpu.VMEM))
        more, sums, *halves = pl.pallas_call(
            functools.partial(
                slab_kernel, side, local_bits, list_length, particles, cap, offset, first, last
            ),
            out_shape=(
                jax.ShapeDtypeStruct((slabs, particles, LANES), jnp.float32),
                pltpu.VMEM((blocks + 8, features), jnp.float32),
            )
            + tuple(jax.ShapeDtypeStruct((length, features), jnp.float32) for length in lengths),
            in_specs=[SMEM_SPEC] * 6 + [VMEM_SPEC] * (len(arguments) - 6),
            out_specs=(VMEM_SPEC, VMEM_SPEC) + (ANY_SPEC,) * len(lengths),
            scratch_shapes=[
                pltpu.VMEM((min(tile, STEP), features), jnp.float32),
                pltpu.SMEM((slabs * tile // min(tile, STEP) + 1,), jnp.int32),
                pltpu.SemaphoreType.DMA((max(1, len(lengths)),)),
            ],
            input_output_aliases=aliases,
            compiler_params=params(24),
            cost_estimate=pl.CostEstimate(flops=0, bytes_accessed=16 * MIB, transcendentals=0),
            name="compare_and_add",
        )(*arguments)
        squares = squares + more
        behind.append(more)
        offset += tile
    mine, *theirs = halves
    partial_sums = jnp.sum(squares, axis=2)
    return mine, theirs, partial_sums, side


def body(*arrays):
    mine, theirs, partial_sums, side = gradient_of_slab(*arrays)
    field, squares = to_field(mine, theirs, partial_sums, side)
    counts = arrays[6]
    return field, squares / (counts.astype(jnp.float32) * 128.0)


def solution(mesh):
    in_specs = (
        P(("groups", "slab"), None),
        P(),
        P(("groups", "slab", "dom"), None, None),
        P(("groups", "slab", "dom"), None, None),
        P(("groups", "slab", "dom"), None),
        P(("groups", "slab", "dom"), None),
        P(("groups", "slab", "dom")),
        P(("groups", "slab", "dom")),
        P(),
        P(("groups", "slab", "dom")),
    )
    out_specs = (P(None, ("groups", "dom"), "slab", None), P(("groups", "slab", "dom")))
    return jax.shard_map(body, mesh=mesh, in_specs=in_specs, out_specs=out_specs, check_vma=False)
```

```python
import functools
import math

import jax
import jax.numpy as jnp
import numpy as np
from jax import lax
from jax.experimental import pallas as pl
from jax.experimental.pallas import tpu as pltpu
from jax.sharding import PartitionSpec as P

LANES = 128
GROUP = 16
UNUSED = 100
STEP = 256
MIB = 1024 * 1024

SMEM_SPEC = pl.BlockSpec(memory_space=pltpu.SMEM)
VMEM_SPEC = pl.BlockSpec(memory_space=pltpu.VMEM)
ANY_SPEC = pl.BlockSpec(memory_space=pl.ANY)


def params(mib):
    return pltpu.CompilerParams(vmem_limit_bytes=mib * MIB)


def bits_of(count):
    return (count - 1).bit_length()


def route_kernel(slabs, cap, local_bits, owner_ref, local_ref, kind_ref, counts_ref, target_ref, word_ref, totals_ref):
    particles, list_length = local_ref.shape
    rows_each = list_length // LANES
    rows = particles * rows_each
    gathered = lambda ref: jnp.concatenate(
        [ref[:, j * LANES:(j + 1) * LANES] for j in range(rows_each)], axis=0
    )
    row_id = lax.broadcasted_iota(jnp.int32, (rows, LANES), 0)
    lane_id = lax.broadcasted_iota(jnp.int32, (rows, LANES), 1)
    particle = row_id % particles
    position = (row_id // particles) * LANES + lane_id
    limit = jnp.zeros((rows, LANES), jnp.int32)
    for i in range(particles):
        limit = jnp.where(particle == i, counts_ref[i], limit)
    owner = jnp.concatenate(
        [owner_ref[pl.ds(j, particles, stride=rows_each), :] for j in range(rows_each)], axis=0
    )
    owner = jnp.where(position < limit, owner, -1)
    up_to = (
        lax.broadcasted_iota(jnp.int32, (LANES, LANES), 0)
        <= lax.broadcasted_iota(jnp.int32, (LANES, LANES), 1)
    ).astype(jnp.bfloat16)
    ones = jnp.ones((LANES, LANES), jnp.bfloat16)
    before = (
        lax.broadcasted_iota(jnp.int32, (rows, rows), 1)
        < lax.broadcasted_iota(jnp.int32, (rows, rows), 0)
    ).astype(jnp.bfloat16)

    def one_slab(slab, target):
        mine = owner == slab
        hits = mine.astype(jnp.float32).astype(jnp.bfloat16)
        inside = jnp.dot(hits, up_to, preferred_element_type=jnp.float32)
        row_sum = jnp.dot(hits, ones, preferred_element_type=jnp.float32)
        above = jnp.dot(before, row_sum.astype(jnp.bfloat16), preferred_element_type=jnp.float32)
        rank = (inside + above).astype(jnp.int32) - 1
        total = (above[rows - 1:rows, :] + row_sum[rows - 1:rows, :]).astype(jnp.int32)
        totals_ref[pl.ds(slab, 1), :] = total
        return jnp.where(mine, slab * (cap + LANES) + rank, target)

    target = lax.fori_loop(0, slabs, one_slab, jnp.full((rows, LANES), cap + UNUSED, jnp.int32))
    target_ref[...] = target
    kind_bits = local_bits
    word = gathered(local_ref) | (gathered(kind_ref) << kind_bits) | (position << (kind_bits + 2))
    word_ref[...] = word | (particle << (kind_bits + 2 + bits_of(list_length)))


def pack_kernel(slabs, cap, list_length, target_ref, word_ref, counts_ref, totals_ref, code_ref, image_ref, meta_ref, *refs):
    out_refs, (wide_ref, staged_ref) = refs[:-2], refs[-2:]
    particles = counts_ref.shape[0]
    stride = cap + LANES
    step = 256

    @pl.loop(0, image_ref.shape[0] // step)
    def _(i):
        at = pl.multiple_of(i * step, step)
        wide_ref[pl.ds(at, step), :] = image_ref[pl.ds(at, step), :].astype(jnp.float32)

    @pl.loop(0, particles)
    def _(particle):
        @pl.loop(0, (counts_ref[particle] + 15) // 16)
        def _(i):
            first = (i // 8) * (particles * LANES) + particle * LANES + (i % 8) * 16
            row = particle * list_length + i * 16
            targets = [target_ref[first + j] for j in range(16)]
            words = [word_ref[first + j] for j in range(16)]
            rows = [wide_ref[pl.ds(row + j, 1), :] for j in range(16)]
            for j in range(16):
                staged_ref[pl.ds(targets[j], 1), :] = rows[j]
                meta_ref[targets[j]] = words[j]

    @pl.loop(0, slabs)
    def _(slab):
        header = slab * stride + cap
        meta_ref[header] = totals_ref[slab, 0]
        for j in range(particles):
            meta_ref[header + 1 + j] = code_ref[j]

    offset = 0
    for out_ref in out_refs:
        width = out_ref.shape[1]

        @pl.loop(0, slabs)
        def _(slab, offset=offset):
            at = pl.multiple_of(slab * stride + offset, LANES)
            out_ref[slab] = staged_ref[pl.ds(at, width), :].astype(jnp.bfloat16)

        offset += width


def decode_kernel(local_bits, dummy, word_ref, live_ref, index_ref):
    rows = word_ref.shape[0]
    live = live_ref[...] != 0
    index = jnp.where(live, word_ref[...] & ((1 << local_bits) - 1), dummy)
    lane = lax.broadcasted_iota(jnp.int32, (rows, LANES), 1)
    clash = jnp.zeros((rows, LANES), jnp.int32)
    for shift in range(1, GROUP):
        earlier = pltpu.roll(index, shift, 1)
        same = (earlier == index) & (lane % GROUP >= shift) & live
        clash = clash | same.astype(jnp.int32)
    shift = 1
    while shift < LANES:
        if shift == GROUP:
            index = index | jnp.where(lane % GROUP == 0, clash << 24, 0)
        clash = clash | pltpu.roll(clash, LANES - shift, 1)
        shift *= 2
    index_ref[0:rows, :] = index | jnp.where(lane == 0, clash << 25, 0)
    index_ref[rows:, :] = jnp.full((index_ref.shape[0] - rows, LANES), dummy, jnp.int32)


def gather_kernel(slabs, cap, index_ref, totals_ref, volume_ref, *refs):
    out_refs, (wide_ref, staged_ref) = refs[:-2], refs[-2:]
    blocks = volume_ref.shape[0]
    step = 256

    @pl.loop(0, blocks // step)
    def _(i):
        at = pl.multiple_of(i * step, step)
        wide_ref[pl.ds(at, step), :] = volume_ref[pl.ds(at, step), :].astype(jnp.float32)

    @pl.loop(0, slabs)
    def _(source):
        live = totals_ref[source]

        @pl.loop(0, (live + 15) // 16)
        def _(i):
            first = source * cap + i * 16
            places = [index_ref[first] & 0xFFFFFF] + [index_ref[first + j] for j in range(1, 16)]
            rows = [wide_ref[pl.ds(places[j], 1), :] for j in range(16)]
            for j in range(16):
                staged_ref[pl.ds(i * 16 + j, 1), :] = rows[j]

        offset = 0
        for out_ref in out_refs:
            width = out_ref.shape[1]

            @pl.when(live > offset)
            def _(offset=offset):
                out_ref[source] = staged_ref[offset:offset + width, :].astype(jnp.bfloat16)

            offset += width


def sine(angle):
    turns = jnp.floor(angle * (1.0 / math.pi) + 0.5)
    rest = angle - turns * 3.140625
    rest = rest - turns * (math.pi - 3.140625)
    odd = turns - 2.0 * jnp.floor(turns * 0.5)
    square = rest * rest
    poly = 2.718121e-6
    poly = poly * square - 1.9839334e-4
    poly = poly * square + 8.3333293e-3
    poly = poly * square - 1.6666667e-1
    value = rest + rest * square * poly
    return value * (1.0 - 2.0 * odd)


def slab_kernel(
    side, local_bits, list_length, particles, cap, offset,
    totals_ref, defocus_ref, phase_ref, scale_ref, index_ref, core_ref,
    word_ref, voxel_ref, image_ref, forward_ref, backward_ref, unit_ref, *rest,
):
    square_ref, out_refs, (sum_ref, staged_ref, steps_ref, sems) = rest[0], rest[1:-4], rest[-4:]
    slabs, _, tile = word_ref.shape
    step = staged_ref.shape[0]
    steps_each = tile // step
    blocks = sum_ref.shape[0] - 8
    features = image_ref.shape[2]
    kinds = forward_ref.shape[0] // features
    position_bits = bits_of(list_length)
    per_row = side // 8
    half = features // 2

    @pl.loop(0, blocks // 256)
    def _(i):
        at = pl.multiple_of(i * 256, 256)
        sum_ref[pl.ds(at, 256), :] = jnp.zeros((256, features), jnp.float32)

    square_ref[...] = jnp.zeros_like(square_ref)
    live_of = lambda source: jnp.clip(totals_ref[source] - offset, 0, tile)

    def list_source(source, count):
        def list_step(i, count):
            steps_ref[count] = source * steps_each + i
            return count + 1

        return lax.fori_loop(0, (live_of(source) + step - 1) // step, list_step, count)

    steps_ref[0] = 0
    count = lax.fori_loop(0, slabs, list_source, 0)

    def compare(number):
        which_step = steps_ref[jnp.minimum(number, jnp.maximum(count - 1, 0))]
        source, at = which_step // steps_each, (which_step % steps_each) * step
        at = pl.multiple_of(at, step)
        live = jnp.where(number < count, live_of(source) - at, 0)
        word = word_ref[source, :, pl.ds(at, step)]
        kind = (word >> local_bits) & 3
        position = (word >> (local_bits + 2)) & (list_length - 1)
        particle = (word >> (local_bits + 2 + position_bits)) & (particles - 1)
        valid = lax.broadcasted_iota(jnp.int32, (1, step), 1) < live
        defocus = jnp.zeros((1, step), jnp.float32)
        phase = jnp.zeros((1, step), jnp.float32)
        scale = jnp.zeros((1, step), jnp.float32)
        for j in range(particles):
            chosen = particle == j
            defocus = jnp.where(chosen, defocus_ref[source * particles + j], defocus)
            phase = jnp.where(chosen, phase_ref[source * particles + j], phase)
            scale = jnp.where(chosen, scale_ref[source * particles + j], scale)
        defocus = defocus * (1.0 / float((side // 2) ** 2))
        cell = lax.broadcasted_iota(jnp.int32, (half, LANES), 0)
        cell_vert, cell_horiz = (cell // 8).astype(jnp.float32), (cell % 8).astype(jnp.float32)
        repeat = lambda table: jnp.concatenate([table] * (step // LANES), axis=1)
        vert = ((position // per_row) * 8 - side // 2).astype(jnp.float32) + repeat(cell_vert)
        horiz = ((position % per_row) * 8 - side // 2).astype(jnp.float32) + repeat(cell_horiz)
        factor = scale * sine(defocus * (vert * vert + horiz * horiz) + phase)
        factor = jnp.concatenate([factor, factor], axis=0)
        contract_last = (((1,), (1,)), ((), ()))
        each_kind = lax.dot_general(
            forward_ref[...], voxel_ref[source, pl.ds(at, step), :], contract_last,
            preferred_element_type=jnp.float32,
        )
        extracted = each_kind[0:features, :]
        for k in range(1, kinds):
            extracted = jnp.where(kind == k, each_kind[k * features:(k + 1) * features, :], extracted)
        picture = lax.dot_general(
            unit_ref[...], image_ref[source, pl.ds(at, step), :], contract_last,
            preferred_element_type=jnp.float32,
        )
        misfit = jnp.where(valid, factor * extracted - picture, 0.0)
        squares = jnp.sum(misfit * misfit, axis=0, keepdims=True)
        which = lax.broadcasted_iota(jnp.int32, (particles, step), 0)
        spread = jnp.where(valid & (particle == which), squares, 0.0)
        folded = spread[:, 0:LANES]
        for i in range(1, step // LANES):
            folded = folded + spread[:, i * LANES:(i + 1) * LANES]
        square_ref[source] = square_ref[source] + folded
        weighted = (factor * misfit).astype(jnp.bfloat16)
        none = jnp.zeros_like(weighted)
        spread_back = jnp.concatenate(
            [jnp.where(kind == k, weighted, none) for k in range(kinds)], axis=0
        )
        terms = jnp.dot(backward_ref[...], spread_back, preferred_element_type=jnp.float32)
        staged_ref[...] = terms.T

    def places_of(base):
        return [index_ref[base] & 0xFFFFFF] + [index_ref[base + j] for j in range(1, GROUP)]

    def add_group(base, at):
        places = places_of(base)
        held = [sum_ref[pl.ds(place, 1), :] for place in places]
        new = [staged_ref[pl.ds(at + j, 1), :] for j in range(GROUP)]
        for j in range(GROUP):
            sum_ref[pl.ds(places[j], 1), :] = held[j] + new[j]

    @pl.loop(0, count + 1)
    def _(number):
        earlier = steps_ref[jnp.maximum(number - 1, 0)]
        base = (earlier // steps_each) * cap + offset + (earlier % steps_each) * step
        base = jnp.where(number > 0, base, slabs * cap)
        marks = index_ref[base]
        for i in range(1, step // LANES):
            marks = marks | index_ref[base + i * LANES]

        @pl.when(marks < (1 << 25))
        def _():
            for g in range(step // GROUP):
                add_group(base + g * GROUP, g * GROUP)
            compare(number)

        @pl.when(marks >= (1 << 25))
        def _():
            @pl.loop(0, step // GROUP)
            def _(g):
                start = base + g * GROUP
                clashes = (index_ref[start] >> 24) & 1

                @pl.when(clashes == 0)
                def _():
                    add_group(start, g * GROUP)

                @pl.when(clashes == 1)
                def _():
                    places = places_of(start)
                    for j in range(GROUP):
                        sum_ref[pl.ds(places[j], 1), :] = (
                            sum_ref[pl.ds(places[j], 1), :] + staged_ref[pl.ds(g * GROUP + j, 1), :]
                        )

            compare(number)

    half = blocks // 2
    start = (1 - core_ref[0]) * half
    places = [core_ref[0] * half]
    for out_ref in out_refs[1:]:
        places.append(start)
        start = start + out_ref.shape[0]
    copies = []
    for i, (place, out_ref) in enumerate(zip(places, out_refs)):
        length = out_ref.shape[0]
        at = pl.multiple_of(place, 8)
        copies.append(pltpu.make_async_copy(sum_ref.at[pl.ds(at, length)], out_ref, sems.at[i]))
    for copy in copies:
        copy.start()
    for copy in copies:
        copy.wait()


def pieces_of(planes):
    if planes < 16:
        return [planes]
    return [4, planes - 4]


def rotated(value, turn, length, sign=None):
    real, imag = value
    if turn == 0 or 4 * turn == length:
        if turn:
            real, imag = -imag, real
        return (real, imag) if sign is None else (real * sign, imag * sign)
    if sign is None and 8 * turn in (length, 3 * length):
        root = math.sqrt(0.5)
        if 8 * turn == length:
            return ((real - imag) * root, (real + imag) * root)
        return ((real + imag) * -root, (real - imag) * root)
    cos, sin = math.cos(2 * math.pi * turn / length), math.sin(2 * math.pi * turn / length)
    if sign is not None:
        cos, sin = cos * sign, sin * sign
    return (real * cos - imag * sin, real * sin + imag * cos)


def small_dft(values):
    length = len(values)
    if length == 1:
        return values
    even, odd = small_dft(values[0::2]), small_dft(values[1::2])
    low, high = [], []
    for k in range(length // 2):
        turned = rotated(odd[k], k, length)
        low.append((even[k][0] + turned[0], even[k][1] + turned[1]))
        high.append((even[k][0] - turned[0], even[k][1] - turned[1]))
    return low + high


def swap_quarters(values):
    lane = lax.broadcasted_iota(jnp.int32, values[0].shape, 1)
    low, even = lane < 64, (lane // 32) % 2 == 0
    roll = lambda value, shift: pltpu.roll(value, shift, 1)
    for first, second, shift, keep in ((0, 2, 64, low), (1, 3, 64, low), (0, 1, 32, even), (2, 3, 32, even)):
        one, two = values[first], values[second]
        values[first] = jnp.where(keep, one, roll(two, shift))
        values[second] = jnp.where(keep, roll(one, LANES - shift), two)
    return values


def in_halves(value):
    high = value.astype(jnp.bfloat16)
    return high, (value - high.astype(jnp.float32)).astype(jnp.bfloat16)


def planes_kernel(halves, *refs):
    half_refs, rest = refs[:halves], refs[halves:]
    zblock_ref, turn_ref, wide_ref, fine_ref, out_ref, high_ref, low_ref = rest
    step = pl.program_id(1)
    count = half_refs[0].shape[1]
    groups, side = out_ref.shape[0], out_ref.shape[4]
    height = side // groups

    @pl.loop(0, count, unroll=8)
    def _(i):
        block = sum(ref[:, i] for ref in half_refs).reshape(LANES, LANES)
        high, low = in_halves(block.T)
        both = jnp.dot(
            jnp.concatenate([high, low, high], axis=1), zblock_ref[...],
            preferred_element_type=jnp.float32,
        )
        by_cos = both[:, :LANES].reshape(8, 2, 8, LANES)
        by_sin = both[:, LANES:].reshape(8, 2, 8, LANES)
        real = by_cos[:, 0] - by_sin[:, 1]
        imag = by_sin[:, 0] + by_cos[:, 1]
        values = []
        for z in range(8):
            cos, sin = turn_ref[0, z:z + 1, :], turn_ref[1, z:z + 1, :]
            values.append((real[z] * cos - imag[z] * sin, real[z] * sin + imag[z] * cos))
        values = [jnp.concatenate(value, axis=0) for value in small_dft(values)]
        at = pl.ds(pl.multiple_of((step * count + i) * 16, 16), 16)
        for half in range(2):
            planes = swap_quarters(values[4 * half:4 * half + 4])
            for x in range(4):
                columns = slice((2 * x + half) * LANES, (2 * x + half + 1) * LANES)
                high, low = in_halves(planes[x])
                high_ref[at, columns] = high
                low_ref[at, columns] = low

    @pl.when(step == pl.num_programs(1) - 1)
    def _():
        @pl.loop(0, 4)
        def _(x):
            columns = pl.ds(pl.multiple_of(x * side, side), side)
            product = functools.partial(jnp.dot, preferred_element_type=jnp.float32)
            high = high_ref[:, columns]
            result = product(wide_ref[...], high) + (
                product(wide_ref[...], low_ref[:, columns]) + product(fine_ref[...], high)
            )
            for part in range(2):
                for group in range(groups):
                    start = part * side + group * height
                    out_ref[group, x, part] = result[start:start + height, :].astype(jnp.bfloat16)


def first_dimension_kernel(slabs, each, core_ref, *refs):
    arrays, (out_ref, mid_ref) = refs[:-2], refs[-2:]
    chunks = len(arrays) // 2
    own, other = arrays[:chunks], arrays[chunks:]
    spots = [(i, at) for i, ref in enumerate(own) for at in range(ref.shape[1])]
    core = core_ref[0]
    is_first = core == 0
    sign = (1 - 2 * core).astype(jnp.float32)

    rows = out_ref.shape[2]
    strips = [slice(at, min(at + 8, rows)) for at in range(0, rows, 8)]

    def plane(x, strip):
        slab, rest = x // (2 * each), x % (2 * each)
        half, inner = rest // each, rest % each
        chunk, at = spots[inner]
        loaded = []
        for part in range(2):
            here, there = own[chunk][slab, at, part], other[chunk][slab, at, part]
            value = jnp.where(is_first, here, there) if half == 0 else jnp.where(is_first, there, here)
            loaded.append(value.astype(jnp.float32)[strip])
        return tuple(loaded)

    for low in range(16):
        for strip in strips:
            values = small_dft([plane(low + 16 * high, strip) for high in range(16)])
            for k in range(16):
                real, imag = rotated(values[k], low * k, 256, sign if low % 2 else None)
                mid_ref[k, low, 0, strip] = real
                mid_ref[k, low, 1, strip] = imag

    @pl.loop(0, 16)
    def _(k):
        for strip in strips:
            values = [(mid_ref[k, low, 0, strip], mid_ref[k, low, 1, strip]) for low in range(16)]
            even, odd = small_dft(values[0::2]), small_dft(values[1::2])
            for m in range(8):
                turned = rotated(odd[m], m, 16)
                out_ref[0, k + 16 * m, strip] = even[m][0] + turned[0]
                out_ref[1, k + 16 * m, strip] = even[m][1] + turned[1]


def host_halves(table):
    high = table.astype(jnp.bfloat16)
    return high, (table - high.astype(np.float64)).astype(jnp.bfloat16)


def transform_tables(side):
    per_row = side // 8
    grid = np.arange(per_row)
    angle = 2 * np.pi * np.outer(grid, grid) / per_row
    zblock = np.concatenate([np.kron(np.eye(4), np.cos(angle)), np.kron(np.eye(4), np.sin(angle))], axis=1)
    high, low = host_halves(zblock)
    zblock = np.concatenate([high, high, low], axis=0)
    angle = 2 * np.pi * np.outer(np.arange(8), grid) / side
    turns = np.stack([np.tile(np.cos(angle), (1, 4)), np.tile(np.sin(angle), (1, 4))]).astype(np.float32)
    cells = np.arange(side)
    angle = 2 * np.pi * (np.outer(cells, cells) % side) / side
    cos, sin = np.cos(angle).reshape(side, per_row, 1, 8), np.sin(angle).reshape(side, per_row, 1, 8)
    matrix = np.concatenate(
        [np.concatenate([cos, -sin], axis=2), np.concatenate([sin, cos], axis=2)], axis=0
    ).reshape(2 * side, 2 * side) / float(side) ** 1.5
    return (zblock, turns) + host_halves(matrix)


def sum_over_slabs(partial_sums):
    slabs = partial_sums.shape[0]
    if slabs <= 8:
        me = lax.axis_index("slab")
        row = lambda i: lax.dynamic_index_in_dim(partial_sums, me ^ i, axis=0, keepdims=True)
        returned = [row(0)] + [
            lax.ppermute(row(i), "slab", [(slab, slab ^ i) for slab in range(slabs)])
            for i in range(1, slabs)
        ]
        returned = jnp.concatenate(returned)
    else:
        returned = lax.all_to_all(partial_sums, "slab", split_axis=0, concat_axis=0, tiled=True)
    return jnp.sum(returned, axis=0)


def to_field(mine, theirs, partial_sums, side):
    slabs = lax.axis_size("slab")
    per_row = side // 8
    each = side // slabs // 2
    height = side // slabs
    groups = slabs if height % 16 == 0 else 1
    tables = [jnp.asarray(table) for table in transform_tables(side)]
    swap = [(0, 1), (1, 0)]
    short = max(0, 4 - each)

    def gridded(half):
        half = half.reshape(-1, per_row, per_row, LANES)
        return jnp.pad(half, ((0, short), (0, 0), (0, 0), (0, 0))) if short else half

    mine = [gridded(half) for half in mine]
    yblocks = 8
    own = []
    first_quad = 0
    before = []
    for chunk, real_planes in enumerate(pieces_of(each)):
        added = [part[chunk] for part in theirs]
        if before:
            added[-1], before[0] = lax.optimization_barrier((added[-1], before[0]))
        added = [gridded(half) for half in added]
        held = real_planes + short
        quads = held // 4
        whole = lambda table: pl.BlockSpec(table.shape, lambda q, y: (0,) * table.ndim)
        sent = pl.pallas_call(
            functools.partial(planes_kernel, len(mine) + len(added)),
            grid=(quads, per_row // yblocks),
            out_shape=jax.ShapeDtypeStruct((groups, held, 2, side // groups, side), jnp.bfloat16),
            in_specs=[
                pl.BlockSpec((4, yblocks, per_row, LANES), lambda q, y, at=first_quad: (at + q, y, 0, 0))
                for _ in mine
            ] + [
                pl.BlockSpec((4, yblocks, per_row, LANES), lambda q, y: (q, y, 0, 0)) for _ in added
            ] + [whole(table) for table in tables],
            out_specs=pl.BlockSpec((groups, 4, 2, side // groups, side), lambda q, y: (0, q, 0, 0, 0)),
            scratch_shapes=[
                pltpu.VMEM((2 * side, 4 * side), jnp.bfloat16),
                pltpu.VMEM((2 * side, 4 * side), jnp.bfloat16),
            ],
            compiler_params=params(56),
            cost_estimate=pl.CostEstimate(
                flops=held * 8 * side**3, bytes_accessed=held * 4 * side**2 * 8, transcendentals=0
            ),
            name="transform_planes",
        )(*mine, *added, *tables)
        if groups != slabs:
            sent = sent.reshape(-1, 2, slabs, height, side).transpose(2, 0, 1, 3, 4)[:, :real_planes]
        first_quad += quads
        if before:
            sent, own[-1] = lax.optimization_barrier((sent, own[-1]))
        if first_quad * 4 >= each:
            sent, partial_sums = lax.optimization_barrier((sent, partial_sums))
        before = [sent]
        got = lax.all_to_all(sent, "slab", split_axis=0, concat_axis=0, tiled=True)
        own.append(got)
    other = [lax.ppermute(got, "dom", swap) for got in own[:-1]]
    own[-1], losses, *other = lax.optimization_barrier((own[-1], sum_over_slabs(partial_sums), *other))
    other.append(lax.ppermute(own[-1], "dom", swap))
    rows = min(16, height)
    arrays = own + other
    field = pl.pallas_call(
        functools.partial(first_dimension_kernel, slabs, each),
        grid=(height // rows, side // LANES),
        out_shape=jax.ShapeDtypeStruct((2, side // 2, height, side), jnp.float32),
        in_specs=[SMEM_SPEC] + [
            pl.BlockSpec(array.shape[:3] + (rows, LANES), lambda y, z: (0, 0, 0, y, z))
            for array in arrays
        ],
        out_specs=pl.BlockSpec((2, side // 2, rows, LANES), lambda y, z: (0, 0, y, z)),
        scratch_shapes=[pltpu.VMEM((16, 16, 2, rows, LANES), jnp.float32)],
        compiler_params=params(28),
        name="transform_first",
    )(lax.axis_index("dom").astype(jnp.int32).reshape(1), *arrays)
    return field, losses


def gradient_of_slab(volume, kernels, images, owners, local_block, kinds, counts, ctf_code, ctf_table, scales):
    slabs = lax.axis_size("slab")
    particles, list_length, features = images.shape
    side = math.isqrt(list_length * 64)
    entries = particles * list_length
    cap = 2 * entries // slabs
    slots = slabs * cap
    blocks = volume.shape[0]
    local_bits = bits_of(blocks)
    kind_count = kernels.shape[0]
    rows = entries // LANES
    int_rows = jax.ShapeDtypeStruct((rows, LANES), jnp.int32)

    target, word, totals = pl.pallas_call(
        functools.partial(route_kernel, slabs, cap, local_bits),
        out_shape=(int_rows, int_rows, jax.ShapeDtypeStruct((slabs, LANES), jnp.int32)),
        in_specs=[VMEM_SPEC, VMEM_SPEC, VMEM_SPEC, SMEM_SPEC],
        out_specs=(VMEM_SPEC, VMEM_SPEC, VMEM_SPEC),
        compiler_params=params(56),
        name="route",
    )(owners.reshape(rows, LANES), local_block, kinds, counts)
    target, word = target.reshape(entries), word.reshape(entries)
    tiles = [cap * 5 // 8, cap * 3 // 8] if cap >= 2048 else [cap]
    parts = len(tiles)
    code = ctf_code | ((scales.astype(jnp.float32) * 256.0).astype(jnp.int32) << 8)
    stride = cap + LANES
    meta, *packed = pl.pallas_call(
        functools.partial(pack_kernel, slabs, cap, list_length),
        out_shape=(jax.ShapeDtypeStruct((slabs * stride,), jnp.int32),)
        + tuple(jax.ShapeDtypeStruct((slabs, tile, features), jnp.bfloat16) for tile in tiles),
        in_specs=[SMEM_SPEC] * 5 + [VMEM_SPEC],
        out_specs=(SMEM_SPEC,) + (VMEM_SPEC,) * parts,
        scratch_shapes=[
            pltpu.VMEM((entries, features), jnp.float32),
            pltpu.VMEM((slabs * stride, features), jnp.float32),
        ],
        compiler_params=params(56),
        name="pack",
    )(target, word, counts, totals, code, images.reshape(entries, features))
    arrived = lax.all_to_all(
        meta.reshape(slabs, stride), "slab", split_axis=0, concat_axis=0, tiled=True
    )
    words = arrived[:, :cap]
    totals_in = arrived[:, cap]
    codes_in = arrived[:, cap + 1:cap + 1 + particles]
    live = (jnp.arange(cap, dtype=jnp.int32)[None, :] < totals_in[:, None]).astype(jnp.int32)
    table_rows = ctf_table[(codes_in & 255).reshape(-1)]
    scale_in = (codes_in >> 8).astype(jnp.float32).reshape(-1) * (1.0 / 256.0)

    index = pl.pallas_call(
        functools.partial(decode_kernel, local_bits, blocks),
        out_shape=jax.ShapeDtypeStruct((slots // LANES + 8, LANES), jnp.int32),
        in_specs=[VMEM_SPEC, VMEM_SPEC],
        out_specs=VMEM_SPEC,
        compiler_params=params(56),
        name="decode",
    )(words.reshape(slots // LANES, LANES), live.reshape(slots // LANES, LANES))
    index = index.reshape(slots + 8 * LANES)
    voxels = list(pl.pallas_call(
        functools.partial(gather_kernel, slabs, cap),
        out_shape=tuple(
            jax.ShapeDtypeStruct((slabs, tile, features), jnp.bfloat16) for tile in tiles
        ),
        in_specs=[SMEM_SPEC, SMEM_SPEC, VMEM_SPEC],
        out_specs=(VMEM_SPEC,) * parts,
        scratch_shapes=[
            pltpu.VMEM((blocks + 8, features), jnp.float32),
            pltpu.VMEM((cap, features), jnp.float32),
        ],
        compiler_params=params(56),
        cost_estimate=pl.CostEstimate(flops=0, bytes_accessed=100 * MIB, transcendentals=0),
        name="read_voxels",
    )(index, totals_in, volume))

    forward = jnp.transpose(kernels, (0, 2, 1)).reshape(kind_count * features, features)
    backward = kernels.reshape(kind_count, 2, 8, 8, features).transpose(3, 1, 2, 0, 4)
    backward = backward.reshape(features, kind_count * features)
    unit = jnp.eye(features, dtype=jnp.bfloat16)
    core = lax.axis_index("dom").astype(jnp.int32).reshape(1)
    plane_blocks = (side // 8) ** 2
    pieces = [planes * plane_blocks for planes in pieces_of(side // slabs // 2)]
    squares, offset, mine, theirs = 0.0, 0, [], []
    lengths = [blocks // 2] + pieces
    for part, tile in enumerate(tiles):
        if part == 1:
            packed[1], voxels[0] = lax.optimization_barrier((packed[1], voxels[0]))
        picture = lax.all_to_all(packed[part], "slab", split_axis=0, concat_axis=0, tiled=True)
        more, own_half, *other_half = pl.pallas_call(
            functools.partial(slab_kernel, side, local_bits, list_length, particles, cap, offset),
            out_shape=(jax.ShapeDtypeStruct((slabs, particles, LANES), jnp.float32),)
            + tuple(jax.ShapeDtypeStruct((length, features), jnp.float32) for length in lengths),
            in_specs=[SMEM_SPEC] * 6 + [VMEM_SPEC] * 6,
            out_specs=(VMEM_SPEC,) + (ANY_SPEC,) * len(lengths),
            scratch_shapes=[
                pltpu.VMEM((blocks + 8, features), jnp.float32),
                pltpu.VMEM((min(tile, STEP), features), jnp.float32),
                pltpu.SMEM((slabs * tile // min(tile, STEP) + 1,), jnp.int32),
                pltpu.SemaphoreType.DMA((len(lengths),)),
            ],
            compiler_params=params(56),
            cost_estimate=pl.CostEstimate(flops=0, bytes_accessed=16 * MIB, transcendentals=0),
            name="compare_and_add",
        )(
            totals_in, table_rows[:, 0], table_rows[:, 1], scale_in, index, core,
            words[:, offset:offset + tile].reshape(slabs, 1, tile), voxels[part], picture,
            forward, backward, unit,
        )
        received = [lax.ppermute(piece, "dom", [(0, 1), (1, 0)]) for piece in other_half]
        if part + 1 < parts:
            voxels[part + 1], more, received[0] = lax.optimization_barrier(
                (voxels[part + 1], more, received[0])
            )
        squares = squares + more
        mine.append(own_half)
        theirs.append(received)
        offset += tile
    partial_sums = jnp.sum(squares, axis=2)
    return mine, theirs, partial_sums, side


def body(*arrays):
    mine, theirs, partial_sums, side = gradient_of_slab(*arrays)
    field, squares = to_field(mine, theirs, partial_sums, side)
    counts = arrays[6]
    return field, squares / (counts.astype(jnp.float32) * 128.0)


def solution(mesh):
    in_specs = (
        P(("groups", "slab"), None),
        P(),
        P(("groups", "slab", "dom"), None, None),
        P(("groups", "slab", "dom"), None, None),
        P(("groups", "slab", "dom"), None),
        P(("groups", "slab", "dom"), None),
        P(("groups", "slab", "dom")),
        P(("groups", "slab", "dom")),
        P(),
        P(("groups", "slab", "dom")),
    )
    out_specs = (P(None, ("groups", "dom"), "slab", None), P(("groups", "slab", "dom")))
    return jax.shard_map(body, mesh=mesh, in_specs=in_specs, out_specs=out_specs, check_vma=False)
```

```python
import functools
import math

import jax
import jax.numpy as jnp
import numpy as np
from jax import lax
from jax.experimental import pallas as pl
from jax.experimental.pallas import tpu as pltpu
from jax.sharding import PartitionSpec as P

LANES = 128
GROUP = 16
UNUSED = 100
STEP = 128
MIB = 1024 * 1024

SMEM_SPEC = pl.BlockSpec(memory_space=pltpu.SMEM)
VMEM_SPEC = pl.BlockSpec(memory_space=pltpu.VMEM)
ANY_SPEC = pl.BlockSpec(memory_space=pl.ANY)


def params(mib):
    return pltpu.CompilerParams(vmem_limit_bytes=mib * MIB)


def bits_of(count):
    return (count - 1).bit_length()


def route_kernel(slabs, cap, local_bits, owner_ref, local_ref, kind_ref, counts_ref, target_ref, word_ref, totals_ref):
    particles, list_length = local_ref.shape
    rows_each = list_length // LANES
    rows = particles * rows_each
    gathered = lambda ref: jnp.concatenate(
        [ref[:, j * LANES:(j + 1) * LANES] for j in range(rows_each)], axis=0
    )
    row_id = lax.broadcasted_iota(jnp.int32, (rows, LANES), 0)
    lane_id = lax.broadcasted_iota(jnp.int32, (rows, LANES), 1)
    particle = row_id % particles
    position = (row_id // particles) * LANES + lane_id
    limit = jnp.zeros((rows, LANES), jnp.int32)
    for i in range(particles):
        limit = jnp.where(particle == i, counts_ref[i], limit)
    owner = jnp.concatenate(
        [owner_ref[pl.ds(j, particles, stride=rows_each), :] for j in range(rows_each)], axis=0
    )
    owner = jnp.where(position < limit, owner, -1)
    up_to = (
        lax.broadcasted_iota(jnp.int32, (LANES, LANES), 0)
        <= lax.broadcasted_iota(jnp.int32, (LANES, LANES), 1)
    ).astype(jnp.bfloat16)
    ones = jnp.ones((LANES, LANES), jnp.bfloat16)
    before = (
        lax.broadcasted_iota(jnp.int32, (rows, rows), 1)
        < lax.broadcasted_iota(jnp.int32, (rows, rows), 0)
    ).astype(jnp.bfloat16)

    def one_slab(slab, target):
        mine = owner == slab
        hits = mine.astype(jnp.float32).astype(jnp.bfloat16)
        inside = jnp.dot(hits, up_to, preferred_element_type=jnp.float32)
        row_sum = jnp.dot(hits, ones, preferred_element_type=jnp.float32)
        above = jnp.dot(before, row_sum.astype(jnp.bfloat16), preferred_element_type=jnp.float32)
        rank = (inside + above).astype(jnp.int32) - 1
        total = (above[rows - 1:rows, :] + row_sum[rows - 1:rows, :]).astype(jnp.int32)
        totals_ref[pl.ds(slab, 1), :] = total
        return jnp.where(mine, slab * (cap + LANES) + rank, target)

    target = lax.fori_loop(0, slabs, one_slab, jnp.full((rows, LANES), cap + UNUSED, jnp.int32))
    target_ref[...] = target
    kind_bits = local_bits
    word = gathered(local_ref) | (gathered(kind_ref) << kind_bits) | (position << (kind_bits + 2))
    word_ref[...] = word | (particle << (kind_bits + 2 + bits_of(list_length)))


def pack_kernel(slabs, cap, list_length, target_ref, word_ref, counts_ref, totals_ref, code_ref, image_ref, meta_ref, *refs):
    out_refs, (wide_ref, staged_ref, narrow_ref, sem) = refs[:-4], refs[-4:]
    particles = counts_ref.shape[0]
    stride = cap + LANES
    step = 256
    turn = 32

    @pl.loop(0, image_ref.shape[0] // step)
    def _(i):
        at = pl.multiple_of(i * step, step)
        wide_ref[pl.ds(at, step), :] = image_ref[pl.ds(at, step), :].astype(jnp.float32)

    @pl.loop(0, particles)
    def _(particle):
        @pl.loop(0, (counts_ref[particle] + turn - 1) // turn)
        def _(i):
            per_row = LANES // turn
            first = (i // per_row) * (particles * LANES) + particle * LANES + (i % per_row) * turn
            row = particle * list_length + i * turn
            targets = [target_ref[first + j] for j in range(turn)]
            words = [word_ref[first + j] for j in range(turn)]
            rows = [wide_ref[pl.ds(row + j, 1), :] for j in range(turn)]
            for j in range(turn):
                staged_ref[pl.ds(targets[j], 1), :] = rows[j]
                meta_ref[targets[j]] = words[j]

    @pl.loop(0, slabs)
    def _(slab):
        header = slab * stride + cap
        meta_ref[header] = totals_ref[slab, 0]
        for j in range(particles):
            meta_ref[header + 1 + j] = code_ref[j]

    def blocks_of(act):
        offset = 0
        for out_ref in out_refs:
            width = out_ref.shape[1]

            @pl.loop(0, slabs)
            def _(slab, offset=offset, width=width, out_ref=out_ref):
                live = jnp.clip(totals_ref[slab, 0] - offset, 0, width)

                @pl.loop(0, (live + LANES - 1) // LANES)
                def _(i):
                    at = pl.multiple_of(slab * cap + offset + i * LANES, LANES)
                    to = pl.multiple_of(i * LANES, LANES)
                    copy = pltpu.make_async_copy(
                        narrow_ref.at[pl.ds(at, LANES)], out_ref.at[slab, pl.ds(to, LANES)], sem
                    )
                    act(copy, at, pl.multiple_of(at + slab * LANES, LANES))

            offset += width

    def convert_and_start(copy, at, staged_at):
        narrow_ref[pl.ds(at, LANES), :] = staged_ref[pl.ds(staged_at, LANES), :].astype(jnp.bfloat16)
        copy.start()

    blocks_of(convert_and_start)
    blocks_of(lambda copy, at, staged_at: copy.wait())


def decode_kernel(local_bits, dummy, word_ref, live_ref, index_ref):
    rows = word_ref.shape[0]
    live = live_ref[...] != 0
    index = jnp.where(live, word_ref[...] & ((1 << local_bits) - 1), dummy)
    lane = lax.broadcasted_iota(jnp.int32, (rows, LANES), 1)
    clash = jnp.zeros((rows, LANES), jnp.int32)
    for shift in range(1, GROUP):
        earlier = pltpu.roll(index, shift, 1)
        same = (earlier == index) & (lane % GROUP >= shift) & live
        clash = clash | same.astype(jnp.int32)
    shift = 1
    while shift < LANES:
        if shift == GROUP:
            index = index | jnp.where(lane % GROUP == 0, clash << 24, 0)
        clash = clash | pltpu.roll(clash, LANES - shift, 1)
        shift *= 2
    index_ref[0:rows, :] = index | jnp.where(lane == 0, clash << 25, 0)
    index_ref[rows:, :] = jnp.full((index_ref.shape[0] - rows, LANES), dummy, jnp.int32)


def gather_kernel(slabs, cap, index_ref, totals_ref, volume_ref, *refs):
    out_refs, (wide_ref, staged_ref) = refs[:-2], refs[-2:]
    blocks = volume_ref.shape[0]
    step = 256

    @pl.loop(0, blocks // step)
    def _(i):
        at = pl.multiple_of(i * step, step)
        wide_ref[pl.ds(at, step), :] = volume_ref[pl.ds(at, step), :].astype(jnp.float32)

    @pl.loop(0, slabs)
    def _(source):
        live = totals_ref[source]

        @pl.loop(0, (live + 15) // 16)
        def _(i):
            first = source * cap + i * 16
            places = [index_ref[first] & 0xFFFFFF] + [index_ref[first + j] for j in range(1, 16)]
            rows = [wide_ref[pl.ds(places[j], 1), :] for j in range(16)]
            for j in range(16):
                staged_ref[pl.ds(i * 16 + j, 1), :] = rows[j]

        offset = 0
        for out_ref in out_refs:
            width = out_ref.shape[1]

            @pl.when(live > offset)
            def _(offset=offset):
                out_ref[source] = staged_ref[offset:offset + width, :].astype(jnp.bfloat16)

            offset += width


def sine(angle):
    turns = jnp.floor(angle * (1.0 / math.pi) + 0.5)
    rest = angle - turns * 3.140625
    rest = rest - turns * (math.pi - 3.140625)
    odd = turns - 2.0 * jnp.floor(turns * 0.5)
    square = rest * rest
    poly = 2.718121e-6
    poly = poly * square - 1.9839334e-4
    poly = poly * square + 8.3333293e-3
    poly = poly * square - 1.6666667e-1
    value = rest + rest * square * poly
    return value * (1.0 - 2.0 * odd)


def slab_kernel(
    side, local_bits, list_length, particles, cap, offset, first, last,
    totals_ref, defocus_ref, phase_ref, scale_ref, index_ref, core_ref,
    word_ref, voxel_ref, image_ref, forward_ref, backward_ref, unit_ref, *rest,
):
    if not first:
        rest = rest[1:]
    square_ref, sum_ref, out_refs, (staged_ref, steps_ref, sems) = rest[0], rest[1], rest[2:-3], rest[-3:]
    slabs, _, tile = word_ref.shape
    step = staged_ref.shape[0]
    steps_each = tile // step
    blocks = sum_ref.shape[0] - 8
    features = image_ref.shape[2]
    kinds = forward_ref.shape[0] // features
    position_bits = bits_of(list_length)
    per_row = side // 8
    half = features // 2

    if first:
        @pl.loop(0, blocks // 256)
        def _(i):
            at = pl.multiple_of(i * 256, 256)
            sum_ref[pl.ds(at, 256), :] = jnp.zeros((256, features), jnp.float32)

    square_ref[...] = jnp.zeros_like(square_ref)
    live_of = lambda source: jnp.clip(totals_ref[source] - offset, 0, tile)

    def list_source(source, count):
        def list_step(i, count):
            steps_ref[count] = source * steps_each + i
            return count + 1

        return lax.fori_loop(0, (live_of(source) + step - 1) // step, list_step, count)

    steps_ref[0] = 0
    count = lax.fori_loop(0, slabs, list_source, 0)

    def compare(number):
        which_step = steps_ref[jnp.minimum(number, jnp.maximum(count - 1, 0))]
        source, at = which_step // steps_each, (which_step % steps_each) * step
        at = pl.multiple_of(at, step)
        live = jnp.where(number < count, live_of(source) - at, 0)
        word = word_ref[source, :, pl.ds(at, step)]
        kind = (word >> local_bits) & 3
        position = (word >> (local_bits + 2)) & (list_length - 1)
        particle = (word >> (local_bits + 2 + position_bits)) & (particles - 1)
        valid = lax.broadcasted_iota(jnp.int32, (1, step), 1) < live
        defocus = jnp.zeros((1, step), jnp.float32)
        phase = jnp.zeros((1, step), jnp.float32)
        scale = jnp.zeros((1, step), jnp.float32)
        for j in range(particles):
            chosen = particle == j
            defocus = jnp.where(chosen, defocus_ref[source * particles + j], defocus)
            phase = jnp.where(chosen, phase_ref[source * particles + j], phase)
            scale = jnp.where(chosen, scale_ref[source * particles + j], scale)
        defocus = defocus * (1.0 / float((side // 2) ** 2))
        cell = lax.broadcasted_iota(jnp.int32, (half, LANES), 0)
        cell_vert, cell_horiz = (cell // 8).astype(jnp.float32), (cell % 8).astype(jnp.float32)
        repeat = lambda table: jnp.concatenate([table] * (step // LANES), axis=1)
        vert = ((position // per_row) * 8 - side // 2).astype(jnp.float32) + repeat(cell_vert)
        horiz = ((position % per_row) * 8 - side // 2).astype(jnp.float32) + repeat(cell_horiz)
        factor = scale * sine(defocus * (vert * vert + horiz * horiz) + phase)
        factor = jnp.concatenate([factor, factor], axis=0)
        contract_last = (((1,), (1,)), ((), ()))
        each_kind = lax.dot_general(
            forward_ref[...], voxel_ref[source, pl.ds(at, step), :], contract_last,
            preferred_element_type=jnp.float32,
        )
        extracted = each_kind[0:features, :]
        for k in range(1, kinds):
            extracted = jnp.where(kind == k, each_kind[k * features:(k + 1) * features, :], extracted)
        picture = lax.dot_general(
            unit_ref[...], image_ref[source, pl.ds(at, step), :], contract_last,
            preferred_element_type=jnp.float32,
        )
        misfit = jnp.where(valid, factor * extracted - picture, 0.0)
        squares = jnp.sum(misfit * misfit, axis=0, keepdims=True)
        which = lax.broadcasted_iota(jnp.int32, (particles, step), 0)
        spread = jnp.where(valid & (particle == which), squares, 0.0)
        folded = spread[:, 0:LANES]
        for i in range(1, step // LANES):
            folded = folded + spread[:, i * LANES:(i + 1) * LANES]
        square_ref[source] = square_ref[source] + folded
        weighted = (factor * misfit).astype(jnp.bfloat16)
        none = jnp.zeros_like(weighted)
        spread_back = jnp.concatenate(
            [jnp.where(kind == k, weighted, none) for k in range(kinds)], axis=0
        )
        terms = jnp.dot(backward_ref[...], spread_back, preferred_element_type=jnp.float32)
        staged_ref[...] = terms.T

    def places_of(base):
        return [index_ref[base] & 0xFFFFFF] + [index_ref[base + j] for j in range(1, GROUP)]

    def add_group(base, at):
        places = places_of(base)
        held = [sum_ref[pl.ds(place, 1), :] for place in places]
        new = [staged_ref[pl.ds(at + j, 1), :] for j in range(GROUP)]
        for j in range(GROUP):
            sum_ref[pl.ds(places[j], 1), :] = held[j] + new[j]

    @pl.loop(0, count + 1)
    def _(number):
        earlier = steps_ref[jnp.maximum(number - 1, 0)]
        base = (earlier // steps_each) * cap + offset + (earlier % steps_each) * step
        base = jnp.where(number > 0, base, slabs * cap)
        marks = index_ref[base]
        for i in range(1, step // LANES):
            marks = marks | index_ref[base + i * LANES]

        @pl.when(marks < (1 << 25))
        def _():
            for g in range(step // GROUP):
                add_group(base + g * GROUP, g * GROUP)
            compare(number)

        @pl.when(marks >= (1 << 25))
        def _():
            @pl.loop(0, step // GROUP)
            def _(g):
                start = base + g * GROUP
                clashes = (index_ref[start] >> 24) & 1

                @pl.when(clashes == 0)
                def _():
                    add_group(start, g * GROUP)

                @pl.when(clashes == 1)
                def _():
                    places = places_of(start)
                    for j in range(GROUP):
                        sum_ref[pl.ds(places[j], 1), :] = (
                            sum_ref[pl.ds(places[j], 1), :] + staged_ref[pl.ds(g * GROUP + j, 1), :]
                        )

            compare(number)

    if last:
        half = blocks // 2
        start = (1 - core_ref[0]) * half
        places = [core_ref[0] * half]
        for out_ref in out_refs[1:]:
            places.append(start)
            start = start + out_ref.shape[0]
        copies = []
        for i, (place, out_ref) in enumerate(zip(places, out_refs)):
            length = out_ref.shape[0]
            at = pl.multiple_of(place, 8)
            copies.append(pltpu.make_async_copy(sum_ref.at[pl.ds(at, length)], out_ref, sems.at[i]))
        for copy in copies:
            copy.start()
        for copy in copies:
            copy.wait()


def pieces_of(planes):
    if planes < 16:
        return [planes]
    return [4, planes - 4]


def rotated(value, turn, length, sign=None):
    real, imag = value
    if turn == 0 or 4 * turn == length:
        if turn:
            real, imag = -imag, real
        return (real, imag) if sign is None else (real * sign, imag * sign)
    if sign is None and 8 * turn in (length, 3 * length):
        root = math.sqrt(0.5)
        if 8 * turn == length:
            return ((real - imag) * root, (real + imag) * root)
        return ((real + imag) * -root, (real - imag) * root)
    cos, sin = math.cos(2 * math.pi * turn / length), math.sin(2 * math.pi * turn / length)
    if sign is not None:
        cos, sin = cos * sign, sin * sign
    return (real * cos - imag * sin, real * sin + imag * cos)


def small_dft(values):
    length = len(values)
    if length == 1:
        return values
    even, odd = small_dft(values[0::2]), small_dft(values[1::2])
    low, high = [], []
    for k in range(length // 2):
        turned = rotated(odd[k], k, length)
        low.append((even[k][0] + turned[0], even[k][1] + turned[1]))
        high.append((even[k][0] - turned[0], even[k][1] - turned[1]))
    return low + high


def swap_quarters(values):
    lane = lax.broadcasted_iota(jnp.int32, values[0].shape, 1)
    low, even = lane < 64, (lane // 32) % 2 == 0
    roll = lambda value, shift: pltpu.roll(value, shift, 1)
    for first, second, shift, keep in ((0, 2, 64, low), (1, 3, 64, low), (0, 1, 32, even), (2, 3, 32, even)):
        one, two = values[first], values[second]
        values[first] = jnp.where(keep, one, roll(two, shift))
        values[second] = jnp.where(keep, roll(one, LANES - shift), two)
    return values


def in_halves(value):
    high = value.astype(jnp.bfloat16)
    return high, (value - high.astype(jnp.float32)).astype(jnp.bfloat16)


def planes_kernel(mine_ref, theirs_ref, zblock_ref, turn_ref, wide_ref, fine_ref, out_ref, high_ref, low_ref):
    step = pl.program_id(1)
    count = mine_ref.shape[1]
    groups, side = out_ref.shape[0], out_ref.shape[4]
    height = side // groups

    @pl.loop(0, count, unroll=8)
    def _(i):
        block = (mine_ref[:, i] + theirs_ref[:, i]).reshape(LANES, LANES)
        high, low = in_halves(block.T)
        both = jnp.dot(
            jnp.concatenate([high, low, high], axis=1), zblock_ref[...],
            preferred_element_type=jnp.float32,
        )
        by_cos = both[:, :LANES].reshape(8, 2, 8, LANES)
        by_sin = both[:, LANES:].reshape(8, 2, 8, LANES)
        real = by_cos[:, 0] - by_sin[:, 1]
        imag = by_sin[:, 0] + by_cos[:, 1]
        values = []
        for z in range(8):
            cos, sin = turn_ref[0, z:z + 1, :], turn_ref[1, z:z + 1, :]
            values.append((real[z] * cos - imag[z] * sin, real[z] * sin + imag[z] * cos))
        values = [jnp.concatenate(value, axis=0) for value in small_dft(values)]
        at = pl.ds(pl.multiple_of((step * count + i) * 16, 16), 16)
        for half in range(2):
            planes = swap_quarters(values[4 * half:4 * half + 4])
            for x in range(4):
                columns = slice((2 * x + half) * LANES, (2 * x + half + 1) * LANES)
                high, low = in_halves(planes[x])
                high_ref[at, columns] = high
                low_ref[at, columns] = low

    @pl.when(step == pl.num_programs(1) - 1)
    def _():
        @pl.loop(0, 4)
        def _(x):
            columns = pl.ds(pl.multiple_of(x * side, side), side)
            product = functools.partial(jnp.dot, preferred_element_type=jnp.float32)
            high = high_ref[:, columns]
            result = product(wide_ref[...], high) + (
                product(wide_ref[...], low_ref[:, columns]) + product(fine_ref[...], high)
            )
            for part in range(2):
                for group in range(groups):
                    start = part * side + group * height
                    out_ref[group, x, part] = result[start:start + height, :].astype(jnp.bfloat16)


def first_dimension_kernel(slabs, each, core_ref, *refs):
    arrays, (out_ref, mid_ref) = refs[:-2], refs[-2:]
    chunks = len(arrays) // 2
    own, other = arrays[:chunks], arrays[chunks:]
    spots = [(i, at) for i, ref in enumerate(own) for at in range(ref.shape[1])]
    core = core_ref[0]
    is_first = core == 0
    sign = (1 - 2 * core).astype(jnp.float32)

    rows = out_ref.shape[2]
    strips = [slice(at, min(at + 8, rows)) for at in range(0, rows, 8)]

    def plane(x, strip):
        slab, rest = x // (2 * each), x % (2 * each)
        half, inner = rest // each, rest % each
        chunk, at = spots[inner]
        loaded = []
        for part in range(2):
            here, there = own[chunk][slab, at, part], other[chunk][slab, at, part]
            value = jnp.where(is_first, here, there) if half == 0 else jnp.where(is_first, there, here)
            loaded.append(value.astype(jnp.float32)[strip])
        return tuple(loaded)

    for low in range(16):
        for strip in strips:
            values = small_dft([plane(low + 16 * high, strip) for high in range(16)])
            for k in range(16):
                real, imag = rotated(values[k], low * k, 256, sign if low % 2 else None)
                mid_ref[k, low, 0, strip] = real
                mid_ref[k, low, 1, strip] = imag

    @pl.loop(0, 16)
    def _(k):
        for strip in strips:
            values = [(mid_ref[k, low, 0, strip], mid_ref[k, low, 1, strip]) for low in range(16)]
            even, odd = small_dft(values[0::2]), small_dft(values[1::2])
            for m in range(8):
                turned = rotated(odd[m], m, 16)
                out_ref[0, k + 16 * m, strip] = even[m][0] + turned[0]
                out_ref[1, k + 16 * m, strip] = even[m][1] + turned[1]


def host_halves(table):
    high = table.astype(jnp.bfloat16)
    return high, (table - high.astype(np.float64)).astype(jnp.bfloat16)


def transform_tables(side):
    per_row = side // 8
    grid = np.arange(per_row)
    angle = 2 * np.pi * np.outer(grid, grid) / per_row
    zblock = np.concatenate([np.kron(np.eye(4), np.cos(angle)), np.kron(np.eye(4), np.sin(angle))], axis=1)
    high, low = host_halves(zblock)
    zblock = np.concatenate([high, high, low], axis=0)
    angle = 2 * np.pi * np.outer(np.arange(8), grid) / side
    turns = np.stack([np.tile(np.cos(angle), (1, 4)), np.tile(np.sin(angle), (1, 4))]).astype(np.float32)
    cells = np.arange(side)
    angle = 2 * np.pi * (np.outer(cells, cells) % side) / side
    cos, sin = np.cos(angle).reshape(side, per_row, 1, 8), np.sin(angle).reshape(side, per_row, 1, 8)
    matrix = np.concatenate(
        [np.concatenate([cos, -sin], axis=2), np.concatenate([sin, cos], axis=2)], axis=0
    ).reshape(2 * side, 2 * side) / float(side) ** 1.5
    return (zblock, turns) + host_halves(matrix)


def sum_over_slabs(partial_sums):
    slabs = partial_sums.shape[0]
    if slabs <= 8:
        me = lax.axis_index("slab")
        row = lambda i: lax.dynamic_index_in_dim(partial_sums, me ^ i, axis=0, keepdims=True)
        returned = [row(0)] + [
            lax.ppermute(row(i), "slab", [(slab, slab ^ i) for slab in range(slabs)])
            for i in range(1, slabs)
        ]
        returned = jnp.concatenate(returned)
    else:
        returned = lax.all_to_all(partial_sums, "slab", split_axis=0, concat_axis=0, tiled=True)
    return jnp.sum(returned, axis=0)


def to_field(mine, theirs_sent, partial_sums, side):
    slabs = lax.axis_size("slab")
    per_row = side // 8
    each = side // slabs // 2
    height = side // slabs
    groups = slabs if height % 16 == 0 else 1
    tables = [jnp.asarray(table) for table in transform_tables(side)]
    swap = [(0, 1), (1, 0)]
    theirs = [lax.ppermute(chunk, "dom", swap) for chunk in theirs_sent]
    grid_shape = (-1, per_row, per_row, LANES)
    mine = mine.reshape(grid_shape)
    short = max(0, 4 - each)
    if short:
        mine = jnp.pad(mine, ((0, short), (0, 0), (0, 0), (0, 0)))
    yblocks = 8
    own = []
    first_quad = 0
    before = []
    for real_planes, added in zip(pieces_of(each), theirs):
        if before:
            added, before[0] = lax.optimization_barrier((added, before[0]))
        added = added.reshape(grid_shape)
        if short:
            added = jnp.pad(added, ((0, short), (0, 0), (0, 0), (0, 0)))
        held = real_planes + short
        quads = held // 4
        whole = lambda table: pl.BlockSpec(table.shape, lambda q, y: (0,) * table.ndim)
        sent = pl.pallas_call(
            planes_kernel,
            grid=(quads, per_row // yblocks),
            out_shape=jax.ShapeDtypeStruct((groups, held, 2, side // groups, side), jnp.bfloat16),
            in_specs=[
                pl.BlockSpec((4, yblocks, per_row, LANES), lambda q, y, at=first_quad: (at + q, y, 0, 0)),
                pl.BlockSpec((4, yblocks, per_row, LANES), lambda q, y: (q, y, 0, 0)),
            ] + [whole(table) for table in tables],
            out_specs=pl.BlockSpec((groups, 4, 2, side // groups, side), lambda q, y: (0, q, 0, 0, 0)),
            scratch_shapes=[
                pltpu.VMEM((2 * side, 4 * side), jnp.bfloat16),
                pltpu.VMEM((2 * side, 4 * side), jnp.bfloat16),
            ],
            compiler_params=params(56),
            cost_estimate=pl.CostEstimate(
                flops=held * 8 * side**3, bytes_accessed=held * 4 * side**2 * 8, transcendentals=0
            ),
            name="transform_planes",
        )(mine, added, *tables)
        if groups != slabs:
            sent = sent.reshape(-1, 2, slabs, height, side).transpose(2, 0, 1, 3, 4)[:, :real_planes]
        first_quad += quads
        if before:
            sent, own[-1] = lax.optimization_barrier((sent, own[-1]))
        if first_quad * 4 >= each:
            sent, partial_sums = lax.optimization_barrier((sent, partial_sums))
        before = [sent]
        got = lax.all_to_all(sent, "slab", split_axis=0, concat_axis=0, tiled=True)
        own.append(got)
    other = [lax.ppermute(got, "dom", swap) for got in own[:-1]]
    own[-1], losses, *other = lax.optimization_barrier((own[-1], sum_over_slabs(partial_sums), *other))
    other.append(lax.ppermute(own[-1], "dom", swap))
    rows = min(16, height)
    arrays = own + other
    field = pl.pallas_call(
        functools.partial(first_dimension_kernel, slabs, each),
        grid=(height // rows, side // LANES),
        out_shape=jax.ShapeDtypeStruct((2, side // 2, height, side), jnp.float32),
        in_specs=[SMEM_SPEC] + [
            pl.BlockSpec(array.shape[:3] + (rows, LANES), lambda y, z: (0, 0, 0, y, z))
            for array in arrays
        ],
        out_specs=pl.BlockSpec((2, side // 2, rows, LANES), lambda y, z: (0, 0, y, z)),
        scratch_shapes=[pltpu.VMEM((16, 16, 2, rows, LANES), jnp.float32)],
        compiler_params=params(28),
        name="transform_first",
    )(lax.axis_index("dom").astype(jnp.int32).reshape(1), *arrays)
    return field, losses


def gradient_of_slab(volume, kernels, images, owners, local_block, kinds, counts, ctf_code, ctf_table, scales):
    slabs = lax.axis_size("slab")
    particles, list_length, features = images.shape
    side = math.isqrt(list_length * 64)
    entries = particles * list_length
    cap = 2 * entries // slabs
    slots = slabs * cap
    blocks = volume.shape[0]
    local_bits = bits_of(blocks)
    kind_count = kernels.shape[0]
    rows = entries // LANES
    int_rows = jax.ShapeDtypeStruct((rows, LANES), jnp.int32)

    target, word, totals = pl.pallas_call(
        functools.partial(route_kernel, slabs, cap, local_bits),
        out_shape=(int_rows, int_rows, jax.ShapeDtypeStruct((slabs, LANES), jnp.int32)),
        in_specs=[VMEM_SPEC, VMEM_SPEC, VMEM_SPEC, SMEM_SPEC],
        out_specs=(VMEM_SPEC, VMEM_SPEC, VMEM_SPEC),
        compiler_params=params(56),
        name="route",
    )(owners.reshape(rows, LANES), local_block, kinds, counts)
    target, word = target.reshape(entries), word.reshape(entries)
    tiles = [cap * 9 // 16, cap * 7 // 16] if cap >= 2048 else [cap]
    parts = len(tiles)
    code = ctf_code | ((scales.astype(jnp.float32) * 256.0).astype(jnp.int32) << 8)
    stride = cap + LANES
    meta, *packed = pl.pallas_call(
        functools.partial(pack_kernel, slabs, cap, list_length),
        out_shape=(jax.ShapeDtypeStruct((slabs * stride,), jnp.int32),)
        + tuple(jax.ShapeDtypeStruct((slabs, tile, features), jnp.bfloat16) for tile in tiles),
        in_specs=[SMEM_SPEC] * 5 + [VMEM_SPEC],
        out_specs=(SMEM_SPEC,) + (ANY_SPEC,) * parts,
        scratch_shapes=[
            pltpu.VMEM((entries, features), jnp.float32),
            pltpu.VMEM((slabs * stride, features), jnp.float32),
            pltpu.VMEM((slots, features), jnp.bfloat16),
            pltpu.SemaphoreType.DMA(()),
        ],
        compiler_params=params(56),
        name="pack",
    )(target, word, counts, totals, code, images.reshape(entries, features))
    arrived = lax.all_to_all(
        meta.reshape(slabs, stride), "slab", split_axis=0, concat_axis=0, tiled=True
    )
    words = arrived[:, :cap]
    totals_in = arrived[:, cap]
    codes_in = arrived[:, cap + 1:cap + 1 + particles]
    live = (jnp.arange(cap, dtype=jnp.int32)[None, :] < totals_in[:, None]).astype(jnp.int32)
    table_rows = ctf_table[(codes_in & 255).reshape(-1)]
    scale_in = (codes_in >> 8).astype(jnp.float32).reshape(-1) * (1.0 / 256.0)

    index = pl.pallas_call(
        functools.partial(decode_kernel, local_bits, blocks),
        out_shape=jax.ShapeDtypeStruct((slots // LANES + 8, LANES), jnp.int32),
        in_specs=[VMEM_SPEC, VMEM_SPEC],
        out_specs=VMEM_SPEC,
        compiler_params=params(56),
        name="decode",
    )(words.reshape(slots // LANES, LANES), live.reshape(slots // LANES, LANES))
    index = index.reshape(slots + 8 * LANES)
    voxels = list(pl.pallas_call(
        functools.partial(gather_kernel, slabs, cap),
        out_shape=tuple(
            jax.ShapeDtypeStruct((slabs, tile, features), jnp.bfloat16) for tile in tiles
        ),
        in_specs=[SMEM_SPEC, SMEM_SPEC, VMEM_SPEC],
        out_specs=(VMEM_SPEC,) * parts,
        scratch_shapes=[
            pltpu.VMEM((blocks + 8, features), jnp.float32),
            pltpu.VMEM((cap, features), jnp.float32),
        ],
        compiler_params=params(56),
        cost_estimate=pl.CostEstimate(flops=0, bytes_accessed=100 * MIB, transcendentals=0),
        name="read_voxels",
    )(index, totals_in, volume))

    forward = jnp.transpose(kernels, (0, 2, 1)).reshape(kind_count * features, features)
    backward = kernels.reshape(kind_count, 2, 8, 8, features).transpose(3, 1, 2, 0, 4)
    backward = backward.reshape(features, kind_count * features)
    unit = jnp.eye(features, dtype=jnp.bfloat16)
    core = lax.axis_index("dom").astype(jnp.int32).reshape(1)
    plane_blocks = (side // 8) ** 2
    pieces = [planes * plane_blocks for planes in pieces_of(side // slabs // 2)]
    squares, sums, behind, offset = 0.0, None, [voxels[0]], 0
    for part, tile in enumerate(tiles):
        first, last = part == 0, part == parts - 1
        if not first:
            packed[part], earlier = lax.optimization_barrier((packed[part], behind[part - 1]))
            if part == 1:
                voxels[0] = earlier
        picture = lax.all_to_all(packed[part], "slab", split_axis=0, concat_axis=0, tiled=True)
        lengths = [blocks // 2] + pieces if last else []
        arguments = [
            totals_in, table_rows[:, 0], table_rows[:, 1], scale_in, index, core,
            words[:, offset:offset + tile].reshape(slabs, 1, tile), voxels[part], picture,
            forward, backward, unit,
        ]
        aliases = {}
        if not first:
            aliases = {len(arguments): 1}
            arguments.append(pltpu.with_memory_space_constraint(sums, pltpu.VMEM))
        more, sums, *halves = pl.pallas_call(
            functools.partial(
                slab_kernel, side, local_bits, list_length, particles, cap, offset, first, last
            ),
            out_shape=(
                jax.ShapeDtypeStruct((slabs, particles, LANES), jnp.float32),
                pltpu.VMEM((blocks + 8, features), jnp.float32),
            )
            + tuple(jax.ShapeDtypeStruct((length, features), jnp.float32) for length in lengths),
            in_specs=[SMEM_SPEC] * 6 + [VMEM_SPEC] * (len(arguments) - 6),
            out_specs=(VMEM_SPEC, VMEM_SPEC) + (ANY_SPEC,) * len(lengths),
            scratch_shapes=[
                pltpu.VMEM((min(tile, STEP), features), jnp.float32),
                pltpu.SMEM((slabs * tile // min(tile, STEP) + 1,), jnp.int32),
                pltpu.SemaphoreType.DMA((max(1, len(lengths)),)),
            ],
            input_output_aliases=aliases,
            compiler_params=params(24),
            cost_estimate=pl.CostEstimate(flops=0, bytes_accessed=16 * MIB, transcendentals=0),
            name="compare_and_add",
        )(*arguments)
        squares = squares + more
        behind.append(more)
        offset += tile
    mine, *theirs = halves
    partial_sums = jnp.sum(squares, axis=2)
    return mine, theirs, partial_sums, side


def body(*arrays):
    mine, theirs, partial_sums, side = gradient_of_slab(*arrays)
    field, squares = to_field(mine, theirs, partial_sums, side)
    counts = arrays[6]
    return field, squares / (counts.astype(jnp.float32) * 128.0)


def solution(mesh):
    in_specs = (
        P(("groups", "slab"), None),
        P(),
        P(("groups", "slab", "dom"), None, None),
        P(("groups", "slab", "dom"), None, None),
        P(("groups", "slab", "dom"), None),
        P(("groups", "slab", "dom"), None),
        P(("groups", "slab", "dom")),
        P(("groups", "slab", "dom")),
        P(),
        P(("groups", "slab", "dom")),
    )
    out_specs = (P(None, ("groups", "dom"), "slab", None), P(("groups", "slab", "dom")))
    return jax.shard_map(body, mesh=mesh, in_specs=in_specs, out_specs=out_specs, check_vma=False)
```

```python
import functools
import math

import jax
import jax.numpy as jnp
import numpy as np
from jax import lax
from jax.experimental import pallas as pl
from jax.experimental.pallas import tpu as pltpu
from jax.sharding import PartitionSpec as P

LANES = 128
GROUP = 16
UNUSED = 100
STEP = 256
PAIR = 2
MIB = 1024 * 1024

SMEM_SPEC = pl.BlockSpec(memory_space=pltpu.SMEM)
VMEM_SPEC = pl.BlockSpec(memory_space=pltpu.VMEM)
ANY_SPEC = pl.BlockSpec(memory_space=pl.ANY)


def params(mib):
    return pltpu.CompilerParams(vmem_limit_bytes=mib * MIB)


def bits_of(count):
    return (count - 1).bit_length()


def route_kernel(slabs, cap, local_bits, owner_ref, local_ref, kind_ref, counts_ref, target_ref, word_ref, totals_ref):
    particles, list_length = local_ref.shape
    rows_each = list_length // LANES
    rows = particles * rows_each
    gathered = lambda ref: jnp.concatenate(
        [ref[:, j * LANES:(j + 1) * LANES] for j in range(rows_each)], axis=0
    )
    row_id = lax.broadcasted_iota(jnp.int32, (rows, LANES), 0)
    lane_id = lax.broadcasted_iota(jnp.int32, (rows, LANES), 1)
    particle = row_id % particles
    position = (row_id // particles) * LANES + lane_id
    limit = jnp.zeros((rows, LANES), jnp.int32)
    for i in range(particles):
        limit = jnp.where(particle == i, counts_ref[i], limit)
    owner = jnp.concatenate(
        [owner_ref[pl.ds(j, particles, stride=rows_each), :] for j in range(rows_each)], axis=0
    )
    owner = jnp.where(position < limit, owner, -1)
    up_to = (
        lax.broadcasted_iota(jnp.int32, (LANES, LANES), 0)
        <= lax.broadcasted_iota(jnp.int32, (LANES, LANES), 1)
    ).astype(jnp.bfloat16)
    ones = jnp.ones((LANES, LANES), jnp.bfloat16)
    before = (
        lax.broadcasted_iota(jnp.int32, (rows, rows), 1)
        < lax.broadcasted_iota(jnp.int32, (rows, rows), 0)
    ).astype(jnp.bfloat16)

    def one_slab(slab, target):
        mine = owner == slab
        hits = mine.astype(jnp.float32).astype(jnp.bfloat16)
        inside = jnp.dot(hits, up_to, preferred_element_type=jnp.float32)
        row_sum = jnp.dot(hits, ones, preferred_element_type=jnp.float32)
        above = jnp.dot(before, row_sum.astype(jnp.bfloat16), preferred_element_type=jnp.float32)
        rank = (inside + above).astype(jnp.int32) - 1
        total = (above[rows - 1:rows, :] + row_sum[rows - 1:rows, :]).astype(jnp.int32)
        totals_ref[pl.ds(slab, 1), :] = total
        return jnp.where(mine, slab * (cap + LANES) + rank, target)

    target = lax.fori_loop(0, slabs, one_slab, jnp.full((rows, LANES), cap + UNUSED, jnp.int32))
    target_ref[...] = target
    kind_bits = local_bits
    word = gathered(local_ref) | (gathered(kind_ref) << kind_bits) | (position << (kind_bits + 2))
    word_ref[...] = word | (particle << (kind_bits + 2 + bits_of(list_length)))


def pack_kernel(slabs, cap, list_length, target_ref, word_ref, counts_ref, totals_ref, code_ref, image_ref, meta_ref, *refs):
    out_refs, (wide_ref, staged_ref, narrow_ref, sem) = refs[:-4], refs[-4:]
    particles = counts_ref.shape[0]
    stride = cap + LANES
    step = 256
    turn = 32

    @pl.loop(0, image_ref.shape[0] // step)
    def _(i):
        at = pl.multiple_of(i * step, step)
        wide_ref[pl.ds(at, step), :] = image_ref[pl.ds(at, step), :].astype(jnp.float32)

    @pl.loop(0, particles)
    def _(particle):
        @pl.loop(0, (counts_ref[particle] + turn - 1) // turn)
        def _(i):
            per_row = LANES // turn
            first = (i // per_row) * (particles * LANES) + particle * LANES + (i % per_row) * turn
            row = particle * list_length + i * turn
            targets = [target_ref[first + j] for j in range(turn)]
            words = [word_ref[first + j] for j in range(turn)]
            rows = [wide_ref[pl.ds(row + j, 1), :] for j in range(turn)]
            for j in range(turn):
                staged_ref[pl.ds(targets[j], 1), :] = rows[j]
                meta_ref[targets[j]] = words[j]

    @pl.loop(0, slabs)
    def _(slab):
        header = slab * stride + cap
        meta_ref[header] = totals_ref[slab, 0]
        for j in range(particles):
            meta_ref[header + 1 + j] = code_ref[j]

    def blocks_of(act):
        offset = 0
        for out_ref in out_refs:
            width = out_ref.shape[1]

            @pl.loop(0, slabs)
            def _(slab, offset=offset, width=width, out_ref=out_ref):
                live = jnp.clip(totals_ref[slab, 0] - offset, 0, width)

                @pl.loop(0, (live + LANES - 1) // LANES)
                def _(i):
                    at = pl.multiple_of(slab * cap + offset + i * LANES, LANES)
                    to = pl.multiple_of(i * LANES, LANES)
                    copy = pltpu.make_async_copy(
                        narrow_ref.at[pl.ds(at, LANES)], out_ref.at[slab, pl.ds(to, LANES)], sem
                    )
                    act(copy, at, pl.multiple_of(at + slab * LANES, LANES))

            offset += width

    def convert_and_start(copy, at, staged_at):
        narrow_ref[pl.ds(at, LANES), :] = staged_ref[pl.ds(staged_at, LANES), :].astype(jnp.bfloat16)
        copy.start()

    blocks_of(convert_and_start)
    blocks_of(lambda copy, at, staged_at: copy.wait())


def decode_kernel(local_bits, dummy, word_ref, live_ref, index_ref):
    rows = word_ref.shape[0]
    live = live_ref[...] != 0
    index = jnp.where(live, word_ref[...] & ((1 << local_bits) - 1), dummy)
    lane = lax.broadcasted_iota(jnp.int32, (rows, LANES), 1)
    clash = jnp.zeros((rows, LANES), jnp.int32)
    for shift in range(1, GROUP):
        earlier = pltpu.roll(index, shift, 1)
        same = (earlier == index) & (lane % GROUP >= shift) & live
        clash = clash | same.astype(jnp.int32)
    shift = 1
    while shift < LANES:
        if shift == GROUP:
            index = index | jnp.where(lane % GROUP == 0, clash << 24, 0)
        clash = clash | pltpu.roll(clash, LANES - shift, 1)
        shift *= 2
    index_ref[0:rows, :] = index | jnp.where(lane == 0, clash << 25, 0)
    index_ref[rows:, :] = jnp.full((index_ref.shape[0] - rows, LANES), dummy, jnp.int32)


def gather_kernel(slabs, cap, index_ref, totals_ref, volume_ref, *refs):
    out_refs, (wide_ref, staged_ref) = refs[:-2], refs[-2:]
    blocks = volume_ref.shape[0]
    step = 256

    @pl.loop(0, blocks // step)
    def _(i):
        at = pl.multiple_of(i * step, step)
        wide_ref[pl.ds(at, step), :] = volume_ref[pl.ds(at, step), :].astype(jnp.float32)

    @pl.loop(0, slabs)
    def _(source):
        live = totals_ref[source]

        @pl.loop(0, (live + 15) // 16)
        def _(i):
            first = source * cap + i * 16
            places = [index_ref[first] & 0xFFFFFF] + [index_ref[first + j] for j in range(1, 16)]
            rows = [wide_ref[pl.ds(places[j], 1), :] for j in range(16)]
            for j in range(16):
                staged_ref[pl.ds(i * 16 + j, 1), :] = rows[j]

        offset = 0
        for out_ref in out_refs:
            width = out_ref.shape[1]

            @pl.when(live > offset)
            def _(offset=offset):
                out_ref[source] = staged_ref[offset:offset + width, :].astype(jnp.bfloat16)

            offset += width


def sine(angle):
    turns = jnp.floor(angle * (1.0 / math.pi) + 0.5)
    rest = angle - turns * 3.140625
    rest = rest - turns * (math.pi - 3.140625)
    odd = turns - 2.0 * jnp.floor(turns * 0.5)
    square = rest * rest
    poly = 2.718121e-6
    poly = poly * square - 1.9839334e-4
    poly = poly * square + 8.3333293e-3
    poly = poly * square - 1.6666667e-1
    value = rest + rest * square * poly
    return value * (1.0 - 2.0 * odd)


def slab_kernel(
    side, local_bits, list_length, particles, cap, offset, first, last,
    totals_ref, defocus_ref, phase_ref, scale_ref, index_ref, core_ref,
    word_ref, voxel_ref, image_ref, forward_ref, backward_ref, unit_ref, *rest,
):
    if not first:
        rest = rest[1:]
    square_ref, sum_ref, out_refs, (staged_ref, steps_ref, sems) = rest[0], rest[1], rest[2:-3], rest[-3:]
    slabs, _, tile = word_ref.shape
    step = staged_ref.shape[0] // PAIR
    steps_each = tile // step
    blocks = sum_ref.shape[0] - 8
    features = image_ref.shape[2]
    kinds = forward_ref.shape[0] // features
    position_bits = bits_of(list_length)
    per_row = side // 8
    half = features // 2

    if first:
        @pl.loop(0, blocks // 256)
        def _(i):
            at = pl.multiple_of(i * 256, 256)
            sum_ref[pl.ds(at, 256), :] = jnp.zeros((256, features), jnp.float32)

    square_ref[...] = jnp.zeros_like(square_ref)
    live_of = lambda source: jnp.clip(totals_ref[source] - offset, 0, tile)

    def list_source(source, count):
        def list_step(i, count):
            steps_ref[count] = source * steps_each + i
            return count + 1

        return lax.fori_loop(0, (live_of(source) + step - 1) // step, list_step, count)

    steps_ref[0] = 0
    count = lax.fori_loop(0, slabs, list_source, 0)

    def compare(number, slot):
        which_step = steps_ref[jnp.minimum(number, jnp.maximum(count - 1, 0))]
        source, at = which_step // steps_each, (which_step % steps_each) * step
        at = pl.multiple_of(at, step)
        live = jnp.where(number < count, live_of(source) - at, 0)
        word = word_ref[source, :, pl.ds(at, step)]
        kind = (word >> local_bits) & 3
        position = (word >> (local_bits + 2)) & (list_length - 1)
        particle = (word >> (local_bits + 2 + position_bits)) & (particles - 1)
        valid = lax.broadcasted_iota(jnp.int32, (1, step), 1) < live
        defocus = jnp.zeros((1, step), jnp.float32)
        phase = jnp.zeros((1, step), jnp.float32)
        scale = jnp.zeros((1, step), jnp.float32)
        for j in range(particles):
            chosen = particle == j
            defocus = jnp.where(chosen, defocus_ref[source * particles + j], defocus)
            phase = jnp.where(chosen, phase_ref[source * particles + j], phase)
            scale = jnp.where(chosen, scale_ref[source * particles + j], scale)
        defocus = defocus * (1.0 / float((side // 2) ** 2))
        cell = lax.broadcasted_iota(jnp.int32, (half, LANES), 0)
        cell_vert, cell_horiz = (cell // 8).astype(jnp.float32), (cell % 8).astype(jnp.float32)
        repeat = lambda table: jnp.concatenate([table] * (step // LANES), axis=1)
        vert = ((position // per_row) * 8 - side // 2).astype(jnp.float32) + repeat(cell_vert)
        horiz = ((position % per_row) * 8 - side // 2).astype(jnp.float32) + repeat(cell_horiz)
        factor = scale * sine(defocus * (vert * vert + horiz * horiz) + phase)
        factor = jnp.concatenate([factor, factor], axis=0)
        contract_last = (((1,), (1,)), ((), ()))
        each_kind = lax.dot_general(
            forward_ref[...], voxel_ref[source, pl.ds(at, step), :], contract_last,
            preferred_element_type=jnp.float32,
        )
        extracted = each_kind[0:features, :]
        for k in range(1, kinds):
            extracted = jnp.where(kind == k, each_kind[k * features:(k + 1) * features, :], extracted)
        picture = lax.dot_general(
            unit_ref[...], image_ref[source, pl.ds(at, step), :], contract_last,
            preferred_element_type=jnp.float32,
        )
        misfit = jnp.where(valid, factor * extracted - picture, 0.0)
        squares = jnp.sum(misfit * misfit, axis=0, keepdims=True)
        which = lax.broadcasted_iota(jnp.int32, (particles, step), 0)
        spread = jnp.where(valid & (particle == which), squares, 0.0)
        folded = spread[:, 0:LANES]
        for i in range(1, step // LANES):
            folded = folded + spread[:, i * LANES:(i + 1) * LANES]
        square_ref[source] = square_ref[source] + folded
        weighted = (factor * misfit).astype(jnp.bfloat16)
        none = jnp.zeros_like(weighted)
        spread_back = jnp.concatenate(
            [jnp.where(kind == k, weighted, none) for k in range(kinds)], axis=0
        )
        terms = jnp.dot(backward_ref[...], spread_back, preferred_element_type=jnp.float32)
        staged_ref[slot * step:(slot + 1) * step, :] = terms.T

    def places_of(base):
        return [index_ref[base] & 0xFFFFFF] + [index_ref[base + j] for j in range(1, GROUP)]

    def add_group(base, at):
        places = places_of(base)
        held = [sum_ref[pl.ds(place, 1), :] for place in places]
        new = [staged_ref[pl.ds(at + j, 1), :] for j in range(GROUP)]
        for j in range(GROUP):
            sum_ref[pl.ds(places[j], 1), :] = held[j] + new[j]

    def base_of(number):
        earlier = steps_ref[jnp.clip(number, 0, jnp.maximum(count - 1, 0))]
        base = (earlier // steps_each) * cap + offset + (earlier % steps_each) * step
        return jnp.where((number >= 0) & (number < count), base, slabs * cap)

    @pl.loop(0, (count + PAIR - 1) // PAIR + 1)
    def _(turn):
        bases = [base_of((turn - 1) * PAIR + slot) for slot in range(PAIR)]
        marks = 0
        for base in bases:
            for i in range(step // LANES):
                marks = marks | index_ref[base + i * LANES]

        @pl.when(marks < (1 << 25))
        def _():
            for slot, base in enumerate(bases):
                for g in range(step // GROUP):
                    add_group(base + g * GROUP, slot * step + g * GROUP)
            for slot in range(PAIR):
                compare(turn * PAIR + slot, slot)

        @pl.when(marks >= (1 << 25))
        def _():
            for slot, base in enumerate(bases):
                @pl.loop(0, step // GROUP)
                def _(g, slot=slot, base=base):
                    start = base + g * GROUP
                    at = slot * step + g * GROUP
                    clashes = (index_ref[start] >> 24) & 1

                    @pl.when(clashes == 0)
                    def _():
                        add_group(start, at)

                    @pl.when(clashes == 1)
                    def _():
                        places = places_of(start)
                        for j in range(GROUP):
                            sum_ref[pl.ds(places[j], 1), :] = (
                                sum_ref[pl.ds(places[j], 1), :] + staged_ref[pl.ds(at + j, 1), :]
                            )

            for slot in range(PAIR):
                compare(turn * PAIR + slot, slot)

    if last:
        half = blocks // 2
        start = (1 - core_ref[0]) * half
        places = [core_ref[0] * half]
        for out_ref in out_refs[1:]:
            places.append(start)
            start = start + out_ref.shape[0]
        copies = []
        for i, (place, out_ref) in enumerate(zip(places, out_refs)):
            length = out_ref.shape[0]
            at = pl.multiple_of(place, 8)
            copies.append(pltpu.make_async_copy(sum_ref.at[pl.ds(at, length)], out_ref, sems.at[i]))
        for copy in copies:
            copy.start()
        for copy in copies:
            copy.wait()


def pieces_of(planes):
    if planes < 16:
        return [planes]
    return [4, planes - 4]


def rotated(value, turn, length, sign=None):
    real, imag = value
    if turn == 0 or 4 * turn == length:
        if turn:
            real, imag = -imag, real
        return (real, imag) if sign is None else (real * sign, imag * sign)
    if sign is None and 8 * turn in (length, 3 * length):
        root = math.sqrt(0.5)
        if 8 * turn == length:
            return ((real - imag) * root, (real + imag) * root)
        return ((real + imag) * -root, (real - imag) * root)
    cos, sin = math.cos(2 * math.pi * turn / length), math.sin(2 * math.pi * turn / length)
    if sign is not None:
        cos, sin = cos * sign, sin * sign
    return (real * cos - imag * sin, real * sin + imag * cos)


def small_dft(values):
    length = len(values)
    if length == 1:
        return values
    even, odd = small_dft(values[0::2]), small_dft(values[1::2])
    low, high = [], []
    for k in range(length // 2):
        turned = rotated(odd[k], k, length)
        low.append((even[k][0] + turned[0], even[k][1] + turned[1]))
        high.append((even[k][0] - turned[0], even[k][1] - turned[1]))
    return low + high


def swap_quarters(values):
    lane = lax.broadcasted_iota(jnp.int32, values[0].shape, 1)
    low, even = lane < 64, (lane // 32) % 2 == 0
    roll = lambda value, shift: pltpu.roll(value, shift, 1)
    for first, second, shift, keep in ((0, 2, 64, low), (1, 3, 64, low), (0, 1, 32, even), (2, 3, 32, even)):
        one, two = values[first], values[second]
        values[first] = jnp.where(keep, one, roll(two, shift))
        values[second] = jnp.where(keep, roll(one, LANES - shift), two)
    return values


def in_halves(value):
    high = value.astype(jnp.bfloat16)
    return high, (value - high.astype(jnp.float32)).astype(jnp.bfloat16)


def planes_kernel(mine_ref, theirs_ref, zblock_ref, turn_ref, wide_ref, fine_ref, out_ref, high_ref, low_ref):
    step = pl.program_id(1)
    count = mine_ref.shape[1]
    groups, side = out_ref.shape[0], out_ref.shape[4]
    height = side // groups

    @pl.loop(0, count, unroll=8)
    def _(i):
        block = (mine_ref[:, i] + theirs_ref[:, i]).reshape(LANES, LANES)
        high, low = in_halves(block.T)
        both = jnp.dot(
            jnp.concatenate([high, low, high], axis=1), zblock_ref[...],
            preferred_element_type=jnp.float32,
        )
        by_cos = both[:, :LANES].reshape(8, 2, 8, LANES)
        by_sin = both[:, LANES:].reshape(8, 2, 8, LANES)
        real = by_cos[:, 0] - by_sin[:, 1]
        imag = by_sin[:, 0] + by_cos[:, 1]
        values = []
        for z in range(8):
            cos, sin = turn_ref[0, z:z + 1, :], turn_ref[1, z:z + 1, :]
            values.append((real[z] * cos - imag[z] * sin, real[z] * sin + imag[z] * cos))
        values = [jnp.concatenate(value, axis=0) for value in small_dft(values)]
        at = pl.ds(pl.multiple_of((step * count + i) * 16, 16), 16)
        for half in range(2):
            planes = swap_quarters(values[4 * half:4 * half + 4])
            for x in range(4):
                columns = slice((2 * x + half) * LANES, (2 * x + half + 1) * LANES)
                high, low = in_halves(planes[x])
                high_ref[at, columns] = high
                low_ref[at, columns] = low

    @pl.when(step == pl.num_programs(1) - 1)
    def _():
        @pl.loop(0, 4)
        def _(x):
            columns = pl.ds(pl.multiple_of(x * side, side), side)
            product = functools.partial(jnp.dot, preferred_element_type=jnp.float32)
            high = high_ref[:, columns]
            result = product(wide_ref[...], high) + (
                product(wide_ref[...], low_ref[:, columns]) + product(fine_ref[...], high)
            )
            for part in range(2):
                for group in range(groups):
                    start = part * side + group * height
                    out_ref[group, x, part] = result[start:start + height, :].astype(jnp.bfloat16)


def first_dimension_kernel(slabs, each, core_ref, *refs):
    arrays, (out_ref, mid_ref) = refs[:-2], refs[-2:]
    chunks = len(arrays) // 2
    own, other = arrays[:chunks], arrays[chunks:]
    spots = [(i, at) for i, ref in enumerate(own) for at in range(ref.shape[1])]
    core = core_ref[0]
    is_first = core == 0
    sign = (1 - 2 * core).astype(jnp.float32)

    rows = out_ref.shape[2]
    strips = [slice(at, min(at + 8, rows)) for at in range(0, rows, 8)]

    def plane(x, strip):
        slab, rest = x // (2 * each), x % (2 * each)
        half, inner = rest // each, rest % each
        chunk, at = spots[inner]
        loaded = []
        for part in range(2):
            here, there = own[chunk][slab, at, part], other[chunk][slab, at, part]
            value = jnp.where(is_first, here, there) if half == 0 else jnp.where(is_first, there, here)
            loaded.append(value.astype(jnp.float32)[strip])
        return tuple(loaded)

    for low in range(16):
        for strip in strips:
            values = small_dft([plane(low + 16 * high, strip) for high in range(16)])
            for k in range(16):
                real, imag = rotated(values[k], low * k, 256, sign if low % 2 else None)
                mid_ref[k, low, 0, strip] = real
                mid_ref[k, low, 1, strip] = imag

    @pl.loop(0, 16)
    def _(k):
        for strip in strips:
            values = [(mid_ref[k, low, 0, strip], mid_ref[k, low, 1, strip]) for low in range(16)]
            even, odd = small_dft(values[0::2]), small_dft(values[1::2])
            for m in range(8):
                turned = rotated(odd[m], m, 16)
                out_ref[0, k + 16 * m, strip] = even[m][0] + turned[0]
                out_ref[1, k + 16 * m, strip] = even[m][1] + turned[1]


def host_halves(table):
    high = table.astype(jnp.bfloat16)
    return high, (table - high.astype(np.float64)).astype(jnp.bfloat16)


def transform_tables(side):
    per_row = side // 8
    grid = np.arange(per_row)
    angle = 2 * np.pi * np.outer(grid, grid) / per_row
    zblock = np.concatenate([np.kron(np.eye(4), np.cos(angle)), np.kron(np.eye(4), np.sin(angle))], axis=1)
    high, low = host_halves(zblock)
    zblock = np.concatenate([high, high, low], axis=0)
    angle = 2 * np.pi * np.outer(np.arange(8), grid) / side
    turns = np.stack([np.tile(np.cos(angle), (1, 4)), np.tile(np.sin(angle), (1, 4))]).astype(np.float32)
    cells = np.arange(side)
    angle = 2 * np.pi * (np.outer(cells, cells) % side) / side
    cos, sin = np.cos(angle).reshape(side, per_row, 1, 8), np.sin(angle).reshape(side, per_row, 1, 8)
    matrix = np.concatenate(
        [np.concatenate([cos, -sin], axis=2), np.concatenate([sin, cos], axis=2)], axis=0
    ).reshape(2 * side, 2 * side) / float(side) ** 1.5
    return (zblock, turns) + host_halves(matrix)


def sum_over_slabs(partial_sums):
    slabs = partial_sums.shape[0]
    if slabs <= 8:
        me = lax.axis_index("slab")
        row = lambda i: lax.dynamic_index_in_dim(partial_sums, me ^ i, axis=0, keepdims=True)
        returned = [row(0)] + [
            lax.ppermute(row(i), "slab", [(slab, slab ^ i) for slab in range(slabs)])
            for i in range(1, slabs)
        ]
        returned = jnp.concatenate(returned)
    else:
        returned = lax.all_to_all(partial_sums, "slab", split_axis=0, concat_axis=0, tiled=True)
    return jnp.sum(returned, axis=0)


def to_field(mine, theirs_sent, partial_sums, side):
    slabs = lax.axis_size("slab")
    per_row = side // 8
    each = side // slabs // 2
    height = side // slabs
    groups = slabs if height % 16 == 0 else 1
    tables = [jnp.asarray(table) for table in transform_tables(side)]
    swap = [(0, 1), (1, 0)]
    theirs = [lax.ppermute(chunk, "dom", swap) for chunk in theirs_sent]
    grid_shape = (-1, per_row, per_row, LANES)
    mine = mine.reshape(grid_shape)
    short = max(0, 4 - each)
    if short:
        mine = jnp.pad(mine, ((0, short), (0, 0), (0, 0), (0, 0)))
    yblocks = 8
    own = []
    first_quad = 0
    before = []
    for real_planes, added in zip(pieces_of(each), theirs):
        if before:
            added, before[0] = lax.optimization_barrier((added, before[0]))
        added = added.reshape(grid_shape)
        if short:
            added = jnp.pad(added, ((0, short), (0, 0), (0, 0), (0, 0)))
        held = real_planes + short
        quads = held // 4
        whole = lambda table: pl.BlockSpec(table.shape, lambda q, y: (0,) * table.ndim)
        sent = pl.pallas_call(
            planes_kernel,
            grid=(quads, per_row // yblocks),
            out_shape=jax.ShapeDtypeStruct((groups, held, 2, side // groups, side), jnp.bfloat16),
            in_specs=[
                pl.BlockSpec((4, yblocks, per_row, LANES), lambda q, y, at=first_quad: (at + q, y, 0, 0)),
                pl.BlockSpec((4, yblocks, per_row, LANES), lambda q, y: (q, y, 0, 0)),
            ] + [whole(table) for table in tables],
            out_specs=pl.BlockSpec((groups, 4, 2, side // groups, side), lambda q, y: (0, q, 0, 0, 0)),
            scratch_shapes=[
                pltpu.VMEM((2 * side, 4 * side), jnp.bfloat16),
                pltpu.VMEM((2 * side, 4 * side), jnp.bfloat16),
            ],
            compiler_params=params(56),
            cost_estimate=pl.CostEstimate(
                flops=held * 8 * side**3, bytes_accessed=held * 4 * side**2 * 8, transcendentals=0
            ),
            name="transform_planes",
        )(mine, added, *tables)
        if groups != slabs:
            sent = sent.reshape(-1, 2, slabs, height, side).transpose(2, 0, 1, 3, 4)[:, :real_planes]
        first_quad += quads
        if before:
            sent, own[-1] = lax.optimization_barrier((sent, own[-1]))
        if first_quad * 4 >= each:
            sent, partial_sums = lax.optimization_barrier((sent, partial_sums))
        before = [sent]
        got = lax.all_to_all(sent, "slab", split_axis=0, concat_axis=0, tiled=True)
        own.append(got)
    other = [lax.ppermute(got, "dom", swap) for got in own[:-1]]
    own[-1], losses, *other = lax.optimization_barrier((own[-1], sum_over_slabs(partial_sums), *other))
    other.append(lax.ppermute(own[-1], "dom", swap))
    rows = min(16, height)
    arrays = own + other
    field = pl.pallas_call(
        functools.partial(first_dimension_kernel, slabs, each),
        grid=(height // rows, side // LANES),
        out_shape=jax.ShapeDtypeStruct((2, side // 2, height, side), jnp.float32),
        in_specs=[SMEM_SPEC] + [
            pl.BlockSpec(array.shape[:3] + (rows, LANES), lambda y, z: (0, 0, 0, y, z))
            for array in arrays
        ],
        out_specs=pl.BlockSpec((2, side // 2, rows, LANES), lambda y, z: (0, 0, y, z)),
        scratch_shapes=[pltpu.VMEM((16, 16, 2, rows, LANES), jnp.float32)],
        compiler_params=params(28),
        name="transform_first",
    )(lax.axis_index("dom").astype(jnp.int32).reshape(1), *arrays)
    return field, losses


def gradient_of_slab(volume, kernels, images, owners, local_block, kinds, counts, ctf_code, ctf_table, scales):
    slabs = lax.axis_size("slab")
    particles, list_length, features = images.shape
    side = math.isqrt(list_length * 64)
    entries = particles * list_length
    cap = 2 * entries // slabs
    slots = slabs * cap
    blocks = volume.shape[0]
    local_bits = bits_of(blocks)
    kind_count = kernels.shape[0]
    rows = entries // LANES
    int_rows = jax.ShapeDtypeStruct((rows, LANES), jnp.int32)

    target, word, totals = pl.pallas_call(
        functools.partial(route_kernel, slabs, cap, local_bits),
        out_shape=(int_rows, int_rows, jax.ShapeDtypeStruct((slabs, LANES), jnp.int32)),
        in_specs=[VMEM_SPEC, VMEM_SPEC, VMEM_SPEC, SMEM_SPEC],
        out_specs=(VMEM_SPEC, VMEM_SPEC, VMEM_SPEC),
        compiler_params=params(56),
        name="route",
    )(owners.reshape(rows, LANES), local_block, kinds, counts)
    target, word = target.reshape(entries), word.reshape(entries)
    tiles = [cap * 5 // 8, cap * 3 // 8] if cap >= 2048 else [cap]
    parts = len(tiles)
    code = ctf_code | ((scales.astype(jnp.float32) * 256.0).astype(jnp.int32) << 8)
    stride = cap + LANES
    meta, *packed = pl.pallas_call(
        functools.partial(pack_kernel, slabs, cap, list_length),
        out_shape=(jax.ShapeDtypeStruct((slabs * stride,), jnp.int32),)
        + tuple(jax.ShapeDtypeStruct((slabs, tile, features), jnp.bfloat16) for tile in tiles),
        in_specs=[SMEM_SPEC] * 5 + [VMEM_SPEC],
        out_specs=(SMEM_SPEC,) + (ANY_SPEC,) * parts,
        scratch_shapes=[
            pltpu.VMEM((entries, features), jnp.float32),
            pltpu.VMEM((slabs * stride, features), jnp.float32),
            pltpu.VMEM((slots, features), jnp.bfloat16),
            pltpu.SemaphoreType.DMA(()),
        ],
        compiler_params=params(56),
        name="pack",
    )(target, word, counts, totals, code, images.reshape(entries, features))
    arrived = lax.all_to_all(
        meta.reshape(slabs, stride), "slab", split_axis=0, concat_axis=0, tiled=True
    )
    words = arrived[:, :cap]
    totals_in = arrived[:, cap]
    codes_in = arrived[:, cap + 1:cap + 1 + particles]
    live = (jnp.arange(cap, dtype=jnp.int32)[None, :] < totals_in[:, None]).astype(jnp.int32)
    table_rows = ctf_table[(codes_in & 255).reshape(-1)]
    scale_in = (codes_in >> 8).astype(jnp.float32).reshape(-1) * (1.0 / 256.0)

    index = pl.pallas_call(
        functools.partial(decode_kernel, local_bits, blocks),
        out_shape=jax.ShapeDtypeStruct((slots // LANES + 8, LANES), jnp.int32),
        in_specs=[VMEM_SPEC, VMEM_SPEC],
        out_specs=VMEM_SPEC,
        compiler_params=params(56),
        name="decode",
    )(words.reshape(slots // LANES, LANES), live.reshape(slots // LANES, LANES))
    index = index.reshape(slots + 8 * LANES)
    voxels = list(pl.pallas_call(
        functools.partial(gather_kernel, slabs, cap),
        out_shape=tuple(
            jax.ShapeDtypeStruct((slabs, tile, features), jnp.bfloat16) for tile in tiles
        ),
        in_specs=[SMEM_SPEC, SMEM_SPEC, VMEM_SPEC],
        out_specs=(VMEM_SPEC,) * parts,
        scratch_shapes=[
            pltpu.VMEM((blocks + 8, features), jnp.float32),
            pltpu.VMEM((cap, features), jnp.float32),
        ],
        compiler_params=params(56),
        cost_estimate=pl.CostEstimate(flops=0, bytes_accessed=100 * MIB, transcendentals=0),
        name="read_voxels",
    )(index, totals_in, volume))

    forward = jnp.transpose(kernels, (0, 2, 1)).reshape(kind_count * features, features)
    backward = kernels.reshape(kind_count, 2, 8, 8, features).transpose(3, 1, 2, 0, 4)
    backward = backward.reshape(features, kind_count * features)
    unit = jnp.eye(features, dtype=jnp.bfloat16)
    core = lax.axis_index("dom").astype(jnp.int32).reshape(1)
    plane_blocks = (side // 8) ** 2
    pieces = [planes * plane_blocks for planes in pieces_of(side // slabs // 2)]
    squares, sums, behind, offset = 0.0, None, [voxels[0]], 0
    for part, tile in enumerate(tiles):
        first, last = part == 0, part == parts - 1
        if not first:
            packed[part], earlier = lax.optimization_barrier((packed[part], behind[part - 1]))
            if part == 1:
                voxels[0] = earlier
        picture = lax.all_to_all(packed[part], "slab", split_axis=0, concat_axis=0, tiled=True)
        lengths = [blocks // 2] + pieces if last else []
        arguments = [
            totals_in, table_rows[:, 0], table_rows[:, 1], scale_in, index, core,
            words[:, offset:offset + tile].reshape(slabs, 1, tile), voxels[part], picture,
            forward, backward, unit,
        ]
        aliases = {}
        if not first:
            aliases = {len(arguments): 1}
            arguments.append(pltpu.with_memory_space_constraint(sums, pltpu.VMEM))
        more, sums, *halves = pl.pallas_call(
            functools.partial(
                slab_kernel, side, local_bits, list_length, particles, cap, offset, first, last
            ),
            out_shape=(
                jax.ShapeDtypeStruct((slabs, particles, LANES), jnp.float32),
                pltpu.VMEM((blocks + 8, features), jnp.float32),
            )
            + tuple(jax.ShapeDtypeStruct((length, features), jnp.float32) for length in lengths),
            in_specs=[SMEM_SPEC] * 6 + [VMEM_SPEC] * (len(arguments) - 6),
            out_specs=(VMEM_SPEC, VMEM_SPEC) + (ANY_SPEC,) * len(lengths),
            scratch_shapes=[
                pltpu.VMEM((PAIR * min(tile, STEP), features), jnp.float32),
                pltpu.SMEM((slabs * tile // min(tile, STEP) + 1,), jnp.int32),
                pltpu.SemaphoreType.DMA((max(1, len(lengths)),)),
            ],
            input_output_aliases=aliases,
            compiler_params=params(24),
            cost_estimate=pl.CostEstimate(flops=0, bytes_accessed=16 * MIB, transcendentals=0),
            name="compare_and_add",
        )(*arguments)
        squares = squares + more
        behind.append(more)
        offset += tile
    mine, *theirs = halves
    partial_sums = jnp.sum(squares, axis=2)
    return mine, theirs, partial_sums, side


def body(*arrays):
    mine, theirs, partial_sums, side = gradient_of_slab(*arrays)
    field, squares = to_field(mine, theirs, partial_sums, side)
    counts = arrays[6]
    return field, squares / (counts.astype(jnp.float32) * 128.0)


def solution(mesh):
    in_specs = (
        P(("groups", "slab"), None),
        P(),
        P(("groups", "slab", "dom"), None, None),
        P(("groups", "slab", "dom"), None, None),
        P(("groups", "slab", "dom"), None),
        P(("groups", "slab", "dom"), None),
        P(("groups", "slab", "dom")),
        P(("groups", "slab", "dom")),
        P(),
        P(("groups", "slab", "dom")),
    )
    out_specs = (P(None, ("groups", "dom"), "slab", None), P(("groups", "slab", "dom")))
    return jax.shard_map(body, mesh=mesh, in_specs=in_specs, out_specs=out_specs, check_vma=False)
```

```python
import functools
import math

import jax
import jax.numpy as jnp
import numpy as np
from jax import lax
from jax.experimental import pallas as pl
from jax.experimental.pallas import tpu as pltpu
from jax.sharding import PartitionSpec as P

LANES = 128
GROUP = 16
UNUSED = 100
STEP = 256
PAIR = 1
MIB = 1024 * 1024

SMEM_SPEC = pl.BlockSpec(memory_space=pltpu.SMEM)
VMEM_SPEC = pl.BlockSpec(memory_space=pltpu.VMEM)
ANY_SPEC = pl.BlockSpec(memory_space=pl.ANY)


def params(mib):
    return pltpu.CompilerParams(vmem_limit_bytes=mib * MIB)


def bits_of(count):
    return (count - 1).bit_length()


def route_kernel(slabs, cap, local_bits, owner_ref, local_ref, kind_ref, counts_ref, target_ref, word_ref, totals_ref):
    particles, list_length = local_ref.shape
    rows_each = list_length // LANES
    rows = particles * rows_each
    gathered = lambda ref: jnp.concatenate(
        [ref[:, j * LANES:(j + 1) * LANES] for j in range(rows_each)], axis=0
    )
    row_id = lax.broadcasted_iota(jnp.int32, (rows, LANES), 0)
    lane_id = lax.broadcasted_iota(jnp.int32, (rows, LANES), 1)
    particle = row_id % particles
    position = (row_id // particles) * LANES + lane_id
    limit = jnp.zeros((rows, LANES), jnp.int32)
    for i in range(particles):
        limit = jnp.where(particle == i, counts_ref[i], limit)
    owner = jnp.concatenate(
        [owner_ref[pl.ds(j, particles, stride=rows_each), :] for j in range(rows_each)], axis=0
    )
    owner = jnp.where(position < limit, owner, -1)
    up_to = (
        lax.broadcasted_iota(jnp.int32, (LANES, LANES), 0)
        <= lax.broadcasted_iota(jnp.int32, (LANES, LANES), 1)
    ).astype(jnp.bfloat16)
    ones = jnp.ones((LANES, LANES), jnp.bfloat16)
    before = (
        lax.broadcasted_iota(jnp.int32, (rows, rows), 1)
        < lax.broadcasted_iota(jnp.int32, (rows, rows), 0)
    ).astype(jnp.bfloat16)

    def one_slab(slab, target):
        mine = owner == slab
        hits = mine.astype(jnp.float32).astype(jnp.bfloat16)
        inside = jnp.dot(hits, up_to, preferred_element_type=jnp.float32)
        row_sum = jnp.dot(hits, ones, preferred_element_type=jnp.float32)
        above = jnp.dot(before, row_sum.astype(jnp.bfloat16), preferred_element_type=jnp.float32)
        rank = (inside + above).astype(jnp.int32) - 1
        total = (above[rows - 1:rows, :] + row_sum[rows - 1:rows, :]).astype(jnp.int32)
        totals_ref[pl.ds(slab, 1), :] = total
        return jnp.where(mine, slab * (cap + LANES) + rank, target)

    target = lax.fori_loop(0, slabs, one_slab, jnp.full((rows, LANES), cap + UNUSED, jnp.int32))
    target_ref[...] = target
    kind_bits = local_bits
    word = gathered(local_ref) | (gathered(kind_ref) << kind_bits) | (position << (kind_bits + 2))
    word_ref[...] = word | (particle << (kind_bits + 2 + bits_of(list_length)))


def pack_kernel(slabs, cap, list_length, target_ref, word_ref, counts_ref, totals_ref, code_ref, image_ref, meta_ref, *refs):
    out_refs, (wide_ref, staged_ref, narrow_ref, sem) = refs[:-4], refs[-4:]
    particles = counts_ref.shape[0]
    stride = cap + LANES
    step = 256
    turn = 32

    @pl.loop(0, image_ref.shape[0] // step)
    def _(i):
        at = pl.multiple_of(i * step, step)
        wide_ref[pl.ds(at, step), :] = image_ref[pl.ds(at, step), :].astype(jnp.float32)

    @pl.loop(0, particles)
    def _(particle):
        @pl.loop(0, (counts_ref[particle] + turn - 1) // turn)
        def _(i):
            per_row = LANES // turn
            first = (i // per_row) * (particles * LANES) + particle * LANES + (i % per_row) * turn
            row = particle * list_length + i * turn
            targets = [target_ref[first + j] for j in range(turn)]
            words = [word_ref[first + j] for j in range(turn)]
            rows = [wide_ref[pl.ds(row + j, 1), :] for j in range(turn)]
            for j in range(turn):
                staged_ref[pl.ds(targets[j], 1), :] = rows[j]
                meta_ref[targets[j]] = words[j]

    @pl.loop(0, slabs)
    def _(slab):
        header = slab * stride + cap
        meta_ref[header] = totals_ref[slab, 0]
        for j in range(particles):
            meta_ref[header + 1 + j] = code_ref[j]

    def blocks_of(act):
        offset = 0
        for out_ref in out_refs:
            width = out_ref.shape[1]

            @pl.loop(0, slabs)
            def _(slab, offset=offset, width=width, out_ref=out_ref):
                live = jnp.clip(totals_ref[slab, 0] - offset, 0, width)

                @pl.loop(0, (live + LANES - 1) // LANES)
                def _(i):
                    at = pl.multiple_of(slab * cap + offset + i * LANES, LANES)
                    to = pl.multiple_of(i * LANES, LANES)
                    copy = pltpu.make_async_copy(
                        narrow_ref.at[pl.ds(at, LANES)], out_ref.at[slab, pl.ds(to, LANES)], sem
                    )
                    act(copy, at, pl.multiple_of(at + slab * LANES, LANES))

            offset += width

    def convert_and_start(copy, at, staged_at):
        narrow_ref[pl.ds(at, LANES), :] = staged_ref[pl.ds(staged_at, LANES), :].astype(jnp.bfloat16)
        copy.start()

    blocks_of(convert_and_start)
    blocks_of(lambda copy, at, staged_at: copy.wait())


def decode_kernel(local_bits, dummy, word_ref, live_ref, index_ref):
    rows = word_ref.shape[0]
    live = live_ref[...] != 0
    index = jnp.where(live, word_ref[...] & ((1 << local_bits) - 1), dummy)
    lane = lax.broadcasted_iota(jnp.int32, (rows, LANES), 1)
    clash = jnp.zeros((rows, LANES), jnp.int32)
    for shift in range(1, GROUP):
        earlier = pltpu.roll(index, shift, 1)
        same = (earlier == index) & (lane % GROUP >= shift) & live
        clash = clash | same.astype(jnp.int32)
    shift = 1
    while shift < LANES:
        if shift == GROUP:
            index = index | jnp.where(lane % GROUP == 0, clash << 24, 0)
        clash = clash | pltpu.roll(clash, LANES - shift, 1)
        shift *= 2
    index_ref[0:rows, :] = index | jnp.where(lane == 0, clash << 25, 0)
    index_ref[rows:, :] = jnp.full((index_ref.shape[0] - rows, LANES), dummy, jnp.int32)


def gather_kernel(slabs, cap, index_ref, totals_ref, volume_ref, *refs):
    out_refs, (wide_ref, staged_ref) = refs[:-2], refs[-2:]
    blocks = volume_ref.shape[0]
    step = 256

    @pl.loop(0, blocks // step)
    def _(i):
        at = pl.multiple_of(i * step, step)
        wide_ref[pl.ds(at, step), :] = volume_ref[pl.ds(at, step), :].astype(jnp.float32)

    @pl.loop(0, slabs)
    def _(source):
        live = totals_ref[source]

        @pl.loop(0, (live + 15) // 16)
        def _(i):
            first = source * cap + i * 16
            places = [index_ref[first] & 0xFFFFFF] + [index_ref[first + j] for j in range(1, 16)]
            rows = [wide_ref[pl.ds(places[j], 1), :] for j in range(16)]
            for j in range(16):
                staged_ref[pl.ds(i * 16 + j, 1), :] = rows[j]

        offset = 0
        for out_ref in out_refs:
            width = out_ref.shape[1]

            @pl.when(live > offset)
            def _(offset=offset):
                out_ref[source] = staged_ref[offset:offset + width, :].astype(jnp.bfloat16)

            offset += width


def sine(angle):
    turns = jnp.floor(angle * (1.0 / math.pi) + 0.5)
    rest = angle - turns * 3.140625
    rest = rest - turns * (math.pi - 3.140625)
    odd = turns - 2.0 * jnp.floor(turns * 0.5)
    square = rest * rest
    poly = 2.718121e-6
    poly = poly * square - 1.9839334e-4
    poly = poly * square + 8.3333293e-3
    poly = poly * square - 1.6666667e-1
    value = rest + rest * square * poly
    return value * (1.0 - 2.0 * odd)


def slab_kernel(
    side, local_bits, list_length, particles, cap, offset, first, last,
    totals_ref, defocus_ref, phase_ref, scale_ref, index_ref, core_ref,
    word_ref, voxel_ref, image_ref, forward_ref, backward_ref, *rest,
):
    if not first:
        rest = rest[1:]
    square_ref, sum_ref, out_refs, (staged_ref, steps_ref, sems) = rest[0], rest[1], rest[2:-3], rest[-3:]
    slabs, _, tile = word_ref.shape
    step = staged_ref.shape[0] // PAIR
    steps_each = tile // step
    blocks = sum_ref.shape[0] - 8
    features = image_ref.shape[2]
    kinds = forward_ref.shape[1] // features
    position_bits = bits_of(list_length)
    per_row = side // 8
    half = features // 2

    if first:
        @pl.loop(0, blocks // 256)
        def _(i):
            at = pl.multiple_of(i * 256, 256)
            sum_ref[pl.ds(at, 256), :] = jnp.zeros((256, features), jnp.float32)

    square_ref[...] = jnp.zeros_like(square_ref)
    live_of = lambda source: jnp.clip(totals_ref[source] - offset, 0, tile)

    def list_source(source, count):
        def list_step(i, count):
            steps_ref[count] = source * steps_each + i
            return count + 1

        return lax.fori_loop(0, (live_of(source) + step - 1) // step, list_step, count)

    steps_ref[0] = 0
    count = lax.fori_loop(0, slabs, list_source, 0)

    def compare(number, slot):
        which_step = steps_ref[jnp.minimum(number, jnp.maximum(count - 1, 0))]
        source, at = which_step // steps_each, (which_step % steps_each) * step
        at = pl.multiple_of(at, step)
        live = jnp.where(number < count, live_of(source) - at, 0)
        word = word_ref[source, :, pl.ds(at, step)]
        kind = (word >> local_bits) & 3
        position = (word >> (local_bits + 2)) & (list_length - 1)
        particle = (word >> (local_bits + 2 + position_bits)) & (particles - 1)
        valid = lax.broadcasted_iota(jnp.int32, (1, step), 1) < live
        defocus = jnp.zeros((1, step), jnp.float32)
        phase = jnp.zeros((1, step), jnp.float32)
        scale = jnp.zeros((1, step), jnp.float32)
        for j in range(particles):
            chosen = particle == j
            defocus = jnp.where(chosen, defocus_ref[source * particles + j], defocus)
            phase = jnp.where(chosen, phase_ref[source * particles + j], phase)
            scale = jnp.where(chosen, scale_ref[source * particles + j], scale)
        defocus = defocus * (1.0 / float((side // 2) ** 2))
        cell = lax.broadcasted_iota(jnp.int32, (half, LANES), 0)
        cell_vert, cell_horiz = (cell // 8).astype(jnp.float32), (cell % 8).astype(jnp.float32)
        repeat = lambda table: jnp.concatenate([table] * (step // LANES), axis=1)
        vert = ((position // per_row) * 8 - side // 2).astype(jnp.float32) + repeat(cell_vert)
        horiz = ((position % per_row) * 8 - side // 2).astype(jnp.float32) + repeat(cell_horiz)
        factor = scale * sine(defocus * (vert * vert + horiz * horiz) + phase)
        factor = jnp.concatenate([factor, factor], axis=0)
        voxel = voxel_ref[source, pl.ds(at, step), :].astype(jnp.float32).T.astype(jnp.bfloat16)
        picture = image_ref[source, pl.ds(at, step), :].astype(jnp.float32).T

        def by_kind(value):
            none = jnp.zeros_like(value)
            return jnp.concatenate([jnp.where(kind == k, value, none) for k in range(kinds)], axis=0)

        extracted = jnp.dot(forward_ref[...], by_kind(voxel), preferred_element_type=jnp.float32)
        misfit = jnp.where(valid, factor * extracted - picture, 0.0)
        squares = jnp.sum(misfit * misfit, axis=0, keepdims=True)
        which = lax.broadcasted_iota(jnp.int32, (particles, step), 0)
        spread = jnp.where(valid & (particle == which), squares, 0.0)
        folded = spread[:, 0:LANES]
        for i in range(1, step // LANES):
            folded = folded + spread[:, i * LANES:(i + 1) * LANES]
        square_ref[source] = square_ref[source] + folded
        weighted = (factor * misfit).astype(jnp.bfloat16)
        terms = jnp.dot(backward_ref[...], by_kind(weighted), preferred_element_type=jnp.float32)
        staged_ref[slot * step:(slot + 1) * step, :] = terms.T

    def places_of(base):
        return [index_ref[base] & 0xFFFFFF] + [index_ref[base + j] for j in range(1, GROUP)]

    def add_group(base, at):
        places = places_of(base)
        held = [sum_ref[pl.ds(place, 1), :] for place in places]
        new = [staged_ref[pl.ds(at + j, 1), :] for j in range(GROUP)]
        for j in range(GROUP):
            sum_ref[pl.ds(places[j], 1), :] = held[j] + new[j]

    def base_of(number):
        earlier = steps_ref[jnp.clip(number, 0, jnp.maximum(count - 1, 0))]
        base = (earlier // steps_each) * cap + offset + (earlier % steps_each) * step
        return jnp.where((number >= 0) & (number < count), base, slabs * cap)

    @pl.loop(0, (count + PAIR - 1) // PAIR + 1)
    def _(turn):
        bases = [base_of((turn - 1) * PAIR + slot) for slot in range(PAIR)]
        marks = 0
        for base in bases:
            for i in range(step // LANES):
                marks = marks | index_ref[base + i * LANES]

        @pl.when(marks < (1 << 25))
        def _():
            for slot, base in enumerate(bases):
                for g in range(step // GROUP):
                    add_group(base + g * GROUP, slot * step + g * GROUP)
            for slot in range(PAIR):
                compare(turn * PAIR + slot, slot)

        @pl.when(marks >= (1 << 25))
        def _():
            for slot, base in enumerate(bases):
                @pl.loop(0, step // GROUP)
                def _(g, slot=slot, base=base):
                    start = base + g * GROUP
                    at = slot * step + g * GROUP
                    clashes = (index_ref[start] >> 24) & 1

                    @pl.when(clashes == 0)
                    def _():
                        add_group(start, at)

                    @pl.when(clashes == 1)
                    def _():
                        places = places_of(start)
                        for j in range(GROUP):
                            sum_ref[pl.ds(places[j], 1), :] = (
                                sum_ref[pl.ds(places[j], 1), :] + staged_ref[pl.ds(at + j, 1), :]
                            )

            for slot in range(PAIR):
                compare(turn * PAIR + slot, slot)

    if last:
        half = blocks // 2
        start = (1 - core_ref[0]) * half
        places = [core_ref[0] * half]
        for out_ref in out_refs[1:]:
            places.append(start)
            start = start + out_ref.shape[0]
        copies = []
        for i, (place, out_ref) in enumerate(zip(places, out_refs)):
            length = out_ref.shape[0]
            at = pl.multiple_of(place, 8)
            copies.append(pltpu.make_async_copy(sum_ref.at[pl.ds(at, length)], out_ref, sems.at[i]))
        for copy in copies:
            copy.start()
        for copy in copies:
            copy.wait()


def pieces_of(planes):
    if planes < 16:
        return [planes]
    return [4, planes - 4]


def rotated(value, turn, length, sign=None):
    real, imag = value
    if turn == 0 or 4 * turn == length:
        if turn:
            real, imag = -imag, real
        return (real, imag) if sign is None else (real * sign, imag * sign)
    if sign is None and 8 * turn in (length, 3 * length):
        root = math.sqrt(0.5)
        if 8 * turn == length:
            return ((real - imag) * root, (real + imag) * root)
        return ((real + imag) * -root, (real - imag) * root)
    cos, sin = math.cos(2 * math.pi * turn / length), math.sin(2 * math.pi * turn / length)
    if sign is not None:
        cos, sin = cos * sign, sin * sign
    return (real * cos - imag * sin, real * sin + imag * cos)


def small_dft(values):
    length = len(values)
    if length == 1:
        return values
    even, odd = small_dft(values[0::2]), small_dft(values[1::2])
    low, high = [], []
    for k in range(length // 2):
        turned = rotated(odd[k], k, length)
        low.append((even[k][0] + turned[0], even[k][1] + turned[1]))
        high.append((even[k][0] - turned[0], even[k][1] - turned[1]))
    return low + high


def swap_quarters(values):
    lane = lax.broadcasted_iota(jnp.int32, values[0].shape, 1)
    low, even = lane < 64, (lane // 32) % 2 == 0
    roll = lambda value, shift: pltpu.roll(value, shift, 1)
    for first, second, shift, keep in ((0, 2, 64, low), (1, 3, 64, low), (0, 1, 32, even), (2, 3, 32, even)):
        one, two = values[first], values[second]
        values[first] = jnp.where(keep, one, roll(two, shift))
        values[second] = jnp.where(keep, roll(one, LANES - shift), two)
    return values


def in_halves(value):
    high = value.astype(jnp.bfloat16)
    return high, (value - high.astype(jnp.float32)).astype(jnp.bfloat16)


def planes_kernel(mine_ref, theirs_ref, zblock_ref, turn_ref, wide_ref, fine_ref, out_ref, high_ref, low_ref):
    step = pl.program_id(1)
    count = mine_ref.shape[1]
    groups, side = out_ref.shape[0], out_ref.shape[4]
    height = side // groups

    @pl.loop(0, count, unroll=8)
    def _(i):
        block = (mine_ref[:, i] + theirs_ref[:, i]).reshape(LANES, LANES)
        high, low = in_halves(block.T)
        both = jnp.dot(
            jnp.concatenate([high, low, high], axis=1), zblock_ref[...],
            preferred_element_type=jnp.float32,
        )
        by_cos = both[:, :LANES].reshape(8, 2, 8, LANES)
        by_sin = both[:, LANES:].reshape(8, 2, 8, LANES)
        real = by_cos[:, 0] - by_sin[:, 1]
        imag = by_sin[:, 0] + by_cos[:, 1]
        values = []
        for z in range(8):
            cos, sin = turn_ref[0, z:z + 1, :], turn_ref[1, z:z + 1, :]
            values.append((real[z] * cos - imag[z] * sin, real[z] * sin + imag[z] * cos))
        values = [jnp.concatenate(value, axis=0) for value in small_dft(values)]
        at = pl.ds(pl.multiple_of((step * count + i) * 16, 16), 16)
        for half in range(2):
            planes = swap_quarters(values[4 * half:4 * half + 4])
            for x in range(4):
                columns = slice((2 * x + half) * LANES, (2 * x + half + 1) * LANES)
                high, low = in_halves(planes[x])
                high_ref[at, columns] = high
                low_ref[at, columns] = low

    @pl.when(step == pl.num_programs(1) - 1)
    def _():
        @pl.loop(0, 4)
        def _(x):
            columns = pl.ds(pl.multiple_of(x * side, side), side)
            product = functools.partial(jnp.dot, preferred_element_type=jnp.float32)
            high = high_ref[:, columns]
            result = product(wide_ref[...], high) + (
                product(wide_ref[...], low_ref[:, columns]) + product(fine_ref[...], high)
            )
            for part in range(2):
                for group in range(groups):
                    start = part * side + group * height
                    out_ref[group, x, part] = result[start:start + height, :].astype(jnp.bfloat16)


def first_dimension_kernel(slabs, each, core_ref, *refs):
    arrays, (out_ref, mid_ref) = refs[:-2], refs[-2:]
    chunks = len(arrays) // 2
    own, other = arrays[:chunks], arrays[chunks:]
    spots = [(i, at) for i, ref in enumerate(own) for at in range(ref.shape[1])]
    core = core_ref[0]
    is_first = core == 0
    sign = (1 - 2 * core).astype(jnp.float32)

    rows = out_ref.shape[2]
    strips = [slice(at, min(at + 8, rows)) for at in range(0, rows, 8)]

    def plane(x, strip):
        slab, rest = x // (2 * each), x % (2 * each)
        half, inner = rest // each, rest % each
        chunk, at = spots[inner]
        loaded = []
        for part in range(2):
            here, there = own[chunk][slab, at, part], other[chunk][slab, at, part]
            value = jnp.where(is_first, here, there) if half == 0 else jnp.where(is_first, there, here)
            loaded.append(value.astype(jnp.float32)[strip])
        return tuple(loaded)

    for low in range(16):
        for strip in strips:
            values = small_dft([plane(low + 16 * high, strip) for high in range(16)])
            for k in range(16):
                real, imag = rotated(values[k], low * k, 256, sign if low % 2 else None)
                mid_ref[k, low, 0, strip] = real
                mid_ref[k, low, 1, strip] = imag

    @pl.loop(0, 16)
    def _(k):
        for strip in strips:
            values = [(mid_ref[k, low, 0, strip], mid_ref[k, low, 1, strip]) for low in range(16)]
            even, odd = small_dft(values[0::2]), small_dft(values[1::2])
            for m in range(8):
                turned = rotated(odd[m], m, 16)
                out_ref[0, k + 16 * m, strip] = even[m][0] + turned[0]
                out_ref[1, k + 16 * m, strip] = even[m][1] + turned[1]


def host_halves(table):
    high = table.astype(jnp.bfloat16)
    return high, (table - high.astype(np.float64)).astype(jnp.bfloat16)


def transform_tables(side):
    per_row = side // 8
    grid = np.arange(per_row)
    angle = 2 * np.pi * np.outer(grid, grid) / per_row
    zblock = np.concatenate([np.kron(np.eye(4), np.cos(angle)), np.kron(np.eye(4), np.sin(angle))], axis=1)
    high, low = host_halves(zblock)
    zblock = np.concatenate([high, high, low], axis=0)
    angle = 2 * np.pi * np.outer(np.arange(8), grid) / side
    turns = np.stack([np.tile(np.cos(angle), (1, 4)), np.tile(np.sin(angle), (1, 4))]).astype(np.float32)
    cells = np.arange(side)
    angle = 2 * np.pi * (np.outer(cells, cells) % side) / side
    cos, sin = np.cos(angle).reshape(side, per_row, 1, 8), np.sin(angle).reshape(side, per_row, 1, 8)
    matrix = np.concatenate(
        [np.concatenate([cos, -sin], axis=2), np.concatenate([sin, cos], axis=2)], axis=0
    ).reshape(2 * side, 2 * side) / float(side) ** 1.5
    return (zblock, turns) + host_halves(matrix)


def sum_over_slabs(partial_sums):
    slabs = partial_sums.shape[0]
    if slabs <= 8:
        me = lax.axis_index("slab")
        row = lambda i: lax.dynamic_index_in_dim(partial_sums, me ^ i, axis=0, keepdims=True)
        returned = [row(0)] + [
            lax.ppermute(row(i), "slab", [(slab, slab ^ i) for slab in range(slabs)])
            for i in range(1, slabs)
        ]
        returned = jnp.concatenate(returned)
    else:
        returned = lax.all_to_all(partial_sums, "slab", split_axis=0, concat_axis=0, tiled=True)
    return jnp.sum(returned, axis=0)


def to_field(mine, theirs_sent, partial_sums, side):
    slabs = lax.axis_size("slab")
    per_row = side // 8
    each = side // slabs // 2
    height = side // slabs
    groups = slabs if height % 16 == 0 else 1
    tables = [jnp.asarray(table) for table in transform_tables(side)]
    swap = [(0, 1), (1, 0)]
    theirs = [lax.ppermute(chunk, "dom", swap) for chunk in theirs_sent]
    grid_shape = (-1, per_row, per_row, LANES)
    mine = mine.reshape(grid_shape)
    short = max(0, 4 - each)
    if short:
        mine = jnp.pad(mine, ((0, short), (0, 0), (0, 0), (0, 0)))
    yblocks = 8
    own = []
    first_quad = 0
    before = []
    for real_planes, added in zip(pieces_of(each), theirs):
        if before:
            added, before[0] = lax.optimization_barrier((added, before[0]))
        added = added.reshape(grid_shape)
        if short:
            added = jnp.pad(added, ((0, short), (0, 0), (0, 0), (0, 0)))
        held = real_planes + short
        quads = held // 4
        whole = lambda table: pl.BlockSpec(table.shape, lambda q, y: (0,) * table.ndim)
        sent = pl.pallas_call(
            planes_kernel,
            grid=(quads, per_row // yblocks),
            out_shape=jax.ShapeDtypeStruct((groups, held, 2, side // groups, side), jnp.bfloat16),
            in_specs=[
                pl.BlockSpec((4, yblocks, per_row, LANES), lambda q, y, at=first_quad: (at + q, y, 0, 0)),
                pl.BlockSpec((4, yblocks, per_row, LANES), lambda q, y: (q, y, 0, 0)),
            ] + [whole(table) for table in tables],
            out_specs=pl.BlockSpec((groups, 4, 2, side // groups, side), lambda q, y: (0, q, 0, 0, 0)),
            scratch_shapes=[
                pltpu.VMEM((2 * side, 4 * side), jnp.bfloat16),
                pltpu.VMEM((2 * side, 4 * side), jnp.bfloat16),
            ],
            compiler_params=params(56),
            cost_estimate=pl.CostEstimate(
                flops=held * 8 * side**3, bytes_accessed=held * 4 * side**2 * 8, transcendentals=0
            ),
            name="transform_planes",
        )(mine, added, *tables)
        if groups != slabs:
            sent = sent.reshape(-1, 2, slabs, height, side).transpose(2, 0, 1, 3, 4)[:, :real_planes]
        first_quad += quads
        if before:
            sent, own[-1] = lax.optimization_barrier((sent, own[-1]))
        if first_quad * 4 >= each:
            sent, partial_sums = lax.optimization_barrier((sent, partial_sums))
        before = [sent]
        got = lax.all_to_all(sent, "slab", split_axis=0, concat_axis=0, tiled=True)
        own.append(got)
    other = [lax.ppermute(got, "dom", swap) for got in own[:-1]]
    own[-1], losses, *other = lax.optimization_barrier((own[-1], sum_over_slabs(partial_sums), *other))
    other.append(lax.ppermute(own[-1], "dom", swap))
    rows = min(16, height)
    arrays = own + other
    field = pl.pallas_call(
        functools.partial(first_dimension_kernel, slabs, each),
        grid=(height // rows, side // LANES),
        out_shape=jax.ShapeDtypeStruct((2, side // 2, height, side), jnp.float32),
        in_specs=[SMEM_SPEC] + [
            pl.BlockSpec(array.shape[:3] + (rows, LANES), lambda y, z: (0, 0, 0, y, z))
            for array in arrays
        ],
        out_specs=pl.BlockSpec((2, side // 2, rows, LANES), lambda y, z: (0, 0, y, z)),
        scratch_shapes=[pltpu.VMEM((16, 16, 2, rows, LANES), jnp.float32)],
        compiler_params=params(28),
        name="transform_first",
    )(lax.axis_index("dom").astype(jnp.int32).reshape(1), *arrays)
    return field, losses


def gradient_of_slab(volume, kernels, images, owners, local_block, kinds, counts, ctf_code, ctf_table, scales):
    slabs = lax.axis_size("slab")
    particles, list_length, features = images.shape
    side = math.isqrt(list_length * 64)
    entries = particles * list_length
    cap = 2 * entries // slabs
    slots = slabs * cap
    blocks = volume.shape[0]
    local_bits = bits_of(blocks)
    kind_count = kernels.shape[0]
    rows = entries // LANES
    int_rows = jax.ShapeDtypeStruct((rows, LANES), jnp.int32)

    target, word, totals = pl.pallas_call(
        functools.partial(route_kernel, slabs, cap, local_bits),
        out_shape=(int_rows, int_rows, jax.ShapeDtypeStruct((slabs, LANES), jnp.int32)),
        in_specs=[VMEM_SPEC, VMEM_SPEC, VMEM_SPEC, SMEM_SPEC],
        out_specs=(VMEM_SPEC, VMEM_SPEC, VMEM_SPEC),
        compiler_params=params(56),
        name="route",
    )(owners.reshape(rows, LANES), local_block, kinds, counts)
    target, word = target.reshape(entries), word.reshape(entries)
    tiles = [cap // 2, cap // 2] if cap >= 2048 else [cap]
    parts = len(tiles)
    code = ctf_code | ((scales.astype(jnp.float32) * 256.0).astype(jnp.int32) << 8)
    stride = cap + LANES
    meta, *packed = pl.pallas_call(
        functools.partial(pack_kernel, slabs, cap, list_length),
        out_shape=(jax.ShapeDtypeStruct((slabs * stride,), jnp.int32),)
        + tuple(jax.ShapeDtypeStruct((slabs, tile, features), jnp.bfloat16) for tile in tiles),
        in_specs=[SMEM_SPEC] * 5 + [VMEM_SPEC],
        out_specs=(SMEM_SPEC,) + (ANY_SPEC,) * parts,
        scratch_shapes=[
            pltpu.VMEM((entries, features), jnp.float32),
            pltpu.VMEM((slabs * stride, features), jnp.float32),
            pltpu.VMEM((slots, features), jnp.bfloat16),
            pltpu.SemaphoreType.DMA(()),
        ],
        compiler_params=params(56),
        name="pack",
    )(target, word, counts, totals, code, images.reshape(entries, features))
    arrived = lax.all_to_all(
        meta.reshape(slabs, stride), "slab", split_axis=0, concat_axis=0, tiled=True
    )
    words = arrived[:, :cap]
    totals_in = arrived[:, cap]
    codes_in = arrived[:, cap + 1:cap + 1 + particles]
    live = (jnp.arange(cap, dtype=jnp.int32)[None, :] < totals_in[:, None]).astype(jnp.int32)
    table_rows = ctf_table[(codes_in & 255).reshape(-1)]
    scale_in = (codes_in >> 8).astype(jnp.float32).reshape(-1) * (1.0 / 256.0)

    index = pl.pallas_call(
        functools.partial(decode_kernel, local_bits, blocks),
        out_shape=jax.ShapeDtypeStruct((slots // LANES + 8, LANES), jnp.int32),
        in_specs=[VMEM_SPEC, VMEM_SPEC],
        out_specs=VMEM_SPEC,
        compiler_params=params(56),
        name="decode",
    )(words.reshape(slots // LANES, LANES), live.reshape(slots // LANES, LANES))
    index = index.reshape(slots + 8 * LANES)
    voxels = list(pl.pallas_call(
        functools.partial(gather_kernel, slabs, cap),
        out_shape=tuple(
            jax.ShapeDtypeStruct((slabs, tile, features), jnp.bfloat16) for tile in tiles
        ),
        in_specs=[SMEM_SPEC, SMEM_SPEC, VMEM_SPEC],
        out_specs=(VMEM_SPEC,) * parts,
        scratch_shapes=[
            pltpu.VMEM((blocks + 8, features), jnp.float32),
            pltpu.VMEM((cap, features), jnp.float32),
        ],
        compiler_params=params(56),
        cost_estimate=pl.CostEstimate(flops=0, bytes_accessed=100 * MIB, transcendentals=0),
        name="read_voxels",
    )(index, totals_in, volume))

    forward = jnp.transpose(kernels, (2, 0, 1)).reshape(features, kind_count * features)
    backward = kernels.reshape(kind_count, 2, 8, 8, features).transpose(3, 1, 2, 0, 4)
    backward = backward.reshape(features, kind_count * features)
    core = lax.axis_index("dom").astype(jnp.int32).reshape(1)
    plane_blocks = (side // 8) ** 2
    pieces = [planes * plane_blocks for planes in pieces_of(side // slabs // 2)]
    squares, sums, behind, offset = 0.0, None, [voxels[0]], 0
    for part, tile in enumerate(tiles):
        first, last = part == 0, part == parts - 1
        if not first:
            packed[part], earlier = lax.optimization_barrier((packed[part], behind[part - 1]))
            if part == 1:
                voxels[0] = earlier
        picture = lax.all_to_all(packed[part], "slab", split_axis=0, concat_axis=0, tiled=True)
        lengths = [blocks // 2] + pieces if last else []
        arguments = [
            totals_in, table_rows[:, 0], table_rows[:, 1], scale_in, index, core,
            words[:, offset:offset + tile].reshape(slabs, 1, tile), voxels[part], picture,
            forward, backward,
        ]
        aliases = {}
        if not first:
            aliases = {len(arguments): 1}
            arguments.append(pltpu.with_memory_space_constraint(sums, pltpu.VMEM))
        more, sums, *halves = pl.pallas_call(
            functools.partial(
                slab_kernel, side, local_bits, list_length, particles, cap, offset, first, last
            ),
            out_shape=(
                jax.ShapeDtypeStruct((slabs, particles, LANES), jnp.float32),
                pltpu.VMEM((blocks + 8, features), jnp.float32),
            )
            + tuple(jax.ShapeDtypeStruct((length, features), jnp.float32) for length in lengths),
            in_specs=[SMEM_SPEC] * 6 + [VMEM_SPEC] * (len(arguments) - 6),
            out_specs=(VMEM_SPEC, VMEM_SPEC) + (ANY_SPEC,) * len(lengths),
            scratch_shapes=[
                pltpu.VMEM((PAIR * min(tile, STEP), features), jnp.float32),
                pltpu.SMEM((slabs * tile // min(tile, STEP) + 1,), jnp.int32),
                pltpu.SemaphoreType.DMA((max(1, len(lengths)),)),
            ],
            input_output_aliases=aliases,
            compiler_params=params(24),
            cost_estimate=pl.CostEstimate(flops=0, bytes_accessed=16 * MIB, transcendentals=0),
            name="compare_and_add",
        )(*arguments)
        squares = squares + more
        behind.append(more)
        offset += tile
    mine, *theirs = halves
    partial_sums = jnp.sum(squares, axis=2)
    return mine, theirs, partial_sums, side


def body(*arrays):
    mine, theirs, partial_sums, side = gradient_of_slab(*arrays)
    field, squares = to_field(mine, theirs, partial_sums, side)
    counts = arrays[6]
    return field, squares / (counts.astype(jnp.float32) * 128.0)


def solution(mesh):
    in_specs = (
        P(("groups", "slab"), None),
        P(),
        P(("groups", "slab", "dom"), None, None),
        P(("groups", "slab", "dom"), None, None),
        P(("groups", "slab", "dom"), None),
        P(("groups", "slab", "dom"), None),
        P(("groups", "slab", "dom")),
        P(("groups", "slab", "dom")),
        P(),
        P(("groups", "slab", "dom")),
    )
    out_specs = (P(None, ("groups", "dom"), "slab", None), P(("groups", "slab", "dom")))
    return jax.shard_map(body, mesh=mesh, in_specs=in_specs, out_specs=out_specs, check_vma=False)
```

```python
import functools
import math

import jax
import jax.numpy as jnp
import numpy as np
from jax import lax
from jax.experimental import pallas as pl
from jax.experimental.pallas import tpu as pltpu
from jax.sharding import PartitionSpec as P

LANES = 128
GROUP = 16
UNUSED = 100
STEP = 256
PAIR = 1
MIB = 1024 * 1024

SMEM_SPEC = pl.BlockSpec(memory_space=pltpu.SMEM)
VMEM_SPEC = pl.BlockSpec(memory_space=pltpu.VMEM)
ANY_SPEC = pl.BlockSpec(memory_space=pl.ANY)


def params(mib):
    return pltpu.CompilerParams(vmem_limit_bytes=mib * MIB)


def bits_of(count):
    return (count - 1).bit_length()


def route_kernel(slabs, cap, local_bits, owner_ref, local_ref, kind_ref, counts_ref, target_ref, word_ref, totals_ref):
    particles, list_length = local_ref.shape
    rows_each = list_length // LANES
    rows = particles * rows_each
    gathered = lambda ref: jnp.concatenate(
        [ref[:, j * LANES:(j + 1) * LANES] for j in range(rows_each)], axis=0
    )
    row_id = lax.broadcasted_iota(jnp.int32, (rows, LANES), 0)
    lane_id = lax.broadcasted_iota(jnp.int32, (rows, LANES), 1)
    particle = row_id % particles
    position = (row_id // particles) * LANES + lane_id
    limit = jnp.zeros((rows, LANES), jnp.int32)
    for i in range(particles):
        limit = jnp.where(particle == i, counts_ref[i], limit)
    owner = jnp.concatenate(
        [owner_ref[pl.ds(j, particles, stride=rows_each), :] for j in range(rows_each)], axis=0
    )
    owner = jnp.where(position < limit, owner, -1)
    up_to = (
        lax.broadcasted_iota(jnp.int32, (LANES, LANES), 0)
        <= lax.broadcasted_iota(jnp.int32, (LANES, LANES), 1)
    ).astype(jnp.bfloat16)
    ones = jnp.ones((LANES, LANES), jnp.bfloat16)
    before = (
        lax.broadcasted_iota(jnp.int32, (rows, rows), 1)
        < lax.broadcasted_iota(jnp.int32, (rows, rows), 0)
    ).astype(jnp.bfloat16)

    def one_slab(slab, target):
        mine = owner == slab
        hits = mine.astype(jnp.float32).astype(jnp.bfloat16)
        inside = jnp.dot(hits, up_to, preferred_element_type=jnp.float32)
        row_sum = jnp.dot(hits, ones, preferred_element_type=jnp.float32)
        above = jnp.dot(before, row_sum.astype(jnp.bfloat16), preferred_element_type=jnp.float32)
        rank = (inside + above).astype(jnp.int32) - 1
        total = (above[rows - 1:rows, :] + row_sum[rows - 1:rows, :]).astype(jnp.int32)
        totals_ref[pl.ds(slab, 1), :] = total
        return jnp.where(mine, slab * (cap + LANES) + rank, target)

    target = lax.fori_loop(0, slabs, one_slab, jnp.full((rows, LANES), cap + UNUSED, jnp.int32))
    target_ref[...] = target
    kind_bits = local_bits
    word = gathered(local_ref) | (gathered(kind_ref) << kind_bits) | (position << (kind_bits + 2))
    word_ref[...] = word | (particle << (kind_bits + 2 + bits_of(list_length)))


def pack_kernel(slabs, cap, list_length, target_ref, word_ref, counts_ref, totals_ref, code_ref, image_ref, meta_ref, *refs):
    out_refs, (wide_ref, staged_ref, narrow_ref, sem) = refs[:-4], refs[-4:]
    particles = counts_ref.shape[0]
    stride = cap + LANES
    step = 256
    turn = 32

    @pl.loop(0, image_ref.shape[0] // step)
    def _(i):
        at = pl.multiple_of(i * step, step)
        wide_ref[pl.ds(at, step), :] = image_ref[pl.ds(at, step), :].astype(jnp.float32)

    @pl.loop(0, particles)
    def _(particle):
        @pl.loop(0, (counts_ref[particle] + turn - 1) // turn)
        def _(i):
            per_row = LANES // turn
            first = (i // per_row) * (particles * LANES) + particle * LANES + (i % per_row) * turn
            row = particle * list_length + i * turn
            targets = [target_ref[first + j] for j in range(turn)]
            words = [word_ref[first + j] for j in range(turn)]
            rows = [wide_ref[pl.ds(row + j, 1), :] for j in range(turn)]
            for j in range(turn):
                staged_ref[pl.ds(targets[j], 1), :] = rows[j]
                meta_ref[targets[j]] = words[j]

    @pl.loop(0, slabs)
    def _(slab):
        header = slab * stride + cap
        meta_ref[header] = totals_ref[slab, 0]
        for j in range(particles):
            meta_ref[header + 1 + j] = code_ref[j]

    def blocks_of(act):
        offset = 0
        for out_ref in out_refs:
            width = out_ref.shape[1]

            @pl.loop(0, slabs)
            def _(slab, offset=offset, width=width, out_ref=out_ref):
                live = jnp.clip(totals_ref[slab, 0] - offset, 0, width)

                @pl.loop(0, (live + LANES - 1) // LANES)
                def _(i):
                    at = pl.multiple_of(slab * cap + offset + i * LANES, LANES)
                    to = pl.multiple_of(i * LANES, LANES)
                    copy = pltpu.make_async_copy(
                        narrow_ref.at[pl.ds(at, LANES)], out_ref.at[slab, pl.ds(to, LANES)], sem
                    )
                    act(copy, at, pl.multiple_of(at + slab * LANES, LANES))

            offset += width

    def convert_and_start(copy, at, staged_at):
        narrow_ref[pl.ds(at, LANES), :] = staged_ref[pl.ds(staged_at, LANES), :].astype(jnp.bfloat16)
        copy.start()

    blocks_of(convert_and_start)
    blocks_of(lambda copy, at, staged_at: copy.wait())


def decode_kernel(local_bits, dummy, word_ref, live_ref, index_ref):
    rows = word_ref.shape[0]
    live = live_ref[...] != 0
    index = jnp.where(live, word_ref[...] & ((1 << local_bits) - 1), dummy)
    lane = lax.broadcasted_iota(jnp.int32, (rows, LANES), 1)
    clash = jnp.zeros((rows, LANES), jnp.int32)
    for shift in range(1, GROUP):
        earlier = pltpu.roll(index, shift, 1)
        same = (earlier == index) & (lane % GROUP >= shift) & live
        clash = clash | same.astype(jnp.int32)
    shift = 1
    while shift < LANES:
        if shift == GROUP:
            index = index | jnp.where(lane % GROUP == 0, clash << 24, 0)
        clash = clash | pltpu.roll(clash, LANES - shift, 1)
        shift *= 2
    index_ref[0:rows, :] = index | jnp.where(lane == 0, clash << 25, 0)
    index_ref[rows:, :] = jnp.full((index_ref.shape[0] - rows, LANES), dummy, jnp.int32)


def gather_kernel(slabs, cap, index_ref, totals_ref, volume_ref, *refs):
    out_refs, (wide_ref, staged_ref) = refs[:-2], refs[-2:]
    blocks = volume_ref.shape[0]
    step = 256

    @pl.loop(0, blocks // step)
    def _(i):
        at = pl.multiple_of(i * step, step)
        wide_ref[pl.ds(at, step), :] = volume_ref[pl.ds(at, step), :].astype(jnp.float32)

    @pl.loop(0, slabs)
    def _(source):
        live = totals_ref[source]

        @pl.loop(0, (live + 15) // 16)
        def _(i):
            first = source * cap + i * 16
            places = [index_ref[first] & 0xFFFFFF] + [index_ref[first + j] for j in range(1, 16)]
            rows = [wide_ref[pl.ds(places[j], 1), :] for j in range(16)]
            for j in range(16):
                staged_ref[pl.ds(i * 16 + j, 1), :] = rows[j]

        offset = 0
        for out_ref in out_refs:
            width = out_ref.shape[1]

            @pl.when(live > offset)
            def _(offset=offset):
                out_ref[source] = staged_ref[offset:offset + width, :].astype(jnp.bfloat16)

            offset += width


def sine(angle):
    turns = jnp.floor(angle * (1.0 / math.pi) + 0.5)
    rest = angle - turns * 3.140625
    rest = rest - turns * (math.pi - 3.140625)
    odd = turns - 2.0 * jnp.floor(turns * 0.5)
    square = rest * rest
    poly = 2.718121e-6
    poly = poly * square - 1.9839334e-4
    poly = poly * square + 8.3333293e-3
    poly = poly * square - 1.6666667e-1
    value = rest + rest * square * poly
    return value * (1.0 - 2.0 * odd)


def slab_kernel(
    side, local_bits, list_length, particles, cap, offset, first, last,
    totals_ref, defocus_ref, phase_ref, scale_ref, index_ref, core_ref,
    word_ref, voxel_ref, image_ref, forward_ref, backward_ref, *rest,
):
    if not first:
        rest = rest[1:]
    square_ref, sum_ref, out_refs, (staged_ref, zero_ref, steps_ref, sems) = rest[0], rest[1], rest[2:-4], rest[-4:]
    slabs, _, tile = word_ref.shape
    step = staged_ref.shape[0] // PAIR
    steps_each = tile // step
    blocks = sum_ref.shape[0] - 8
    features = image_ref.shape[2]
    kinds = forward_ref.shape[1] // features
    position_bits = bits_of(list_length)
    per_row = side // 8
    half = features // 2

    if first:
        zero_ref[...] = jnp.zeros_like(zero_ref)
        length = zero_ref.shape[0]
        clear = lambda i: pltpu.make_async_copy(
            zero_ref, sum_ref.at[pl.ds(pl.multiple_of(i * length, length), length)], sems.at[0]
        )

        @pl.loop(0, blocks // length)
        def _(i):
            clear(i).start()

        @pl.loop(0, blocks // length)
        def _(i):
            clear(i).wait()

    square_ref[...] = jnp.zeros_like(square_ref)
    live_of = lambda source: jnp.clip(totals_ref[source] - offset, 0, tile)

    def list_source(source, count):
        def list_step(i, count):
            steps_ref[count] = source * steps_each + i
            return count + 1

        return lax.fori_loop(0, (live_of(source) + step - 1) // step, list_step, count)

    steps_ref[0] = 0
    count = lax.fori_loop(0, slabs, list_source, 0)

    def compare(number, slot):
        which_step = steps_ref[jnp.minimum(number, jnp.maximum(count - 1, 0))]
        source, at = which_step // steps_each, (which_step % steps_each) * step
        at = pl.multiple_of(at, step)
        live = jnp.where(number < count, live_of(source) - at, 0)
        word = word_ref[source, :, pl.ds(at, step)]
        kind = (word >> local_bits) & 3
        position = (word >> (local_bits + 2)) & (list_length - 1)
        particle = (word >> (local_bits + 2 + position_bits)) & (particles - 1)
        valid = lax.broadcasted_iota(jnp.int32, (1, step), 1) < live
        defocus = jnp.zeros((1, step), jnp.float32)
        phase = jnp.zeros((1, step), jnp.float32)
        scale = jnp.zeros((1, step), jnp.float32)
        for j in range(particles):
            chosen = particle == j
            defocus = jnp.where(chosen, defocus_ref[source * particles + j], defocus)
            phase = jnp.where(chosen, phase_ref[source * particles + j], phase)
            scale = jnp.where(chosen, scale_ref[source * particles + j], scale)
        defocus = defocus * (1.0 / float((side // 2) ** 2))
        cell = lax.broadcasted_iota(jnp.int32, (half, LANES), 0)
        cell_vert, cell_horiz = (cell // 8).astype(jnp.float32), (cell % 8).astype(jnp.float32)
        repeat = lambda table: jnp.concatenate([table] * (step // LANES), axis=1)
        vert = ((position // per_row) * 8 - side // 2).astype(jnp.float32) + repeat(cell_vert)
        horiz = ((position % per_row) * 8 - side // 2).astype(jnp.float32) + repeat(cell_horiz)
        factor = scale * sine(defocus * (vert * vert + horiz * horiz) + phase)
        factor = jnp.concatenate([factor, factor], axis=0)
        voxel = voxel_ref[source, pl.ds(at, step), :].astype(jnp.float32).T.astype(jnp.bfloat16)
        picture = image_ref[source, pl.ds(at, step), :].astype(jnp.float32).T

        def by_kind(value):
            none = jnp.zeros_like(value)
            return jnp.concatenate([jnp.where(kind == k, value, none) for k in range(kinds)], axis=0)

        extracted = jnp.dot(forward_ref[...], by_kind(voxel), preferred_element_type=jnp.float32)
        misfit = jnp.where(valid, factor * extracted - picture, 0.0)
        squares = jnp.sum(misfit * misfit, axis=0, keepdims=True)
        which = lax.broadcasted_iota(jnp.int32, (particles, step), 0)
        spread = jnp.where(valid & (particle == which), squares, 0.0)
        folded = spread[:, 0:LANES]
        for i in range(1, step // LANES):
            folded = folded + spread[:, i * LANES:(i + 1) * LANES]
        square_ref[source] = square_ref[source] + folded
        weighted = (factor * misfit).astype(jnp.bfloat16)
        terms = jnp.dot(backward_ref[...], by_kind(weighted), preferred_element_type=jnp.float32)
        staged_ref[slot * step:(slot + 1) * step, :] = terms.T

    def places_of(base):
        return [index_ref[base] & 0xFFFFFF] + [index_ref[base + j] for j in range(1, GROUP)]

    def add_group(base, at):
        places = places_of(base)
        held = [sum_ref[place] for place in places]
        new = [staged_ref[pl.ds(at + j, 1), :] for j in range(GROUP)]
        for j in range(GROUP):
            sum_ref[places[j]] = held[j] + new[j]

    def base_of(number):
        earlier = steps_ref[jnp.clip(number, 0, jnp.maximum(count - 1, 0))]
        base = (earlier // steps_each) * cap + offset + (earlier % steps_each) * step
        return jnp.where((number >= 0) & (number < count), base, slabs * cap)

    @pl.loop(0, (count + PAIR - 1) // PAIR + 1)
    def _(turn):
        bases = [base_of((turn - 1) * PAIR + slot) for slot in range(PAIR)]
        marks = 0
        for base in bases:
            for i in range(step // LANES):
                marks = marks | index_ref[base + i * LANES]

        @pl.when(marks < (1 << 25))
        def _():
            for slot, base in enumerate(bases):
                for g in range(step // GROUP):
                    add_group(base + g * GROUP, slot * step + g * GROUP)
            for slot in range(PAIR):
                compare(turn * PAIR + slot, slot)

        @pl.when(marks >= (1 << 25))
        def _():
            for slot, base in enumerate(bases):
                @pl.loop(0, step // GROUP)
                def _(g, slot=slot, base=base):
                    start = base + g * GROUP
                    at = slot * step + g * GROUP
                    clashes = (index_ref[start] >> 24) & 1

                    @pl.when(clashes == 0)
                    def _():
                        add_group(start, at)

                    @pl.when(clashes == 1)
                    def _():
                        places = places_of(start)
                        for j in range(GROUP):
                            sum_ref[places[j]] = sum_ref[places[j]] + staged_ref[pl.ds(at + j, 1), :]

            for slot in range(PAIR):
                compare(turn * PAIR + slot, slot)

    if last:
        half = blocks // 2
        start = (1 - core_ref[0]) * half
        places = [core_ref[0] * half]
        for out_ref in out_refs[1:]:
            places.append(start)
            start = start + out_ref.shape[0]
        copies = []
        for i, (place, out_ref) in enumerate(zip(places, out_refs)):
            length = out_ref.shape[0]
            at = pl.multiple_of(place, 8)
            copies.append(pltpu.make_async_copy(sum_ref.at[pl.ds(at, length)], out_ref, sems.at[i]))
        for copy in copies:
            copy.start()
        for copy in copies:
            copy.wait()


def pieces_of(planes):
    if planes < 16:
        return [planes]
    return [4, planes - 4]


def rotated(value, turn, length, sign=None):
    real, imag = value
    if turn == 0 or 4 * turn == length:
        if turn:
            real, imag = -imag, real
        return (real, imag) if sign is None else (real * sign, imag * sign)
    if sign is None and 8 * turn in (length, 3 * length):
        root = math.sqrt(0.5)
        if 8 * turn == length:
            return ((real - imag) * root, (real + imag) * root)
        return ((real + imag) * -root, (real - imag) * root)
    cos, sin = math.cos(2 * math.pi * turn / length), math.sin(2 * math.pi * turn / length)
    if sign is not None:
        cos, sin = cos * sign, sin * sign
    return (real * cos - imag * sin, real * sin + imag * cos)


def small_dft(values):
    length = len(values)
    if length == 1:
        return values
    even, odd = small_dft(values[0::2]), small_dft(values[1::2])
    low, high = [], []
    for k in range(length // 2):
        turned = rotated(odd[k], k, length)
        low.append((even[k][0] + turned[0], even[k][1] + turned[1]))
        high.append((even[k][0] - turned[0], even[k][1] - turned[1]))
    return low + high


def swap_quarters(values):
    lane = lax.broadcasted_iota(jnp.int32, values[0].shape, 1)
    low, even = lane < 64, (lane // 32) % 2 == 0
    roll = lambda value, shift: pltpu.roll(value, shift, 1)
    for first, second, shift, keep in ((0, 2, 64, low), (1, 3, 64, low), (0, 1, 32, even), (2, 3, 32, even)):
        one, two = values[first], values[second]
        values[first] = jnp.where(keep, one, roll(two, shift))
        values[second] = jnp.where(keep, roll(one, LANES - shift), two)
    return values


def in_halves(value):
    high = value.astype(jnp.bfloat16)
    return high, (value - high.astype(jnp.float32)).astype(jnp.bfloat16)


def planes_kernel(mine_ref, theirs_ref, zblock_ref, turn_ref, wide_ref, fine_ref, out_ref, high_ref, low_ref):
    step = pl.program_id(1)
    count = mine_ref.shape[1]
    groups, side = out_ref.shape[0], out_ref.shape[4]
    height = side // groups

    @pl.loop(0, count, unroll=8)
    def _(i):
        block = (mine_ref[:, i] + theirs_ref[:, i]).reshape(LANES, LANES)
        high, low = in_halves(block.T)
        both = jnp.dot(
            jnp.concatenate([high, low, high], axis=1), zblock_ref[...],
            preferred_element_type=jnp.float32,
        )
        by_cos = both[:, :LANES].reshape(8, 2, 8, LANES)
        by_sin = both[:, LANES:].reshape(8, 2, 8, LANES)
        real = by_cos[:, 0] - by_sin[:, 1]
        imag = by_sin[:, 0] + by_cos[:, 1]
        values = []
        for z in range(8):
            cos, sin = turn_ref[0, z:z + 1, :], turn_ref[1, z:z + 1, :]
            values.append((real[z] * cos - imag[z] * sin, real[z] * sin + imag[z] * cos))
        values = [jnp.concatenate(value, axis=0) for value in small_dft(values)]
        at = pl.ds(pl.multiple_of((step * count + i) * 16, 16), 16)
        for half in range(2):
            planes = swap_quarters(values[4 * half:4 * half + 4])
            for x in range(4):
                columns = slice((2 * x + half) * LANES, (2 * x + half + 1) * LANES)
                high, low = in_halves(planes[x])
                high_ref[at, columns] = high
                low_ref[at, columns] = low

    @pl.when(step == pl.num_programs(1) - 1)
    def _():
        @pl.loop(0, 4)
        def _(x):
            columns = pl.ds(pl.multiple_of(x * side, side), side)
            product = functools.partial(jnp.dot, preferred_element_type=jnp.float32)
            high = high_ref[:, columns]
            result = product(wide_ref[...], high) + (
                product(wide_ref[...], low_ref[:, columns]) + product(fine_ref[...], high)
            )
            for part in range(2):
                for group in range(groups):
                    start = part * side + group * height
                    out_ref[group, x, part] = result[start:start + height, :].astype(jnp.bfloat16)


def first_dimension_kernel(slabs, each, core_ref, *refs):
    arrays, (out_ref, mid_ref) = refs[:-2], refs[-2:]
    chunks = len(arrays) // 2
    own, other = arrays[:chunks], arrays[chunks:]
    spots = [(i, at) for i, ref in enumerate(own) for at in range(ref.shape[1])]
    core = core_ref[0]
    is_first = core == 0
    sign = (1 - 2 * core).astype(jnp.float32)

    rows = out_ref.shape[2]
    strips = [slice(at, min(at + 8, rows)) for at in range(0, rows, 8)]

    def plane(x, strip):
        slab, rest = x // (2 * each), x % (2 * each)
        half, inner = rest // each, rest % each
        chunk, at = spots[inner]
        loaded = []
        for part in range(2):
            here, there = own[chunk][slab, at, part], other[chunk][slab, at, part]
            value = jnp.where(is_first, here, there) if half == 0 else jnp.where(is_first, there, here)
            loaded.append(value.astype(jnp.float32)[strip])
        return tuple(loaded)

    for low in range(16):
        for strip in strips:
            values = small_dft([plane(low + 16 * high, strip) for high in range(16)])
            for k in range(16):
                real, imag = rotated(values[k], low * k, 256, sign if low % 2 else None)
                mid_ref[k, low, 0, strip] = real
                mid_ref[k, low, 1, strip] = imag

    @pl.loop(0, 16)
    def _(k):
        for strip in strips:
            values = [(mid_ref[k, low, 0, strip], mid_ref[k, low, 1, strip]) for low in range(16)]
            even, odd = small_dft(values[0::2]), small_dft(values[1::2])
            for m in range(8):
                turned = rotated(odd[m], m, 16)
                out_ref[0, k + 16 * m, strip] = even[m][0] + turned[0]
                out_ref[1, k + 16 * m, strip] = even[m][1] + turned[1]


def host_halves(table):
    high = table.astype(jnp.bfloat16)
    return high, (table - high.astype(np.float64)).astype(jnp.bfloat16)


def transform_tables(side):
    per_row = side // 8
    grid = np.arange(per_row)
    angle = 2 * np.pi * np.outer(grid, grid) / per_row
    zblock = np.concatenate([np.kron(np.eye(4), np.cos(angle)), np.kron(np.eye(4), np.sin(angle))], axis=1)
    high, low = host_halves(zblock)
    zblock = np.concatenate([high, high, low], axis=0)
    angle = 2 * np.pi * np.outer(np.arange(8), grid) / side
    turns = np.stack([np.tile(np.cos(angle), (1, 4)), np.tile(np.sin(angle), (1, 4))]).astype(np.float32)
    cells = np.arange(side)
    angle = 2 * np.pi * (np.outer(cells, cells) % side) / side
    cos, sin = np.cos(angle).reshape(side, per_row, 1, 8), np.sin(angle).reshape(side, per_row, 1, 8)
    matrix = np.concatenate(
        [np.concatenate([cos, -sin], axis=2), np.concatenate([sin, cos], axis=2)], axis=0
    ).reshape(2 * side, 2 * side) / float(side) ** 1.5
    return (zblock, turns) + host_halves(matrix)


def sum_over_slabs(partial_sums):
    slabs = partial_sums.shape[0]
    if slabs <= 8:
        me = lax.axis_index("slab")
        row = lambda i: lax.dynamic_index_in_dim(partial_sums, me ^ i, axis=0, keepdims=True)
        returned = [row(0)] + [
            lax.ppermute(row(i), "slab", [(slab, slab ^ i) for slab in range(slabs)])
            for i in range(1, slabs)
        ]
        returned = jnp.concatenate(returned)
    else:
        returned = lax.all_to_all(partial_sums, "slab", split_axis=0, concat_axis=0, tiled=True)
    return jnp.sum(returned, axis=0)


def to_field(mine, theirs_sent, partial_sums, side):
    slabs = lax.axis_size("slab")
    per_row = side // 8
    each = side // slabs // 2
    height = side // slabs
    groups = slabs if height % 16 == 0 else 1
    tables = [jnp.asarray(table) for table in transform_tables(side)]
    swap = [(0, 1), (1, 0)]
    theirs = [lax.ppermute(chunk, "dom", swap) for chunk in theirs_sent]
    grid_shape = (-1, per_row, per_row, LANES)
    mine = mine.reshape(grid_shape)
    short = max(0, 4 - each)
    if short:
        mine = jnp.pad(mine, ((0, short), (0, 0), (0, 0), (0, 0)))
    yblocks = 8
    own = []
    first_quad = 0
    before = []
    for real_planes, added in zip(pieces_of(each), theirs):
        if before:
            added, before[0] = lax.optimization_barrier((added, before[0]))
        added = added.reshape(grid_shape)
        if short:
            added = jnp.pad(added, ((0, short), (0, 0), (0, 0), (0, 0)))
        held = real_planes + short
        quads = held // 4
        whole = lambda table: pl.BlockSpec(table.shape, lambda q, y: (0,) * table.ndim)
        sent = pl.pallas_call(
            planes_kernel,
            grid=(quads, per_row // yblocks),
            out_shape=jax.ShapeDtypeStruct((groups, held, 2, side // groups, side), jnp.bfloat16),
            in_specs=[
                pl.BlockSpec((4, yblocks, per_row, LANES), lambda q, y, at=first_quad: (at + q, y, 0, 0)),
                pl.BlockSpec((4, yblocks, per_row, LANES), lambda q, y: (q, y, 0, 0)),
            ] + [whole(table) for table in tables],
            out_specs=pl.BlockSpec((groups, 4, 2, side // groups, side), lambda q, y: (0, q, 0, 0, 0)),
            scratch_shapes=[
                pltpu.VMEM((2 * side, 4 * side), jnp.bfloat16),
                pltpu.VMEM((2 * side, 4 * side), jnp.bfloat16),
            ],
            compiler_params=params(56),
            cost_estimate=pl.CostEstimate(
                flops=held * 8 * side**3, bytes_accessed=held * 4 * side**2 * 8, transcendentals=0
            ),
            name="transform_planes",
        )(mine, added, *tables)
        if groups != slabs:
            sent = sent.reshape(-1, 2, slabs, height, side).transpose(2, 0, 1, 3, 4)[:, :real_planes]
        first_quad += quads
        if before:
            sent, own[-1] = lax.optimization_barrier((sent, own[-1]))
        if first_quad * 4 >= each:
            sent, partial_sums = lax.optimization_barrier((sent, partial_sums))
        before = [sent]
        got = lax.all_to_all(sent, "slab", split_axis=0, concat_axis=0, tiled=True)
        own.append(got)
    other = [lax.ppermute(got, "dom", swap) for got in own[:-1]]
    own[-1], losses, *other = lax.optimization_barrier((own[-1], sum_over_slabs(partial_sums), *other))
    other.append(lax.ppermute(own[-1], "dom", swap))
    rows = min(16, height)
    arrays = own + other
    field = pl.pallas_call(
        functools.partial(first_dimension_kernel, slabs, each),
        grid=(height // rows, side // LANES),
        out_shape=jax.ShapeDtypeStruct((2, side // 2, height, side), jnp.float32),
        in_specs=[SMEM_SPEC] + [
            pl.BlockSpec(array.shape[:3] + (rows, LANES), lambda y, z: (0, 0, 0, y, z))
            for array in arrays
        ],
        out_specs=pl.BlockSpec((2, side // 2, rows, LANES), lambda y, z: (0, 0, y, z)),
        scratch_shapes=[pltpu.VMEM((16, 16, 2, rows, LANES), jnp.float32)],
        compiler_params=params(28),
        name="transform_first",
    )(lax.axis_index("dom").astype(jnp.int32).reshape(1), *arrays)
    return field, losses


def gradient_of_slab(volume, kernels, images, owners, local_block, kinds, counts, ctf_code, ctf_table, scales):
    slabs = lax.axis_size("slab")
    particles, list_length, features = images.shape
    side = math.isqrt(list_length * 64)
    entries = particles * list_length
    cap = 2 * entries // slabs
    slots = slabs * cap
    blocks = volume.shape[0]
    local_bits = bits_of(blocks)
    kind_count = kernels.shape[0]
    rows = entries // LANES
    int_rows = jax.ShapeDtypeStruct((rows, LANES), jnp.int32)

    target, word, totals = pl.pallas_call(
        functools.partial(route_kernel, slabs, cap, local_bits),
        out_shape=(int_rows, int_rows, jax.ShapeDtypeStruct((slabs, LANES), jnp.int32)),
        in_specs=[VMEM_SPEC, VMEM_SPEC, VMEM_SPEC, SMEM_SPEC],
        out_specs=(VMEM_SPEC, VMEM_SPEC, VMEM_SPEC),
        compiler_params=params(56),
        name="route",
    )(owners.reshape(rows, LANES), local_block, kinds, counts)
    target, word = target.reshape(entries), word.reshape(entries)
    tiles = [cap // 2, cap // 2] if cap >= 2048 else [cap]
    parts = len(tiles)
    code = ctf_code | ((scales.astype(jnp.float32) * 256.0).astype(jnp.int32) << 8)
    stride = cap + LANES
    meta, *packed = pl.pallas_call(
        functools.partial(pack_kernel, slabs, cap, list_length),
        out_shape=(jax.ShapeDtypeStruct((slabs * stride,), jnp.int32),)
        + tuple(jax.ShapeDtypeStruct((slabs, tile, features), jnp.bfloat16) for tile in tiles),
        in_specs=[SMEM_SPEC] * 5 + [VMEM_SPEC],
        out_specs=(SMEM_SPEC,) + (ANY_SPEC,) * parts,
        scratch_shapes=[
            pltpu.VMEM((entries, features), jnp.float32),
            pltpu.VMEM((slabs * stride, features), jnp.float32),
            pltpu.VMEM((slots, features), jnp.bfloat16),
            pltpu.SemaphoreType.DMA(()),
        ],
        compiler_params=params(56),
        name="pack",
    )(target, word, counts, totals, code, images.reshape(entries, features))
    arrived = lax.all_to_all(
        meta.reshape(slabs, stride), "slab", split_axis=0, concat_axis=0, tiled=True
    )
    words = arrived[:, :cap]
    totals_in = arrived[:, cap]
    codes_in = arrived[:, cap + 1:cap + 1 + particles]
    live = (jnp.arange(cap, dtype=jnp.int32)[None, :] < totals_in[:, None]).astype(jnp.int32)
    table_rows = ctf_table[(codes_in & 255).reshape(-1)]
    scale_in = (codes_in >> 8).astype(jnp.float32).reshape(-1) * (1.0 / 256.0)

    index = pl.pallas_call(
        functools.partial(decode_kernel, local_bits, blocks),
        out_shape=jax.ShapeDtypeStruct((slots // LANES + 8, LANES), jnp.int32),
        in_specs=[VMEM_SPEC, VMEM_SPEC],
        out_specs=VMEM_SPEC,
        compiler_params=params(56),
        name="decode",
    )(words.reshape(slots // LANES, LANES), live.reshape(slots // LANES, LANES))
    index = index.reshape(slots + 8 * LANES)
    voxels = list(pl.pallas_call(
        functools.partial(gather_kernel, slabs, cap),
        out_shape=tuple(
            jax.ShapeDtypeStruct((slabs, tile, features), jnp.bfloat16) for tile in tiles
        ),
        in_specs=[SMEM_SPEC, SMEM_SPEC, VMEM_SPEC],
        out_specs=(VMEM_SPEC,) * parts,
        scratch_shapes=[
            pltpu.VMEM((blocks + 8, features), jnp.float32),
            pltpu.VMEM((cap, features), jnp.float32),
        ],
        compiler_params=params(56),
        cost_estimate=pl.CostEstimate(flops=0, bytes_accessed=100 * MIB, transcendentals=0),
        name="read_voxels",
    )(index, totals_in, volume))

    forward = jnp.transpose(kernels, (2, 0, 1)).reshape(features, kind_count * features)
    backward = kernels.reshape(kind_count, 2, 8, 8, features).transpose(3, 1, 2, 0, 4)
    backward = backward.reshape(features, kind_count * features)
    core = lax.axis_index("dom").astype(jnp.int32).reshape(1)
    plane_blocks = (side // 8) ** 2
    pieces = [planes * plane_blocks for planes in pieces_of(side // slabs // 2)]
    squares, sums, behind, offset = 0.0, None, [voxels[0]], 0
    for part, tile in enumerate(tiles):
        first, last = part == 0, part == parts - 1
        if not first:
            packed[part], earlier = lax.optimization_barrier((packed[part], behind[part - 1]))
            if part == 1:
                voxels[0] = earlier
        picture = lax.all_to_all(packed[part], "slab", split_axis=0, concat_axis=0, tiled=True)
        lengths = [blocks // 2] + pieces if last else []
        arguments = [
            totals_in, table_rows[:, 0], table_rows[:, 1], scale_in, index, core,
            words[:, offset:offset + tile].reshape(slabs, 1, tile), voxels[part], picture,
            forward, backward,
        ]
        aliases = {}
        if not first:
            aliases = {len(arguments): 1}
            arguments.append(pltpu.with_memory_space_constraint(sums, pltpu.VMEM))
        more, sums, *halves = pl.pallas_call(
            functools.partial(
                slab_kernel, side, local_bits, list_length, particles, cap, offset, first, last
            ),
            out_shape=(
                jax.ShapeDtypeStruct((slabs, particles, LANES), jnp.float32),
                pltpu.VMEM((blocks + 8, 1, features), jnp.float32),
            )
            + tuple(jax.ShapeDtypeStruct((length, 1, features), jnp.float32) for length in lengths),
            in_specs=[SMEM_SPEC] * 6 + [VMEM_SPEC] * (len(arguments) - 6),
            out_specs=(VMEM_SPEC, VMEM_SPEC) + (ANY_SPEC,) * len(lengths),
            scratch_shapes=[
                pltpu.VMEM((PAIR * min(tile, STEP), features), jnp.float32),
                pltpu.VMEM((256, 1, features), jnp.float32),
                pltpu.SMEM((slabs * tile // min(tile, STEP) + 1,), jnp.int32),
                pltpu.SemaphoreType.DMA((max(1, len(lengths)),)),
            ],
            input_output_aliases=aliases,
            compiler_params=params(24),
            cost_estimate=pl.CostEstimate(flops=0, bytes_accessed=16 * MIB, transcendentals=0),
            name="compare_and_add",
        )(*arguments)
        squares = squares + more
        behind.append(more)
        offset += tile
    mine, *theirs = [half.reshape(-1, features) for half in halves]
    partial_sums = jnp.sum(squares, axis=2)
    return mine, theirs, partial_sums, side


def body(*arrays):
    mine, theirs, partial_sums, side = gradient_of_slab(*arrays)
    field, squares = to_field(mine, theirs, partial_sums, side)
    counts = arrays[6]
    return field, squares / (counts.astype(jnp.float32) * 128.0)


def solution(mesh):
    in_specs = (
        P(("groups", "slab"), None),
        P(),
        P(("groups", "slab", "dom"), None, None),
        P(("groups", "slab", "dom"), None, None),
        P(("groups", "slab", "dom"), None),
        P(("groups", "slab", "dom"), None),
        P(("groups", "slab", "dom")),
        P(("groups", "slab", "dom")),
        P(),
        P(("groups", "slab", "dom")),
    )
    out_specs = (P(None, ("groups", "dom"), "slab", None), P(("groups", "slab", "dom")))
    return jax.shard_map(body, mesh=mesh, in_specs=in_specs, out_specs=out_specs, check_vma=False)
```

```python
import functools
import math

import jax
import jax.numpy as jnp
import numpy as np
from jax import lax
from jax.experimental import pallas as pl
from jax.experimental.pallas import tpu as pltpu
from jax.sharding import PartitionSpec as P

LANES = 128
GROUP = 16
UNUSED = 100
STEP = 256
PAIR = 1
MIB = 1024 * 1024

SMEM_SPEC = pl.BlockSpec(memory_space=pltpu.SMEM)
VMEM_SPEC = pl.BlockSpec(memory_space=pltpu.VMEM)
ANY_SPEC = pl.BlockSpec(memory_space=pl.ANY)


def params(mib):
    return pltpu.CompilerParams(vmem_limit_bytes=mib * MIB)


def bits_of(count):
    return (count - 1).bit_length()


def route_kernel(slabs, cap, local_bits, owner_ref, local_ref, kind_ref, counts_ref, target_ref, word_ref, totals_ref):
    particles, list_length = local_ref.shape
    rows_each = list_length // LANES
    rows = particles * rows_each
    gathered = lambda ref: jnp.concatenate(
        [ref[:, j * LANES:(j + 1) * LANES] for j in range(rows_each)], axis=0
    )
    row_id = lax.broadcasted_iota(jnp.int32, (rows, LANES), 0)
    lane_id = lax.broadcasted_iota(jnp.int32, (rows, LANES), 1)
    particle = row_id % particles
    position = (row_id // particles) * LANES + lane_id
    limit = jnp.zeros((rows, LANES), jnp.int32)
    for i in range(particles):
        limit = jnp.where(particle == i, counts_ref[i], limit)
    owner = jnp.concatenate(
        [owner_ref[pl.ds(j, particles, stride=rows_each), :] for j in range(rows_each)], axis=0
    )
    owner = jnp.where(position < limit, owner, -1)
    up_to = (
        lax.broadcasted_iota(jnp.int32, (LANES, LANES), 0)
        <= lax.broadcasted_iota(jnp.int32, (LANES, LANES), 1)
    ).astype(jnp.bfloat16)
    ones = jnp.ones((LANES, LANES), jnp.bfloat16)
    before = (
        lax.broadcasted_iota(jnp.int32, (rows, rows), 1)
        < lax.broadcasted_iota(jnp.int32, (rows, rows), 0)
    ).astype(jnp.bfloat16)

    def one_slab(slab, target):
        mine = owner == slab
        hits = mine.astype(jnp.float32).astype(jnp.bfloat16)
        inside = jnp.dot(hits, up_to, preferred_element_type=jnp.float32)
        row_sum = jnp.dot(hits, ones, preferred_element_type=jnp.float32)
        above = jnp.dot(before, row_sum.astype(jnp.bfloat16), preferred_element_type=jnp.float32)
        rank = (inside + above).astype(jnp.int32) - 1
        total = (above[rows - 1:rows, :] + row_sum[rows - 1:rows, :]).astype(jnp.int32)
        totals_ref[pl.ds(slab, 1), :] = total
        return jnp.where(mine, slab * (cap + LANES) + rank, target)

    target = lax.fori_loop(0, slabs, one_slab, jnp.full((rows, LANES), cap + UNUSED, jnp.int32))
    target_ref[...] = target
    kind_bits = local_bits
    word = gathered(local_ref) | (gathered(kind_ref) << kind_bits) | (position << (kind_bits + 2))
    word_ref[...] = word | (particle << (kind_bits + 2 + bits_of(list_length)))


def pack_kernel(slabs, cap, list_length, target_ref, word_ref, counts_ref, totals_ref, code_ref, image_ref, meta_ref, *refs):
    out_refs, (wide_ref, staged_ref, narrow_ref, sem) = refs[:-4], refs[-4:]
    particles = counts_ref.shape[0]
    stride = cap + LANES
    step = 256
    turn = 32

    @pl.loop(0, image_ref.shape[0] // step)
    def _(i):
        at = pl.multiple_of(i * step, step)
        wide_ref[pl.ds(at, step), :] = image_ref[pl.ds(at, step), :].astype(jnp.float32)

    @pl.loop(0, particles)
    def _(particle):
        @pl.loop(0, (counts_ref[particle] + turn - 1) // turn)
        def _(i):
            per_row = LANES // turn
            first = (i // per_row) * (particles * LANES) + particle * LANES + (i % per_row) * turn
            row = particle * list_length + i * turn
            targets = [target_ref[first + j] for j in range(turn)]
            words = [word_ref[first + j] for j in range(turn)]
            rows = [wide_ref[pl.ds(row + j, 1), :] for j in range(turn)]
            for j in range(turn):
                staged_ref[pl.ds(targets[j], 1), :] = rows[j]
                meta_ref[targets[j]] = words[j]

    @pl.loop(0, slabs)
    def _(slab):
        header = slab * stride + cap
        meta_ref[header] = totals_ref[slab, 0]
        for j in range(particles):
            meta_ref[header + 1 + j] = code_ref[j]

    def blocks_of(act):
        offset = 0
        for out_ref in out_refs:
            width = out_ref.shape[1]

            @pl.loop(0, slabs)
            def _(slab, offset=offset, width=width, out_ref=out_ref):
                live = jnp.clip(totals_ref[slab, 0] - offset, 0, width)

                @pl.loop(0, (live + LANES - 1) // LANES)
                def _(i):
                    at = pl.multiple_of(slab * cap + offset + i * LANES, LANES)
                    to = pl.multiple_of(i * LANES, LANES)
                    copy = pltpu.make_async_copy(
                        narrow_ref.at[pl.ds(at, LANES)], out_ref.at[slab, pl.ds(to, LANES)], sem
                    )
                    act(copy, at, pl.multiple_of(at + slab * LANES, LANES))

            offset += width

    def convert_and_start(copy, at, staged_at):
        narrow_ref[pl.ds(at, LANES), :] = staged_ref[pl.ds(staged_at, LANES), :].astype(jnp.bfloat16)
        copy.start()

    blocks_of(convert_and_start)
    blocks_of(lambda copy, at, staged_at: copy.wait())


def decode_kernel(local_bits, dummy, word_ref, live_ref, index_ref):
    rows = word_ref.shape[0]
    live = live_ref[...] != 0
    index = jnp.where(live, word_ref[...] & ((1 << local_bits) - 1), dummy)
    lane = lax.broadcasted_iota(jnp.int32, (rows, LANES), 1)
    clash = jnp.zeros((rows, LANES), jnp.int32)
    for shift in range(1, GROUP):
        earlier = pltpu.roll(index, shift, 1)
        same = (earlier == index) & (lane % GROUP >= shift) & live
        clash = clash | same.astype(jnp.int32)
    shift = 1
    while shift < LANES:
        if shift == GROUP:
            index = index | jnp.where(lane % GROUP == 0, clash << 24, 0)
        clash = clash | pltpu.roll(clash, LANES - shift, 1)
        shift *= 2
    index_ref[0:rows, :] = index | jnp.where(lane == 0, clash << 25, 0)
    index_ref[rows:, :] = jnp.full((index_ref.shape[0] - rows, LANES), dummy, jnp.int32)


def gather_kernel(slabs, cap, index_ref, totals_ref, volume_ref, *refs):
    out_refs, (wide_ref, staged_ref) = refs[:-2], refs[-2:]
    blocks = volume_ref.shape[0]
    step = 256

    @pl.loop(0, blocks // step)
    def _(i):
        at = pl.multiple_of(i * step, step)
        wide_ref[pl.ds(at, step), :] = volume_ref[pl.ds(at, step), :].astype(jnp.float32)

    @pl.loop(0, slabs)
    def _(source):
        live = totals_ref[source]

        @pl.loop(0, (live + 15) // 16)
        def _(i):
            first = source * cap + i * 16
            places = [index_ref[first] & 0xFFFFFF] + [index_ref[first + j] for j in range(1, 16)]
            rows = [wide_ref[pl.ds(places[j], 1), :] for j in range(16)]
            for j in range(16):
                staged_ref[pl.ds(i * 16 + j, 1), :] = rows[j]

        offset = 0
        for out_ref in out_refs:
            width = out_ref.shape[1]

            @pl.when(live > offset)
            def _(offset=offset):
                out_ref[source] = staged_ref[offset:offset + width, :].astype(jnp.bfloat16)

            offset += width


def sine(angle):
    turns = jnp.floor(angle * (1.0 / math.pi) + 0.5)
    rest = angle - turns * 3.140625
    rest = rest - turns * (math.pi - 3.140625)
    odd = turns - 2.0 * jnp.floor(turns * 0.5)
    square = rest * rest
    poly = 2.718121e-6
    poly = poly * square - 1.9839334e-4
    poly = poly * square + 8.3333293e-3
    poly = poly * square - 1.6666667e-1
    value = rest + rest * square * poly
    return value * (1.0 - 2.0 * odd)


def slab_kernel(
    side, local_bits, list_length, particles, cap, offset, first, last,
    totals_ref, defocus_ref, phase_ref, scale_ref, index_ref, core_ref,
    word_ref, voxel_ref, image_ref, forward_ref, backward_ref, *rest,
):
    if not first:
        rest = rest[1:]
    square_ref, sum_ref, out_refs, (staged_ref, steps_ref, sems) = rest[0], rest[1], rest[2:-3], rest[-3:]
    slabs, _, tile = word_ref.shape
    step = staged_ref.shape[0] // PAIR
    steps_each = tile // step
    blocks = sum_ref.shape[0] - 8
    features = image_ref.shape[2]
    kinds = forward_ref.shape[1] // features
    position_bits = bits_of(list_length)
    per_row = side // 8
    half = features // 2

    if first:
        @pl.loop(0, blocks // 256)
        def _(i):
            at = pl.multiple_of(i * 256, 256)
            sum_ref[pl.ds(at, 256), :] = jnp.zeros((256, features), jnp.float32)

    square_ref[...] = jnp.zeros_like(square_ref)
    live_of = lambda source: jnp.clip(totals_ref[source] - offset, 0, tile)

    def list_source(source, count):
        def list_step(i, count):
            steps_ref[count] = source * steps_each + i
            return count + 1

        return lax.fori_loop(0, (live_of(source) + step - 1) // step, list_step, count)

    steps_ref[0] = 0
    count = lax.fori_loop(0, slabs, list_source, 0)

    def compare(number, slot):
        which_step = steps_ref[jnp.minimum(number, jnp.maximum(count - 1, 0))]
        source, at = which_step // steps_each, (which_step % steps_each) * step
        at = pl.multiple_of(at, step)
        live = jnp.where(number < count, live_of(source) - at, 0)
        word = word_ref[source, :, pl.ds(at, step)]
        kind = (word >> local_bits) & 3
        position = (word >> (local_bits + 2)) & (list_length - 1)
        particle = (word >> (local_bits + 2 + position_bits)) & (particles - 1)
        valid = lax.broadcasted_iota(jnp.int32, (1, step), 1) < live
        defocus = jnp.zeros((1, step), jnp.float32)
        phase = jnp.zeros((1, step), jnp.float32)
        scale = jnp.zeros((1, step), jnp.float32)
        for j in range(particles):
            chosen = particle == j
            defocus = jnp.where(chosen, defocus_ref[source * particles + j], defocus)
            phase = jnp.where(chosen, phase_ref[source * particles + j], phase)
            scale = jnp.where(chosen, scale_ref[source * particles + j], scale)
        defocus = defocus * (1.0 / float((side // 2) ** 2))
        cell = lax.broadcasted_iota(jnp.int32, (half, LANES), 0)
        cell_vert, cell_horiz = (cell // 8).astype(jnp.float32), (cell % 8).astype(jnp.float32)
        repeat = lambda table: jnp.concatenate([table] * (step // LANES), axis=1)
        vert = ((position // per_row) * 8 - side // 2).astype(jnp.float32) + repeat(cell_vert)
        horiz = ((position % per_row) * 8 - side // 2).astype(jnp.float32) + repeat(cell_horiz)
        factor = scale * sine(defocus * (vert * vert + horiz * horiz) + phase)
        factor = jnp.concatenate([factor, factor], axis=0)
        voxel = voxel_ref[source, pl.ds(at, step), :].astype(jnp.float32).T.astype(jnp.bfloat16)
        picture = image_ref[source, pl.ds(at, step), :].astype(jnp.float32).T

        def by_kind(value):
            none = jnp.zeros_like(value)
            return jnp.concatenate([jnp.where(kind == k, value, none) for k in range(kinds)], axis=0)

        extracted = jnp.dot(forward_ref[...], by_kind(voxel), preferred_element_type=jnp.float32)
        misfit = jnp.where(valid, factor * extracted - picture, 0.0)
        squares = jnp.sum(misfit * misfit, axis=0, keepdims=True)
        which = lax.broadcasted_iota(jnp.int32, (particles, step), 0)
        spread = jnp.where(valid & (particle == which), squares, 0.0)
        folded = spread[:, 0:LANES]
        for i in range(1, step // LANES):
            folded = folded + spread[:, i * LANES:(i + 1) * LANES]
        square_ref[source] = square_ref[source] + folded
        weighted = (factor * misfit).astype(jnp.bfloat16)
        terms = jnp.dot(backward_ref[...], by_kind(weighted), preferred_element_type=jnp.float32)
        staged_ref[slot * step:(slot + 1) * step, :] = terms.T

    def places_of(base):
        return [index_ref[base] & 0xFFFFFF] + [index_ref[base + j] for j in range(1, GROUP)]

    def add_group(base, at):
        places = places_of(base)
        held = [sum_ref[pl.ds(place, 1), :] for place in places]
        new = [staged_ref[pl.ds(at + j, 1), :] for j in range(GROUP)]
        for j in range(GROUP):
            sum_ref[pl.ds(places[j], 1), :] = held[j] + new[j]

    def base_of(number):
        earlier = steps_ref[jnp.clip(number, 0, jnp.maximum(count - 1, 0))]
        base = (earlier // steps_each) * cap + offset + (earlier % steps_each) * step
        return jnp.where((number >= 0) & (number < count), base, slabs * cap)

    @pl.loop(0, (count + PAIR - 1) // PAIR + 1)
    def _(turn):
        bases = [base_of((turn - 1) * PAIR + slot) for slot in range(PAIR)]
        marks = 0
        for base in bases:
            for i in range(step // LANES):
                marks = marks | index_ref[base + i * LANES]

        @pl.when(marks < (1 << 25))
        def _():
            for slot, base in enumerate(bases):
                for g in range(step // GROUP):
                    add_group(base + g * GROUP, slot * step + g * GROUP)
            for slot in range(PAIR):
                compare(turn * PAIR + slot, slot)

        @pl.when(marks >= (1 << 25))
        def _():
            for slot, base in enumerate(bases):
                @pl.loop(0, step // GROUP)
                def _(g, slot=slot, base=base):
                    start = base + g * GROUP
                    at = slot * step + g * GROUP
                    clashes = (index_ref[start] >> 24) & 1

                    @pl.when(clashes == 0)
                    def _():
                        add_group(start, at)

                    @pl.when(clashes == 1)
                    def _():
                        places = places_of(start)
                        for j in range(GROUP):
                            sum_ref[pl.ds(places[j], 1), :] = (
                                sum_ref[pl.ds(places[j], 1), :] + staged_ref[pl.ds(at + j, 1), :]
                            )

            for slot in range(PAIR):
                compare(turn * PAIR + slot, slot)

    if last:
        half = blocks // 2
        start = (1 - core_ref[0]) * half
        places = [core_ref[0] * half]
        for out_ref in out_refs[1:]:
            places.append(start)
            start = start + out_ref.shape[0]
        copies = []
        for i, (place, out_ref) in enumerate(zip(places, out_refs)):
            length = out_ref.shape[0]
            at = pl.multiple_of(place, 8)
            copies.append(pltpu.make_async_copy(sum_ref.at[pl.ds(at, length)], out_ref, sems.at[i]))
        for copy in copies:
            copy.start()
        for copy in copies:
            copy.wait()


def pieces_of(planes):
    if planes < 16:
        return [planes]
    return [4, planes - 4]


def rotated(value, turn, length, sign=None):
    real, imag = value
    if turn == 0 or 4 * turn == length:
        if turn:
            real, imag = -imag, real
        return (real, imag) if sign is None else (real * sign, imag * sign)
    if sign is None and 8 * turn in (length, 3 * length):
        root = math.sqrt(0.5)
        if 8 * turn == length:
            return ((real - imag) * root, (real + imag) * root)
        return ((real + imag) * -root, (real - imag) * root)
    cos, sin = math.cos(2 * math.pi * turn / length), math.sin(2 * math.pi * turn / length)
    if sign is not None:
        cos, sin = cos * sign, sin * sign
    return (real * cos - imag * sin, real * sin + imag * cos)


def small_dft(values):
    length = len(values)
    if length == 1:
        return values
    even, odd = small_dft(values[0::2]), small_dft(values[1::2])
    low, high = [], []
    for k in range(length // 2):
        turned = rotated(odd[k], k, length)
        low.append((even[k][0] + turned[0], even[k][1] + turned[1]))
        high.append((even[k][0] - turned[0], even[k][1] - turned[1]))
    return low + high


def swap_quarters(values):
    lane = lax.broadcasted_iota(jnp.int32, values[0].shape, 1)
    low, even = lane < 64, (lane // 32) % 2 == 0
    roll = lambda value, shift: pltpu.roll(value, shift, 1)
    for first, second, shift, keep in ((0, 2, 64, low), (1, 3, 64, low), (0, 1, 32, even), (2, 3, 32, even)):
        one, two = values[first], values[second]
        values[first] = jnp.where(keep, one, roll(two, shift))
        values[second] = jnp.where(keep, roll(one, LANES - shift), two)
    return values


def in_halves(value):
    high = value.astype(jnp.bfloat16)
    return high, (value - high.astype(jnp.float32)).astype(jnp.bfloat16)


def planes_kernel(mine_ref, theirs_ref, zblock_ref, turn_ref, wide_ref, fine_ref, out_ref, high_ref, low_ref):
    step = pl.program_id(1)
    count = mine_ref.shape[1]
    groups, side = out_ref.shape[0], out_ref.shape[4]
    height = side // groups

    @pl.loop(0, count, unroll=8)
    def _(i):
        block = (mine_ref[:, i] + theirs_ref[:, i]).reshape(LANES, LANES)
        high, low = in_halves(block.T)
        both = jnp.dot(
            jnp.concatenate([high, low, high], axis=1), zblock_ref[...],
            preferred_element_type=jnp.float32,
        )
        by_cos = both[:, :LANES].reshape(8, 2, 8, LANES)
        by_sin = both[:, LANES:].reshape(8, 2, 8, LANES)
        real = by_cos[:, 0] - by_sin[:, 1]
        imag = by_sin[:, 0] + by_cos[:, 1]
        values = []
        for z in range(8):
            cos, sin = turn_ref[0, z:z + 1, :], turn_ref[1, z:z + 1, :]
            values.append((real[z] * cos - imag[z] * sin, real[z] * sin + imag[z] * cos))
        values = [jnp.concatenate(value, axis=0) for value in small_dft(values)]
        at = pl.ds(pl.multiple_of((step * count + i) * 16, 16), 16)
        for half in range(2):
            planes = swap_quarters(values[4 * half:4 * half + 4])
            for x in range(4):
                columns = slice((2 * x + half) * LANES, (2 * x + half + 1) * LANES)
                high, low = in_halves(planes[x])
                high_ref[at, columns] = high
                low_ref[at, columns] = low

    @pl.when(step == pl.num_programs(1) - 1)
    def _():
        @pl.loop(0, 4)
        def _(x):
            columns = pl.ds(pl.multiple_of(x * side, side), side)
            product = functools.partial(jnp.dot, preferred_element_type=jnp.float32)
            high = high_ref[:, columns]
            result = product(wide_ref[...], high) + (
                product(wide_ref[...], low_ref[:, columns]) + product(fine_ref[...], high)
            )
            for part in range(2):
                for group in range(groups):
                    start = part * side + group * height
                    out_ref[group, x, part] = result[start:start + height, :].astype(jnp.bfloat16)


def first_dimension_kernel(slabs, each, core_ref, *refs):
    arrays, (out_ref, mid_ref) = refs[:-2], refs[-2:]
    chunks = len(arrays) // 2
    own, other = arrays[:chunks], arrays[chunks:]
    spots = [(i, at) for i, ref in enumerate(own) for at in range(ref.shape[1])]
    core = core_ref[0]
    is_first = core == 0
    sign = (1 - 2 * core).astype(jnp.float32)

    rows = out_ref.shape[2]
    strips = [slice(at, min(at + 8, rows)) for at in range(0, rows, 8)]

    def plane(x, strip):
        slab, rest = x // (2 * each), x % (2 * each)
        half, inner = rest // each, rest % each
        chunk, at = spots[inner]
        loaded = []
        for part in range(2):
            here, there = own[chunk][slab, at, part], other[chunk][slab, at, part]
            value = jnp.where(is_first, here, there) if half == 0 else jnp.where(is_first, there, here)
            loaded.append(value.astype(jnp.float32)[strip])
        return tuple(loaded)

    for low in range(16):
        for strip in strips:
            values = small_dft([plane(low + 16 * high, strip) for high in range(16)])
            for k in range(16):
                real, imag = rotated(values[k], low * k, 256, sign if low % 2 else None)
                mid_ref[k, low, 0, strip] = real
                mid_ref[k, low, 1, strip] = imag

    @pl.loop(0, 16)
    def _(k):
        for strip in strips:
            values = [(mid_ref[k, low, 0, strip], mid_ref[k, low, 1, strip]) for low in range(16)]
            even, odd = small_dft(values[0::2]), small_dft(values[1::2])
            for m in range(8):
                turned = rotated(odd[m], m, 16)
                out_ref[0, k + 16 * m, strip] = even[m][0] + turned[0]
                out_ref[1, k + 16 * m, strip] = even[m][1] + turned[1]


def host_halves(table):
    high = table.astype(jnp.bfloat16)
    return high, (table - high.astype(np.float64)).astype(jnp.bfloat16)


def transform_tables(side):
    per_row = side // 8
    grid = np.arange(per_row)
    angle = 2 * np.pi * np.outer(grid, grid) / per_row
    zblock = np.concatenate([np.kron(np.eye(4), np.cos(angle)), np.kron(np.eye(4), np.sin(angle))], axis=1)
    high, low = host_halves(zblock)
    zblock = np.concatenate([high, high, low], axis=0)
    angle = 2 * np.pi * np.outer(np.arange(8), grid) / side
    turns = np.stack([np.tile(np.cos(angle), (1, 4)), np.tile(np.sin(angle), (1, 4))]).astype(np.float32)
    cells = np.arange(side)
    angle = 2 * np.pi * (np.outer(cells, cells) % side) / side
    cos, sin = np.cos(angle).reshape(side, per_row, 1, 8), np.sin(angle).reshape(side, per_row, 1, 8)
    matrix = np.concatenate(
        [np.concatenate([cos, -sin], axis=2), np.concatenate([sin, cos], axis=2)], axis=0
    ).reshape(2 * side, 2 * side) / float(side) ** 1.5
    return (zblock, turns) + host_halves(matrix)


def sum_over_slabs(partial_sums):
    slabs = partial_sums.shape[0]
    if slabs <= 8:
        me = lax.axis_index("slab")
        row = lambda i: lax.dynamic_index_in_dim(partial_sums, me ^ i, axis=0, keepdims=True)
        returned = [row(0)] + [
            lax.ppermute(row(i), "slab", [(slab, slab ^ i) for slab in range(slabs)])
            for i in range(1, slabs)
        ]
        returned = jnp.concatenate(returned)
    else:
        returned = lax.all_to_all(partial_sums, "slab", split_axis=0, concat_axis=0, tiled=True)
    return jnp.sum(returned, axis=0)


def to_field(mine, theirs_sent, partial_sums, side):
    slabs = lax.axis_size("slab")
    per_row = side // 8
    each = side // slabs // 2
    height = side // slabs
    groups = slabs if height % 16 == 0 else 1
    tables = [jnp.asarray(table) for table in transform_tables(side)]
    swap = [(0, 1), (1, 0)]
    theirs = [lax.ppermute(chunk, "dom", swap) for chunk in theirs_sent]
    grid_shape = (-1, per_row, per_row, LANES)
    mine = mine.reshape(grid_shape)
    short = max(0, 4 - each)
    if short:
        mine = jnp.pad(mine, ((0, short), (0, 0), (0, 0), (0, 0)))
    yblocks = 8
    own = []
    first_quad = 0
    before = []
    for real_planes, added in zip(pieces_of(each), theirs):
        if before:
            added, before[0] = lax.optimization_barrier((added, before[0]))
        added = added.reshape(grid_shape)
        if short:
            added = jnp.pad(added, ((0, short), (0, 0), (0, 0), (0, 0)))
        held = real_planes + short
        quads = held // 4
        whole = lambda table: pl.BlockSpec(table.shape, lambda q, y: (0,) * table.ndim)
        sent = pl.pallas_call(
            planes_kernel,
            grid=(quads, per_row // yblocks),
            out_shape=jax.ShapeDtypeStruct((groups, held, 2, side // groups, side), jnp.bfloat16),
            in_specs=[
                pl.BlockSpec((4, yblocks, per_row, LANES), lambda q, y, at=first_quad: (at + q, y, 0, 0)),
                pl.BlockSpec((4, yblocks, per_row, LANES), lambda q, y: (q, y, 0, 0)),
            ] + [whole(table) for table in tables],
            out_specs=pl.BlockSpec((groups, 4, 2, side // groups, side), lambda q, y: (0, q, 0, 0, 0)),
            scratch_shapes=[
                pltpu.VMEM((2 * side, 4 * side), jnp.bfloat16),
                pltpu.VMEM((2 * side, 4 * side), jnp.bfloat16),
            ],
            compiler_params=params(56),
            cost_estimate=pl.CostEstimate(
                flops=held * 8 * side**3, bytes_accessed=held * 4 * side**2 * 8, transcendentals=0
            ),
            name="transform_planes",
        )(mine, added, *tables)
        if groups != slabs:
            sent = sent.reshape(-1, 2, slabs, height, side).transpose(2, 0, 1, 3, 4)[:, :real_planes]
        first_quad += quads
        if before:
            sent, own[-1] = lax.optimization_barrier((sent, own[-1]))
        if first_quad * 4 >= each:
            sent, partial_sums = lax.optimization_barrier((sent, partial_sums))
        before = [sent]
        got = lax.all_to_all(sent, "slab", split_axis=0, concat_axis=0, tiled=True)
        own.append(got)
    other = [lax.ppermute(got, "dom", swap) for got in own[:-1]]
    own[-1], losses, *other = lax.optimization_barrier((own[-1], sum_over_slabs(partial_sums), *other))
    other.append(lax.ppermute(own[-1], "dom", swap))
    rows = min(16, height)
    arrays = own + other
    field = pl.pallas_call(
        functools.partial(first_dimension_kernel, slabs, each),
        grid=(height // rows, side // LANES),
        out_shape=jax.ShapeDtypeStruct((2, side // 2, height, side), jnp.float32),
        in_specs=[SMEM_SPEC] + [
            pl.BlockSpec(array.shape[:3] + (rows, LANES), lambda y, z: (0, 0, 0, y, z))
            for array in arrays
        ],
        out_specs=pl.BlockSpec((2, side // 2, rows, LANES), lambda y, z: (0, 0, y, z)),
        scratch_shapes=[pltpu.VMEM((16, 16, 2, rows, LANES), jnp.float32)],
        compiler_params=params(28),
        name="transform_first",
    )(lax.axis_index("dom").astype(jnp.int32).reshape(1), *arrays)
    return field, losses


def gradient_of_slab(volume, kernels, images, owners, local_block, kinds, counts, ctf_code, ctf_table, scales):
    slabs = lax.axis_size("slab")
    particles, list_length, features = images.shape
    side = math.isqrt(list_length * 64)
    entries = particles * list_length
    cap = 2 * entries // slabs
    slots = slabs * cap
    blocks = volume.shape[0]
    local_bits = bits_of(blocks)
    kind_count = kernels.shape[0]
    rows = entries // LANES
    int_rows = jax.ShapeDtypeStruct((rows, LANES), jnp.int32)

    target, word, totals = pl.pallas_call(
        functools.partial(route_kernel, slabs, cap, local_bits),
        out_shape=(int_rows, int_rows, jax.ShapeDtypeStruct((slabs, LANES), jnp.int32)),
        in_specs=[VMEM_SPEC, VMEM_SPEC, VMEM_SPEC, SMEM_SPEC],
        out_specs=(VMEM_SPEC, VMEM_SPEC, VMEM_SPEC),
        compiler_params=params(56),
        name="route",
    )(owners.reshape(rows, LANES), local_block, kinds, counts)
    target, word = target.reshape(entries), word.reshape(entries)
    tiles = [cap * 5 // 8, cap * 3 // 8] if cap >= 2048 else [cap]
    parts = len(tiles)
    code = ctf_code | ((scales.astype(jnp.float32) * 256.0).astype(jnp.int32) << 8)
    stride = cap + LANES
    meta, *packed = pl.pallas_call(
        functools.partial(pack_kernel, slabs, cap, list_length),
        out_shape=(jax.ShapeDtypeStruct((slabs * stride,), jnp.int32),)
        + tuple(jax.ShapeDtypeStruct((slabs, tile, features), jnp.bfloat16) for tile in tiles),
        in_specs=[SMEM_SPEC] * 5 + [VMEM_SPEC],
        out_specs=(SMEM_SPEC,) + (ANY_SPEC,) * parts,
        scratch_shapes=[
            pltpu.VMEM((entries, features), jnp.float32),
            pltpu.VMEM((slabs * stride, features), jnp.float32),
            pltpu.VMEM((slots, features), jnp.bfloat16),
            pltpu.SemaphoreType.DMA(()),
        ],
        compiler_params=params(56),
        name="pack",
    )(target, word, counts, totals, code, images.reshape(entries, features))
    arrived = lax.all_to_all(
        meta.reshape(slabs, stride), "slab", split_axis=0, concat_axis=0, tiled=True
    )
    words = arrived[:, :cap]
    totals_in = arrived[:, cap]
    codes_in = arrived[:, cap + 1:cap + 1 + particles]
    live = (jnp.arange(cap, dtype=jnp.int32)[None, :] < totals_in[:, None]).astype(jnp.int32)
    table_rows = ctf_table[(codes_in & 255).reshape(-1)]
    scale_in = (codes_in >> 8).astype(jnp.float32).reshape(-1) * (1.0 / 256.0)

    index = pl.pallas_call(
        functools.partial(decode_kernel, local_bits, blocks),
        out_shape=jax.ShapeDtypeStruct((slots // LANES + 8, LANES), jnp.int32),
        in_specs=[VMEM_SPEC, VMEM_SPEC],
        out_specs=VMEM_SPEC,
        compiler_params=params(56),
        name="decode",
    )(words.reshape(slots // LANES, LANES), live.reshape(slots // LANES, LANES))
    index = index.reshape(slots + 8 * LANES)
    voxels = list(pl.pallas_call(
        functools.partial(gather_kernel, slabs, cap),
        out_shape=tuple(
            jax.ShapeDtypeStruct((slabs, tile, features), jnp.bfloat16) for tile in tiles
        ),
        in_specs=[SMEM_SPEC, SMEM_SPEC, VMEM_SPEC],
        out_specs=(VMEM_SPEC,) * parts,
        scratch_shapes=[
            pltpu.VMEM((blocks + 8, features), jnp.float32),
            pltpu.VMEM((cap, features), jnp.float32),
        ],
        compiler_params=params(56),
        cost_estimate=pl.CostEstimate(flops=0, bytes_accessed=100 * MIB, transcendentals=0),
        name="read_voxels",
    )(index, totals_in, volume))

    forward = jnp.transpose(kernels, (2, 0, 1)).reshape(features, kind_count * features)
    backward = kernels.reshape(kind_count, 2, 8, 8, features).transpose(3, 1, 2, 0, 4)
    backward = backward.reshape(features, kind_count * features)
    core = lax.axis_index("dom").astype(jnp.int32).reshape(1)
    plane_blocks = (side // 8) ** 2
    pieces = [planes * plane_blocks for planes in pieces_of(side // slabs // 2)]
    squares, sums, behind, offset = 0.0, None, [voxels[0]], 0
    for part, tile in enumerate(tiles):
        first, last = part == 0, part == parts - 1
        if not first:
            packed[part], earlier = lax.optimization_barrier((packed[part], behind[part - 1]))
            if part == 1:
                voxels[0] = earlier
        picture = lax.all_to_all(packed[part], "slab", split_axis=0, concat_axis=0, tiled=True)
        lengths = [blocks // 2] + pieces if last else []
        arguments = [
            totals_in, table_rows[:, 0], table_rows[:, 1], scale_in, index, core,
            words[:, offset:offset + tile].reshape(slabs, 1, tile), voxels[part], picture,
            forward, backward,
        ]
        aliases = {}
        if not first:
            aliases = {len(arguments): 1}
            arguments.append(pltpu.with_memory_space_constraint(sums, pltpu.VMEM))
        more, sums, *halves = pl.pallas_call(
            functools.partial(
                slab_kernel, side, local_bits, list_length, particles, cap, offset, first, last
            ),
            out_shape=(
                jax.ShapeDtypeStruct((slabs, particles, LANES), jnp.float32),
                pltpu.VMEM((blocks + 8, features), jnp.float32),
            )
            + tuple(jax.ShapeDtypeStruct((length, features), jnp.float32) for length in lengths),
            in_specs=[SMEM_SPEC] * 6 + [VMEM_SPEC] * (len(arguments) - 6),
            out_specs=(VMEM_SPEC, VMEM_SPEC) + (ANY_SPEC,) * len(lengths),
            scratch_shapes=[
                pltpu.VMEM((PAIR * min(tile, STEP), features), jnp.float32),
                pltpu.SMEM((slabs * tile // min(tile, STEP) + 1,), jnp.int32),
                pltpu.SemaphoreType.DMA((max(1, len(lengths)),)),
            ],
            input_output_aliases=aliases,
            compiler_params=params(24),
            cost_estimate=pl.CostEstimate(flops=0, bytes_accessed=16 * MIB, transcendentals=0),
            name="compare_and_add",
        )(*arguments)
        squares = squares + more
        behind.append(more)
        offset += tile
    mine, *theirs = halves
    partial_sums = jnp.sum(squares, axis=2)
    return mine, theirs, partial_sums, side


def body(*arrays):
    mine, theirs, partial_sums, side = gradient_of_slab(*arrays)
    field, squares = to_field(mine, theirs, partial_sums, side)
    counts = arrays[6]
    return field, squares / (counts.astype(jnp.float32) * 128.0)


def solution(mesh):
    in_specs = (
        P(("groups", "slab"), None),
        P(),
        P(("groups", "slab", "dom"), None, None),
        P(("groups", "slab", "dom"), None, None),
        P(("groups", "slab", "dom"), None),
        P(("groups", "slab", "dom"), None),
        P(("groups", "slab", "dom")),
        P(("groups", "slab", "dom")),
        P(),
        P(("groups", "slab", "dom")),
    )
    out_specs = (P(None, ("groups", "dom"), "slab", None), P(("groups", "slab", "dom")))
    return jax.shard_map(body, mesh=mesh, in_specs=in_specs, out_specs=out_specs, check_vma=False)
```

```python
import functools
import math

import jax
import jax.numpy as jnp
import numpy as np
from jax import lax
from jax.experimental import pallas as pl
from jax.experimental.pallas import tpu as pltpu
from jax.sharding import PartitionSpec as P

LANES = 128
GROUP = 16
UNUSED = 100
STEP = 256
PAIR = 2
MIB = 1024 * 1024

SMEM_SPEC = pl.BlockSpec(memory_space=pltpu.SMEM)
VMEM_SPEC = pl.BlockSpec(memory_space=pltpu.VMEM)
ANY_SPEC = pl.BlockSpec(memory_space=pl.ANY)


def params(mib):
    return pltpu.CompilerParams(vmem_limit_bytes=mib * MIB)


def bits_of(count):
    return (count - 1).bit_length()


def route_kernel(slabs, cap, local_bits, owner_ref, local_ref, kind_ref, counts_ref, target_ref, word_ref, totals_ref):
    particles, list_length = local_ref.shape
    rows_each = list_length // LANES
    rows = particles * rows_each
    gathered = lambda ref: jnp.concatenate(
        [ref[:, j * LANES:(j + 1) * LANES] for j in range(rows_each)], axis=0
    )
    row_id = lax.broadcasted_iota(jnp.int32, (rows, LANES), 0)
    lane_id = lax.broadcasted_iota(jnp.int32, (rows, LANES), 1)
    particle = row_id % particles
    position = (row_id // particles) * LANES + lane_id
    limit = jnp.zeros((rows, LANES), jnp.int32)
    for i in range(particles):
        limit = jnp.where(particle == i, counts_ref[i], limit)
    owner = jnp.concatenate(
        [owner_ref[pl.ds(j, particles, stride=rows_each), :] for j in range(rows_each)], axis=0
    )
    owner = jnp.where(position < limit, owner, -1)
    up_to = (
        lax.broadcasted_iota(jnp.int32, (LANES, LANES), 0)
        <= lax.broadcasted_iota(jnp.int32, (LANES, LANES), 1)
    ).astype(jnp.bfloat16)
    ones = jnp.ones((LANES, LANES), jnp.bfloat16)
    before = (
        lax.broadcasted_iota(jnp.int32, (rows, rows), 1)
        < lax.broadcasted_iota(jnp.int32, (rows, rows), 0)
    ).astype(jnp.bfloat16)

    def one_slab(slab, target):
        mine = owner == slab
        hits = mine.astype(jnp.float32).astype(jnp.bfloat16)
        inside = jnp.dot(hits, up_to, preferred_element_type=jnp.float32)
        row_sum = jnp.dot(hits, ones, preferred_element_type=jnp.float32)
        above = jnp.dot(before, row_sum.astype(jnp.bfloat16), preferred_element_type=jnp.float32)
        rank = (inside + above).astype(jnp.int32) - 1
        total = (above[rows - 1:rows, :] + row_sum[rows - 1:rows, :]).astype(jnp.int32)
        totals_ref[pl.ds(slab, 1), :] = total
        return jnp.where(mine, slab * (cap + LANES) + rank, target)

    target = lax.fori_loop(0, slabs, one_slab, jnp.full((rows, LANES), cap + UNUSED, jnp.int32))
    target_ref[...] = target
    kind_bits = local_bits
    word = gathered(local_ref) | (gathered(kind_ref) << kind_bits) | (position << (kind_bits + 2))
    word_ref[...] = word | (particle << (kind_bits + 2 + bits_of(list_length)))


def pack_kernel(slabs, cap, list_length, target_ref, word_ref, counts_ref, totals_ref, code_ref, image_ref, meta_ref, *refs):
    out_refs, (wide_ref, staged_ref, narrow_ref, sem) = refs[:-4], refs[-4:]
    particles = counts_ref.shape[0]
    stride = cap + LANES
    step = 256
    turn = 32

    @pl.loop(0, image_ref.shape[0] // step)
    def _(i):
        at = pl.multiple_of(i * step, step)
        wide_ref[pl.ds(at, step), :] = image_ref[pl.ds(at, step), :].astype(jnp.float32)

    @pl.loop(0, particles)
    def _(particle):
        @pl.loop(0, (counts_ref[particle] + turn - 1) // turn)
        def _(i):
            per_row = LANES // turn
            first = (i // per_row) * (particles * LANES) + particle * LANES + (i % per_row) * turn
            row = particle * list_length + i * turn
            targets = [target_ref[first + j] for j in range(turn)]
            words = [word_ref[first + j] for j in range(turn)]
            rows = [wide_ref[pl.ds(row + j, 1), :] for j in range(turn)]
            for j in range(turn):
                staged_ref[pl.ds(targets[j], 1), :] = rows[j]
                meta_ref[targets[j]] = words[j]

    @pl.loop(0, slabs)
    def _(slab):
        header = slab * stride + cap
        meta_ref[header] = totals_ref[slab, 0]
        for j in range(particles):
            meta_ref[header + 1 + j] = code_ref[j]

    def blocks_of(act):
        offset = 0
        for out_ref in out_refs:
            width = out_ref.shape[1]

            @pl.loop(0, slabs)
            def _(slab, offset=offset, width=width, out_ref=out_ref):
                live = jnp.clip(totals_ref[slab, 0] - offset, 0, width)

                @pl.loop(0, (live + LANES - 1) // LANES)
                def _(i):
                    at = pl.multiple_of(slab * cap + offset + i * LANES, LANES)
                    to = pl.multiple_of(i * LANES, LANES)
                    copy = pltpu.make_async_copy(
                        narrow_ref.at[pl.ds(at, LANES)], out_ref.at[slab, pl.ds(to, LANES)], sem
                    )
                    act(copy, at, pl.multiple_of(at + slab * LANES, LANES))

            offset += width

    def convert_and_start(copy, at, staged_at):
        narrow_ref[pl.ds(at, LANES), :] = staged_ref[pl.ds(staged_at, LANES), :].astype(jnp.bfloat16)
        copy.start()

    blocks_of(convert_and_start)
    blocks_of(lambda copy, at, staged_at: copy.wait())


def decode_kernel(local_bits, dummy, word_ref, live_ref, index_ref):
    rows = word_ref.shape[0]
    live = live_ref[...] != 0
    index = jnp.where(live, word_ref[...] & ((1 << local_bits) - 1), dummy)
    lane = lax.broadcasted_iota(jnp.int32, (rows, LANES), 1)
    clash = jnp.zeros((rows, LANES), jnp.int32)
    for shift in range(1, GROUP):
        earlier = pltpu.roll(index, shift, 1)
        same = (earlier == index) & (lane % GROUP >= shift) & live
        clash = clash | same.astype(jnp.int32)
    shift = 1
    while shift < LANES:
        if shift == GROUP:
            index = index | jnp.where(lane % GROUP == 0, clash << 24, 0)
        clash = clash | pltpu.roll(clash, LANES - shift, 1)
        shift *= 2
    index_ref[0:rows, :] = index | jnp.where(lane == 0, clash << 25, 0)
    index_ref[rows:, :] = jnp.full((index_ref.shape[0] - rows, LANES), dummy, jnp.int32)


def gather_kernel(slabs, cap, index_ref, totals_ref, volume_ref, *refs):
    out_refs, (wide_ref, staged_ref) = refs[:-2], refs[-2:]
    blocks = volume_ref.shape[0]
    step = 256

    @pl.loop(0, blocks // step)
    def _(i):
        at = pl.multiple_of(i * step, step)
        wide_ref[pl.ds(at, step), :] = volume_ref[pl.ds(at, step), :].astype(jnp.float32)

    @pl.loop(0, slabs)
    def _(source):
        live = totals_ref[source]

        @pl.loop(0, (live + 15) // 16)
        def _(i):
            first = source * cap + i * 16
            places = [index_ref[first] & 0xFFFFFF] + [index_ref[first + j] for j in range(1, 16)]
            rows = [wide_ref[pl.ds(places[j], 1), :] for j in range(16)]
            for j in range(16):
                staged_ref[pl.ds(i * 16 + j, 1), :] = rows[j]

        offset = 0
        for out_ref in out_refs:
            width = out_ref.shape[1]

            @pl.when(live > offset)
            def _(offset=offset):
                out_ref[source] = staged_ref[offset:offset + width, :].astype(jnp.bfloat16)

            offset += width


def sine(angle):
    turns = jnp.floor(angle * (1.0 / math.pi) + 0.5)
    rest = angle - turns * 3.140625
    rest = rest - turns * (math.pi - 3.140625)
    odd = turns - 2.0 * jnp.floor(turns * 0.5)
    square = rest * rest
    poly = 2.718121e-6
    poly = poly * square - 1.9839334e-4
    poly = poly * square + 8.3333293e-3
    poly = poly * square - 1.6666667e-1
    value = rest + rest * square * poly
    return value * (1.0 - 2.0 * odd)


def slab_kernel(
    side, local_bits, list_length, particles, cap, offset, first, last,
    totals_ref, defocus_ref, phase_ref, scale_ref, index_ref, core_ref,
    word_ref, voxel_ref, image_ref, forward_ref, backward_ref, *rest,
):
    if not first:
        rest = rest[1:]
    square_ref, sum_ref, out_refs, (staged_ref, steps_ref, sems) = rest[0], rest[1], rest[2:-3], rest[-3:]
    slabs, _, tile = word_ref.shape
    step = staged_ref.shape[0] // PAIR
    blocks = sum_ref.shape[0] - 8
    features = image_ref.shape[2]
    kinds = forward_ref.shape[1] // features
    position_bits = bits_of(list_length)
    per_row = side // 8
    half = features // 2

    if first:
        @pl.loop(0, blocks // 256)
        def _(i):
            at = pl.multiple_of(i * 256, 256)
            sum_ref[pl.ds(at, 256), :] = jnp.zeros((256, features), jnp.float32)

    square_ref[...] = jnp.zeros_like(square_ref)
    live_of = lambda source: jnp.clip(totals_ref[source] - offset, 0, tile)

    def list_source(source, count):
        def list_step(i, count):
            steps_ref[2 * count] = source
            steps_ref[2 * count + 1] = i * step
            return count + 1

        return lax.fori_loop(0, (live_of(source) + step - 1) // step, list_step, count)

    steps_ref[0] = 0
    steps_ref[1] = 0
    count = lax.fori_loop(0, slabs, list_source, 0)

    def compare(number, slot):
        spot = 2 * jnp.minimum(number, jnp.maximum(count - 1, 0))
        source, at = steps_ref[spot], pl.multiple_of(steps_ref[spot + 1], step)
        live = jnp.where(number < count, live_of(source) - at, 0)
        word = word_ref[source, :, pl.ds(at, step)]
        kind = (word >> local_bits) & 3
        position = (word >> (local_bits + 2)) & (list_length - 1)
        particle = (word >> (local_bits + 2 + position_bits)) & (particles - 1)
        valid = lax.broadcasted_iota(jnp.int32, (1, step), 1) < live
        defocus = jnp.zeros((1, step), jnp.float32)
        phase = jnp.zeros((1, step), jnp.float32)
        scale = jnp.zeros((1, step), jnp.float32)
        for j in range(particles):
            chosen = particle == j
            defocus = jnp.where(chosen, defocus_ref[source * particles + j], defocus)
            phase = jnp.where(chosen, phase_ref[source * particles + j], phase)
            scale = jnp.where(chosen, scale_ref[source * particles + j], scale)
        defocus = defocus * (1.0 / float((side // 2) ** 2))
        cell = lax.broadcasted_iota(jnp.int32, (half, LANES), 0)
        cell_vert, cell_horiz = (cell // 8).astype(jnp.float32), (cell % 8).astype(jnp.float32)
        repeat = lambda table: jnp.concatenate([table] * (step // LANES), axis=1)
        vert = ((position // per_row) * 8 - side // 2).astype(jnp.float32) + repeat(cell_vert)
        horiz = ((position % per_row) * 8 - side // 2).astype(jnp.float32) + repeat(cell_horiz)
        factor = scale * sine(defocus * (vert * vert + horiz * horiz) + phase)
        factor = jnp.concatenate([factor, factor], axis=0)
        voxel = voxel_ref[source, pl.ds(at, step), :].astype(jnp.float32).T.astype(jnp.bfloat16)
        picture = image_ref[source, pl.ds(at, step), :].astype(jnp.float32).T

        def by_kind(value):
            none = jnp.zeros_like(value)
            return jnp.concatenate([jnp.where(kind == k, value, none) for k in range(kinds)], axis=0)

        extracted = jnp.dot(forward_ref[...], by_kind(voxel), preferred_element_type=jnp.float32)
        misfit = jnp.where(valid, factor * extracted - picture, 0.0)
        squares = jnp.sum(misfit * misfit, axis=0, keepdims=True)
        which = lax.broadcasted_iota(jnp.int32, (particles, step), 0)
        spread = jnp.where(valid & (particle == which), squares, 0.0)
        folded = spread[:, 0:LANES]
        for i in range(1, step // LANES):
            folded = folded + spread[:, i * LANES:(i + 1) * LANES]
        square_ref[source] = square_ref[source] + folded
        weighted = (factor * misfit).astype(jnp.bfloat16)
        terms = jnp.dot(backward_ref[...], by_kind(weighted), preferred_element_type=jnp.float32)
        staged_ref[slot * step:(slot + 1) * step, :] = terms.T

    def places_of(base):
        return [index_ref[base] & 0xFFFFFF] + [index_ref[base + j] for j in range(1, GROUP)]

    def add_group(base, at):
        places = places_of(base)
        held = [sum_ref[pl.ds(place, 1), :] for place in places]
        new = [staged_ref[pl.ds(at + j, 1), :] for j in range(GROUP)]
        for j in range(GROUP):
            sum_ref[pl.ds(places[j], 1), :] = held[j] + new[j]

    def base_of(number):
        spot = 2 * jnp.clip(number, 0, jnp.maximum(count - 1, 0))
        base = steps_ref[spot] * cap + offset + steps_ref[spot + 1]
        return jnp.where((number >= 0) & (number < count), base, slabs * cap)

    @pl.loop(0, (count + PAIR - 1) // PAIR + 1)
    def _(turn):
        bases = [base_of((turn - 1) * PAIR + slot) for slot in range(PAIR)]
        marks = 0
        for base in bases:
            for i in range(step // LANES):
                marks = marks | index_ref[base + i * LANES]

        @pl.when(marks < (1 << 25))
        def _():
            for slot, base in enumerate(bases):
                for g in range(step // GROUP):
                    add_group(base + g * GROUP, slot * step + g * GROUP)
            for slot in range(PAIR):
                compare(turn * PAIR + slot, slot)

        @pl.when(marks >= (1 << 25))
        def _():
            for slot, base in enumerate(bases):
                @pl.loop(0, step // GROUP)
                def _(g, slot=slot, base=base):
                    start = base + g * GROUP
                    at = slot * step + g * GROUP
                    clashes = (index_ref[start] >> 24) & 1

                    @pl.when(clashes == 0)
                    def _():
                        add_group(start, at)

                    @pl.when(clashes == 1)
                    def _():
                        places = places_of(start)
                        for j in range(GROUP):
                            sum_ref[pl.ds(places[j], 1), :] = (
                                sum_ref[pl.ds(places[j], 1), :] + staged_ref[pl.ds(at + j, 1), :]
                            )

            for slot in range(PAIR):
                compare(turn * PAIR + slot, slot)

    if last:
        half = blocks // 2
        start = (1 - core_ref[0]) * half
        places = [core_ref[0] * half]
        for out_ref in out_refs[1:]:
            places.append(start)
            start = start + out_ref.shape[0]
        copies = []
        for i, (place, out_ref) in enumerate(zip(places, out_refs)):
            length = out_ref.shape[0]
            at = pl.multiple_of(place, 8)
            copies.append(pltpu.make_async_copy(sum_ref.at[pl.ds(at, length)], out_ref, sems.at[i]))
        for copy in copies:
            copy.start()
        for copy in copies:
            copy.wait()


def pieces_of(planes):
    if planes < 16:
        return [planes]
    return [4, planes - 4]


def rotated(value, turn, length, sign=None):
    real, imag = value
    if turn == 0 or 4 * turn == length:
        if turn:
            real, imag = -imag, real
        return (real, imag) if sign is None else (real * sign, imag * sign)
    if sign is None and 8 * turn in (length, 3 * length):
        root = math.sqrt(0.5)
        if 8 * turn == length:
            return ((real - imag) * root, (real + imag) * root)
        return ((real + imag) * -root, (real - imag) * root)
    cos, sin = math.cos(2 * math.pi * turn / length), math.sin(2 * math.pi * turn / length)
    if sign is not None:
        cos, sin = cos * sign, sin * sign
    return (real * cos - imag * sin, real * sin + imag * cos)


def small_dft(values):
    length = len(values)
    if length == 1:
        return values
    even, odd = small_dft(values[0::2]), small_dft(values[1::2])
    low, high = [], []
    for k in range(length // 2):
        turned = rotated(odd[k], k, length)
        low.append((even[k][0] + turned[0], even[k][1] + turned[1]))
        high.append((even[k][0] - turned[0], even[k][1] - turned[1]))
    return low + high


def swap_quarters(values):
    lane = lax.broadcasted_iota(jnp.int32, values[0].shape, 1)
    low, even = lane < 64, (lane // 32) % 2 == 0
    roll = lambda value, shift: pltpu.roll(value, shift, 1)
    for first, second, shift, keep in ((0, 2, 64, low), (1, 3, 64, low), (0, 1, 32, even), (2, 3, 32, even)):
        one, two = values[first], values[second]
        values[first] = jnp.where(keep, one, roll(two, shift))
        values[second] = jnp.where(keep, roll(one, LANES - shift), two)
    return values


def in_halves(value):
    high = value.astype(jnp.bfloat16)
    return high, (value - high.astype(jnp.float32)).astype(jnp.bfloat16)


def planes_kernel(mine_ref, theirs_ref, zblock_ref, turn_ref, wide_ref, fine_ref, out_ref, high_ref, low_ref):
    step = pl.program_id(1)
    count = mine_ref.shape[1]
    groups, side = out_ref.shape[0], out_ref.shape[4]
    height = side // groups

    @pl.loop(0, count, unroll=8)
    def _(i):
        block = (mine_ref[:, i] + theirs_ref[:, i]).reshape(LANES, LANES)
        high, low = in_halves(block.T)
        both = jnp.dot(
            jnp.concatenate([high, low, high], axis=1), zblock_ref[...],
            preferred_element_type=jnp.float32,
        )
        by_cos = both[:, :LANES].reshape(8, 2, 8, LANES)
        by_sin = both[:, LANES:].reshape(8, 2, 8, LANES)
        real = by_cos[:, 0] - by_sin[:, 1]
        imag = by_sin[:, 0] + by_cos[:, 1]
        values = []
        for z in range(8):
            cos, sin = turn_ref[0, z:z + 1, :], turn_ref[1, z:z + 1, :]
            values.append((real[z] * cos - imag[z] * sin, real[z] * sin + imag[z] * cos))
        values = [jnp.concatenate(value, axis=0) for value in small_dft(values)]
        at = pl.ds(pl.multiple_of((step * count + i) * 16, 16), 16)
        for half in range(2):
            planes = swap_quarters(values[4 * half:4 * half + 4])
            for x in range(4):
                columns = slice((2 * x + half) * LANES, (2 * x + half + 1) * LANES)
                high, low = in_halves(planes[x])
                high_ref[at, columns] = high
                low_ref[at, columns] = low

    @pl.when(step == pl.num_programs(1) - 1)
    def _():
        @pl.loop(0, 4)
        def _(x):
            columns = pl.ds(pl.multiple_of(x * side, side), side)
            product = functools.partial(jnp.dot, preferred_element_type=jnp.float32)
            high = high_ref[:, columns]
            result = product(wide_ref[...], high) + (
                product(wide_ref[...], low_ref[:, columns]) + product(fine_ref[...], high)
            )
            for part in range(2):
                for group in range(groups):
                    start = part * side + group * height
                    out_ref[group, x, part] = result[start:start + height, :].astype(jnp.bfloat16)


def first_dimension_kernel(slabs, each, core_ref, *refs):
    arrays, (out_ref, mid_ref) = refs[:-2], refs[-2:]
    chunks = len(arrays) // 2
    own, other = arrays[:chunks], arrays[chunks:]
    spots = [(i, at) for i, ref in enumerate(own) for at in range(ref.shape[1])]
    core = core_ref[0]
    is_first = core == 0
    sign = (1 - 2 * core).astype(jnp.float32)

    rows = out_ref.shape[2]
    strips = [slice(at, min(at + 8, rows)) for at in range(0, rows, 8)]

    def plane(x, strip):
        slab, rest = x // (2 * each), x % (2 * each)
        half, inner = rest // each, rest % each
        chunk, at = spots[inner]
        loaded = []
        for part in range(2):
            here, there = own[chunk][slab, at, part], other[chunk][slab, at, part]
            value = jnp.where(is_first, here, there) if half == 0 else jnp.where(is_first, there, here)
            loaded.append(value.astype(jnp.float32)[strip])
        return tuple(loaded)

    for low in range(16):
        for strip in strips:
            values = small_dft([plane(low + 16 * high, strip) for high in range(16)])
            for k in range(16):
                real, imag = rotated(values[k], low * k, 256, sign if low % 2 else None)
                mid_ref[k, low, 0, strip] = real
                mid_ref[k, low, 1, strip] = imag

    @pl.loop(0, 16)
    def _(k):
        for strip in strips:
            values = [(mid_ref[k, low, 0, strip], mid_ref[k, low, 1, strip]) for low in range(16)]
            even, odd = small_dft(values[0::2]), small_dft(values[1::2])
            for m in range(8):
                turned = rotated(odd[m], m, 16)
                out_ref[0, k + 16 * m, strip] = even[m][0] + turned[0]
                out_ref[1, k + 16 * m, strip] = even[m][1] + turned[1]


def host_halves(table):
    high = table.astype(jnp.bfloat16)
    return high, (table - high.astype(np.float64)).astype(jnp.bfloat16)


def transform_tables(side):
    per_row = side // 8
    grid = np.arange(per_row)
    angle = 2 * np.pi * np.outer(grid, grid) / per_row
    zblock = np.concatenate([np.kron(np.eye(4), np.cos(angle)), np.kron(np.eye(4), np.sin(angle))], axis=1)
    high, low = host_halves(zblock)
    zblock = np.concatenate([high, high, low], axis=0)
    angle = 2 * np.pi * np.outer(np.arange(8), grid) / side
    turns = np.stack([np.tile(np.cos(angle), (1, 4)), np.tile(np.sin(angle), (1, 4))]).astype(np.float32)
    cells = np.arange(side)
    angle = 2 * np.pi * (np.outer(cells, cells) % side) / side
    cos, sin = np.cos(angle).reshape(side, per_row, 1, 8), np.sin(angle).reshape(side, per_row, 1, 8)
    matrix = np.concatenate(
        [np.concatenate([cos, -sin], axis=2), np.concatenate([sin, cos], axis=2)], axis=0
    ).reshape(2 * side, 2 * side) / float(side) ** 1.5
    return (zblock, turns) + host_halves(matrix)


def sum_over_slabs(partial_sums):
    slabs = partial_sums.shape[0]
    if slabs <= 8:
        me = lax.axis_index("slab")
        row = lambda i: lax.dynamic_index_in_dim(partial_sums, me ^ i, axis=0, keepdims=True)
        returned = [row(0)] + [
            lax.ppermute(row(i), "slab", [(slab, slab ^ i) for slab in range(slabs)])
            for i in range(1, slabs)
        ]
        returned = jnp.concatenate(returned)
    else:
        returned = lax.all_to_all(partial_sums, "slab", split_axis=0, concat_axis=0, tiled=True)
    return jnp.sum(returned, axis=0)


def to_field(mine, theirs_sent, partial_sums, side):
    slabs = lax.axis_size("slab")
    per_row = side // 8
    each = side // slabs // 2
    height = side // slabs
    groups = slabs if height % 16 == 0 else 1
    tables = [jnp.asarray(table) for table in transform_tables(side)]
    swap = [(0, 1), (1, 0)]
    theirs = [lax.ppermute(chunk, "dom", swap) for chunk in theirs_sent]
    grid_shape = (-1, per_row, per_row, LANES)
    mine = mine.reshape(grid_shape)
    short = max(0, 4 - each)
    if short:
        mine = jnp.pad(mine, ((0, short), (0, 0), (0, 0), (0, 0)))
    yblocks = 8
    own = []
    first_quad = 0
    before = []
    for real_planes, added in zip(pieces_of(each), theirs):
        if before:
            added, before[0] = lax.optimization_barrier((added, before[0]))
        added = added.reshape(grid_shape)
        if short:
            added = jnp.pad(added, ((0, short), (0, 0), (0, 0), (0, 0)))
        held = real_planes + short
        quads = held // 4
        whole = lambda table: pl.BlockSpec(table.shape, lambda q, y: (0,) * table.ndim)
        sent = pl.pallas_call(
            planes_kernel,
            grid=(quads, per_row // yblocks),
            out_shape=jax.ShapeDtypeStruct((groups, held, 2, side // groups, side), jnp.bfloat16),
            in_specs=[
                pl.BlockSpec((4, yblocks, per_row, LANES), lambda q, y, at=first_quad: (at + q, y, 0, 0)),
                pl.BlockSpec((4, yblocks, per_row, LANES), lambda q, y: (q, y, 0, 0)),
            ] + [whole(table) for table in tables],
            out_specs=pl.BlockSpec((groups, 4, 2, side // groups, side), lambda q, y: (0, q, 0, 0, 0)),
            scratch_shapes=[
                pltpu.VMEM((2 * side, 4 * side), jnp.bfloat16),
                pltpu.VMEM((2 * side, 4 * side), jnp.bfloat16),
            ],
            compiler_params=params(56),
            cost_estimate=pl.CostEstimate(
                flops=held * 8 * side**3, bytes_accessed=held * 4 * side**2 * 8, transcendentals=0
            ),
            name="transform_planes",
        )(mine, added, *tables)
        if groups != slabs:
            sent = sent.reshape(-1, 2, slabs, height, side).transpose(2, 0, 1, 3, 4)[:, :real_planes]
        first_quad += quads
        if before:
            sent, own[-1] = lax.optimization_barrier((sent, own[-1]))
        if first_quad * 4 >= each:
            sent, partial_sums = lax.optimization_barrier((sent, partial_sums))
        before = [sent]
        got = lax.all_to_all(sent, "slab", split_axis=0, concat_axis=0, tiled=True)
        own.append(got)
    other = [lax.ppermute(got, "dom", swap) for got in own[:-1]]
    own[-1], losses, *other = lax.optimization_barrier((own[-1], sum_over_slabs(partial_sums), *other))
    other.append(lax.ppermute(own[-1], "dom", swap))
    rows = min(16, height)
    arrays = own + other
    field = pl.pallas_call(
        functools.partial(first_dimension_kernel, slabs, each),
        grid=(height // rows, side // LANES),
        out_shape=jax.ShapeDtypeStruct((2, side // 2, height, side), jnp.float32),
        in_specs=[SMEM_SPEC] + [
            pl.BlockSpec(array.shape[:3] + (rows, LANES), lambda y, z: (0, 0, 0, y, z))
            for array in arrays
        ],
        out_specs=pl.BlockSpec((2, side // 2, rows, LANES), lambda y, z: (0, 0, y, z)),
        scratch_shapes=[pltpu.VMEM((16, 16, 2, rows, LANES), jnp.float32)],
        compiler_params=params(28),
        name="transform_first",
    )(lax.axis_index("dom").astype(jnp.int32).reshape(1), *arrays)
    return field, losses


def gradient_of_slab(volume, kernels, images, owners, local_block, kinds, counts, ctf_code, ctf_table, scales):
    slabs = lax.axis_size("slab")
    particles, list_length, features = images.shape
    side = math.isqrt(list_length * 64)
    entries = particles * list_length
    cap = 2 * entries // slabs
    slots = slabs * cap
    blocks = volume.shape[0]
    local_bits = bits_of(blocks)
    kind_count = kernels.shape[0]
    rows = entries // LANES
    int_rows = jax.ShapeDtypeStruct((rows, LANES), jnp.int32)

    target, word, totals = pl.pallas_call(
        functools.partial(route_kernel, slabs, cap, local_bits),
        out_shape=(int_rows, int_rows, jax.ShapeDtypeStruct((slabs, LANES), jnp.int32)),
        in_specs=[VMEM_SPEC, VMEM_SPEC, VMEM_SPEC, SMEM_SPEC],
        out_specs=(VMEM_SPEC, VMEM_SPEC, VMEM_SPEC),
        compiler_params=params(56),
        name="route",
    )(owners.reshape(rows, LANES), local_block, kinds, counts)
    target, word = target.reshape(entries), word.reshape(entries)
    tiles = [cap * 5 // 8, cap * 3 // 8] if cap >= 2048 else [cap]
    parts = len(tiles)
    code = ctf_code | ((scales.astype(jnp.float32) * 256.0).astype(jnp.int32) << 8)
    stride = cap + LANES
    meta, *packed = pl.pallas_call(
        functools.partial(pack_kernel, slabs, cap, list_length),
        out_shape=(jax.ShapeDtypeStruct((slabs * stride,), jnp.int32),)
        + tuple(jax.ShapeDtypeStruct((slabs, tile, features), jnp.bfloat16) for tile in tiles),
        in_specs=[SMEM_SPEC] * 5 + [VMEM_SPEC],
        out_specs=(SMEM_SPEC,) + (ANY_SPEC,) * parts,
        scratch_shapes=[
            pltpu.VMEM((entries, features), jnp.float32),
            pltpu.VMEM((slabs * stride, features), jnp.float32),
            pltpu.VMEM((slots, features), jnp.bfloat16),
            pltpu.SemaphoreType.DMA(()),
        ],
        compiler_params=params(56),
        name="pack",
    )(target, word, counts, totals, code, images.reshape(entries, features))
    arrived = lax.all_to_all(
        meta.reshape(slabs, stride), "slab", split_axis=0, concat_axis=0, tiled=True
    )
    words = arrived[:, :cap]
    totals_in = arrived[:, cap]
    codes_in = arrived[:, cap + 1:cap + 1 + particles]
    live = (jnp.arange(cap, dtype=jnp.int32)[None, :] < totals_in[:, None]).astype(jnp.int32)
    table_rows = ctf_table[(codes_in & 255).reshape(-1)]
    scale_in = (codes_in >> 8).astype(jnp.float32).reshape(-1) * (1.0 / 256.0)

    index = pl.pallas_call(
        functools.partial(decode_kernel, local_bits, blocks),
        out_shape=jax.ShapeDtypeStruct((slots // LANES + 8, LANES), jnp.int32),
        in_specs=[VMEM_SPEC, VMEM_SPEC],
        out_specs=VMEM_SPEC,
        compiler_params=params(56),
        name="decode",
    )(words.reshape(slots // LANES, LANES), live.reshape(slots // LANES, LANES))
    index = index.reshape(slots + 8 * LANES)
    voxels = list(pl.pallas_call(
        functools.partial(gather_kernel, slabs, cap),
        out_shape=tuple(
            jax.ShapeDtypeStruct((slabs, tile, features), jnp.bfloat16) for tile in tiles
        ),
        in_specs=[SMEM_SPEC, SMEM_SPEC, VMEM_SPEC],
        out_specs=(VMEM_SPEC,) * parts,
        scratch_shapes=[
            pltpu.VMEM((blocks + 8, features), jnp.float32),
            pltpu.VMEM((cap, features), jnp.float32),
        ],
        compiler_params=params(56),
        cost_estimate=pl.CostEstimate(flops=0, bytes_accessed=100 * MIB, transcendentals=0),
        name="read_voxels",
    )(index, totals_in, volume))

    forward = jnp.transpose(kernels, (2, 0, 1)).reshape(features, kind_count * features)
    backward = kernels.reshape(kind_count, 2, 8, 8, features).transpose(3, 1, 2, 0, 4)
    backward = backward.reshape(features, kind_count * features)
    core = lax.axis_index("dom").astype(jnp.int32).reshape(1)
    plane_blocks = (side // 8) ** 2
    pieces = [planes * plane_blocks for planes in pieces_of(side // slabs // 2)]
    squares, sums, behind, offset = 0.0, None, [voxels[0]], 0
    for part, tile in enumerate(tiles):
        first, last = part == 0, part == parts - 1
        if not first:
            packed[part], earlier = lax.optimization_barrier((packed[part], behind[part - 1]))
            if part == 1:
                voxels[0] = earlier
        picture = lax.all_to_all(packed[part], "slab", split_axis=0, concat_axis=0, tiled=True)
        lengths = [blocks // 2] + pieces if last else []
        arguments = [
            totals_in, table_rows[:, 0], table_rows[:, 1], scale_in, index, core,
            words[:, offset:offset + tile].reshape(slabs, 1, tile), voxels[part], picture,
            forward, backward,
        ]
        aliases = {}
        if not first:
            aliases = {len(arguments): 1}
            arguments.append(pltpu.with_memory_space_constraint(sums, pltpu.VMEM))
        more, sums, *halves = pl.pallas_call(
            functools.partial(
                slab_kernel, side, local_bits, list_length, particles, cap, offset, first, last
            ),
            out_shape=(
                jax.ShapeDtypeStruct((slabs, particles, LANES), jnp.float32),
                pltpu.VMEM((blocks + 8, features), jnp.float32),
            )
            + tuple(jax.ShapeDtypeStruct((length, features), jnp.float32) for length in lengths),
            in_specs=[SMEM_SPEC] * 6 + [VMEM_SPEC] * (len(arguments) - 6),
            out_specs=(VMEM_SPEC, VMEM_SPEC) + (ANY_SPEC,) * len(lengths),
            scratch_shapes=[
                pltpu.VMEM((PAIR * min(tile, STEP), features), jnp.float32),
                pltpu.SMEM((2 * (slabs * tile // min(tile, STEP) + 1),), jnp.int32),
                pltpu.SemaphoreType.DMA((max(1, len(lengths)),)),
            ],
            input_output_aliases=aliases,
            compiler_params=params(24),
            cost_estimate=pl.CostEstimate(flops=0, bytes_accessed=16 * MIB, transcendentals=0),
            name="compare_and_add",
        )(*arguments)
        squares = squares + more
        behind.append(more)
        offset += tile
    mine, *theirs = halves
    partial_sums = jnp.sum(squares, axis=2)
    return mine, theirs, partial_sums, side


def body(*arrays):
    mine, theirs, partial_sums, side = gradient_of_slab(*arrays)
    field, squares = to_field(mine, theirs, partial_sums, side)
    counts = arrays[6]
    return field, squares / (counts.astype(jnp.float32) * 128.0)


def solution(mesh):
    in_specs = (
        P(("groups", "slab"), None),
        P(),
        P(("groups", "slab", "dom"), None, None),
        P(("groups", "slab", "dom"), None, None),
        P(("groups", "slab", "dom"), None),
        P(("groups", "slab", "dom"), None),
        P(("groups", "slab", "dom")),
        P(("groups", "slab", "dom")),
        P(),
        P(("groups", "slab", "dom")),
    )
    out_specs = (P(None, ("groups", "dom"), "slab", None), P(("groups", "slab", "dom")))
    return jax.shard_map(body, mesh=mesh, in_specs=in_specs, out_specs=out_specs, check_vma=False)
```
